32 devices in a mesh: ctx: 16 (over z, y, x), wa: 2 (over core).
Axes of the slice: x: 2, y: 2, z: 4, core: 2. Of those that a mesh axis runs over, the one named last changes fastest.
Arguments:
- tokens: bfloat16 [16384, 640], P('ctx'), may hold values from -6 to 6
- cotangent: bfloat16 [16384, 640], P('ctx'), may hold values from -6 to 6
- seq_ids: int32 [16384], P('ctx'), may hold values from 0 to 7, as said below
- w_query: bfloat16 [640, 1024], P(None, 'wa'), may hold values from -0.5 to 0.5
- w_keyval: bfloat16 [2, 640, 256], replicated, may hold values from -0.25 to 0.25
- w_out: bfloat16 [1024, 640], P('wa'), may hold values from -0.1875 to 0.1875
- w_gateup: bfloat16 [2, 640, 2048], P(None, None, 'wa'), may hold values from -0.25 to 0.25
- w_down: bfloat16 [2048, 640], P('wa'), may hold values from -0.125 to 0.125
- norm_gains: float32 [4, 640], replicated, may hold values from -0.5 to 0.5
- mom_query: float32 [640, 1024], P('ctx', 'wa'), may hold values from -600 to 600
- mom_keyval: float32 [2, 640, 256], P(None, 'ctx', 'wa'), may hold values from -600 to 600
- mom_out: float32 [1024, 640], P('wa', 'ctx'), may hold values from -600 to 600
- mom_gateup: float32 [2, 640, 2048], P(None, 'ctx', 'wa'), may hold values from -600 to 600
- mom_down: float32 [2048, 640], P('wa', 'ctx'), may hold values from -600 to 600
- gain_first: float32 [4, 640], P(None, 'ctx'), may hold values from -180 to 180
- gain_second: float32 [4, 640], P(None, 'ctx'), may hold values from 1000 to 10000
Outputs:
- block_out: bfloat16 [16384, 640], P('ctx')
- input_grad: float32 [16384, 640], P('ctx')
- grad_query: float32 [640, 1024], P('ctx', 'wa')
- grad_keyval: float32 [2, 640, 256], P(None, 'ctx', 'wa')
- grad_out: float32 [1024, 640], P('wa', 'ctx')
- grad_gateup: float32 [2, 640, 2048], P(None, 'ctx', 'wa')
- grad_down: float32 [2048, 640], P('wa', 'ctx')
- grad_gains: float32 [4, 640], P(None, 'ctx')
- new_mom_query: float32 [640, 1024], P('ctx', 'wa')
- new_mom_keyval: float32 [2, 640, 256], P(None, 'ctx', 'wa')
- new_mom_out: float32 [1024, 640], P('wa', 'ctx')
- new_mom_gateup: float32 [2, 640, 2048], P(None, 'ctx', 'wa')
- new_mom_down: float32 [2048, 640], P('wa', 'ctx')
- upd_query: float32 [640, 1024], P('ctx', 'wa')
- upd_keyval: float32 [2, 640, 256], P(None, 'ctx', 'wa')
- upd_out: float32 [1024, 640], P('wa', 'ctx')
- upd_gateup: float32 [2, 640, 2048], P(None, 'ctx', 'wa')
- upd_down: float32 [2048, 640], P('wa', 'ctx')
- new_gain_first: float32 [4, 640], P(None, 'ctx')
- new_gain_second: float32 [4, 640], P(None, 'ctx')
- gain_update: float32 [4, 640], P(None, 'ctx')
The draws below stay inside these ranges and needn't reach their ends.
Inputs may be any that keep to these rules, and one draw needn't show every extreme that they name: `seq_ids`: never falling along the tokens; each value marks one sequence of 1024 to 4096 tokens; the first sequence has 4096 tokens.
All inputs are finite; a program needn't handle non-finite values.
Results may differ from the reference program's by a relative error of at most 0.024.
Values may be sent and summed in bfloat16 or wider, within the bound.
A program may use at most 384 MiB of HBM per device.

```python
import math
import jax
import jax.numpy as jnp
from jax import lax

D = 640
FF = 2048
HEADS = 4
HD = 256
WINDOW = 512
SOFT_CAP = 10
SPAN = 4096
NS_STEPS = 5
TOKENS = 16384
HQ = 1024


def draw_seq_ids(key, part):
    span_count = TOKENS // SPAN
    split_key = jax.random.fold_in(key, 11)
    cut_key = jax.random.fold_in(key, 23)
    span_index = jnp.arange(span_count, dtype=jnp.int32)
    split_flag = jax.random.randint(split_key, (span_count,), 0, 2, dtype=jnp.int32)
    split_flag = jnp.where(span_index == 0, 0, jnp.where(span_index == span_count - 1, 1, split_flag))
    cut_at = SPAN // 4 + SPAN // 16 * jax.random.randint(cut_key, (span_count,), 0, 9, dtype=jnp.int32)
    inner_pos = jnp.arange(SPAN, dtype=jnp.int32)
    later_part = (inner_pos[None, :] >= cut_at[:, None]).astype(jnp.int32)
    seq_ids = 2 * span_index[:, None] + split_flag[:, None] * later_part
    return seq_ids.reshape(-1).astype(jnp.int32)


def spiked(result, key, source, target, parts, factor):
    def block_of(position):
        return (jnp.arange(result.shape[position]) // (result.shape[position] // parts)).reshape((-1,) + (1,) * (result.ndim - 1 - position))

    first = jax.random.permutation(key, parts)[block_of(target)]
    second = (block_of(target) + parts // 2) % parts
    return jnp.where((block_of(source) == first) | (block_of(source) == second), factor * result, result)


def shard_levels(rng, shape, cuts, smallest, high):
    loudness = 1.0
    for dim, shards_of in cuts:
        draws = jax.random.uniform(jax.random.fold_in(jax.random.fold_in(rng, 6), dim), (shards_of,), jnp.float32, smallest / len(cuts), high / len(cuts))
        loudness = loudness * jnp.repeat(jnp.exp(draws), shape[dim] // shards_of).reshape((-1,) + (1,) * (len(shape) - 1 - dim))
    return loudness


def centred(stream_key, extent, scale, bound, cuts=(), held_as=jnp.bfloat16):
    drawn = scale * jax.random.normal(stream_key, extent, jnp.float32)
    if cuts:
        drawn = drawn * shard_levels(stream_key, extent, cuts, -0.22, 0.18)
    return jnp.clip(drawn, -bound, bound).astype(held_as)


def bell_draw_with(rng, extent, deviation, reach, split, heavy, kind=jnp.bfloat16):
    entries = deviation * jax.random.normal(rng, extent, jnp.float32)
    if split:
        entries = entries * shard_levels(rng, extent, split, -0.22, 0.18)
    return jnp.clip(spiked(entries, jax.random.fold_in(rng, 3), *heavy), -reach, reach).astype(kind)


def setup_inputs(seed: int = 0) -> dict:
    arg_keys = jax.random.split(jax.random.key(seed), 17)
    tokens = centred(arg_keys[0], (TOKENS, D), 1.0, 6.0, ((0, 16),))
    cotangent = bell_draw_with(arg_keys[1], (TOKENS, D), 1.0, 6.0, ((0, 16),), (0, 1, 16, 2.0))
    seq_ids = draw_seq_ids(jax.random.fold_in(arg_keys[16], 71), 0)
    w_query = centred(arg_keys[3], (D, HQ), (D // 4) ** -0.5, 0.5, ((1, 2),))
    w_keyval = centred(arg_keys[4], (2, D, HD), D ** -0.5, 0.25)
    w_out = centred(arg_keys[5], (HQ, D), HQ ** -0.5, 0.1875, ((0, 2),))
    w_gateup = centred(arg_keys[6], (2, D, FF), D ** -0.5, 0.25, ((2, 2),))
    w_down = centred(arg_keys[7], (FF, D), FF ** -0.5, 0.125, ((0, 2),))
    norm_gains = jnp.clip(jax.random.uniform(arg_keys[8], (4, D), jnp.float32, -0.5, 0.5), -0.5, 0.5)
    mom_query = centred(arg_keys[9], (D, HQ), 100.0, 600.0, ((0, 16), (1, 2)), jnp.float32)
    mom_keyval = centred(arg_keys[10], (2, D, HD), 100.0, 600.0, ((1, 16), (2, 2)), jnp.float32)
    mom_out = centred(arg_keys[11], (HQ, D), 100.0, 600.0, ((0, 2), (1, 16)), jnp.float32)
    mom_gateup = centred(arg_keys[12], (2, D, FF), 100.0, 600.0, ((1, 16), (2, 2)), jnp.float32)
    mom_down = centred(arg_keys[13], (FF, D), 100.0, 600.0, ((0, 2), (1, 16)), jnp.float32)
    gain_first = centred(arg_keys[14], (4, D), 30.0, 180.0, ((1, 16),), jnp.float32)
    gain_second = jnp.clip(jnp.exp(math.log(10000.0) - 2.3025851 * jax.random.uniform(arg_keys[15], (4, D), jnp.float32) ** shard_levels(arg_keys[15], (4, D), ((1, 16),), -0.2, 0.2)), 1000.0, 10000.0)
    return dict(tokens=tokens, cotangent=cotangent, seq_ids=seq_ids, w_query=w_query, w_keyval=w_keyval, w_out=w_out, w_gateup=w_gateup, w_down=w_down, norm_gains=norm_gains, mom_query=mom_query, mom_keyval=mom_keyval, mom_out=mom_out, mom_gateup=mom_gateup, mom_down=mom_down, gain_first=gain_first, gain_second=gain_second)


EPS_NORM = 1e-06
ROPE_BASE = 10000.0
MOMENTUM = 0.95
MUON_RATE = 0.2
ADAM_ONE = 0.9
ADAM_TWO = 0.95
ADAM_EPS = 1e-08
GAIN_RATE = 0.1
QUINTIC_A = 3.4445
QUINTIC_B = -4.775
QUINTIC_C = 2.0315
MASK_FILL = -1e+30
HIGHEST_PREC = lax.Precision.HIGHEST

@jax.custom_vjp
def low(v):
    return lax.optimization_barrier(v.astype(jnp.bfloat16)).astype(jnp.float32)

@jax.custom_vjp
def low_back(v):
    return v

def low_keep(v):
    return (low(v), None)

def low_pass(kept, grad):
    return (grad,)

def back_keep(v):
    return (v, None)

def back_low(kept, grad):
    return (low(grad),)
low.defvjp(low_keep, low_pass)
low_back.defvjp(back_keep, back_low)

def rms_scale(activation, gain_row):
    return activation * lax.rsqrt(lax.optimization_barrier(jnp.mean(activation * activation, axis=-1, keepdims=True)) + EPS_NORM) * (1.0 + gain_row)

def inverse_freq():
    return jnp.power(ROPE_BASE, -2.0 * jnp.arange(HD // 2, dtype=jnp.float32) / HD)

def rotate(vectors, angles):
    half_dim = vectors.shape[-1] // 2
    cosine_tab = jnp.cos(angles)
    sine_tab = jnp.sin(angles)
    if vectors.ndim == 3:
        cosine_tab = cosine_tab[:, None, :]
        sine_tab = sine_tab[:, None, :]
    left_part = vectors[..., :half_dim]
    right_part = vectors[..., half_dim:]
    return jnp.concatenate([left_part * cosine_tab - right_part * sine_tab, right_part * cosine_tab + left_part * sine_tab], axis=-1)

def positions_of(seq_ids):
    return jnp.arange(seq_ids.shape[0], dtype=jnp.int32)

def attend_block(query_blk, key_blk, value_blk, query_pos, query_ids, key_pos, key_ids):
    raw_scores = low_back(jnp.einsum('bhd,sd->hbs', query_blk, key_blk, precision=HIGHEST_PREC))
    capped = SOFT_CAP * jnp.tanh(raw_scores / SOFT_CAP)
    pos_gap = query_pos[:, None] - key_pos[None, :]
    allowed = (query_ids[:, None] == key_ids[None, :]) & (pos_gap >= 0) & (pos_gap < WINDOW)
    masked = jnp.where(allowed[None], capped, MASK_FILL)
    probs_f = jax.nn.softmax(masked, axis=-1)
    return jnp.einsum('hbs,sd->bhd', low(probs_f), value_blk, precision=HIGHEST_PREC)

def attention(query_rot, key_rot, value_low, positions, seq_ids):
    row_count = query_rot.shape[0]
    block_rows = min(512, row_count)
    pad_keys = jnp.concatenate([jnp.zeros((WINDOW, HD), jnp.float32), key_rot])
    pad_values = jnp.concatenate([jnp.zeros((WINDOW, HD), jnp.float32), value_low])
    pad_pos = jnp.concatenate([jnp.zeros((WINDOW,), jnp.int32), positions])
    pad_ids = jnp.concatenate([jnp.full((WINDOW,), -1, jnp.int32), seq_ids])

    def one_block(block_idx):
        start_row = (block_idx * block_rows).astype(jnp.int32)
        query_blk = lax.dynamic_slice_in_dim(query_rot, start_row, block_rows, 0)
        query_pos = lax.dynamic_slice_in_dim(positions, start_row, block_rows, 0)
        query_ids = lax.dynamic_slice_in_dim(seq_ids, start_row, block_rows, 0)
        key_blk = lax.dynamic_slice_in_dim(pad_keys, start_row, block_rows + WINDOW, 0)
        value_blk = lax.dynamic_slice_in_dim(pad_values, start_row, block_rows + WINDOW, 0)
        key_pos = lax.dynamic_slice_in_dim(pad_pos, start_row, block_rows + WINDOW, 0)
        key_ids = lax.dynamic_slice_in_dim(pad_ids, start_row, block_rows + WINDOW, 0)
        return attend_block(query_blk, key_blk, value_blk, query_pos, query_ids, key_pos, key_ids)
    blocks = lax.map(jax.checkpoint(one_block), jnp.arange(row_count // block_rows, dtype=jnp.int32))
    return blocks.reshape(row_count, HEADS, HD)

def layer_forward(tok_f, query_w, keyval_w, out_w, gateup_w, down_w, gains_all, positions, seq_ids):
    row_count = tok_f.shape[0]
    angles = positions.astype(jnp.float32)[:, None] * inverse_freq()[None, :]
    normed = low(rms_scale(tok_f, gains_all[0]))
    query_proj = low_back(jnp.dot(normed, query_w, precision=HIGHEST_PREC))
    key_proj = low_back(jnp.dot(normed, keyval_w[0], precision=HIGHEST_PREC))
    value_proj = low_back(jnp.dot(normed, keyval_w[1], precision=HIGHEST_PREC))
    query_rot = low(rotate(query_proj.reshape(row_count, HEADS, HD), angles) * HD ** (-0.5))
    key_rot = low(rotate(key_proj, angles))
    value_low = low(value_proj)
    attended = attention(query_rot, key_rot, value_low, positions, seq_ids)
    attended = low(low_back(attended.reshape(row_count, HEADS * HD)))
    attn_proj = low_back(jnp.dot(attended, out_w, precision=HIGHEST_PREC))
    hidden_one = tok_f + rms_scale(attn_proj, gains_all[1])
    ffn_in = low(rms_scale(hidden_one, gains_all[2]))
    gate_pre = low_back(jnp.dot(ffn_in, gateup_w[0], precision=HIGHEST_PREC))
    up_proj = low_back(jnp.dot(ffn_in, gateup_w[1], precision=HIGHEST_PREC))
    inner_act = low(jax.nn.gelu(gate_pre, approximate=True) * up_proj)
    down_proj = low_back(jnp.dot(inner_act, down_w, precision=HIGHEST_PREC))
    return hidden_one + rms_scale(down_proj, gains_all[3])

def orthogonalize(matrix):
    flipped = matrix.shape[0] > matrix.shape[1]
    iterate = matrix.T if flipped else matrix
    iterate = iterate / (jnp.sqrt(jnp.sum(iterate * iterate)) + 1e-07)
    for sweep in range(NS_STEPS):
        gram_mat = jnp.dot(iterate, iterate.T, precision=HIGHEST_PREC)
        poly_mat = QUINTIC_B * gram_mat + QUINTIC_C * jnp.dot(gram_mat, gram_mat, precision=HIGHEST_PREC)
        iterate = QUINTIC_A * iterate + jnp.dot(poly_mat, iterate, precision=HIGHEST_PREC)
    return iterate.T if flipped else iterate

def muon_update(matrix):
    return -MUON_RATE * 0.2 * math.sqrt(max(matrix.shape[0], matrix.shape[1])) * orthogonalize(matrix)

def reference(tokens, cotangent, seq_ids, w_query, w_keyval, w_out, w_gateup, w_down, norm_gains, mom_query, mom_keyval, mom_out, mom_gateup, mom_down, gain_first, gain_second):
    positions = positions_of(seq_ids)

    def forward_fn(tok_f, query_w, keyval_w, out_w, gateup_w, down_w, gains_all):
        return layer_forward(tok_f, query_w, keyval_w, out_w, gateup_w, down_w, gains_all, positions, seq_ids)
    layer_out, pullback = jax.vjp(forward_fn, tokens.astype(jnp.float32), w_query.astype(jnp.float32), w_keyval.astype(jnp.float32), w_out.astype(jnp.float32), w_gateup.astype(jnp.float32), w_down.astype(jnp.float32), norm_gains)
    input_grad, grad_query, grad_keyval, grad_out, grad_gateup, grad_down, grad_gains = pullback(cotangent.astype(jnp.float32))
    new_mom_query = MOMENTUM * mom_query + grad_query
    new_mom_keyval = MOMENTUM * mom_keyval + grad_keyval
    new_mom_out = MOMENTUM * mom_out + grad_out
    new_mom_gateup = MOMENTUM * mom_gateup + grad_gateup
    new_mom_down = MOMENTUM * mom_down + grad_down
    upd_query = muon_update(new_mom_query)
    upd_keyval = jnp.stack([muon_update(new_mom_keyval[0]), muon_update(new_mom_keyval[1])])
    upd_out = muon_update(new_mom_out)
    upd_gateup = jnp.stack([muon_update(new_mom_gateup[0]), muon_update(new_mom_gateup[1])])
    upd_down = muon_update(new_mom_down)
    new_gain_first = ADAM_ONE * gain_first + (1.0 - ADAM_ONE) * grad_gains
    new_gain_second = ADAM_TWO * gain_second + (1.0 - ADAM_TWO) * grad_gains * grad_gains
    gain_update = -GAIN_RATE * new_gain_first / (jnp.sqrt(new_gain_second) + ADAM_EPS)
    return (layer_out.astype(jnp.bfloat16), input_grad, grad_query, grad_keyval, grad_out, grad_gateup, grad_down, grad_gains, new_mom_query, new_mom_keyval, new_mom_out, new_mom_gateup, new_mom_down, upd_query, upd_keyval, upd_out, upd_gateup, upd_down, new_gain_first, new_gain_second, gain_update)
```

```python
from functools import partial
import math

import jax
import jax.numpy as jnp
from jax import lax
from jax.experimental import pallas as pl
from jax.experimental.pallas import tpu as pltpu
from jax.sharding import PartitionSpec as P

D = 640
FF = 2048
HD = 256
WINDOW = 512
SOFT_CAP = 10
NS_STEPS = 5
HQ = 1024


EPS_NORM = 1e-06
ROPE_BASE = 10000.0
MOMENTUM = 0.95
MUON_RATE = 0.2
ADAM_ONE = 0.9
ADAM_TWO = 0.95
ADAM_EPS = 1e-08
GAIN_RATE = 0.1
QUINTIC_A = 3.4445
QUINTIC_B = -4.775
QUINTIC_C = 2.0315
MASK_FILL = -1e30
HIGHEST_PREC = lax.Precision.HIGHEST
MATRIX_COUNT = 7


def shifted(block, axis, distance):
    devices = range(lax.axis_size(axis))
    route = [(i - distance, i) for i in devices if i - distance in devices]
    return lax.ppermute(block, axis, route)


def rms_scale(activation, gain_row):
    return (
        activation
        * lax.rsqrt(jnp.mean(activation * activation, axis=-1, keepdims=True) + EPS_NORM)
        * (1.0 + gain_row)
    )


def geglu(gate_pre, up_proj):
    return jax.nn.gelu(gate_pre, approximate=True) * up_proj


def inverse_freq():
    return jnp.power(ROPE_BASE, -2.0 * jnp.arange(HD // 2, dtype=jnp.float32) / HD)


def angle_tables(vectors, angles):
    cosine_tab = jnp.cos(angles)
    sine_tab = jnp.sin(angles)
    if vectors.ndim == 3:
        cosine_tab = cosine_tab[:, None, :]
        sine_tab = sine_tab[:, None, :]
    return (cosine_tab, sine_tab)


def rotate(vectors, angles):
    half_dim = vectors.shape[-1] // 2
    cosine_tab, sine_tab = angle_tables(vectors, angles)
    left_part = vectors[..., :half_dim]
    right_part = vectors[..., half_dim:]
    return jnp.concatenate(
        [
            left_part * cosine_tab - right_part * sine_tab,
            right_part * cosine_tab + left_part * sine_tab,
        ],
        axis=-1,
    )


def rotate_back(grads_rot, angles):
    half_dim = grads_rot.shape[-1] // 2
    cosine_tab, sine_tab = angle_tables(grads_rot, angles)
    left_part = grads_rot[..., :half_dim]
    right_part = grads_rot[..., half_dim:]
    return jnp.concatenate(
        [
            left_part * cosine_tab + right_part * sine_tab,
            right_part * cosine_tab - left_part * sine_tab,
        ],
        axis=-1,
    )


def local_positions(seq_ids, ctx_index):
    tok_count = seq_ids.shape[0]
    begin_at = ctx_index * tok_count
    return begin_at + jnp.arange(tok_count, dtype=jnp.int32)


def block_scores(query_blk, key_blk, query_pos, query_ids, key_pos, key_ids):
    raw_scores = jnp.einsum("bhd,sd->hbs", query_blk, key_blk, preferred_element_type=jnp.float32)
    tanh_cap = jnp.tanh(raw_scores / SOFT_CAP)
    pos_gap = query_pos[:, None] - key_pos[None, :]
    allowed = (query_ids[:, None] == key_ids[None, :]) & (pos_gap >= 0) & (pos_gap < WINDOW)
    masked = jnp.where(allowed[None], SOFT_CAP * tanh_cap, MASK_FILL)
    return (masked, tanh_cap)


def take_block(array_in, along_dim, block_index, block_size):
    return lax.dynamic_slice_in_dim(array_in, block_index * block_size, block_size, along_dim)


MESH = pl.DeviceIdType.MESH
BF = jnp.bfloat16
F32 = jnp.float32
IN_COUNT = 4
NAMES = ("down", "gate", "up", "out", "query", "key", "value")
WIDTHS = (FF, FF, FF, HQ, HQ, HD, HD)
OWNERS = (7, 4, 8, 5, 11, 9, 10)
CHUNK_SETS = ((0,), (1,), (2,), (3, 4, 5, 6))
TILE = 256


def layout(wa_count):
    halves = [w // wa_count for w in WIDTHS]
    offs = [sum(halves[:i]) for i in range(len(halves))]
    return halves, offs, sum(halves)


def dot32(a, b):
    return jnp.dot(a, b, preferred_element_type=F32)


def eye_mask(n):
    return (
        lax.broadcasted_iota(jnp.int32, (n, n), 0) == lax.broadcasted_iota(jnp.int32, (n, n), 1)
    )


def pad_rows(v, rows):
    if v.shape[0] == rows:
        return v
    return jnp.concatenate([v, jnp.zeros((rows - v.shape[0], v.shape[1]), v.dtype)], axis=0)


def split_into(v, hi, lo):
    top = v.astype(BF)
    hi[...] = top
    lo[...] = (v - top.astype(F32)).astype(BF)


def mm3(h1, l1, h2, l2):
    return dot32(h1[...], h2[...]) + dot32(h1[...], l2[...]) + dot32(l1[...], h2[...])


def tail_kernel(
    ctx_count,
    wa_count,
    g_ref,
    mom_ref,
    sum_ref,
    nm_ref,
    upd_ref,
    own,
    pr,
    s3,
    ls,
    lr,
    mb,
    xb,
    xf,
    xc,
    ob,
    ub,
    am,
    ah,
    al,
    ph,
    plo,
    qh,
    ql,
    own_sem,
    psend,
    precv,
    lsend,
    lrecv,
    gsend,
    grecv,
    usend,
    urecv,
):
    c = lax.axis_index("ctx")
    w = lax.axis_index("wa")
    n_in = IN_COUNT
    n_out = ctx_count // n_in
    n_dev = ctx_count * wa_count
    p = lax.rem(c, n_in)
    z = lax.div(c, n_in)
    rows = D // ctx_count
    rp = xb.shape[1]
    halves, offs, cols = layout(wa_count)
    chunks = [(offs[s[0]], sum(halves[m] for m in s)) for s in CHUNK_SETS]
    me = c * wa_count + w

    barrier = pltpu.get_barrier_semaphore()

    def greet(i, carry):
        other = lax.rem(me + i, n_dev)
        pl.semaphore_signal(
            barrier,
            inc=1,
            device_id=(lax.div(other, wa_count), lax.rem(other, wa_count)),
            device_id_type=MESH,
        )
        return carry

    lax.fori_loop(1, n_dev, greet, 0)
    pl.semaphore_wait(barrier, n_dev - 1)

    def plane_copy(ci, k):
        off, wid = chunks[ci]
        q = lax.rem(p + k, n_in)
        return pltpu.make_async_remote_copy(
            g_ref.at[q, :, pl.ds(off, wid)],
            pr.at[k - 1, :, pl.ds(off, wid)],
            psend.at[ci, k - 1],
            precv.at[ci, k - 1],
            device_id=(z * n_in + q, w),
            device_id_type=MESH,
        )

    def own_copy(ci):
        off, wid = chunks[ci]
        return pltpu.make_async_copy(
            g_ref.at[p, :, pl.ds(off, wid)], own.at[:, pl.ds(off, wid)], own_sem.at[ci]
        )

    def line_copy(ci, k):
        off, wid = chunks[ci]
        j = lax.rem(z + k, n_out)
        return pltpu.make_async_remote_copy(
            ls.at[j, :, pl.ds(off, wid)],
            lr.at[k - 1, :, pl.ds(off, wid)],
            lsend.at[ci, k - 1],
            lrecv.at[ci, k - 1],
            device_id=(j * n_in + p, w),
            device_id_type=MESH,
        )

    def gather_remote(m):
        return pltpu.make_async_remote_copy(
            mb.at[:, pl.ds(offs[m], halves[m])],
            xb.at[c, :, pl.ds(pl.multiple_of(w * halves[m], 128), halves[m])],
            gsend.at[m],
            grecv,
            device_id=(OWNERS[m], 0),
            device_id_type=MESH,
        )

    def gather_local(m):
        return pltpu.make_async_copy(
            mb.at[:, pl.ds(offs[m], halves[m])],
            xb.at[c, :, pl.ds(pl.multiple_of(w * halves[m], 128), halves[m])],
            grecv,
        )

    for ci in range(len(chunks)):
        own_copy(ci).start()
        for k in range(1, n_in):
            plane_copy(ci, k).start()

    for ci, (off, wid) in enumerate(chunks):
        own_copy(ci).wait()
        for k in range(1, n_in):
            plane_copy(ci, k).wait_recv()

        def plane_sum(t, carry, off=off):
            cs = pl.ds(pl.multiple_of(off + t * TILE, TILE), TILE)
            s = own[:, cs].astype(F32)
            for k in range(n_in - 1):
                s = s + pr[k, :, cs].astype(F32)
            for j in range(n_out):
                slab = s[j * rows : (j + 1) * rows]
                s3[j, :, cs] = slab
                ls[j, :, cs] = pad_rows(slab, rp).astype(BF)
            return carry

        lax.fori_loop(0, wid // TILE, plane_sum, 0)
        for k in range(1, n_out):
            line_copy(ci, k).start()

    for ci, (off, wid) in enumerate(chunks):
        for k in range(1, n_out):
            line_copy(ci, k).wait_recv()

        def line_sum(t, carry, off=off):
            cs = pl.ds(pl.multiple_of(off + t * TILE, TILE), TILE)
            s = s3[z, :, cs]
            for k in range(n_out - 1):
                s = s + lr[k, :, cs][:rows].astype(F32)
            sum_ref[:, cs] = s
            nm = MOMENTUM * mom_ref[:, cs] + s
            nm_ref[:, cs] = nm
            mb[:, cs] = pad_rows(nm, rp).astype(BF)
            return carry

        lax.fori_loop(0, wid // TILE, line_sum, 0)
        for m in CHUNK_SETS[ci]:
            mine = me == OWNERS[m] * wa_count

            @pl.when(mine)
            def _(m=m):
                gather_local(m).start()

            @pl.when(jnp.logical_not(mine))
            def _(m=m):
                gather_remote(m).start()

    is_owner = me == OWNERS[0] * wa_count
    for m in range(1, MATRIX_COUNT):
        is_owner = jnp.logical_or(is_owner, me == OWNERS[m] * wa_count)
    is_small = jnp.logical_or(me == OWNERS[5] * wa_count, me == OWNERS[6] * wa_count)
    is_wide = me == OWNERS[0] * wa_count
    for m in (1, 2):
        is_wide = jnp.logical_or(is_wide, me == OWNERS[m] * wa_count)
    tiles = jnp.where(is_small, HD // TILE, jnp.where(is_wide, FF // TILE, HQ // TILE))

    for m in range(MATRIX_COUNT):

        @pl.when(me == OWNERS[m] * wa_count)
        def _(m=m):
            whole = xb.at[:, :, pl.ds(0, halves[m] * wa_count)]
            pltpu.make_async_copy(whole, whole, grecv).wait()

    @pl.when(is_owner)
    def _():
        am[...] = jnp.zeros_like(am)

        def gram(t, carry):
            cs = pl.ds(pl.multiple_of(t * TILE, TILE), TILE)
            for i in range(ctx_count):
                xf[i * rows : (i + 1) * rows, :] = xb[i, :, cs][:rows].astype(F32)
            x = xf[...].astype(BF)
            xc[:, cs] = x

            @pl.when(jnp.logical_not(is_small))
            def _():
                am[...] += lax.dot_general(
                    x, x, (((1,), (1,)), ((), ())), preferred_element_type=F32
                )

            @pl.when(is_small)
            def _():
                am[0:HD, 0:HD] = lax.dot_general(
                    x, x, (((0,), (0,)), ((), ())), preferred_element_type=F32
                )

            return carry

        lax.fori_loop(0, tiles, gram, 0)
        diag = eye_mask(D)
        norm2 = jnp.sum(jnp.where(diag, am[...], 0.0), keepdims=True)
        inv = 1.0 / (jnp.sqrt(norm2) + 1e-07)
        am[...] = am[...] * (inv * inv)

        def poly():
            split_into(am[...], ah, al)
            return (
                QUINTIC_B * am[...]
                + QUINTIC_C * mm3(ah, al, ah, al)
                + jnp.where(eye_mask(D), QUINTIC_A, 0.0)
            )

        def advance():
            b = mm3(ph, plo, ah, al)
            split_into(b, ah, al)
            am[...] = mm3(ah, al, ph, plo)

        first = poly()
        split_into(first, ph, plo)
        split_into(first, qh, ql)
        advance()

        def sweep(i, carry):
            split_into(poly(), ph, plo)
            split_into(mm3(ph, plo, qh, ql), qh, ql)

            @pl.when(i < NS_STEPS - 2)
            def _():
                advance()

            return carry

        lax.fori_loop(0, NS_STEPS - 1, sweep, 0)
        wide_rate = -MUON_RATE * 0.2 * math.sqrt(FF)
        mid_rate = -MUON_RATE * 0.2 * math.sqrt(HQ)
        low_rate = -MUON_RATE * 0.2 * math.sqrt(D)
        rate = jnp.where(is_small, low_rate, jnp.where(is_wide, wide_rate, mid_rate))
        scale = rate * inv

        def back(t, carry):
            cs = pl.ds(pl.multiple_of(t * TILE, TILE), TILE)

            @pl.when(jnp.logical_not(is_small))
            def _():
                xf[...] = dot32(qh[...], xc[:, cs]) * scale

            @pl.when(is_small)
            def _():
                xf[...] = dot32(xc[:, cs], qh[0:HD, 0:HD]) * scale

            for i in range(ctx_count):
                ob[i, :, cs] = pad_rows(xf[i * rows : (i + 1) * rows, :], rp).astype(BF)
            return carry

        lax.fori_loop(0, tiles, back, 0)

    for m in range(MATRIX_COUNT):

        def pieces(t, m=m):
            i = lax.div(t, wa_count)
            v = lax.rem(t, wa_count)
            src = ob.at[i, :, pl.ds(pl.multiple_of(v * halves[m], 128), halves[m])]
            return i, v, src

        def remote_piece(t, m=m):
            i, v, src = pieces(t, m)
            return pltpu.make_async_remote_copy(
                src,
                ub.at[:, pl.ds(offs[m], halves[m])],
                usend.at[t],
                urecv.at[m],
                device_id=(i, v),
                device_id_type=MESH,
            )

        def local_piece(t, m=m):
            i, v, src = pieces(t, m)
            return pltpu.make_async_copy(src, ub.at[:, pl.ds(offs[m], halves[m])], urecv.at[m])

        owner_flat = OWNERS[m] * wa_count

        @pl.when(me == owner_flat)
        def _(m=m, owner_flat=owner_flat, remote_piece=remote_piece, local_piece=local_piece):
            def send(t, carry):
                remote_piece(lax.rem(owner_flat + t, n_dev)).start()
                return carry

            local_piece(owner_flat).start()
            lax.fori_loop(1, n_dev, send, 0)

    for m in range(MATRIX_COUNT):
        piece = ub.at[:, pl.ds(offs[m], halves[m])]
        pltpu.make_async_copy(piece, piece, urecv.at[m]).wait()
    for t in range(cols // TILE):
        cs = slice(t * TILE, (t + 1) * TILE)
        upd_ref[:, cs] = ub[:, cs][:rows].astype(F32)

    for ci in range(len(chunks)):
        for k in range(1, n_in):
            plane_copy(ci, k).wait_send()
        for k in range(1, n_out):
            line_copy(ci, k).wait_send()
    for m in range(MATRIX_COUNT):

        @pl.when(me != OWNERS[m] * wa_count)
        def _(m=m):
            gather_remote(m).wait_send()

        owner_flat = OWNERS[m] * wa_count

        @pl.when(me == owner_flat)
        def _(m=m, owner_flat=owner_flat):
            def done(t, carry):
                o = lax.rem(owner_flat + t, n_dev)
                i, v = lax.div(o, wa_count), lax.rem(o, wa_count)
                pltpu.make_async_remote_copy(
                    ob.at[i, :, pl.ds(pl.multiple_of(v * halves[m], 128), halves[m])],
                    ub.at[:, pl.ds(offs[m], halves[m])],
                    usend.at[o],
                    urecv.at[m],
                    device_id=(i, v),
                    device_id_type=MESH,
                ).wait_send()
                return carry

            lax.fori_loop(1, n_dev, done, 0)


def run_tail(grads, moments, ctx_count, wa_count):
    n_in = IN_COUNT
    n_out = ctx_count // n_in
    rows = D // ctx_count
    rp = -(-rows // 16) * 16
    cols = layout(wa_count)[2]
    n_ch = len(CHUNK_SETS)
    n_dev = ctx_count * wa_count
    square = lambda dt: pltpu.VMEM((D, D), dt)
    dma = pltpu.SemaphoreType.DMA
    shard = jax.ShapeDtypeStruct((rows, cols), F32)
    in_vmem = pl.BlockSpec(memory_space=pltpu.VMEM)
    return pl.pallas_call(
        partial(tail_kernel, ctx_count, wa_count),
        out_shape=(shard, shard, shard),
        in_specs=[pl.BlockSpec(memory_space=pl.ANY), in_vmem],
        out_specs=(in_vmem, in_vmem, in_vmem),
        scratch_shapes=[
            pltpu.VMEM((D // n_in, cols), BF),
            pltpu.VMEM((n_in - 1, D // n_in, cols), BF),
            pltpu.VMEM((n_out, rows, cols), F32),
            pltpu.VMEM((n_out, rp, cols), BF),
            pltpu.VMEM((n_out - 1, rp, cols), BF),
            pltpu.VMEM((rp, cols), BF),
            pltpu.VMEM((ctx_count, rp, FF), BF),
            pltpu.VMEM((D, TILE), F32),
            pltpu.VMEM((D, FF), BF),
            pltpu.VMEM((ctx_count, rp, FF), BF),
            pltpu.VMEM((rp, cols), BF),
            square(F32),
            square(BF),
            square(BF),
            square(BF),
            square(BF),
            square(BF),
            square(BF),
            dma((n_ch,)),
            dma((n_ch, n_in - 1)),
            dma((n_ch, n_in - 1)),
            dma((n_ch, n_out - 1)),
            dma((n_ch, n_out - 1)),
            dma((MATRIX_COUNT,)),
            dma,
            dma((n_dev,)),
            dma((MATRIX_COUNT,)),
        ],
        compiler_params=pltpu.CompilerParams(
            collective_id=0, has_side_effects=True, vmem_limit_bytes=60 << 20
        ),
        name="tail",
    )(grads, moments)


def per_device(
    tokens,
    cotangent,
    seq_ids,
    w_query,
    w_keyval,
    w_out,
    w_gateup,
    w_down,
    norm_gains,
    mom_query,
    mom_keyval,
    mom_out,
    mom_gateup,
    mom_down,
    gain_first,
    gain_second,
):
    ctx_index = lax.axis_index("ctx")
    wa_index = lax.axis_index("wa")
    ctx_count = lax.axis_size("ctx")
    wa_count = lax.axis_size("wa")
    tok_count = tokens.shape[0]
    head_local = w_query.shape[1] // HD
    block_rows = min(512, tok_count)
    key_span = block_rows + WINDOW
    block_total = tok_count // block_rows
    positions = local_positions(seq_ids, ctx_index)
    angles = positions.astype(jnp.float32)[:, None] * inverse_freq()[None, :]
    resid_in = tokens.astype(jnp.float32)
    normed = rms_scale(resid_in, norm_gains[0]).astype(jnp.bfloat16)
    query_proj = jnp.dot(normed, w_query, preferred_element_type=jnp.float32)
    key_proj = jnp.dot(normed, w_keyval[0], preferred_element_type=jnp.float32)
    value_proj = jnp.dot(normed, w_keyval[1], preferred_element_type=jnp.float32)
    query_rot = (
        rotate(query_proj.reshape(tok_count, head_local, HD), angles) * HD ** (-0.5)
    ).astype(jnp.bfloat16)
    key_rot = rotate(key_proj, angles).astype(jnp.bfloat16)
    value_low = value_proj.astype(jnp.bfloat16)
    prev_key, prev_value, prev_pos, prev_ids = shifted(
        (key_rot, value_low, positions, seq_ids), "ctx", 1
    )
    prev_ids = jnp.where(ctx_index > 0, prev_ids, -1)
    keys_all = jnp.concatenate([prev_key, key_rot])
    values_all = jnp.concatenate([prev_value, value_low])
    pos_all = jnp.concatenate([prev_pos, positions])
    ids_all = jnp.concatenate([prev_ids, seq_ids])
    attended_parts = []
    lse_parts = []
    for block_idx in range(block_total):
        q_start = block_idx * block_rows
        k_start = tok_count + q_start - WINDOW
        masked, tanh_cap = block_scores(
            query_rot[q_start : q_start + block_rows],
            keys_all[k_start : k_start + key_span],
            positions[q_start : q_start + block_rows],
            seq_ids[q_start : q_start + block_rows],
            pos_all[k_start : k_start + key_span],
            ids_all[k_start : k_start + key_span],
        )
        row_max = jnp.max(masked, axis=-1, keepdims=True)
        exp_terms = jnp.exp(masked - row_max)
        row_total = jnp.sum(exp_terms, axis=-1, keepdims=True)
        prob_low = (exp_terms / row_total).astype(jnp.bfloat16)
        attended_parts.append(
            jnp.einsum(
                "hbs,sd->bhd",
                prob_low,
                values_all[k_start : k_start + key_span],
                preferred_element_type=jnp.float32,
            )
        )
        lse_parts.append(row_max + jnp.log(row_total))
    att_low = (
        jnp.concatenate(attended_parts).reshape(tok_count, head_local * HD).astype(jnp.bfloat16)
    )
    attn_part = jnp.dot(att_low, w_out, preferred_element_type=jnp.float32)
    attn_proj = lax.psum(attn_part, "wa")
    hidden_one = resid_in + rms_scale(attn_proj, norm_gains[1])
    ffn_in = rms_scale(hidden_one, norm_gains[2]).astype(jnp.bfloat16)
    gate_up = jnp.einsum("td,gdf->gtf", ffn_in, w_gateup, preferred_element_type=jnp.float32)
    inner_act = geglu(gate_up[0], gate_up[1]).astype(jnp.bfloat16)
    down_part = jnp.dot(inner_act, w_down, preferred_element_type=jnp.float32)
    down_proj = lax.psum(down_part, "wa")
    layer_out = hidden_one + rms_scale(down_proj, norm_gains[3])
    block_out = layer_out.astype(jnp.bfloat16)
    out_grad = cotangent.astype(jnp.float32)
    post_ffn_pull = jax.vjp(rms_scale, down_proj, norm_gains[3])[1]
    d_down, d_gain3 = post_ffn_pull(out_grad)
    d_down_low = d_down.astype(jnp.bfloat16)
    grad_down = jnp.dot(inner_act.T, d_down_low, preferred_element_type=jnp.float32)
    d_inner = jnp.dot(d_down_low, w_down.T, preferred_element_type=jnp.float32)
    act_pull = jax.vjp(geglu, gate_up[0], gate_up[1])[1]
    d_gate, d_up = act_pull(d_inner)
    d_gateup_low = jnp.stack([d_gate, d_up]).astype(jnp.bfloat16)
    grad_gateup = jnp.einsum(
        "td,gtf->gdf", ffn_in, d_gateup_low, preferred_element_type=jnp.float32
    )
    d_ffn_part = jnp.einsum(
        "gtf,gdf->td", d_gateup_low, w_gateup, preferred_element_type=jnp.float32
    )
    d_ffn = lax.psum(d_ffn_part, "wa")
    pre_ffn_pull = jax.vjp(rms_scale, hidden_one, norm_gains[2])[1]
    d_hidden_b, d_gain2 = pre_ffn_pull(d_ffn)
    d_hidden = out_grad + d_hidden_b
    post_attn_pull = jax.vjp(rms_scale, attn_proj, norm_gains[1])[1]
    d_attn, d_gain1 = post_attn_pull(d_hidden)
    d_attn_low = d_attn.astype(jnp.bfloat16)
    grad_out = jnp.dot(att_low.T, d_attn_low, preferred_element_type=jnp.float32)
    d_att_low = (
        jnp.dot(d_attn_low, w_out.T, preferred_element_type=jnp.float32)
        .astype(jnp.bfloat16)
        .reshape(tok_count, head_local, HD)
    )
    d_query_parts = []
    d_keys_all = jnp.zeros((2 * tok_count, HD), jnp.float32)
    d_values_all = jnp.zeros((2 * tok_count, HD), jnp.float32)
    for block_idx in range(block_total):
        q_start = block_idx * block_rows
        k_start = tok_count + q_start - WINDOW
        query_blk = query_rot[q_start : q_start + block_rows]
        key_blk = keys_all[k_start : k_start + key_span]
        value_blk = values_all[k_start : k_start + key_span]
        masked, tanh_cap = block_scores(
            query_blk,
            key_blk,
            positions[q_start : q_start + block_rows],
            seq_ids[q_start : q_start + block_rows],
            pos_all[k_start : k_start + key_span],
            ids_all[k_start : k_start + key_span],
        )
        prob_f32 = jnp.exp(masked - lse_parts[block_idx])
        prob_low = prob_f32.astype(jnp.bfloat16)
        d_att_blk = d_att_low[q_start : q_start + block_rows]
        d_probs = jnp.einsum(
            "bhd,sd->hbs", d_att_blk, value_blk, preferred_element_type=jnp.float32
        )
        inner_sum = jnp.sum(prob_f32 * d_probs, axis=-1, keepdims=True)
        d_raw = (prob_f32 * (d_probs - inner_sum) * (1.0 - tanh_cap * tanh_cap)).astype(
            jnp.bfloat16
        )
        d_query_parts.append(
            jnp.einsum("hbs,sd->bhd", d_raw, key_blk, preferred_element_type=jnp.float32)
        )
        d_key_blk = jnp.einsum("hbs,bhd->sd", d_raw, query_blk, preferred_element_type=jnp.float32)
        d_value_blk = jnp.einsum(
            "hbs,bhd->sd", prob_low, d_att_blk, preferred_element_type=jnp.float32
        )
        d_keys_all = d_keys_all.at[k_start : k_start + key_span].add(d_key_blk)
        d_values_all = d_values_all.at[k_start : k_start + key_span].add(d_value_blk)
    from_next = (
        shifted(d_keys_all[:tok_count].astype(jnp.bfloat16), "ctx", -1).astype(jnp.float32),
        shifted(d_values_all[:tok_count].astype(jnp.bfloat16), "ctx", -1).astype(jnp.float32),
    )
    d_key_own = d_keys_all[tok_count:] + from_next[0]
    d_value_own = d_values_all[tok_count:] + from_next[1]
    d_key_sum, d_value_sum = (
        lax.psum(d_key_own.astype(jnp.bfloat16), "wa").astype(jnp.float32),
        lax.psum(d_value_own.astype(jnp.bfloat16), "wa").astype(jnp.float32),
    )
    d_key_low = rotate_back(d_key_sum, angles).astype(jnp.bfloat16)
    d_value_low = d_value_sum.astype(jnp.bfloat16)
    d_query_rot = jnp.concatenate(d_query_parts)
    d_query_low = (
        (rotate_back(d_query_rot, angles) * HD ** (-0.5))
        .reshape(tok_count, head_local * HD)
        .astype(jnp.bfloat16)
    )
    half_kv = HD // wa_count
    key_half = take_block(d_key_low, 1, wa_index, half_kv)
    value_half = take_block(d_value_low, 1, wa_index, half_kv)
    w_key_half = take_block(w_keyval[0], 1, wa_index, half_kv)
    w_value_half = take_block(w_keyval[1], 1, wa_index, half_kv)
    grad_query = jnp.dot(normed.T, d_query_low, preferred_element_type=jnp.float32)
    grad_keyval = jnp.stack(
        [
            jnp.dot(normed.T, key_half, preferred_element_type=jnp.float32),
            jnp.dot(normed.T, value_half, preferred_element_type=jnp.float32),
        ]
    )
    d_normed_part = jnp.dot(d_query_low, w_query.T, preferred_element_type=jnp.float32)
    d_normed_part = d_normed_part + jnp.dot(
        key_half, w_key_half.T, preferred_element_type=jnp.float32
    )
    d_normed_part = d_normed_part + jnp.dot(
        value_half, w_value_half.T, preferred_element_type=jnp.float32
    )
    d_normed = lax.psum(d_normed_part.astype(jnp.bfloat16), "wa").astype(jnp.float32)
    pre_attn_pull = jax.vjp(rms_scale, resid_in, norm_gains[0])[1]
    d_tokens, d_gain0 = pre_attn_pull(d_normed)
    input_grad = d_hidden + d_tokens
    grad_gains = jnp.stack([d_gain0, d_gain1, d_gain2, d_gain3])
    stack = jnp.concatenate(
        [
            grad_down.T,
            grad_gateup[0],
            grad_gateup[1],
            grad_out.T,
            grad_query,
            grad_keyval[0],
            grad_keyval[1],
        ],
        axis=1,
    ).astype(jnp.bfloat16)
    cols = stack.shape[1]
    rows = D // ctx_count
    stack = (
        stack.reshape(ctx_count // IN_COUNT, IN_COUNT, rows, cols)
        .transpose(1, 0, 2, 3)
        .reshape(IN_COUNT, D // IN_COUNT, cols)
    )
    moments = jnp.concatenate(
        [
            mom_down.T,
            mom_gateup[0],
            mom_gateup[1],
            mom_out.T,
            mom_query,
            mom_keyval[0],
            mom_keyval[1],
        ],
        axis=1,
    )
    sums, fresh, updates = run_tail(stack, moments, ctx_count, wa_count)
    halves, offs, _ = layout(wa_count)

    def unstack(flat):
        down, gate, up, out, query, key, value = [
            flat[:, o : o + h] for o, h in zip(offs, halves)
        ]
        return (query, jnp.stack([key, value]), out.T, jnp.stack([gate, up]), down.T)

    sum_query, sum_keyval, sum_out, sum_gateup, sum_down = unstack(sums)
    new_mom_query, new_mom_keyval, new_mom_out, new_mom_gateup, new_mom_down = unstack(fresh)
    upd_query, upd_keyval, upd_out, upd_gateup, upd_down = unstack(updates)
    sum_gains = lax.psum_scatter(grad_gains, "ctx", scatter_dimension=1, tiled=True)
    new_gain_first = ADAM_ONE * gain_first + (1.0 - ADAM_ONE) * sum_gains
    new_gain_second = ADAM_TWO * gain_second + (1.0 - ADAM_TWO) * sum_gains * sum_gains
    gain_update = -GAIN_RATE * new_gain_first / (jnp.sqrt(new_gain_second) + ADAM_EPS)
    return (
        block_out,
        input_grad,
        sum_query,
        sum_keyval,
        sum_out,
        sum_gateup,
        sum_down,
        sum_gains,
        new_mom_query,
        new_mom_keyval,
        new_mom_out,
        new_mom_gateup,
        new_mom_down,
        upd_query,
        upd_keyval,
        upd_out,
        upd_gateup,
        upd_down,
        new_gain_first,
        new_gain_second,
        gain_update,
    )


def solution(mesh):
    in_specs = (
        P("ctx", None),
        P("ctx", None),
        P("ctx"),
        P(None, "wa"),
        P(),
        P("wa", None),
        P(None, None, "wa"),
        P("wa", None),
        P(),
        P("ctx", "wa"),
        P(None, "ctx", "wa"),
        P("wa", "ctx"),
        P(None, "ctx", "wa"),
        P("wa", "ctx"),
        P(None, "ctx"),
        P(None, "ctx"),
    )
    out_specs = (
        P("ctx", None),
        P("ctx", None),
        P("ctx", "wa"),
        P(None, "ctx", "wa"),
        P("wa", "ctx"),
        P(None, "ctx", "wa"),
        P("wa", "ctx"),
        P(None, "ctx"),
        P("ctx", "wa"),
        P(None, "ctx", "wa"),
        P("wa", "ctx"),
        P(None, "ctx", "wa"),
        P("wa", "ctx"),
        P("ctx", "wa"),
        P(None, "ctx", "wa"),
        P("wa", "ctx"),
        P(None, "ctx", "wa"),
        P("wa", "ctx"),
        P(None, "ctx"),
        P(None, "ctx"),
        P(None, "ctx"),
    )
    return jax.shard_map(
        per_device, mesh=mesh, in_specs=in_specs, out_specs=out_specs, check_vma=False
    )
```

```python
from functools import partial
import math

import jax
import jax.numpy as jnp
import numpy as np
from jax import lax
from jax.experimental import pallas as pl
from jax.experimental.pallas import tpu as pltpu
from jax.sharding import PartitionSpec as P

D = 640
FF = 2048
HD = 256
WINDOW = 512
SOFT_CAP = 10
NS_STEPS = 5
HQ = 1024


EPS_NORM = 1e-06
ROPE_BASE = 10000.0
MOMENTUM = 0.95
ADAM_ONE = 0.9
ADAM_TWO = 0.95
ADAM_EPS = 1e-08
GAIN_RATE = 0.1
QUINTIC_A = 3.4445
QUINTIC_B = -4.775
QUINTIC_C = 2.0315
MATRIX_COUNT = 7
MUON_RATE = 0.2

MESH = pl.DeviceIdType.MESH
BF = jnp.bfloat16
F32 = jnp.float32
IN_COUNT = 4
NAMES = ("down", "gate", "up", "out", "query", "key", "value")
WIDTHS = (FF, FF, FF, HQ, HQ, HD, HD)
OWNERS = (7, 4, 8, 5, 11, 9, 10)
CHUNK_SETS = ((0,), (1,), (2,), (3, 4, 5, 6))
TILE = 256


def layout(wa_count):
    halves = [w // wa_count for w in WIDTHS]
    offs = [sum(halves[:i]) for i in range(len(halves))]
    return halves, offs, sum(halves)


def dot32(a, b):
    return jnp.dot(a, b, preferred_element_type=F32)


def eye_mask(n):
    return (
        lax.broadcasted_iota(jnp.int32, (n, n), 0) == lax.broadcasted_iota(jnp.int32, (n, n), 1)
    )


def pad_rows(v, rows):
    if v.shape[0] == rows:
        return v
    return jnp.concatenate([v, jnp.zeros((rows - v.shape[0], v.shape[1]), v.dtype)], axis=0)


def split_into(v, hi, lo):
    top = v.astype(BF)
    hi[...] = top
    lo[...] = (v - top.astype(F32)).astype(BF)


def mm3(h1, l1, h2, l2):
    return dot32(h1[...], h2[...]) + dot32(h1[...], l2[...]) + dot32(l1[...], h2[...])


def tail_kernel(
    ctx_count,
    wa_count,
    g_ref,
    mom_ref,
    dg_ref,
    sum_ref,
    nm_ref,
    upd_ref,
    gs_ref,
    own,
    pr,
    s3,
    ls,
    lr,
    mb,
    xb,
    xf,
    xc,
    ob,
    ub,
    am,
    ah,
    al,
    ph,
    plo,
    qh,
    ql,
    own_sem,
    psend,
    precv,
    lsend,
    lrecv,
    gsend,
    grecv,
    usend,
    urecv,
    dgs,
    dgr,
    dsend,
    drecv,
):
    c = lax.axis_index("ctx")
    w = lax.axis_index("wa")
    n_in = IN_COUNT
    n_out = ctx_count // n_in
    n_dev = ctx_count * wa_count
    p = lax.rem(c, n_in)
    z = lax.div(c, n_in)
    rows = D // ctx_count
    rp = xb.shape[1]
    halves, offs, cols = layout(wa_count)
    chunks = [(offs[s[0]], sum(halves[m] for m in s)) for s in CHUNK_SETS]
    me = c * wa_count + w

    barrier = pltpu.get_barrier_semaphore()

    def greet(i, carry):
        other = lax.rem(me + i, n_dev)
        pl.semaphore_signal(
            barrier,
            inc=1,
            device_id=(lax.div(other, wa_count), lax.rem(other, wa_count)),
            device_id_type=MESH,
        )
        return carry

    lax.fori_loop(1, n_dev, greet, 0)
    pl.semaphore_wait(barrier, n_dev - 1)

    def plane_copy(ci, k):
        off, wid = chunks[ci]
        q = lax.rem(p + k, n_in)
        return pltpu.make_async_remote_copy(
            g_ref.at[q, :, pl.ds(off, wid)],
            pr.at[k - 1, :, pl.ds(off, wid)],
            psend.at[ci, k - 1],
            precv.at[ci, k - 1],
            device_id=(z * n_in + q, w),
            device_id_type=MESH,
        )

    def own_copy(ci):
        off, wid = chunks[ci]
        return pltpu.make_async_copy(
            g_ref.at[p, :, pl.ds(off, wid)], own.at[:, pl.ds(off, wid)], own_sem.at[ci]
        )

    def line_copy(ci, k):
        off, wid = chunks[ci]
        j = lax.rem(z + k, n_out)
        return pltpu.make_async_remote_copy(
            ls.at[j, :, pl.ds(off, wid)],
            lr.at[k - 1, :, pl.ds(off, wid)],
            lsend.at[ci, k - 1],
            lrecv.at[ci, k - 1],
            device_id=(j * n_in + p, w),
            device_id_type=MESH,
        )

    def gather_remote(m):
        return pltpu.make_async_remote_copy(
            mb.at[:, pl.ds(offs[m], halves[m])],
            xb.at[c, :, pl.ds(pl.multiple_of(w * halves[m], 128), halves[m])],
            gsend.at[m],
            grecv,
            device_id=(OWNERS[m], 0),
            device_id_type=MESH,
        )

    def gather_local(m):
        return pltpu.make_async_copy(
            mb.at[:, pl.ds(offs[m], halves[m])],
            xb.at[c, :, pl.ds(pl.multiple_of(w * halves[m], 128), halves[m])],
            grecv,
        )

    for ci in range(len(chunks)):
        own_copy(ci).start()
        for k in range(1, n_in):
            plane_copy(ci, k).start()

    for i in range(ctx_count):
        dgs[i, :, 0:rows] = dg_ref[:, i * rows : (i + 1) * rows]

    def gain_copy(t):
        i, v = lax.div(t, wa_count), lax.rem(t, wa_count)
        return pltpu.make_async_remote_copy(
            dgs.at[i], dgr.at[me], dsend.at[t], drecv, device_id=(i, v), device_id_type=MESH
        )

    def gain_send(t, carry):
        gain_copy(lax.rem(me + t, n_dev)).start()
        return carry

    def gain_sent(t, carry):
        gain_copy(lax.rem(me + t, n_dev)).wait_send()
        return carry

    pltpu.make_async_copy(dgs.at[c], dgr.at[me], drecv).start()
    lax.fori_loop(1, n_dev, gain_send, 0)

    for ci, (off, wid) in enumerate(chunks):
        own_copy(ci).wait()
        for k in range(1, n_in):
            plane_copy(ci, k).wait_recv()

        def plane_sum(t, carry, off=off):
            cs = pl.ds(pl.multiple_of(off + t * TILE, TILE), TILE)
            s = own[:, cs].astype(F32)
            for k in range(n_in - 1):
                s = s + pr[k, :, cs].astype(F32)
            for j in range(n_out):
                slab = s[j * rows : (j + 1) * rows]
                s3[j, :, cs] = slab
                ls[j, :, cs] = pad_rows(slab, rp).astype(BF)
            return carry

        lax.fori_loop(0, wid // TILE, plane_sum, 0)
        for k in range(1, n_out):
            line_copy(ci, k).start()

    for ci, (off, wid) in enumerate(chunks):
        for k in range(1, n_out):
            line_copy(ci, k).wait_recv()

        def line_sum(t, carry, off=off):
            cs = pl.ds(pl.multiple_of(off + t * TILE, TILE), TILE)
            s = s3[z, :, cs]
            for k in range(n_out - 1):
                s = s + lr[k, :, cs][:rows].astype(F32)
            sum_ref[:, cs] = s
            nm = MOMENTUM * mom_ref[:, cs] + s
            nm_ref[:, cs] = nm
            mb[:, cs] = pad_rows(nm, rp).astype(BF)
            return carry

        lax.fori_loop(0, wid // TILE, line_sum, 0)
        for m in CHUNK_SETS[ci]:
            mine = me == OWNERS[m] * wa_count

            @pl.when(mine)
            def _(m=m):
                gather_local(m).start()

            @pl.when(jnp.logical_not(mine))
            def _(m=m):
                gather_remote(m).start()

    pltpu.make_async_copy(dgr, dgr, drecv).wait()
    gs_ref[...] = jnp.sum(dgr[...], axis=0)
    is_owner = me == OWNERS[0] * wa_count
    for m in range(1, MATRIX_COUNT):
        is_owner = jnp.logical_or(is_owner, me == OWNERS[m] * wa_count)
    is_small = jnp.logical_or(me == OWNERS[5] * wa_count, me == OWNERS[6] * wa_count)
    is_wide = me == OWNERS[0] * wa_count
    for m in (1, 2):
        is_wide = jnp.logical_or(is_wide, me == OWNERS[m] * wa_count)
    tiles = jnp.where(is_small, HD // TILE, jnp.where(is_wide, FF // TILE, HQ // TILE))

    for m in range(MATRIX_COUNT):

        @pl.when(me == OWNERS[m] * wa_count)
        def _(m=m):
            whole = xb.at[:, :, pl.ds(0, halves[m] * wa_count)]
            pltpu.make_async_copy(whole, whole, grecv).wait()

    @pl.when(is_owner)
    def _():
        am[...] = jnp.zeros_like(am)

        def gram(t, carry):
            cs = pl.ds(pl.multiple_of(t * TILE, TILE), TILE)
            for i in range(ctx_count):
                xf[i * rows : (i + 1) * rows, :] = xb[i, :, cs][:rows].astype(F32)
            x = xf[...].astype(BF)
            xc[:, cs] = x

            @pl.when(jnp.logical_not(is_small))
            def _():
                am[...] += lax.dot_general(
                    x, x, (((1,), (1,)), ((), ())), preferred_element_type=F32
                )

            @pl.when(is_small)
            def _():
                am[0:HD, 0:HD] = lax.dot_general(
                    x, x, (((0,), (0,)), ((), ())), preferred_element_type=F32
                )

            return carry

        lax.fori_loop(0, tiles, gram, 0)
        diag = eye_mask(D)
        norm2 = jnp.sum(jnp.where(diag, am[...], 0.0), keepdims=True)
        inv = 1.0 / (jnp.sqrt(norm2) + 1e-07)
        am[...] = am[...] * (inv * inv)

        def poly():
            split_into(am[...], ah, al)
            return (
                QUINTIC_B * am[...]
                + QUINTIC_C * mm3(ah, al, ah, al)
                + jnp.where(eye_mask(D), QUINTIC_A, 0.0)
            )

        def advance():
            b = mm3(ph, plo, ah, al)
            split_into(b, ah, al)
            am[...] = mm3(ah, al, ph, plo)

        first = poly()
        split_into(first, ph, plo)
        split_into(first, qh, ql)
        advance()

        def sweep(i, carry):
            split_into(poly(), ph, plo)
            split_into(mm3(ph, plo, qh, ql), qh, ql)

            @pl.when(i < NS_STEPS - 2)
            def _():
                advance()

            return carry

        lax.fori_loop(0, NS_STEPS - 1, sweep, 0)
        wide_rate = -MUON_RATE * 0.2 * math.sqrt(FF)
        mid_rate = -MUON_RATE * 0.2 * math.sqrt(HQ)
        low_rate = -MUON_RATE * 0.2 * math.sqrt(D)
        rate = jnp.where(is_small, low_rate, jnp.where(is_wide, wide_rate, mid_rate))
        scale = rate * inv

        def back(t, carry):
            cs = pl.ds(pl.multiple_of(t * TILE, TILE), TILE)

            @pl.when(jnp.logical_not(is_small))
            def _():
                xf[...] = dot32(qh[...], xc[:, cs]) * scale

            @pl.when(is_small)
            def _():
                xf[...] = dot32(xc[:, cs], qh[0:HD, 0:HD]) * scale

            for i in range(ctx_count):
                ob[i, :, cs] = pad_rows(xf[i * rows : (i + 1) * rows, :], rp).astype(BF)
            return carry

        lax.fori_loop(0, tiles, back, 0)

    for m in range(MATRIX_COUNT):

        def pieces(t, m=m):
            i = lax.div(t, wa_count)
            v = lax.rem(t, wa_count)
            src = ob.at[i, :, pl.ds(pl.multiple_of(v * halves[m], 128), halves[m])]
            return i, v, src

        def remote_piece(t, m=m):
            i, v, src = pieces(t, m)
            return pltpu.make_async_remote_copy(
                src,
                ub.at[:, pl.ds(offs[m], halves[m])],
                usend.at[t],
                urecv.at[m],
                device_id=(i, v),
                device_id_type=MESH,
            )

        def local_piece(t, m=m):
            i, v, src = pieces(t, m)
            return pltpu.make_async_copy(src, ub.at[:, pl.ds(offs[m], halves[m])], urecv.at[m])

        owner_flat = OWNERS[m] * wa_count

        @pl.when(me == owner_flat)
        def _(m=m, owner_flat=owner_flat, remote_piece=remote_piece, local_piece=local_piece):
            def send(t, carry):
                remote_piece(lax.rem(owner_flat + t, n_dev)).start()
                return carry

            local_piece(owner_flat).start()
            lax.fori_loop(1, n_dev, send, 0)

    for m in range(MATRIX_COUNT):
        piece = ub.at[:, pl.ds(offs[m], halves[m])]
        pltpu.make_async_copy(piece, piece, urecv.at[m]).wait()
    for t in range(cols // TILE):
        cs = slice(t * TILE, (t + 1) * TILE)
        upd_ref[:, cs] = ub[:, cs][:rows].astype(F32)

    lax.fori_loop(1, n_dev, gain_sent, 0)
    for ci in range(len(chunks)):
        for k in range(1, n_in):
            plane_copy(ci, k).wait_send()
        for k in range(1, n_out):
            line_copy(ci, k).wait_send()
    for m in range(MATRIX_COUNT):

        @pl.when(me != OWNERS[m] * wa_count)
        def _(m=m):
            gather_remote(m).wait_send()

        owner_flat = OWNERS[m] * wa_count

        @pl.when(me == owner_flat)
        def _(m=m, owner_flat=owner_flat):
            def done(t, carry):
                o = lax.rem(owner_flat + t, n_dev)
                i, v = lax.div(o, wa_count), lax.rem(o, wa_count)
                pltpu.make_async_remote_copy(
                    ob.at[i, :, pl.ds(pl.multiple_of(v * halves[m], 128), halves[m])],
                    ub.at[:, pl.ds(offs[m], halves[m])],
                    usend.at[o],
                    urecv.at[m],
                    device_id=(i, v),
                    device_id_type=MESH,
                ).wait_send()
                return carry

            lax.fori_loop(1, n_dev, done, 0)


def run_tail(grads, moments, gain_grads, ctx_count, wa_count):
    n_in = IN_COUNT
    n_out = ctx_count // n_in
    rows = D // ctx_count
    rp = -(-rows // 16) * 16
    cols = layout(wa_count)[2]
    n_ch = len(CHUNK_SETS)
    n_dev = ctx_count * wa_count
    square = lambda dt: pltpu.VMEM((D, D), dt)
    dma = pltpu.SemaphoreType.DMA
    shard = jax.ShapeDtypeStruct((rows, cols), F32)
    in_vmem = pl.BlockSpec(memory_space=pltpu.VMEM)
    return pl.pallas_call(
        partial(tail_kernel, ctx_count, wa_count),
        out_shape=(shard, shard, shard, jax.ShapeDtypeStruct((8, 128), F32)),
        in_specs=[pl.BlockSpec(memory_space=pl.ANY), in_vmem, in_vmem],
        out_specs=(in_vmem,) * 4,
        scratch_shapes=[
            pltpu.VMEM((D // n_in, cols), BF),
            pltpu.VMEM((n_in - 1, D // n_in, cols), BF),
            pltpu.VMEM((n_out, rows, cols), F32),
            pltpu.VMEM((n_out, rp, cols), BF),
            pltpu.VMEM((n_out - 1, rp, cols), BF),
            pltpu.VMEM((rp, cols), BF),
            pltpu.VMEM((ctx_count, rp, FF), BF),
            pltpu.VMEM((D, TILE), F32),
            pltpu.VMEM((D, FF), BF),
            pltpu.VMEM((ctx_count, rp, FF), BF),
            pltpu.VMEM((rp, cols), BF),
            square(F32),
            square(BF),
            square(BF),
            square(BF),
            square(BF),
            square(BF),
            square(BF),
            dma((n_ch,)),
            dma((n_ch, n_in - 1)),
            dma((n_ch, n_in - 1)),
            dma((n_ch, n_out - 1)),
            dma((n_ch, n_out - 1)),
            dma((MATRIX_COUNT,)),
            dma,
            dma((n_dev,)),
            dma((MATRIX_COUNT,)),
            pltpu.VMEM((ctx_count, 8, 128), F32),
            pltpu.VMEM((n_dev, 8, 128), F32),
            dma((n_dev,)),
            dma,
        ],
        compiler_params=pltpu.CompilerParams(
            collective_id=0, has_side_effects=True, vmem_limit_bytes=60 << 20
        ),
        name="tail",
    )(grads, moments, gain_grads)


class Refs:
    pass


def dot_nt(a, b):
    return lax.dot_general(a, b, (((1,), (1,)), ((), ())), preferred_element_type=F32)


def dot_tn(a, b):
    return lax.dot_general(a, b, (((0,), (0,)), ((), ())), preferred_element_type=F32)


def aligned(start, size):
    return pl.ds(pl.multiple_of(start, size), size)


def norm_parts(v, gain):
    r = lax.rsqrt(jnp.mean(v * v, axis=-1, keepdims=True) + EPS_NORM)
    return r, v * r, 1.0 + gain


def norm_back(v, gain, e):
    r, zed, g1 = norm_parts(v, gain)
    e1 = e * g1
    dv = r * (e1 - zed * jnp.mean(e1 * zed, axis=-1, keepdims=True))
    return dv, jnp.sum(e * zed, axis=0, keepdims=True)


def layer_scratch(tok):
    v = pltpu.VMEM
    dma = pltpu.SemaphoreType.DMA
    cols = sum(WIDTHS) // 2
    heads = HQ // HD
    tiles = tok // TILE
    win = WINDOW + TILE
    return dict(
        wq=v((2, D, HQ // 2), BF),
        wo=v((HQ, D), BF),
        wg=v((2, D, FF // 2), BF),
        wu=v((2, D, FF // 2), BF),
        wd=v((FF, D), BF),
        tk=v((tok, D), BF),
        ct=v((tok, D), BF),
        xa=v((tok, D), BF),
        xat=v((D, tok), BF),
        fit=v((D, tok), BF),
        ddn=v((tok, D), BF),
        ddnt=v((D, tok), BF),
        cs=v((tok, HD // 2), F32),
        sn=v((tok, HD // 2), F32),
        ka=v((WINDOW + tok, HD), BF),
        va=v((WINDOW + tok, HD), BF),
        idown=v((8, tok), jnp.int32),
        idprev=v((8, tok), jnp.int32),
        qs=v((tiles * heads, TILE, HD), BF),
        mk=v((tiles, TILE, win), BF),
        ps=v((tiles * heads, TILE, win), F32),
        ts=v((tiles * heads, TILE, win), BF),
        att=v((tok, HQ), BF),
        ao=v((tok, D), F32),
        h1=v((tok, D), F32),
        dn=v((tok, D), F32),
        dh1=v((tok, D), F32),
        yb=v((tok, D), BF),
        hid=v((2, tok, FF // 2), BF),
        a1=v((2, tok, FF // 2), BF),
        a2=v((2, tok, FF // 2), BF),
        datt=v((tok, HQ), BF),
        dka=v((WINDOW + tok, HD), F32),
        dva=v((WINDOW + tok, HD), F32),
        dks=v((2, tok, HD), BF),
        dkr=v((2, tok, HD), BF),
        dkv=v((2, tok, HD), BF),
        sb=v((IN_COUNT, D // IN_COUNT, cols), BF),
        gb=v((IN_COUNT, D // IN_COUNT, cols), BF),
        wsend=dma((5,)),
        wrecv=dma((5,)),
        wown=dma((5,)),
        ksend=dma((3,)),
        krecv=dma((3,)),
        dsend=dma((2,)),
        drecv=dma((2,)),
        csend=dma((MATRIX_COUNT, 4)),
        crecv=dma((MATRIX_COUNT, 4)),
        osend=dma((2,)),
        orecv=dma((2,)),
        oown=dma((2,)),
        tsem=dma((2,)),
    )


def layer_phases(s, ctx_count, wa_count):
    c = lax.axis_index("ctx")
    w = lax.axis_index("wa")
    other = 1 - w
    flat = c * wa_count + w
    n_dev = ctx_count * wa_count
    tok = s.xa.shape[0]
    rows = D // ctx_count
    n_out = ctx_count // IN_COUNT
    heads = HQ // HD
    tiles = tok // TILE
    win = WINDOW + TILE
    half_ff = FF // 2
    halves, offs, cols = layout(wa_count)
    step = 128
    partner = (c, other)
    follow = jnp.minimum(flat + 1, n_dev - 1)
    ahead = jnp.maximum(flat - 1, 0)
    next_id = (lax.div(follow, wa_count), lax.rem(follow, wa_count))
    prev_id = (lax.div(ahead, wa_count), lax.rem(ahead, wa_count))
    order = [zz * IN_COUNT + pp for pp in range(IN_COUNT) for zz in range(n_out)]

    def remote(src, dst, send, recv, where):
        return pltpu.make_async_remote_copy(
            src, dst, send, recv, device_id=where, device_id_type=MESH
        )

    def permuted(v):
        t = v.astype(BF).astype(F32).T
        return jnp.concatenate([t[i * rows : (i + 1) * rows] for i in order], axis=0).astype(BF)

    def per_rows(body):
        def run(i, carry):
            body(aligned(i * step, step))
            return carry

        lax.fori_loop(0, tok // step, run, 0)

    out_rows = aligned(w * tok, tok)
    tok_in = pltpu.make_async_copy(s.tok_ref.at[out_rows], s.tk, s.tsem.at[0])
    cot_in = pltpu.make_async_copy(s.cot_ref.at[out_rows], s.ct, s.tsem.at[1])
    tok_in.start()
    cot_in.start()

    wk_refs = (
        (s.wq_ref, s.wq.at[w]),
        (s.wo_ref, s.wo.at[aligned(w * (HQ // 2), HQ // 2)]),
        (s.wgu_ref.at[0], s.wg.at[w]),
        (s.wgu_ref.at[1], s.wu.at[w]),
        (s.wd_ref, s.wd.at[aligned(w * half_ff, half_ff)]),
    )
    w_far = [remote(a, b, s.wsend.at[i], s.wrecv.at[i], partner) for i, (a, b) in enumerate(wk_refs)]
    w_own = [pltpu.make_async_copy(a, b, s.wown.at[i]) for i, (a, b) in enumerate(wk_refs)]
    for far, own in zip(w_far, w_own):
        far.start()
        own.start()

    def weights_ready(i):
        w_own[i].wait()
        w_far[i].wait_recv()

    tok_in.wait()

    def first(rs):
        x = s.tk[rs].astype(F32)
        _, zed, g1 = norm_parts(x, s.gain_ref[0:1])
        n = zed * g1
        s.xa[rs] = n.astype(BF)
        s.xat[:, rs] = permuted(n)

    per_rows(first)

    cb, sb_ = s.cosb_ref[pl.ds(flat, 1), :], s.sinb_ref[pl.ds(flat, 1), :]
    s.cs[...] = cb * s.cosi_ref[...] - sb_ * s.sini_ref[...]
    s.sn[...] = sb_ * s.cosi_ref[...] + cb * s.sini_ref[...]
    hh = HD // 2

    def turn(v, cosine, sine):
        a, b = v[:, :hh], v[:, hh:]
        return jnp.concatenate([a * cosine - b * sine, b * cosine + a * sine], axis=1)

    def turn_back(v, cosine, sine):
        a, b = v[:, :hh], v[:, hh:]
        return jnp.concatenate([a * cosine + b * sine, b * cosine - a * sine], axis=1)

    s.ka[WINDOW:, :] = turn(dot32(s.xa[...], s.wkv_ref[0]), s.cs[...], s.sn[...]).astype(BF)
    s.va[WINDOW:, :] = dot32(s.xa[...], s.wkv_ref[1]).astype(BF)
    s.idown[...] = jnp.broadcast_to(s.ids_ref[pl.ds(w, 1), :], (8, tok))

    halo = [
        remote(s.ka.at[pl.ds(tok, WINDOW)], s.ka.at[pl.ds(0, WINDOW)], s.ksend.at[0], s.krecv.at[0], next_id),
        remote(s.va.at[pl.ds(tok, WINDOW)], s.va.at[pl.ds(0, WINDOW)], s.ksend.at[1], s.krecv.at[1], next_id),
        remote(s.idown, s.idprev, s.ksend.at[2], s.krecv.at[2], next_id),
    ]

    @pl.when(flat < n_dev - 1)
    def _():
        for cp in halo:
            cp.start()

    weights_ready(0)

    def project(h, carry):
        v, u = lax.div(h, heads // 2), lax.rem(h, heads // 2)
        q = dot32(s.xa[...], s.wq[v, :, aligned(u * HD, HD)])
        q = (turn(q, s.cs[...], s.sn[...]) * HD ** (-0.5)).astype(BF)
        for a in range(tiles):
            s.qs[a * heads + h] = q[a * TILE : (a + 1) * TILE]
        return carry

    lax.fori_loop(0, heads, project, 0)

    @pl.when(flat > 0)
    def _():
        for cp in halo:
            cp.wait_recv()

    @pl.when(flat == 0)
    def _():
        s.ka[0:WINDOW, :] = jnp.zeros((WINDOW, HD), BF)
        s.va[0:WINDOW, :] = jnp.zeros((WINDOW, HD), BF)
        s.idprev[...] = jnp.full((8, tok), -1, jnp.int32)

    row_ids = jnp.concatenate([s.idprev[0:1, :], s.idown[0:1, :]], axis=1)
    own_col = jnp.broadcast_to(s.idown[0:1, :], (128, tok)).T[:, 0:1]
    gap = lax.broadcasted_iota(jnp.int32, (TILE, win), 1) - lax.broadcasted_iota(
        jnp.int32, (TILE, win), 0
    )
    for a in range(tiles):
        same = own_col[a * TILE : (a + 1) * TILE] == row_ids[:, a * TILE : a * TILE + win]
        ok = jnp.logical_and(same, jnp.logical_and(gap > 0, gap <= WINDOW))
        s.mk[a] = jnp.where(ok, 1.0, 0.0).astype(BF)

    def attend(i, carry):
        a, h = lax.div(i, heads), lax.rem(i, heads)
        ks = pl.ds(pl.multiple_of(a * TILE, TILE), win)
        t = jnp.tanh(dot_nt(s.qs[i], s.ka[ks, :]) * (1.0 / SOFT_CAP))
        e = jnp.exp(SOFT_CAP * t) * s.mk[a].astype(F32)
        pr = e * (1.0 / jnp.sum(e, axis=-1, keepdims=True))
        s.ps[i] = pr
        s.ts[i] = (1.0 - t * t).astype(BF)
        o = dot32(pr.astype(BF), s.va[ks, :])
        s.att[aligned(a * TILE, TILE), aligned(h * HD, HD)] = o.astype(BF)
        return carry

    lax.fori_loop(0, tiles * heads, attend, 0)

    weights_ready(1)
    s.ao[...] = dot32(s.att[...], s.wo[...])

    def second(rs):
        _, zed, g1 = norm_parts(s.ao[rs], s.gain_ref[1:2])
        h = s.tk[rs].astype(F32) + zed * g1
        s.h1[rs] = h
        _, zed, g1 = norm_parts(h, s.gain_ref[2:3])
        n = zed * g1
        s.xa[rs] = n.astype(BF)
        s.fit[:, rs] = permuted(n)

    per_rows(second)

    weights_ready(2)
    weights_ready(3)
    root = 0.7978845608028654

    def forward(i, carry):
        v, u = lax.div(i, 4), lax.rem(i, 4)
        us = aligned(u * TILE, TILE)
        gt = dot32(s.xa[...], s.wg[v, :, us])
        up = dot32(s.xa[...], s.wu[v, :, us])
        g2 = gt * gt
        th = jnp.tanh(root * gt * (1.0 + 0.044715 * g2))
        lift = 0.5 * (1.0 + th)
        act = gt * lift
        slope = lift + 0.5 * gt * (1.0 - th * th) * (root * (1.0 + 3.0 * 0.044715 * g2))
        s.hid[v, :, us] = (act * up).astype(BF)
        s.a1[v, :, us] = (up * slope).astype(BF)
        s.a2[v, :, us] = act.astype(BF)
        return carry

    lax.fori_loop(0, 8, forward, 0)
    weights_ready(4)
    s.dn[...] = dot32(s.hid[0], s.wd[:half_ff]) + dot32(s.hid[1], s.wd[half_ff:])
    s.dg_ref[...] = jnp.zeros_like(s.dg_ref)

    def third(rs):
        dn = s.dn[rs]
        _, zed, g1 = norm_parts(dn, s.gain_ref[3:4])
        s.yb[rs] = (s.h1[rs] + zed * g1).astype(BF)
        dv, dg = norm_back(dn, s.gain_ref[3:4], s.ct[rs].astype(F32))
        s.dg_ref[3:4] += dg
        s.ddn[rs] = dv.astype(BF)
        s.ddnt[:, rs] = permuted(dv)

    cot_in.wait()
    per_rows(third)
    y_far = remote(s.yb, s.y_ref.at[out_rows], s.osend.at[0], s.orecv.at[0], partner)
    y_own = pltpu.make_async_copy(s.yb, s.y_ref.at[out_rows], s.oown.at[0])
    y_far.start()
    y_own.start()

    def part(m, u, width):
        return pl.ds(pl.multiple_of(offs[m] + u * width, 128), width)

    def exchange(m, u, width):
        ps = part(m, u, width)
        return remote(s.sb.at[:, :, ps], s.gb.at[:, :, ps], s.csend.at[m, u], s.crecv.at[m, u], partner)

    def give(m, u, width, value):
        s.sb[:, :, part(m, u, width)] = value.astype(BF).reshape(IN_COUNT, D // IN_COUNT, width)
        exchange(m, u, width).start()

    def keep(m, u, width, value):
        ps = part(m, u, width)
        exchange(m, u, width).wait_recv()
        total = value.reshape(IN_COUNT, D // IN_COUNT, width) + s.gb[:, :, ps].astype(F32)
        s.gb[:, :, ps] = total.astype(BF)

    def ffn_back(v, put):
        def run(u, carry):
            us = aligned(u * TILE, TILE)
            dh = dot_nt(s.ddn[...], s.wd[aligned((v * 4 + u) * TILE, TILE), :])
            dgt = (dh * s.a1[v, :, us].astype(F32)).astype(BF)
            dup = (dh * s.a2[v, :, us].astype(F32)).astype(BF)
            s.a1[v, :, us] = dgt
            s.a2[v, :, us] = dup
            put(0, u, TILE, dot32(s.ddnt[...], s.hid[v, :, us]))
            put(1, u, TILE, dot32(s.fit[...], dgt))
            put(2, u, TILE, dot32(s.fit[...], dup))
            return carry

        lax.fori_loop(0, 4, run, 0)

    ffn_back(other, give)
    ffn_back(w, keep)
    s.chunk_done(0)
    s.chunk_done(1)
    s.chunk_done(2)
    s.dn[...] = (
        dot_nt(s.a1[0], s.wg[0])
        + dot_nt(s.a1[1], s.wg[1])
        + dot_nt(s.a2[0], s.wu[0])
        + dot_nt(s.a2[1], s.wu[1])
    )

    def fourth(rs):
        dv, dg = norm_back(s.h1[rs], s.gain_ref[2:3], s.dn[rs])
        s.dg_ref[2:3] += dg
        dh = s.ct[rs].astype(F32) + dv
        s.dh1[rs] = dh
        dv, dg = norm_back(s.ao[rs], s.gain_ref[1:2], dh)
        s.dg_ref[1:2] += dg
        s.ddn[rs] = dv.astype(BF)
        s.ddnt[:, rs] = permuted(dv)

    per_rows(fourth)

    def out_back(v, put):
        def run(u, carry):
            hs = aligned((v * 2 + u) * HD, HD)
            s.datt[:, hs] = dot_nt(s.ddn[...], s.wo[hs, :]).astype(BF)
            put(3, u, HD, dot32(s.ddnt[...], s.att[:, hs]))
            return carry

        lax.fori_loop(0, 2, run, 0)

    out_back(other, give)
    out_back(w, keep)

    s.dka[...] = jnp.zeros_like(s.dka)
    s.dva[...] = jnp.zeros_like(s.dva)

    def attend_back(i, carry):
        a, h = lax.div(i, heads), lax.rem(i, heads)
        ks = pl.ds(pl.multiple_of(a * TILE, TILE), win)
        qr = aligned(a * TILE, TILE)
        hs = aligned(h * HD, HD)
        do = s.datt[qr, hs]
        pr = s.ps[i]
        s.dva[ks, :] += dot_tn(pr.astype(BF), do)
        dp = dot_nt(do, s.va[ks, :])
        inner = jnp.sum(pr * dp, axis=-1, keepdims=True)
        ds = (pr * (dp - inner) * s.ts[i].astype(F32)).astype(BF)
        s.dka[ks, :] += dot_tn(ds, s.qs[i])
        dq = dot32(ds, s.ka[ks, :])
        s.datt[qr, hs] = (turn_back(dq, s.cs[qr], s.sn[qr]) * HD ** (-0.5)).astype(BF)
        return carry

    lax.fori_loop(0, tiles * heads, attend_back, 0)

    s.dks[0] = s.dka[0:WINDOW, :].astype(BF)
    s.dks[1] = s.dva[0:WINDOW, :].astype(BF)
    d_halo = [
        remote(s.dks.at[i], s.dkr.at[i], s.dsend.at[i], s.drecv.at[i], prev_id) for i in range(2)
    ]

    @pl.when(flat > 0)
    def _():
        for cp in d_halo:
            cp.start()

    def query_back(v, put):
        def run(u, carry):
            hs = aligned((v * 2 + u) * HD, HD)
            put(4, u, HD, dot32(s.xat[...], s.datt[:, hs]))
            return carry

        lax.fori_loop(0, 2, run, 0)

    query_back(other, give)
    s.dn[...] = dot_nt(s.datt[:, : HQ // 2], s.wq[0]) + dot_nt(s.datt[:, HQ // 2 :], s.wq[1])
    query_back(w, keep)

    @pl.when(flat < n_dev - 1)
    def _():
        for cp in d_halo:
            cp.wait_recv()

    @pl.when(flat == n_dev - 1)
    def _():
        s.dkr[...] = jnp.zeros_like(s.dkr)

    dk = s.dka[tok:, :] + s.dkr[0].astype(F32)
    s.dkv[0] = turn_back(dk, s.cs[...], s.sn[...]).astype(BF)
    s.dkv[1] = (s.dva[tok:, :] + s.dkr[1].astype(F32)).astype(BF)
    kvw = HD // 2
    for i in range(2):
        give(5 + i, 0, kvw, dot32(s.xat[...], s.dkv[i, :, aligned(other * kvw, kvw)]))
    for i in range(2):
        keep(5 + i, 0, kvw, dot32(s.xat[...], s.dkv[i, :, aligned(w * kvw, kvw)]))
    s.chunk_done(3)
    s.dn[...] += dot_nt(s.dkv[0], s.wkv_ref[0]) + dot_nt(s.dkv[1], s.wkv_ref[1])

    def fifth(rs):
        dv, dg = norm_back(s.tk[rs].astype(F32), s.gain_ref[0:1], s.dn[rs])
        s.dg_ref[0:1] += dg
        s.h1[rs] = s.dh1[rs] + dv

    per_rows(fifth)
    x_far = remote(s.h1, s.x_ref.at[out_rows], s.osend.at[1], s.orecv.at[1], partner)
    x_own = pltpu.make_async_copy(s.h1, s.x_ref.at[out_rows], s.oown.at[1])
    x_far.start()
    x_own.start()

    def finish():
        for cp in w_far:
            cp.wait_send()

        @pl.when(flat < n_dev - 1)
        def _():
            for cp in halo:
                cp.wait_send()

        @pl.when(flat > 0)
        def _():
            for cp in d_halo:
                cp.wait_send()

        for m, count, width in ((0, 4, TILE), (1, 4, TILE), (2, 4, TILE), (3, 2, HD), (4, 2, HD), (5, 1, kvw), (6, 1, kvw)):
            for u in range(count):
                exchange(m, u, width).wait_send()
        y_own.wait()
        x_own.wait()
        y_far.wait()
        x_far.wait()

    return finish


LAYER_INPUTS = (
    "tok_ref",
    "cot_ref",
    "ids_ref",
    "gain_ref",
    "wkv_ref",
    "cosi_ref",
    "sini_ref",
    "cosb_ref",
    "sinb_ref",
    "wq_ref",
    "wo_ref",
    "wgu_ref",
    "wd_ref",
)


def layer_kernel(ctx_count, wa_count, names, *refs):
    s = Refs()
    for name, ref in zip(names, refs):
        setattr(s, name, ref)
    s.chunk_done = lambda ci: None
    c = lax.axis_index("ctx")
    w = lax.axis_index("wa")
    flat = c * wa_count + w
    n_dev = ctx_count * wa_count
    barrier = pltpu.get_barrier_semaphore()

    def greet(i, carry):
        other = lax.rem(flat + i, n_dev)
        pl.semaphore_signal(
            barrier,
            inc=1,
            device_id=(lax.div(other, wa_count), lax.rem(other, wa_count)),
            device_id_type=MESH,
        )
        return carry

    lax.fori_loop(1, n_dev, greet, 0)
    pl.semaphore_wait(barrier, n_dev - 1)
    finish = layer_phases(s, ctx_count, wa_count)
    out = pltpu.make_async_copy(s.gb, s.g_ref, s.gout)
    out.start()
    finish()
    out.wait()


def rotation_tables(tok, n_dev):
    freq = ROPE_BASE ** (-2.0 * np.arange(HD // 2) / HD)
    inner = np.arange(tok)[:, None] * freq[None, :]
    base = (np.arange(n_dev) * tok)[:, None] * freq[None, :]
    return [jnp.asarray(f(a), F32) for a in (inner, base) for f in (np.cos, np.sin)]


def run_layer(tokens, cotangent, seq_ids, gains, wkv, wq, wo, wgu, wd, ctx_count, wa_count):
    block = tokens.shape[0]
    tok = block // wa_count
    n_dev = ctx_count * wa_count
    scratch = layer_scratch(tok)
    scratch["gout"] = pltpu.SemaphoreType.DMA
    names = LAYER_INPUTS + ("y_ref", "x_ref", "g_ref", "dg_ref") + tuple(scratch)
    any_space = pl.BlockSpec(memory_space=pl.ANY)
    vmem = pl.BlockSpec(memory_space=pltpu.VMEM)
    cols = layout(wa_count)[2]
    return pl.pallas_call(
        partial(layer_kernel, ctx_count, wa_count, names),
        out_shape=(
            jax.ShapeDtypeStruct((block, D), BF),
            jax.ShapeDtypeStruct((block, D), F32),
            jax.ShapeDtypeStruct((IN_COUNT, D // IN_COUNT, cols), BF),
            jax.ShapeDtypeStruct((8, D), F32),
        ),
        in_specs=[any_space] * 2 + [vmem] * 7 + [any_space] * 4,
        out_specs=(any_space, any_space, any_space, vmem),
        scratch_shapes=list(scratch.values()),
        compiler_params=pltpu.CompilerParams(
            collective_id=1, has_side_effects=True, vmem_limit_bytes=61 << 20
        ),
        name="layer",
    )(
        tokens,
        cotangent,
        seq_ids.reshape(wa_count, tok),
        gains,
        wkv,
        *rotation_tables(tok, n_dev),
        wq,
        wo,
        wgu,
        wd,
    )


def per_device(
    tokens,
    cotangent,
    seq_ids,
    w_query,
    w_keyval,
    w_out,
    w_gateup,
    w_down,
    norm_gains,
    mom_query,
    mom_keyval,
    mom_out,
    mom_gateup,
    mom_down,
    gain_first,
    gain_second,
):
    ctx_count = lax.axis_size("ctx")
    wa_count = lax.axis_size("wa")
    block_out, input_grad, stack, grad_gains = run_layer(
        tokens,
        cotangent,
        seq_ids,
        norm_gains,
        w_keyval,
        w_query,
        w_out,
        w_gateup,
        w_down,
        ctx_count,
        wa_count,
    )
    moments = jnp.concatenate(
        [
            mom_down.T,
            mom_gateup[0],
            mom_gateup[1],
            mom_out.T,
            mom_query,
            mom_keyval[0],
            mom_keyval[1],
        ],
        axis=1,
    )
    sums, fresh, updates, sum_gains = run_tail(stack, moments, grad_gains, ctx_count, wa_count)
    halves, offs, _ = layout(wa_count)

    def unstack(flat):
        down, gate, up, out, query, key, value = [
            flat[:, o : o + h] for o, h in zip(offs, halves)
        ]
        return (query, jnp.stack([key, value]), out.T, jnp.stack([gate, up]), down.T)

    sum_query, sum_keyval, sum_out, sum_gateup, sum_down = unstack(sums)
    new_mom_query, new_mom_keyval, new_mom_out, new_mom_gateup, new_mom_down = unstack(fresh)
    upd_query, upd_keyval, upd_out, upd_gateup, upd_down = unstack(updates)
    sum_gains = sum_gains[:4, : D // ctx_count]
    new_gain_first = ADAM_ONE * gain_first + (1.0 - ADAM_ONE) * sum_gains
    new_gain_second = ADAM_TWO * gain_second + (1.0 - ADAM_TWO) * sum_gains * sum_gains
    gain_update = -GAIN_RATE * new_gain_first / (jnp.sqrt(new_gain_second) + ADAM_EPS)
    return (
        block_out,
        input_grad,
        sum_query,
        sum_keyval,
        sum_out,
        sum_gateup,
        sum_down,
        sum_gains,
        new_mom_query,
        new_mom_keyval,
        new_mom_out,
        new_mom_gateup,
        new_mom_down,
        upd_query,
        upd_keyval,
        upd_out,
        upd_gateup,
        upd_down,
        new_gain_first,
        new_gain_second,
        gain_update,
    )


def solution(mesh):
    in_specs = (
        P("ctx", None),
        P("ctx", None),
        P("ctx"),
        P(None, "wa"),
        P(),
        P("wa", None),
        P(None, None, "wa"),
        P("wa", None),
        P(),
        P("ctx", "wa"),
        P(None, "ctx", "wa"),
        P("wa", "ctx"),
        P(None, "ctx", "wa"),
        P("wa", "ctx"),
        P(None, "ctx"),
        P(None, "ctx"),
    )
    out_specs = (
        P("ctx", None),
        P("ctx", None),
        P("ctx", "wa"),
        P(None, "ctx", "wa"),
        P("wa", "ctx"),
        P(None, "ctx", "wa"),
        P("wa", "ctx"),
        P(None, "ctx"),
        P("ctx", "wa"),
        P(None, "ctx", "wa"),
        P("wa", "ctx"),
        P(None, "ctx", "wa"),
        P("wa", "ctx"),
        P("ctx", "wa"),
        P(None, "ctx", "wa"),
        P("wa", "ctx"),
        P(None, "ctx", "wa"),
        P("wa", "ctx"),
        P(None, "ctx"),
        P(None, "ctx"),
        P(None, "ctx"),
    )
    return jax.shard_map(
        per_device, mesh=mesh, in_specs=in_specs, out_specs=out_specs, check_vma=False
    )
```

```python
from functools import partial
import math

import jax
import jax.numpy as jnp
import numpy as np
from jax import lax
from jax.experimental import pallas as pl
from jax.experimental.pallas import tpu as pltpu
from jax.sharding import PartitionSpec as P

D = 640
FF = 2048
HD = 256
WINDOW = 512
SOFT_CAP = 10
NS_STEPS = 5
HQ = 1024


EPS_NORM = 1e-06
ROPE_BASE = 10000.0
MOMENTUM = 0.95
ADAM_ONE = 0.9
ADAM_TWO = 0.95
ADAM_EPS = 1e-08
GAIN_RATE = 0.1
QUINTIC_A = 3.4445
QUINTIC_B = -4.775
QUINTIC_C = 2.0315
MATRIX_COUNT = 7
MUON_RATE = 0.2

MESH = pl.DeviceIdType.MESH
BF = jnp.bfloat16
F32 = jnp.float32
IN_COUNT = 4
NAMES = ("down", "gate", "up", "out", "query", "key", "value")
WIDTHS = (FF, FF, FF, HQ, HQ, HD, HD)
OWNERS = (7, 4, 8, 5, 11, 9, 10)
CHUNK_SETS = ((0,), (1,), (2,), (3, 4), (5, 6))
TILE = 256


def layout(wa_count):
    halves = [w // wa_count for w in WIDTHS]
    offs = [sum(halves[:i]) for i in range(len(halves))]
    return halves, offs, sum(halves)


def dot32(a, b):
    return jnp.dot(a, b, preferred_element_type=F32)


def eye_mask(n):
    return (
        lax.broadcasted_iota(jnp.int32, (n, n), 0) == lax.broadcasted_iota(jnp.int32, (n, n), 1)
    )


def pad_rows(v, rows):
    if v.shape[0] == rows:
        return v
    return jnp.concatenate([v, jnp.zeros((rows - v.shape[0], v.shape[1]), v.dtype)], axis=0)


def split_into(v, hi, lo):
    top = v.astype(BF)
    hi[...] = top
    lo[...] = (v - top.astype(F32)).astype(BF)


SYM_TILES = ((0, 256), (256, 512), (512, 640))


def sym_tiles(out, block):
    for a, b in SYM_TILES:
        v = block(a, b)
        out[a:, a:b] = v
        if b < D:
            out[a:b, b:] = v[b - a :].T


def prod3(h1, l1, h2, l2):
    return lambda a, b: (
        dot32(h1[a:], h2[:, a:b]) + dot32(h1[a:], l2[:, a:b]) + dot32(l1[a:], h2[:, a:b])
    )


def tail_scratch(ctx_count, wa_count):
    v = pltpu.VMEM
    dma = pltpu.SemaphoreType.DMA
    n_in = IN_COUNT
    n_out = ctx_count // n_in
    rows = D // ctx_count
    rp = -(-rows // 16) * 16
    n_dev = ctx_count * wa_count
    n_ch = len(CHUNK_SETS)
    cols = layout(wa_count)[2]
    return dict(
        mb=v((rp, cols), BF),
        xb=v((ctx_count, rp, FF), BF),
        am=v((D, D), F32),
        dg_ref=v((8, D), F32),
        dgs=v((ctx_count, 8, 128), F32),
        dgr=v((n_dev, 8, 128), F32),
        psend=dma((n_ch, n_in - 1)),
        precv=dma((n_ch, n_in - 1)),
        lsend=dma((n_ch, n_out - 1)),
        lrecv=dma((n_ch, n_out - 1)),
        gsend=dma((MATRIX_COUNT,)),
        grecv=dma,
        usend=dma((n_dev,)),
        urecv=dma((MATRIX_COUNT,)),
        gnsend=dma((n_dev,)),
        gnrecv=dma,
        msem=dma((MATRIX_COUNT,)),
        pfree=pltpu.SemaphoreType.REGULAR,
        lfree=pltpu.SemaphoreType.REGULAR,
    )


def tail_phases(s, ctx_count, wa_count):
    c = lax.axis_index("ctx")
    w = lax.axis_index("wa")
    n_in = IN_COUNT
    n_out = ctx_count // n_in
    n_dev = ctx_count * wa_count
    p = lax.rem(c, n_in)
    z = lax.div(c, n_in)
    rows = D // ctx_count
    rp = s.xb.shape[1]
    block = D // n_in
    halves, offs, cols = layout(wa_count)
    chunks = [(offs[m[0]], sum(halves[i] for i in m)) for m in CHUNK_SETS]
    me = c * wa_count + w
    per = ctx_count // 2

    def plane_slot(ci, k):
        i = min(ci, 4) * (n_in - 1) + (k - 1 if ci < 4 else 0)
        buf = (s.wg, s.wu)[i // 8]
        lanes = pl.ds(0, chunks[ci][1]) if ci < 4 else pl.ds((k - 1) * TILE, TILE)
        return buf.at[i % 8 // 4, pl.ds(i % 4 * block, block), lanes]

    def line_slot(base, ci, j):
        wid = chunks[ci][1]
        if ci < 4:
            start = ci % 2 * 256 + j * rp
            return s.ffb.at[base * 2 + ci // 2, pl.ds(pl.multiple_of(start, 16), rp), pl.ds(0, wid)]
        return s.ffb.at[4 + base, pl.ds(pl.multiple_of(j * rp, 16), rp), pl.ds(0, wid)]

    def plane_copy(ci, k):
        off, wid = chunks[ci]
        q = lax.rem(p + k, n_in)
        return pltpu.make_async_remote_copy(
            s.gb.at[q, :, pl.ds(off, wid)],
            plane_slot(ci, k),
            s.psend.at[ci, k - 1],
            s.precv.at[ci, k - 1],
            device_id=(z * n_in + q, w),
            device_id_type=MESH,
        )

    def line_copy(ci, k):
        j = lax.rem(z + k, n_out)
        return pltpu.make_async_remote_copy(
            line_slot(0, ci, j),
            line_slot(1, ci, k - 1),
            s.lsend.at[ci, k - 1],
            s.lrecv.at[ci, k - 1],
            device_id=(j * n_in + p, w),
            device_id_type=MESH,
        )

    def buffers_free():
        for k in range(1, n_in):
            pl.semaphore_signal(
                s.pfree,
                inc=1,
                device_id=(z * n_in + lax.rem(p + k, n_in), w),
                device_id_type=MESH,
            )
        for k in range(1, n_out):
            pl.semaphore_signal(
                s.lfree,
                inc=1,
                device_id=(lax.rem(z + k, n_out) * n_in + p, w),
                device_id_type=MESH,
            )

    def plane_start(ci):
        for k in range(1, n_in):
            plane_copy(ci, k).start()

    def first_sends():
        pl.semaphore_wait(s.pfree, n_in - 1)
        for ci in range(3):
            plane_start(ci)

    def plane_finish(ci):
        off, wid = chunks[ci]
        for k in range(1, n_in):
            plane_copy(ci, k).wait_recv()

        def plane_sum(t, carry):
            cs = aligned(off + t * TILE, TILE)
            here = aligned(t * TILE, TILE)
            total = s.gb[p, :, cs].astype(F32)
            for k in range(1, n_in):
                total = total + plane_slot(ci, k)[:, here].astype(F32)
            for j in range(n_out):
                slab = total[j * rows : (j + 1) * rows]

                @pl.when(z == j)
                def _():
                    s.sum_ref[:, cs] = slab

                line_slot(0, ci, j)[:, here] = pad_rows(slab, rp).astype(BF)
            return carry

        lax.fori_loop(0, wid // TILE, plane_sum, 0)
        if ci == 0:
            pl.semaphore_wait(s.lfree, n_out - 1)
        for k in range(1, n_out):
            line_copy(ci, k).start()

    def gather_copy(m, local):
        src = s.mb.at[:, pl.ds(offs[m], halves[m])]
        dst = s.xb.at[c, :, pl.ds(pl.multiple_of(w * halves[m], 128), halves[m])]
        if local:
            return pltpu.make_async_copy(src, dst, s.grecv)
        return pltpu.make_async_remote_copy(
            src, dst, s.gsend.at[m], s.grecv, device_id=(OWNERS[m], 0), device_id_type=MESH
        )

    def line_finish(ci):
        off, wid = chunks[ci]
        for k in range(1, n_out):
            line_copy(ci, k).wait_recv()

        def line_sum(t, carry):
            cs = aligned(off + t * TILE, TILE)
            here = aligned(t * TILE, TILE)
            total = s.sum_ref[:, cs]
            for k in range(n_out - 1):
                total = total + line_slot(1, ci, k)[:, here][:rows].astype(F32)
            s.sum_ref[:, cs] = total
            fresh = MOMENTUM * s.nm_ref[:, cs] + total
            s.nm_ref[:, cs] = fresh
            s.mb[:, cs] = pad_rows(fresh, rp).astype(BF)
            return carry

        lax.fori_loop(0, wid // TILE, line_sum, 0)
        for m in CHUNK_SETS[ci]:
            mine = me == OWNERS[m] * wa_count

            @pl.when(mine)
            def _():
                gather_copy(m, True).start()

            @pl.when(jnp.logical_not(mine))
            def _():
                gather_copy(m, False).start()

    s.buffers_free = buffers_free
    s.first_sends = first_sends
    s.plane_start = plane_start
    s.plane_finish = plane_finish

    sources = (
        s.md_ref,
        s.mgu_ref.at[0],
        s.mgu_ref.at[1],
        s.mo_ref,
        s.mq_ref,
        s.mkv_ref.at[0],
        s.mkv_ref.at[1],
    )
    moms = [
        pltpu.make_async_copy(src, s.nm_ref.at[:, pl.ds(offs[m], halves[m])], s.msem.at[m])
        for m, src in enumerate(sources)
    ]
    for cp in moms:
        cp.start()

    def rest():
        for i in range(ctx_count):
            s.dgs[i, :, 0:rows] = s.dg_ref[:, i * rows : (i + 1) * rows]

        def gain_copy(t):
            i, v = lax.div(t, wa_count), lax.rem(t, wa_count)
            return pltpu.make_async_remote_copy(
                s.dgs.at[i],
                s.dgr.at[me],
                s.gnsend.at[t],
                s.gnrecv,
                device_id=(i, v),
                device_id_type=MESH,
            )

        def gain_send(t, carry):
            gain_copy(lax.rem(me + t, n_dev)).start()
            return carry

        def gain_sent(t, carry):
            gain_copy(lax.rem(me + t, n_dev)).wait_send()
            return carry

        for cp in moms:
            cp.wait()
        plane_finish(2)
        line_finish(0)
        line_finish(1)
        plane_finish(3)
        plane_finish(4)
        line_finish(2)
        pltpu.make_async_copy(s.dgs.at[c], s.dgr.at[me], s.gnrecv).start()
        lax.fori_loop(1, n_dev, gain_send, 0)
        line_finish(3)
        line_finish(4)
        for ci in range(len(chunks)):
            for k in range(1, n_in):
                plane_copy(ci, k).wait_send()
            for k in range(1, n_out):
                line_copy(ci, k).wait_send()
        solve()
        pltpu.make_async_copy(s.dgr, s.dgr, s.gnrecv).wait()
        s.gs_ref[...] = jnp.sum(s.dgr[...], axis=0)
        lax.fori_loop(1, n_dev, gain_sent, 0)
        updates_back()

    def owned_by(*which):
        hit = me == OWNERS[which[0]] * wa_count
        for m in which[1:]:
            hit = jnp.logical_or(hit, me == OWNERS[m] * wa_count)
        return hit

    def solve():
        is_owner = owned_by(*range(MATRIX_COUNT))
        is_small = owned_by(5, 6)
        is_wide = owned_by(0, 1, 2)
        tiles = jnp.where(is_small, HD // TILE, jnp.where(is_wide, FF // TILE, HQ // TILE))
        am, xf = s.am, s.dka.at[pl.ds(0, D)]
        ah = s.wd.at[pl.ds(0, D)]
        al = s.wd.at[pl.ds(D, D)]
        ph = s.wd.at[pl.ds(2 * D, D)]
        plo = s.wo.at[pl.ds(0, D)]
        qh = s.wu.at[0, :, pl.ds(0, D)]

        def tile_of(t):
            return s.wg.at[lax.div(t, 4), :, aligned(lax.rem(t, 4) * TILE, TILE)]

        for m in range(MATRIX_COUNT):

            @pl.when(me == OWNERS[m] * wa_count)
            def _(m=m):
                whole = s.xb.at[:, :, pl.ds(0, halves[m] * wa_count)]
                pltpu.make_async_copy(whole, whole, s.grecv).wait()

        @pl.when(is_owner)
        def _():
            am[...] = jnp.zeros_like(am)

            def gram(t, carry):
                cs = aligned(t * TILE, TILE)
                for i in range(ctx_count):
                    xf[i * rows : (i + 1) * rows, :] = s.xb[i, :, cs][:rows].astype(F32)
                x = xf[...].astype(BF)
                tile_of(t)[...] = x

                @pl.when(jnp.logical_not(is_small))
                def _():
                    for a, b in SYM_TILES:
                        am[a:, a:b] += dot_nt(x[a:], x[a:b])

                @pl.when(is_small)
                def _():
                    am[0:HD, 0:HD] = dot_tn(x, x)

                return carry

            lax.fori_loop(0, tiles, gram, 0)
            norm2 = jnp.sum(jnp.where(eye_mask(D), am[...], 0.0), keepdims=True)
            inv = 1.0 / (jnp.sqrt(norm2) + 1e-07)
            inv2 = inv * inv
            sym_tiles(am, lambda a, b: am[a:, a:b] * inv2)

            def shifted(a, b, square):
                rest = QUINTIC_B * am[a:, a:b] + QUINTIC_C * square
                top = rest[: b - a] + jnp.where(eye_mask(b - a), QUINTIC_A, 0.0)
                return jnp.concatenate([top, rest[b - a :]], axis=0) if b < D else top

            def poly():
                split_into(am[...], ah, al)
                square = prod3(ah, al, ah, al)
                sym_tiles(am, lambda a, b: shifted(a, b, square(a, b)))

            def advance():
                sym_tiles(am, prod3(ph, plo, ah, al))
                split_into(am[...], ah, al)
                sym_tiles(am, prod3(ah, al, ph, plo))

            def grow():
                sym_tiles(am, lambda a, b: dot32(ph[a:], qh[:, a:b]))
                qh[...] = am[...].astype(BF)

            poly()
            split_into(am[...], ph, plo)
            qh[...] = ph[...]
            advance()

            def sweep(i, carry):
                poly()
                split_into(am[...], ph, plo)
                grow()
                advance()
                return carry

            lax.fori_loop(0, NS_STEPS - 2, sweep, 0)
            ah[...] = am[...].astype(BF)
            sym_tiles(am, lambda a, b: shifted(a, b, dot32(ah[a:], ah[:, a:b])))
            ph[...] = am[...].astype(BF)
            grow()
            rates = [-MUON_RATE * 0.2 * math.sqrt(n) for n in (D, FF, HQ)]
            rate = jnp.where(is_small, rates[0], jnp.where(is_wide, rates[1], rates[2]))
            scale = rate * inv

            def put(v, lanes, value):
                for i in range(ctx_count):
                    s.ffb[v * 2 + i // per, i % per * rp : (i % per + 1) * rp, lanes] = pad_rows(
                        value[i * rows : (i + 1) * rows], rp
                    ).astype(BF)

            def back(v, t):
                @pl.when(jnp.logical_not(is_small))
                def _():
                    whole = v * jnp.where(is_wide, 4, 2) + t
                    xf[...] = dot32(qh[...], tile_of(whole)[...]) * scale
                    put(v, aligned(t * TILE, TILE), xf)

                @pl.when(is_small)
                def _():
                    xf[...] = dot32(tile_of(t)[...], s.wu[0, 0:HD, 0:HD]) * scale
                    for half in range(2):
                        lanes = slice(half * (HD // 2), (half + 1) * (HD // 2))
                        put(half, pl.ds(0, HD // 2), xf[:, lanes])

            for v in range(2):
                count = jnp.where(is_small, 1 - v, jnp.where(is_wide, 4, 2))

                def run(t, carry, v=v):
                    back(v, t)
                    return carry

                lax.fori_loop(0, count, run, 0)
                for m in range(MATRIX_COUNT):

                    @pl.when(me == OWNERS[m] * wa_count)
                    def _(m=m, v=v):
                        def send(i, carry):
                            there = lax.rem(c + i, ctx_count)
                            update_copy(m, there * wa_count + v, False).start()
                            return carry

                        if v == 0:
                            update_copy(m, c * wa_count, True).start()
                            lax.fori_loop(1, ctx_count, send, 0)
                        else:
                            lax.fori_loop(0, ctx_count, send, 0)

    def update_copy(m, t, local):
        i, v = lax.div(t, wa_count), lax.rem(t, wa_count)
        start = pl.multiple_of(lax.rem(i, per) * rp, 16)
        src = s.ffb.at[v * 2 + lax.div(i, per), pl.ds(start, rp), pl.ds(0, halves[m])]
        dst = s.ub.at[:, pl.ds(offs[m], halves[m])]
        if local:
            return pltpu.make_async_copy(src, dst, s.urecv.at[m])
        return pltpu.make_async_remote_copy(
            src, dst, s.usend.at[t], s.urecv.at[m], device_id=(i, v), device_id_type=MESH
        )

    def updates_back():
        for m in range(MATRIX_COUNT):
            piece = s.ub.at[:, pl.ds(offs[m], halves[m])]
            pltpu.make_async_copy(piece, piece, s.urecv.at[m]).wait()

        for m in range(MATRIX_COUNT):
            owner = OWNERS[m] * wa_count

            @pl.when(me != owner)
            def _(m=m):
                gather_copy(m, False).wait_send()

            @pl.when(me == owner)
            def _(m=m, owner=owner):
                def done(t, carry):
                    update_copy(m, lax.rem(owner + t, n_dev), False).wait_send()
                    return carry

                lax.fori_loop(1, n_dev, done, 0)

    return rest


class Refs:
    pass


def dot_nt(a, b):
    return lax.dot_general(a, b, (((1,), (1,)), ((), ())), preferred_element_type=F32)


def dot_tn(a, b):
    return lax.dot_general(a, b, (((0,), (0,)), ((), ())), preferred_element_type=F32)


def aligned(start, size):
    return pl.ds(pl.multiple_of(start, size), size)


def norm_parts(v, gain):
    r = lax.rsqrt(jnp.mean(v * v, axis=-1, keepdims=True) + EPS_NORM)
    return r, v * r, 1.0 + gain


def norm_back(v, gain, e):
    r, zed, g1 = norm_parts(v, gain)
    e1 = e * g1
    dv = r * (e1 - zed * jnp.mean(e1 * zed, axis=-1, keepdims=True))
    return dv, jnp.sum(e * zed, axis=0, keepdims=True)


def layer_scratch(tok):
    v = pltpu.VMEM
    dma = pltpu.SemaphoreType.DMA
    cols = sum(WIDTHS) // 2
    heads = HQ // HD
    tiles = tok // TILE
    win = WINDOW + TILE
    return dict(
        wq=v((2, D, HQ // 2), BF),
        wo=v((HQ, D), BF),
        wg=v((2, D, FF // 2), BF),
        wu=v((2, D, FF // 2), BF),
        wd=v((FF, D), BF),
        tk=v((tok, D), BF),
        ct=v((tok, D), BF),
        xa=v((tok, D), BF),
        xat=v((D, tok), BF),
        fit=v((D, tok), BF),
        ddn=v((tok, D), BF),
        ddnt=v((D, tok), BF),
        cs=v((tok, HD // 2), F32),
        sn=v((tok, HD // 2), F32),
        ka=v((WINDOW + tok, HD), BF),
        va=v((WINDOW + tok, HD), BF),
        idown=v((8, tok), jnp.int32),
        idprev=v((8, tok), jnp.int32),
        qs=v((tiles * heads, TILE, HD), BF),
        ps=v((tiles * heads, TILE, win), BF),
        ts=v((tiles * heads, TILE, win), BF),
        att=v((tok, HQ), BF),
        ao=v((tok, D), F32),
        h1=v((tok, D), F32),
        dn=v((tok, D), F32),
        ffb=v((6, tok, FF // 2), BF),
        datt=v((tok, HQ), BF),
        dka=v((WINDOW + tok, HD), F32),
        dva=v((WINDOW + tok, HD), F32),
        dks=v((2, tok, HD), BF),
        dkr=v((2, tok, HD), BF),
        dkv=v((2, tok, HD), BF),
        sb=v((6, IN_COUNT, D // IN_COUNT, TILE), BF),
        gb=v((IN_COUNT, D // IN_COUNT, cols), BF),
        wsend=dma((5,)),
        wrecv=dma((5,)),
        wown=dma((5,)),
        ksend=dma((3,)),
        krecv=dma((3,)),
        dsend=dma((2,)),
        drecv=dma((2,)),
        csend=dma((MATRIX_COUNT, 4)),
        crecv=dma((MATRIX_COUNT, 4)),
        osend=dma((2,)),
        orecv=dma((2,)),
        oown=dma((2,)),
        tsem=dma((4,)),
    )


def layer_phases(s, ctx_count, wa_count):
    c = lax.axis_index("ctx")
    w = lax.axis_index("wa")
    other = 1 - w
    flat = c * wa_count + w
    n_dev = ctx_count * wa_count
    tok = s.xa.shape[0]
    rows = D // ctx_count
    n_out = ctx_count // IN_COUNT
    heads = HQ // HD
    tiles = tok // TILE
    win = WINDOW + TILE
    half_ff = FF // 2
    halves, offs, cols = layout(wa_count)
    step = 128
    partner = (c, other)
    follow = jnp.minimum(flat + 1, n_dev - 1)
    ahead = jnp.maximum(flat - 1, 0)
    next_id = (lax.div(follow, wa_count), lax.rem(follow, wa_count))
    prev_id = (lax.div(ahead, wa_count), lax.rem(ahead, wa_count))
    order = [zz * IN_COUNT + pp for pp in range(IN_COUNT) for zz in range(n_out)]

    def remote(src, dst, send, recv, where):
        return pltpu.make_async_remote_copy(
            src, dst, send, recv, device_id=where, device_id_type=MESH
        )

    def permuted(v):
        t = v.astype(BF).astype(F32).T
        return jnp.concatenate([t[i * rows : (i + 1) * rows] for i in order], axis=0).astype(BF)

    def per_rows(body):
        def run(i, carry):
            body(aligned(i * step, step))
            return carry

        lax.fori_loop(0, tok // step, run, 0)

    out_rows = aligned(w * tok, tok)
    tok_in = pltpu.make_async_copy(s.tok_ref.at[out_rows], s.tk, s.tsem.at[0])
    cot_in = pltpu.make_async_copy(s.cot_ref.at[out_rows], s.ct, s.tsem.at[1])
    tables = [
        pltpu.make_async_copy(s.cosi_ref, s.cs, s.tsem.at[2]),
        pltpu.make_async_copy(s.sini_ref, s.sn, s.tsem.at[3]),
    ]
    tok_in.start()
    for cp in tables:
        cp.start()
    cot_in.start()

    wk_refs = (
        (s.wq_ref, s.wq.at[w]),
        (s.wo_ref, s.wo.at[aligned(w * (HQ // 2), HQ // 2)]),
        (s.wgu_ref.at[0], s.wg.at[w]),
        (s.wgu_ref.at[1], s.wu.at[w]),
        (s.wd_ref, s.wd.at[aligned(w * half_ff, half_ff)]),
    )
    w_far = [remote(a, b, s.wsend.at[i], s.wrecv.at[i], partner) for i, (a, b) in enumerate(wk_refs)]
    w_own = [pltpu.make_async_copy(a, b, s.wown.at[i]) for i, (a, b) in enumerate(wk_refs)]
    for far, own in zip(w_far, w_own):
        far.start()
        own.start()

    def weights_ready(i):
        w_own[i].wait()
        w_far[i].wait_recv()

    tok_in.wait()

    def first(rs):
        x = s.tk[rs].astype(F32)
        _, zed, g1 = norm_parts(x, s.gain_ref[0:1])
        n = zed * g1
        s.xa[rs] = n.astype(BF)
        s.xat[:, rs] = permuted(n)

    per_rows(first)

    cb, sb_ = s.cosb_ref[pl.ds(flat, 1), :], s.sinb_ref[pl.ds(flat, 1), :]
    for cp in tables:
        cp.wait()
    cosi, sini = s.cs[...], s.sn[...]
    s.cs[...] = cb * cosi - sb_ * sini
    s.sn[...] = sb_ * cosi + cb * sini
    hh = HD // 2

    def turn(v, cosine, sine):
        a, b = v[:, :hh], v[:, hh:]
        return jnp.concatenate([a * cosine - b * sine, b * cosine + a * sine], axis=1)

    def turn_back(v, cosine, sine):
        a, b = v[:, :hh], v[:, hh:]
        return jnp.concatenate([a * cosine + b * sine, b * cosine - a * sine], axis=1)

    s.ka[WINDOW:, :] = turn(dot32(s.xa[...], s.wkv_ref[0]), s.cs[...], s.sn[...]).astype(BF)
    s.va[WINDOW:, :] = dot32(s.xa[...], s.wkv_ref[1]).astype(BF)
    s.idown[...] = jnp.broadcast_to(s.ids_ref[pl.ds(w, 1), :], (8, tok))

    halo = [
        remote(s.ka.at[pl.ds(tok, WINDOW)], s.ka.at[pl.ds(0, WINDOW)], s.ksend.at[0], s.krecv.at[0], next_id),
        remote(s.va.at[pl.ds(tok, WINDOW)], s.va.at[pl.ds(0, WINDOW)], s.ksend.at[1], s.krecv.at[1], next_id),
        remote(s.idown, s.idprev, s.ksend.at[2], s.krecv.at[2], next_id),
    ]

    @pl.when(flat < n_dev - 1)
    def _():
        for cp in halo:
            cp.start()

    weights_ready(0)

    def project(h, carry):
        v, u = lax.div(h, heads // 2), lax.rem(h, heads // 2)
        q = dot32(s.xa[...], s.wq[v, :, aligned(u * HD, HD)])
        q = (turn(q, s.cs[...], s.sn[...]) * HD ** (-0.5)).astype(BF)
        for a in range(tiles):
            s.qs[a * heads + h] = q[a * TILE : (a + 1) * TILE]
        return carry

    lax.fori_loop(0, heads, project, 0)

    @pl.when(flat > 0)
    def _():
        for cp in halo:
            cp.wait_recv()

    @pl.when(flat == 0)
    def _():
        s.ka[0:WINDOW, :] = jnp.zeros((WINDOW, HD), BF)
        s.va[0:WINDOW, :] = jnp.zeros((WINDOW, HD), BF)
        s.idprev[...] = jnp.full((8, tok), -1, jnp.int32)

    row_ids = jnp.concatenate([s.idprev[0:1, :], s.idown[0:1, :]], axis=1)
    own_col = jnp.broadcast_to(s.idown[0:1, :], (128, tok)).T[:, 0:1]
    gap = lax.broadcasted_iota(jnp.int32, (TILE, win), 1) - lax.broadcasted_iota(
        jnp.int32, (TILE, win), 0
    )
    for a in range(tiles):
        same = own_col[a * TILE : (a + 1) * TILE] == row_ids[:, a * TILE : a * TILE + win]
        ok = jnp.logical_and(same, jnp.logical_and(gap > 0, gap <= WINDOW))
        s.ffb[a, 0:TILE, 0:win] = jnp.where(ok, 1.0, 0.0).astype(BF)

    def attend(i, carry):
        a, h = lax.div(i, heads), lax.rem(i, heads)
        ks = pl.ds(pl.multiple_of(a * TILE, TILE), win)
        t = jnp.tanh(dot_nt(s.qs[i], s.ka[ks, :]) * (1.0 / SOFT_CAP))
        e = jnp.exp(SOFT_CAP * t) * s.ffb[a, 0:TILE, 0:win].astype(F32)
        pr = e * (1.0 / jnp.sum(e, axis=-1, keepdims=True))
        pr = pr.astype(BF)
        s.ps[i] = pr
        s.ts[i] = (1.0 - t * t).astype(BF)
        o = dot32(pr, s.va[ks, :])
        s.att[aligned(a * TILE, TILE), aligned(h * HD, HD)] = o.astype(BF)
        return carry

    lax.fori_loop(0, tiles * heads, attend, 0)

    weights_ready(1)
    s.ao[...] = dot32(s.att[...], s.wo[...])

    def second(rs):
        _, zed, g1 = norm_parts(s.ao[rs], s.gain_ref[1:2])
        h = s.tk[rs].astype(F32) + zed * g1
        s.h1[rs] = h
        _, zed, g1 = norm_parts(h, s.gain_ref[2:3])
        n = zed * g1
        s.xa[rs] = n.astype(BF)
        s.fit[:, rs] = permuted(n)

    per_rows(second)

    weights_ready(2)
    weights_ready(3)
    root = 0.7978845608028654

    def forward(i, carry):
        v, u = lax.div(i, 4), lax.rem(i, 4)
        us = aligned(u * TILE, TILE)
        gt = dot32(s.xa[...], s.wg[v, :, us])
        up = dot32(s.xa[...], s.wu[v, :, us])
        g2 = gt * gt
        th = jnp.tanh(root * gt * (1.0 + 0.044715 * g2))
        lift = 0.5 * (1.0 + th)
        act = gt * lift
        slope = lift + 0.5 * gt * (1.0 - th * th) * (root * (1.0 + 3.0 * 0.044715 * g2))
        s.ffb[v, :, us] = (act * up).astype(BF)
        s.ffb[2 + v, :, us] = (up * slope).astype(BF)
        s.ffb[4 + v, :, us] = act.astype(BF)
        return carry

    lax.fori_loop(0, 8, forward, 0)
    weights_ready(4)
    s.dn[...] = dot32(s.ffb[0], s.wd[:half_ff]) + dot32(s.ffb[1], s.wd[half_ff:])
    s.dg_ref[...] = jnp.zeros_like(s.dg_ref)

    def third(rs):
        dn = s.dn[rs]
        _, zed, g1 = norm_parts(dn, s.gain_ref[3:4])
        s.xa[rs] = (s.h1[rs] + zed * g1).astype(BF)
        dv, dg = norm_back(dn, s.gain_ref[3:4], s.ct[rs].astype(F32))
        s.dg_ref[3:4] += dg
        s.ddn[rs] = dv.astype(BF)
        s.ddnt[:, rs] = permuted(dv)

    cot_in.wait()
    per_rows(third)
    y_far = remote(s.xa, s.y_ref.at[out_rows], s.osend.at[0], s.orecv.at[0], partner)
    y_own = pltpu.make_async_copy(s.xa, s.y_ref.at[out_rows], s.oown.at[0])
    y_far.start()
    y_own.start()

    def part(m, u, width):
        return pl.ds(pl.multiple_of(offs[m] + u * width, 128), width)

    def slot(m, u):
        return lax.rem(u, 2) * 3 + m if m < 3 else (0, 2, 4, 5)[m - 3] + u

    def exchange(m, u, width):
        return remote(
            s.sb.at[slot(m, u), :, :, pl.ds(0, width)],
            s.gb.at[:, :, part(m, u, width)],
            s.csend.at[m, u],
            s.crecv.at[m, u],
            partner,
        )

    def give(m, u, width, value):
        if m < 3:

            @pl.when(u >= 2)
            def _():
                exchange(m, u - 2, width).wait_send()

        s.sb[slot(m, u), :, :, 0:width] = value.astype(BF).reshape(
            IN_COUNT, D // IN_COUNT, width
        )
        exchange(m, u, width).start()

    def keep(m, u, width, value):
        ps = part(m, u, width)
        exchange(m, u, width).wait_recv()
        total = value.reshape(IN_COUNT, D // IN_COUNT, width) + s.gb[:, :, ps].astype(F32)
        s.gb[:, :, ps] = total.astype(BF)

    def ffn_back(v, put):
        def run(u, carry):
            us = aligned(u * TILE, TILE)
            dh = dot_nt(s.ddn[...], s.wd[aligned((v * 4 + u) * TILE, TILE), :])
            dgt = (dh * s.ffb[2 + v, :, us].astype(F32)).astype(BF)
            dup = (dh * s.ffb[4 + v, :, us].astype(F32)).astype(BF)
            s.ffb[2 + v, :, us] = dgt
            s.ffb[4 + v, :, us] = dup
            put(0, u, TILE, dot32(s.ddnt[...], s.ffb[v, :, us]))
            put(1, u, TILE, dot32(s.fit[...], dgt))
            put(2, u, TILE, dot32(s.fit[...], dup))
            return carry

        lax.fori_loop(0, 4, run, 0)

    ffn_back(other, give)
    ffn_back(w, keep)
    s.dn[...] = (
        dot_nt(s.ffb[2], s.wg[0])
        + dot_nt(s.ffb[3], s.wg[1])
        + dot_nt(s.ffb[4], s.wu[0])
        + dot_nt(s.ffb[5], s.wu[1])
    )

    s.buffers_free()

    def fourth(rs):
        dv, dg = norm_back(s.h1[rs], s.gain_ref[2:3], s.dn[rs])
        s.dg_ref[2:3] += dg
        dh = s.ct[rs].astype(F32) + dv
        s.h1[rs] = dh
        dv, dg = norm_back(s.ao[rs], s.gain_ref[1:2], dh)
        s.dg_ref[1:2] += dg
        s.ddn[rs] = dv.astype(BF)
        s.ddnt[:, rs] = permuted(dv)

    per_rows(fourth)
    s.first_sends()
    for m in range(3):
        for u in (2, 3):
            exchange(m, u, TILE).wait_send()

    def out_back(v, put):
        def run(u, carry):
            hs = aligned((v * 2 + u) * HD, HD)
            s.datt[:, hs] = dot_nt(s.ddn[...], s.wo[hs, :]).astype(BF)
            put(3, u, HD, dot32(s.ddnt[...], s.att[:, hs]))
            return carry

        lax.fori_loop(0, 2, run, 0)

    out_back(other, give)
    out_back(w, keep)

    s.dka[...] = jnp.zeros_like(s.dka)
    s.dva[...] = jnp.zeros_like(s.dva)

    def attend_back(i, carry):
        a, h = lax.div(i, heads), lax.rem(i, heads)
        ks = pl.ds(pl.multiple_of(a * TILE, TILE), win)
        qr = aligned(a * TILE, TILE)
        hs = aligned(h * HD, HD)
        do = s.datt[qr, hs]
        pr = s.ps[i]
        s.dva[ks, :] += dot_tn(pr, do)
        dp = dot_nt(do, s.va[ks, :])
        pr = pr.astype(F32)
        inner = jnp.sum(pr * dp, axis=-1, keepdims=True)
        ds = (pr * (dp - inner) * s.ts[i].astype(F32)).astype(BF)
        s.dka[ks, :] += dot_tn(ds, s.qs[i])
        dq = dot32(ds, s.ka[ks, :])
        s.datt[qr, hs] = (turn_back(dq, s.cs[qr], s.sn[qr]) * HD ** (-0.5)).astype(BF)
        return carry

    lax.fori_loop(0, heads, attend_back, 0)
    s.plane_finish(0)
    lax.fori_loop(heads, tiles * heads, attend_back, 0)
    s.plane_finish(1)

    s.dks[0] = s.dka[0:WINDOW, :].astype(BF)
    s.dks[1] = s.dva[0:WINDOW, :].astype(BF)
    d_halo = [
        remote(s.dks.at[i], s.dkr.at[i], s.dsend.at[i], s.drecv.at[i], prev_id) for i in range(2)
    ]

    @pl.when(flat > 0)
    def _():
        for cp in d_halo:
            cp.start()

    def query_back(v, put):
        def run(u, carry):
            hs = aligned((v * 2 + u) * HD, HD)
            put(4, u, HD, dot32(s.xat[...], s.datt[:, hs]))
            return carry

        lax.fori_loop(0, 2, run, 0)

    query_back(other, give)
    s.dn[...] = dot_nt(s.datt[:, : HQ // 2], s.wq[0]) + dot_nt(s.datt[:, HQ // 2 :], s.wq[1])
    query_back(w, keep)
    s.plane_start(3)

    @pl.when(flat < n_dev - 1)
    def _():
        for cp in d_halo:
            cp.wait_recv()

    @pl.when(flat == n_dev - 1)
    def _():
        s.dkr[...] = jnp.zeros_like(s.dkr)

    dk = s.dka[tok:, :] + s.dkr[0].astype(F32)
    s.dkv[0] = turn_back(dk, s.cs[...], s.sn[...]).astype(BF)
    s.dkv[1] = (s.dva[tok:, :] + s.dkr[1].astype(F32)).astype(BF)
    kvw = HD // 2
    for i in range(2):
        give(5 + i, 0, kvw, dot32(s.xat[...], s.dkv[i, :, aligned(other * kvw, kvw)]))
    for i in range(2):
        keep(5 + i, 0, kvw, dot32(s.xat[...], s.dkv[i, :, aligned(w * kvw, kvw)]))
    s.plane_start(4)
    s.dn[...] += dot_nt(s.dkv[0], s.wkv_ref[0]) + dot_nt(s.dkv[1], s.wkv_ref[1])

    def fifth(rs):
        dv, dg = norm_back(s.tk[rs].astype(F32), s.gain_ref[0:1], s.dn[rs])
        s.dg_ref[0:1] += dg
        s.h1[rs] = s.h1[rs] + dv

    per_rows(fifth)
    x_far = remote(s.h1, s.x_ref.at[out_rows], s.osend.at[1], s.orecv.at[1], partner)
    x_own = pltpu.make_async_copy(s.h1, s.x_ref.at[out_rows], s.oown.at[1])
    x_far.start()
    x_own.start()

    def finish():
        for cp in w_far:
            cp.wait_send()

        @pl.when(flat < n_dev - 1)
        def _():
            for cp in halo:
                cp.wait_send()

        @pl.when(flat > 0)
        def _():
            for cp in d_halo:
                cp.wait_send()

        for m, count, width in ((3, 2, HD), (4, 2, HD), (5, 1, kvw), (6, 1, kvw)):
            for u in range(count):
                exchange(m, u, width).wait_send()
        y_own.wait()
        x_own.wait()
        y_far.wait()
        x_far.wait()

    return finish


LAYER_INPUTS = (
    "tok_ref",
    "cot_ref",
    "cosi_ref",
    "sini_ref",
    "mq_ref",
    "mkv_ref",
    "mgu_ref",
    "mo_ref",
    "md_ref",
    "ids_ref",
    "gain_ref",
    "wkv_ref",
    "cosb_ref",
    "sinb_ref",
    "wq_ref",
    "wo_ref",
    "wgu_ref",
    "wd_ref",
)
LAYER_OUTPUTS = ("y_ref", "x_ref", "sum_ref", "nm_ref", "ub", "gs_ref")
VMEM_BYTES = 63 << 20


def whole_kernel(ctx_count, wa_count, names, *refs):
    s = Refs()
    for name, ref in zip(names, refs):
        setattr(s, name, ref)
    c = lax.axis_index("ctx")
    w = lax.axis_index("wa")
    flat = c * wa_count + w
    n_dev = ctx_count * wa_count
    barrier = pltpu.get_barrier_semaphore()

    def greet(i, carry):
        other = lax.rem(flat + i, n_dev)
        pl.semaphore_signal(
            barrier,
            inc=1,
            device_id=(lax.div(other, wa_count), lax.rem(other, wa_count)),
            device_id_type=MESH,
        )
        return carry

    lax.fori_loop(1, n_dev, greet, 0)
    pl.semaphore_wait(barrier, n_dev - 1)
    tail = tail_phases(s, ctx_count, wa_count)
    finish = layer_phases(s, ctx_count, wa_count)
    tail()
    finish()


def rotation_tables(tok, n_dev):
    freq = ROPE_BASE ** (-2.0 * np.arange(HD // 2) / HD)
    inner = np.arange(tok)[:, None] * freq[None, :]
    base = (np.arange(n_dev) * tok)[:, None] * freq[None, :]
    return [jnp.asarray(f(a), F32) for a in (inner, base) for f in (np.cos, np.sin)]


def run_whole(
    tokens, cotangent, seq_ids, gains, wkv, moms, wq, wo, wgu, wd, ctx_count, wa_count
):
    block = tokens.shape[0]
    tok = block // wa_count
    n_dev = ctx_count * wa_count
    mom_query, mom_keyval, mom_out, mom_gateup, mom_down = moms
    cosi, sini, cosb, sinb = rotation_tables(tok, n_dev)
    scratch = layer_scratch(tok) | tail_scratch(ctx_count, wa_count)
    names = LAYER_INPUTS + LAYER_OUTPUTS + tuple(scratch)
    any_space = pl.BlockSpec(memory_space=pl.ANY)
    vmem = pl.BlockSpec(memory_space=pltpu.VMEM)
    cols = layout(wa_count)[2]
    shard = jax.ShapeDtypeStruct((D // ctx_count, cols), F32)
    return pl.pallas_call(
        partial(whole_kernel, ctx_count, wa_count, names),
        out_shape=(
            jax.ShapeDtypeStruct((block, D), BF),
            jax.ShapeDtypeStruct((block, D), F32),
            shard,
            shard,
            jax.ShapeDtypeStruct((-(-(D // ctx_count) // 16) * 16, cols), BF),
            jax.ShapeDtypeStruct((8, 128), F32),
        ),
        in_specs=[any_space] * 9 + [vmem] * 5 + [any_space] * 4,
        out_specs=(any_space, any_space, vmem, vmem, vmem, vmem),
        scratch_shapes=list(scratch.values()),
        compiler_params=pltpu.CompilerParams(
            collective_id=0, has_side_effects=True, vmem_limit_bytes=VMEM_BYTES
        ),
        name="whole",
    )(
        tokens,
        cotangent,
        cosi,
        sini,
        mom_query,
        mom_keyval,
        mom_gateup,
        mom_out.T,
        mom_down.T,
        seq_ids.reshape(wa_count, tok),
        gains,
        wkv,
        cosb,
        sinb,
        wq,
        wo,
        wgu,
        wd,
    )


def format_kernel(
    ctx_count,
    wa_count,
    sum_ref,
    nm_ref,
    ub_ref,
    gs_ref,
    first_ref,
    second_ref,
    y_ref,
    x_ref,
    *rest,
):
    outs, (ubv, gsv, fv, sv, sem) = rest[:21], rest[21:]
    y_out, x_out = outs[:2]
    rows = D // ctx_count
    halves, offs, _ = layout(wa_count)
    late = [
        pltpu.make_async_copy(src, dst, sem.at[i])
        for i, (src, dst) in enumerate(
            ((ub_ref, ubv), (gs_ref, gsv), (first_ref, fv), (second_ref, sv))
        )
    ]

    def places(group):
        query, keyval, out, gateup, down = group
        return (down, gateup.at[0], gateup.at[1], out, query, keyval.at[0], keyval.at[1])

    pairs = [(x_ref, x_out), (y_ref, y_out)]
    for src, group in ((sum_ref, outs[2:7]), (nm_ref, outs[8:13])):
        for m, dst in enumerate(places(group)):
            pairs.append((src.at[:, pl.ds(offs[m], halves[m])], dst))
    copies = [pltpu.make_async_copy(a, b, sem.at[4 + i]) for i, (a, b) in enumerate(pairs)]
    for cp in late + copies:
        cp.start()
    for cp in late:
        cp.wait()
    for m, dst in enumerate(places(outs[13:18])):
        dst[...] = ubv[0:rows, offs[m] : offs[m] + halves[m]].astype(F32)
    g = gsv[0:4, 0:rows]
    first = ADAM_ONE * fv[...] + (1.0 - ADAM_ONE) * g
    second = ADAM_TWO * sv[...] + (1.0 - ADAM_TWO) * g * g
    outs[7][...] = g
    outs[18][...] = first
    outs[19][...] = second
    outs[20][...] = -GAIN_RATE * first / (jnp.sqrt(second) + ADAM_EPS)
    for cp in copies:
        cp.wait()


def run_format(sums, fresh, updates, gsum, gain_first, gain_second, y, x, ctx_count, wa_count):
    rows = D // ctx_count
    halves = layout(wa_count)[0]
    down, gate, _, out, query, key, _ = halves
    f = lambda *shape: jax.ShapeDtypeStruct(shape, F32)
    weights = [f(rows, query), f(2, rows, key), f(rows, out), f(2, rows, gate), f(rows, down)]
    any_space = pl.BlockSpec(memory_space=pl.ANY)
    vmem = pl.BlockSpec(memory_space=pltpu.VMEM)
    gain = f(4, rows)
    shapes = [jax.ShapeDtypeStruct(y.shape, y.dtype), jax.ShapeDtypeStruct(x.shape, x.dtype)]
    shapes += weights + [gain] + weights + weights + [gain] * 3
    outs = pl.pallas_call(
        partial(format_kernel, ctx_count, wa_count),
        out_shape=shapes,
        in_specs=[any_space] * 8,
        out_specs=[any_space] * 7 + [vmem] + [any_space] * 5 + [vmem] * 8,
        scratch_shapes=[
            pltpu.VMEM(updates.shape, updates.dtype),
            pltpu.VMEM(gsum.shape, F32),
            pltpu.VMEM(gain_first.shape, F32),
            pltpu.VMEM(gain_second.shape, F32),
            pltpu.SemaphoreType.DMA((20,)),
        ],
        compiler_params=pltpu.CompilerParams(vmem_limit_bytes=VMEM_BYTES),
        name="format",
    )(sums, fresh, updates, gsum, gain_first, gain_second, y, x)
    return tuple(o.T if i in (4, 6, 10, 12, 15, 17) else o for i, o in enumerate(outs))


def per_device(
    tokens,
    cotangent,
    seq_ids,
    w_query,
    w_keyval,
    w_out,
    w_gateup,
    w_down,
    norm_gains,
    mom_query,
    mom_keyval,
    mom_out,
    mom_gateup,
    mom_down,
    gain_first,
    gain_second,
):
    ctx_count = lax.axis_size("ctx")
    wa_count = lax.axis_size("wa")
    y, x, sums, fresh, updates, gsum = run_whole(
        tokens,
        cotangent,
        seq_ids,
        norm_gains,
        w_keyval,
        (mom_query, mom_keyval, mom_out, mom_gateup, mom_down),
        w_query,
        w_out,
        w_gateup,
        w_down,
        ctx_count,
        wa_count,
    )
    return tuple(
        run_format(
            sums, fresh, updates, gsum, gain_first, gain_second, y, x, ctx_count, wa_count
        )
    )


def solution(mesh):
    in_specs = (
        P("ctx", None),
        P("ctx", None),
        P("ctx"),
        P(None, "wa"),
        P(),
        P("wa", None),
        P(None, None, "wa"),
        P("wa", None),
        P(),
        P("ctx", "wa"),
        P(None, "ctx", "wa"),
        P("wa", "ctx"),
        P(None, "ctx", "wa"),
        P("wa", "ctx"),
        P(None, "ctx"),
        P(None, "ctx"),
    )
    out_specs = (
        P("ctx", None),
        P("ctx", None),
        P("ctx", "wa"),
        P(None, "ctx", "wa"),
        P("wa", "ctx"),
        P(None, "ctx", "wa"),
        P("wa", "ctx"),
        P(None, "ctx"),
        P("ctx", "wa"),
        P(None, "ctx", "wa"),
        P("wa", "ctx"),
        P(None, "ctx", "wa"),
        P("wa", "ctx"),
        P("ctx", "wa"),
        P(None, "ctx", "wa"),
        P("wa", "ctx"),
        P(None, "ctx", "wa"),
        P("wa", "ctx"),
        P(None, "ctx"),
        P(None, "ctx"),
        P(None, "ctx"),
    )
    return jax.shard_map(
        per_device, mesh=mesh, in_specs=in_specs, out_specs=out_specs, check_vma=False
    )
```

```python
from functools import partial
import math

import jax
import jax.numpy as jnp
import numpy as np
from jax import lax
from jax.experimental import pallas as pl
from jax.experimental.pallas import tpu as pltpu
from jax.sharding import PartitionSpec as P

D = 640
FF = 2048
HD = 256
WINDOW = 512
SOFT_CAP = 10
NS_STEPS = 5
HQ = 1024


EPS_NORM = 1e-06
ROPE_BASE = 10000.0
MOMENTUM = 0.95
ADAM_ONE = 0.9
ADAM_TWO = 0.95
ADAM_EPS = 1e-08
GAIN_RATE = 0.1
QUINTIC_A = 3.4445
QUINTIC_B = -4.775
QUINTIC_C = 2.0315
MATRIX_COUNT = 7
MUON_RATE = 0.2

MESH = pl.DeviceIdType.MESH
BF = jnp.bfloat16
F32 = jnp.float32
IN_COUNT = 4
NAMES = ("down", "gate", "up", "out", "query", "key", "value")
WIDTHS = (FF, FF, FF, HQ, HQ, HD, HD)
OWNERS = (7, 4, 8, 5, 11, 9, 10)
CHUNK_SETS = ((0,), (1,), (2,), (3, 4), (5, 6))
TILE = 256


def layout(wa_count):
    halves = [w // wa_count for w in WIDTHS]
    offs = [sum(halves[:i]) for i in range(len(halves))]
    return halves, offs, sum(halves)


def dot32(a, b):
    return jnp.dot(a, b, preferred_element_type=F32)


def eye_mask(n):
    return (
        lax.broadcasted_iota(jnp.int32, (n, n), 0) == lax.broadcasted_iota(jnp.int32, (n, n), 1)
    )


def pad_rows(v, rows):
    if v.shape[0] == rows:
        return v
    return jnp.concatenate([v, jnp.zeros((rows - v.shape[0], v.shape[1]), v.dtype)], axis=0)


def split_into(v, hi, lo):
    top = v.astype(BF)
    hi[...] = top
    lo[...] = (v - top.astype(F32)).astype(BF)


SYM_TILES = ((0, 256), (256, 512), (512, 640))


def sym_tiles(out, block):
    for a, b in SYM_TILES:
        v = block(a, b)
        out[a:, a:b] = v
        if b < D:
            out[a:b, b:] = v[b - a :].T


def prod3(h1, l1, h2, l2):
    return lambda a, b: (
        dot32(h1[a:], h2[:, a:b]) + dot32(h1[a:], l2[:, a:b]) + dot32(l1[a:], h2[:, a:b])
    )


def tail_scratch(ctx_count, wa_count):
    v = pltpu.VMEM
    dma = pltpu.SemaphoreType.DMA
    n_in = IN_COUNT
    n_out = ctx_count // n_in
    rows = D // ctx_count
    rp = -(-rows // 16) * 16
    n_dev = ctx_count * wa_count
    n_ch = len(CHUNK_SETS)
    cols = layout(wa_count)[2]
    return dict(
        mb=v((rp, cols), BF),
        xb=v((ctx_count, rp, FF), BF),
        am=v((D, D), F32),
        dg_ref=v((8, D), F32),
        dgs=v((ctx_count, 8, 128), F32),
        dgr=v((n_dev, 8, 128), F32),
        psend=dma((n_ch, n_in - 1)),
        precv=dma((n_ch, n_in - 1)),
        lsend=dma((n_ch, n_out - 1)),
        lrecv=dma((n_ch, n_out - 1)),
        gsend=dma((MATRIX_COUNT,)),
        grecv=dma,
        usend=dma((n_dev,)),
        urecv=dma((MATRIX_COUNT,)),
        gnsend=dma((n_dev,)),
        gnrecv=dma,
        msem=dma((MATRIX_COUNT,)),
        pfree=pltpu.SemaphoreType.REGULAR,
        lfree=pltpu.SemaphoreType.REGULAR,
    )


def tail_phases(s, ctx_count, wa_count):
    c = lax.axis_index("ctx")
    w = lax.axis_index("wa")
    n_in = IN_COUNT
    n_out = ctx_count // n_in
    n_dev = ctx_count * wa_count
    p = lax.rem(c, n_in)
    z = lax.div(c, n_in)
    rows = D // ctx_count
    rp = s.xb.shape[1]
    block = D // n_in
    halves, offs, cols = layout(wa_count)
    chunks = [(offs[m[0]], sum(halves[i] for i in m)) for m in CHUNK_SETS]
    me = c * wa_count + w
    per = ctx_count // 2

    def plane_slot(ci, k):
        i = min(ci, 4) * (n_in - 1) + (k - 1 if ci < 4 else 0)
        buf = (s.wg, s.wu)[i // 8]
        lanes = pl.ds(0, chunks[ci][1]) if ci < 4 else pl.ds((k - 1) * TILE, TILE)
        return buf.at[i % 8 // 4, pl.ds(i % 4 * block, block), lanes]

    def line_slot(base, ci, j):
        wid = chunks[ci][1]
        if ci < 4:
            start = ci % 2 * 256 + j * rp
            return s.ffb.at[base * 2 + ci // 2, pl.ds(pl.multiple_of(start, 16), rp), pl.ds(0, wid)]
        return s.ffb.at[4 + base, pl.ds(pl.multiple_of(j * rp, 16), rp), pl.ds(0, wid)]

    def plane_copy(ci, k):
        off, wid = chunks[ci]
        q = lax.rem(p + k, n_in)
        return pltpu.make_async_remote_copy(
            s.gb.at[q, :, pl.ds(off, wid)],
            plane_slot(ci, k),
            s.psend.at[ci, k - 1],
            s.precv.at[ci, k - 1],
            device_id=(z * n_in + q, w),
            device_id_type=MESH,
        )

    def line_copy(ci, k):
        j = lax.rem(z + k, n_out)
        return pltpu.make_async_remote_copy(
            line_slot(0, ci, j),
            line_slot(1, ci, k - 1),
            s.lsend.at[ci, k - 1],
            s.lrecv.at[ci, k - 1],
            device_id=(j * n_in + p, w),
            device_id_type=MESH,
        )

    def buffers_free():
        for k in range(1, n_in):
            pl.semaphore_signal(
                s.pfree,
                inc=1,
                device_id=(z * n_in + lax.rem(p + k, n_in), w),
                device_id_type=MESH,
            )
        for k in range(1, n_out):
            pl.semaphore_signal(
                s.lfree,
                inc=1,
                device_id=(lax.rem(z + k, n_out) * n_in + p, w),
                device_id_type=MESH,
            )

    def plane_start(ci):
        for k in range(1, n_in):
            plane_copy(ci, k).start()

    def first_sends():
        pl.semaphore_wait(s.pfree, n_in - 1)
        for ci in range(3):
            plane_start(ci)

    def plane_finish(ci):
        off, wid = chunks[ci]
        for k in range(1, n_in):
            plane_copy(ci, k).wait_recv()

        def plane_sum(t, carry):
            cs = aligned(off + t * TILE, TILE)
            here = aligned(t * TILE, TILE)
            total = s.gb[p, :, cs].astype(F32)
            for k in range(1, n_in):
                total = total + plane_slot(ci, k)[:, here].astype(F32)
            for j in range(n_out):
                slab = total[j * rows : (j + 1) * rows]

                @pl.when(z == j)
                def _():
                    s.sum_ref[:, cs] = slab

                line_slot(0, ci, j)[:, here] = pad_rows(slab, rp).astype(BF)
            return carry

        lax.fori_loop(0, wid // TILE, plane_sum, 0)
        if ci == 0:
            pl.semaphore_wait(s.lfree, n_out - 1)
        for k in range(1, n_out):
            line_copy(ci, k).start()

    def gather_copy(m, local):
        src = s.mb.at[:, pl.ds(offs[m], halves[m])]
        dst = s.xb.at[c, :, pl.ds(pl.multiple_of(w * halves[m], 128), halves[m])]
        if local:
            return pltpu.make_async_copy(src, dst, s.grecv)
        return pltpu.make_async_remote_copy(
            src, dst, s.gsend.at[m], s.grecv, device_id=(OWNERS[m], 0), device_id_type=MESH
        )

    def line_finish(ci):
        off, wid = chunks[ci]
        for k in range(1, n_out):
            line_copy(ci, k).wait_recv()

        def line_sum(t, carry):
            cs = aligned(off + t * TILE, TILE)
            here = aligned(t * TILE, TILE)
            total = s.sum_ref[:, cs]
            for k in range(n_out - 1):
                total = total + line_slot(1, ci, k)[:, here][:rows].astype(F32)
            s.sum_ref[:, cs] = total
            fresh = MOMENTUM * s.nm_ref[:, cs] + total
            s.nm_ref[:, cs] = fresh
            s.mb[:, cs] = pad_rows(fresh, rp).astype(BF)
            return carry

        lax.fori_loop(0, wid // TILE, line_sum, 0)
        for m in CHUNK_SETS[ci]:
            mine = me == OWNERS[m] * wa_count

            @pl.when(mine)
            def _():
                gather_copy(m, True).start()

            @pl.when(jnp.logical_not(mine))
            def _():
                gather_copy(m, False).start()

    s.buffers_free = buffers_free
    s.first_sends = first_sends
    s.plane_start = plane_start
    s.plane_finish = plane_finish

    sources = (
        s.md_ref,
        s.mgu_ref.at[0],
        s.mgu_ref.at[1],
        s.mo_ref,
        s.mq_ref,
        s.mkv_ref.at[0],
        s.mkv_ref.at[1],
    )
    moms = [
        pltpu.make_async_copy(src, s.nm_ref.at[:, pl.ds(offs[m], halves[m])], s.msem.at[m])
        for m, src in enumerate(sources)
    ]
    for cp in moms:
        cp.start()

    def rest():
        for i in range(ctx_count):
            s.dgs[i, :, 0:rows] = s.dg_ref[:, i * rows : (i + 1) * rows]

        def gain_copy(t):
            i, v = lax.div(t, wa_count), lax.rem(t, wa_count)
            return pltpu.make_async_remote_copy(
                s.dgs.at[i],
                s.dgr.at[me],
                s.gnsend.at[t],
                s.gnrecv,
                device_id=(i, v),
                device_id_type=MESH,
            )

        def gain_send(t, carry):
            gain_copy(lax.rem(me + t, n_dev)).start()
            return carry

        def gain_sent(t, carry):
            gain_copy(lax.rem(me + t, n_dev)).wait_send()
            return carry

        for cp in moms:
            cp.wait()
        plane_finish(2)
        line_finish(0)
        line_finish(1)
        plane_finish(3)
        plane_finish(4)
        line_finish(2)
        pltpu.make_async_copy(s.dgs.at[c], s.dgr.at[me], s.gnrecv).start()
        lax.fori_loop(1, n_dev, gain_send, 0)
        line_finish(3)
        line_finish(4)
        for ci in range(len(chunks)):
            for k in range(1, n_in):
                plane_copy(ci, k).wait_send()
            for k in range(1, n_out):
                line_copy(ci, k).wait_send()
        solve()
        pltpu.make_async_copy(s.dgr, s.dgr, s.gnrecv).wait()
        s.gs_ref[...] = jnp.sum(s.dgr[...], axis=0)
        lax.fori_loop(1, n_dev, gain_sent, 0)
        updates_back()

    def owned_by(*which):
        hit = me == OWNERS[which[0]] * wa_count
        for m in which[1:]:
            hit = jnp.logical_or(hit, me == OWNERS[m] * wa_count)
        return hit

    def solve():
        is_owner = owned_by(*range(MATRIX_COUNT))
        is_small = owned_by(5, 6)
        is_wide = owned_by(0, 1, 2)
        tiles = jnp.where(is_small, HD // TILE, jnp.where(is_wide, FF // TILE, HQ // TILE))
        am, xf = s.am, s.dka.at[pl.ds(0, D)]
        ah = s.wd.at[pl.ds(0, D)]
        al = s.wd.at[pl.ds(D, D)]
        ph = s.wd.at[pl.ds(2 * D, D)]
        plo = s.wo.at[pl.ds(0, D)]
        qh = s.wu.at[0, :, pl.ds(0, D)]

        def tile_of(t):
            return s.wg.at[lax.div(t, 4), :, aligned(lax.rem(t, 4) * TILE, TILE)]

        for m in range(MATRIX_COUNT):

            @pl.when(me == OWNERS[m] * wa_count)
            def _(m=m):
                whole = s.xb.at[:, :, pl.ds(0, halves[m] * wa_count)]
                pltpu.make_async_copy(whole, whole, s.grecv).wait()

        @pl.when(is_owner)
        def _():
            am[...] = jnp.zeros_like(am)

            def gram(t, carry):
                cs = aligned(t * TILE, TILE)
                for i in range(ctx_count):
                    xf[i * rows : (i + 1) * rows, :] = s.xb[i, :, cs][:rows].astype(F32)
                x = xf[...].astype(BF)
                tile_of(t)[...] = x

                @pl.when(jnp.logical_not(is_small))
                def _():
                    for a, b in SYM_TILES:
                        am[a:, a:b] += dot_nt(x[a:], x[a:b])

                @pl.when(is_small)
                def _():
                    am[0:HD, 0:HD] = dot_tn(x, x)

                return carry

            lax.fori_loop(0, tiles, gram, 0)
            norm2 = jnp.sum(jnp.where(eye_mask(D), am[...], 0.0), keepdims=True)
            inv = 1.0 / (jnp.sqrt(norm2) + 1e-07)
            inv2 = inv * inv
            sym_tiles(am, lambda a, b: am[a:, a:b] * inv2)

            def shifted(a, b, square):
                rest = QUINTIC_B * am[a:, a:b] + QUINTIC_C * square
                top = rest[: b - a] + jnp.where(eye_mask(b - a), QUINTIC_A, 0.0)
                return jnp.concatenate([top, rest[b - a :]], axis=0) if b < D else top

            def poly():
                split_into(am[...], ah, al)
                square = prod3(ah, al, ah, al)
                sym_tiles(am, lambda a, b: shifted(a, b, square(a, b)))

            def advance():
                sym_tiles(am, prod3(ph, plo, ah, al))
                split_into(am[...], ah, al)
                sym_tiles(am, prod3(ah, al, ph, plo))

            def grow():
                sym_tiles(am, lambda a, b: dot32(ph[a:], qh[:, a:b]))
                qh[...] = am[...].astype(BF)

            poly()
            split_into(am[...], ph, plo)
            qh[...] = ph[...]
            advance()

            def sweep(i, carry):
                poly()
                split_into(am[...], ph, plo)
                grow()
                advance()
                return carry

            lax.fori_loop(0, NS_STEPS - 2, sweep, 0)
            ah[...] = am[...].astype(BF)
            sym_tiles(am, lambda a, b: shifted(a, b, dot32(ah[a:], ah[:, a:b])))
            ph[...] = am[...].astype(BF)
            grow()
            rates = [-MUON_RATE * 0.2 * math.sqrt(n) for n in (D, FF, HQ)]
            rate = jnp.where(is_small, rates[0], jnp.where(is_wide, rates[1], rates[2]))
            scale = rate * inv

            def put(v, lanes, value):
                for i in range(ctx_count):
                    s.ffb[v * 2 + i // per, i % per * rp : (i % per + 1) * rp, lanes] = pad_rows(
                        value[i * rows : (i + 1) * rows], rp
                    ).astype(BF)

            def back(v, t):
                @pl.when(jnp.logical_not(is_small))
                def _():
                    whole = v * jnp.where(is_wide, 4, 2) + t
                    xf[...] = dot32(qh[...], tile_of(whole)[...]) * scale
                    put(v, aligned(t * TILE, TILE), xf)

                @pl.when(is_small)
                def _():
                    xf[...] = dot32(tile_of(t)[...], s.wu[0, 0:HD, 0:HD]) * scale
                    for half in range(2):
                        lanes = slice(half * (HD // 2), (half + 1) * (HD // 2))
                        put(half, pl.ds(0, HD // 2), xf[:, lanes])

            for v in range(2):
                count = jnp.where(is_small, 1 - v, jnp.where(is_wide, 4, 2))

                def run(t, carry, v=v):
                    back(v, t)
                    return carry

                lax.fori_loop(0, count, run, 0)
                for m in range(MATRIX_COUNT):

                    @pl.when(me == OWNERS[m] * wa_count)
                    def _(m=m, v=v):
                        def send(i, carry):
                            there = lax.rem(c + i, ctx_count)
                            update_copy(m, there * wa_count + v, False).start()
                            return carry

                        if v == 0:
                            update_copy(m, c * wa_count, True).start()
                            lax.fori_loop(1, ctx_count, send, 0)
                        else:
                            lax.fori_loop(0, ctx_count, send, 0)

    def update_copy(m, t, local):
        i, v = lax.div(t, wa_count), lax.rem(t, wa_count)
        start = pl.multiple_of(lax.rem(i, per) * rp, 16)
        src = s.ffb.at[v * 2 + lax.div(i, per), pl.ds(start, rp), pl.ds(0, halves[m])]
        dst = s.ub.at[:, pl.ds(offs[m], halves[m])]
        if local:
            return pltpu.make_async_copy(src, dst, s.urecv.at[m])
        return pltpu.make_async_remote_copy(
            src, dst, s.usend.at[t], s.urecv.at[m], device_id=(i, v), device_id_type=MESH
        )

    def updates_back():
        for m in range(MATRIX_COUNT):
            piece = s.ub.at[:, pl.ds(offs[m], halves[m])]
            pltpu.make_async_copy(piece, piece, s.urecv.at[m]).wait()

        for m in range(MATRIX_COUNT):
            owner = OWNERS[m] * wa_count

            @pl.when(me != owner)
            def _(m=m):
                gather_copy(m, False).wait_send()

            @pl.when(me == owner)
            def _(m=m, owner=owner):
                def done(t, carry):
                    update_copy(m, lax.rem(owner + t, n_dev), False).wait_send()
                    return carry

                lax.fori_loop(1, n_dev, done, 0)

    return rest


class Refs:
    pass


def dot_nt(a, b):
    return lax.dot_general(a, b, (((1,), (1,)), ((), ())), preferred_element_type=F32)


def dot_tn(a, b):
    return lax.dot_general(a, b, (((0,), (0,)), ((), ())), preferred_element_type=F32)


def aligned(start, size):
    return pl.ds(pl.multiple_of(start, size), size)


def norm_parts(v, gain):
    r = lax.rsqrt(jnp.mean(v * v, axis=-1, keepdims=True) + EPS_NORM)
    return r, v * r, 1.0 + gain


def norm_back(v, gain, e):
    r, zed, g1 = norm_parts(v, gain)
    e1 = e * g1
    dv = r * (e1 - zed * jnp.mean(e1 * zed, axis=-1, keepdims=True))
    return dv, jnp.sum(e * zed, axis=0, keepdims=True)


def layer_scratch(tok):
    v = pltpu.VMEM
    dma = pltpu.SemaphoreType.DMA
    cols = sum(WIDTHS) // 2
    heads = HQ // HD
    tiles = tok // TILE
    win = WINDOW + TILE
    return dict(
        wq=v((2, D, HQ // 2), BF),
        wo=v((HQ, D), BF),
        wg=v((2, D, FF // 2), BF),
        wu=v((2, D, FF // 2), BF),
        wd=v((FF, D), BF),
        tk=v((tok, D), BF),
        ct=v((tok, D), BF),
        xa=v((tok, D), BF),
        xat=v((D, tok), BF),
        fit=v((D, tok), BF),
        ddn=v((tok, D), BF),
        ddnt=v((D, tok), BF),
        cs=v((tok, HD // 2), F32),
        sn=v((tok, HD // 2), F32),
        ka=v((WINDOW + tok, HD), BF),
        va=v((WINDOW + tok, HD), BF),
        idown=v((8, tok), jnp.int32),
        idprev=v((8, tok), jnp.int32),
        qs=v((tiles * heads, TILE, HD), BF),
        ps=v((tiles * heads, TILE, win), BF),
        ts=v((tiles * heads, TILE, win), BF),
        att=v((tok, HQ), BF),
        ao=v((tok, D), F32),
        h1=v((tok, D), F32),
        dn=v((tok, D), F32),
        ffb=v((6, tok, FF // 2), BF),
        datt=v((tok, HQ), BF),
        dka=v((WINDOW + tok, HD), F32),
        dva=v((WINDOW + tok, HD), F32),
        dks=v((2, tok, HD), BF),
        dkr=v((2, tok, HD), BF),
        dkv=v((2, tok, HD), BF),
        sb=v((6, IN_COUNT, D // IN_COUNT, TILE), BF),
        gb=v((IN_COUNT, D // IN_COUNT, cols), BF),
        wsend=dma((5,)),
        wrecv=dma((5,)),
        wown=dma((5,)),
        ksend=dma((3,)),
        krecv=dma((3,)),
        dsend=dma((2,)),
        drecv=dma((2,)),
        csend=dma((MATRIX_COUNT, 4)),
        crecv=dma((MATRIX_COUNT, 4)),
        osend=dma((2,)),
        orecv=dma((2,)),
        oown=dma((2,)),
        tsem=dma((4,)),
    )


def layer_phases(s, ctx_count, wa_count):
    c = lax.axis_index("ctx")
    w = lax.axis_index("wa")
    other = 1 - w
    flat = c * wa_count + w
    n_dev = ctx_count * wa_count
    tok = s.xa.shape[0]
    rows = D // ctx_count
    n_out = ctx_count // IN_COUNT
    heads = HQ // HD
    tiles = tok // TILE
    win = WINDOW + TILE
    half_ff = FF // 2
    halves, offs, cols = layout(wa_count)
    step = 128
    partner = (c, other)
    follow = jnp.minimum(flat + 1, n_dev - 1)
    ahead = jnp.maximum(flat - 1, 0)
    next_id = (lax.div(follow, wa_count), lax.rem(follow, wa_count))
    prev_id = (lax.div(ahead, wa_count), lax.rem(ahead, wa_count))
    order = [zz * IN_COUNT + pp for pp in range(IN_COUNT) for zz in range(n_out)]

    def remote(src, dst, send, recv, where):
        return pltpu.make_async_remote_copy(
            src, dst, send, recv, device_id=where, device_id_type=MESH
        )

    def permuted(v):
        t = v.astype(BF).astype(F32).T
        return jnp.concatenate([t[i * rows : (i + 1) * rows] for i in order], axis=0).astype(BF)

    def per_rows(body):
        def run(i, carry):
            body(aligned(i * step, step))
            return carry

        lax.fori_loop(0, tok // step, run, 0)

    out_rows = aligned(w * tok, tok)
    tok_in = pltpu.make_async_copy(s.tok_ref.at[out_rows], s.tk, s.tsem.at[0])
    cot_in = pltpu.make_async_copy(s.cot_ref.at[out_rows], s.ct, s.tsem.at[1])
    tables = [
        pltpu.make_async_copy(s.cosi_ref, s.cs, s.tsem.at[2]),
        pltpu.make_async_copy(s.sini_ref, s.sn, s.tsem.at[3]),
    ]
    tok_in.start()
    for cp in tables:
        cp.start()
    cot_in.start()

    wk_refs = (
        (s.wq_ref, s.wq.at[w]),
        (s.wo_ref, s.wo.at[aligned(w * (HQ // 2), HQ // 2)]),
        (s.wgu_ref.at[0], s.wg.at[w]),
        (s.wgu_ref.at[1], s.wu.at[w]),
        (s.wd_ref, s.wd.at[aligned(w * half_ff, half_ff)]),
    )
    w_far = [remote(a, b, s.wsend.at[i], s.wrecv.at[i], partner) for i, (a, b) in enumerate(wk_refs)]
    w_own = [pltpu.make_async_copy(a, b, s.wown.at[i]) for i, (a, b) in enumerate(wk_refs)]
    for far, own in zip(w_far, w_own):
        far.start()
        own.start()

    def weights_ready(i):
        w_own[i].wait()
        w_far[i].wait_recv()

    tok_in.wait()

    def first(rs):
        x = s.tk[rs].astype(F32)
        _, zed, g1 = norm_parts(x, s.gain_ref[0:1])
        n = zed * g1
        s.xa[rs] = n.astype(BF)
        s.xat[:, rs] = permuted(n)

    per_rows(first)

    cb, sb_ = s.cosb_ref[pl.ds(flat, 1), :], s.sinb_ref[pl.ds(flat, 1), :]
    for cp in tables:
        cp.wait()
    cosi, sini = s.cs[...], s.sn[...]
    s.cs[...] = cb * cosi - sb_ * sini
    s.sn[...] = sb_ * cosi + cb * sini
    hh = HD // 2

    def turn(v, cosine, sine):
        a, b = v[:, :hh], v[:, hh:]
        return jnp.concatenate([a * cosine - b * sine, b * cosine + a * sine], axis=1)

    def turn_back(v, cosine, sine):
        a, b = v[:, :hh], v[:, hh:]
        return jnp.concatenate([a * cosine + b * sine, b * cosine - a * sine], axis=1)

    s.ka[WINDOW:, :] = turn(dot32(s.xa[...], s.wkv_ref[0]), s.cs[...], s.sn[...]).astype(BF)
    s.va[WINDOW:, :] = dot32(s.xa[...], s.wkv_ref[1]).astype(BF)
    s.idown[...] = jnp.broadcast_to(s.ids_ref[pl.ds(w, 1), :], (8, tok))

    halo = [
        remote(s.ka.at[pl.ds(tok, WINDOW)], s.ka.at[pl.ds(0, WINDOW)], s.ksend.at[0], s.krecv.at[0], next_id),
        remote(s.va.at[pl.ds(tok, WINDOW)], s.va.at[pl.ds(0, WINDOW)], s.ksend.at[1], s.krecv.at[1], next_id),
        remote(s.idown, s.idprev, s.ksend.at[2], s.krecv.at[2], next_id),
    ]

    @pl.when(flat < n_dev - 1)
    def _():
        for cp in halo:
            cp.start()

    weights_ready(0)

    def project(h, carry):
        v, u = lax.div(h, heads // 2), lax.rem(h, heads // 2)
        q = dot32(s.xa[...], s.wq[v, :, aligned(u * HD, HD)])
        q = (turn(q, s.cs[...], s.sn[...]) * HD ** (-0.5)).astype(BF)
        for a in range(tiles):
            s.qs[a * heads + h] = q[a * TILE : (a + 1) * TILE]
        return carry

    lax.fori_loop(0, heads, project, 0)

    @pl.when(flat > 0)
    def _():
        for cp in halo:
            cp.wait_recv()

    @pl.when(flat == 0)
    def _():
        s.ka[0:WINDOW, :] = jnp.zeros((WINDOW, HD), BF)
        s.va[0:WINDOW, :] = jnp.zeros((WINDOW, HD), BF)
        s.idprev[...] = jnp.full((8, tok), -1, jnp.int32)

    row_ids = jnp.concatenate([s.idprev[0:1, :], s.idown[0:1, :]], axis=1)
    own_col = jnp.broadcast_to(s.idown[0:1, :], (128, tok)).T[:, 0:1]
    gap = lax.broadcasted_iota(jnp.int32, (TILE, win), 1) - lax.broadcasted_iota(
        jnp.int32, (TILE, win), 0
    )
    for a in range(tiles):
        same = own_col[a * TILE : (a + 1) * TILE] == row_ids[:, a * TILE : a * TILE + win]
        ok = jnp.logical_and(same, jnp.logical_and(gap > 0, gap <= WINDOW))
        s.ffb[a, 0:TILE, 0:win] = jnp.where(ok, 1.0, 0.0).astype(BF)

    def attend(i, carry):
        a, h = lax.div(i, heads), lax.rem(i, heads)
        ks = pl.ds(pl.multiple_of(a * TILE, TILE), win)
        t = jnp.tanh(dot_nt(s.qs[i], s.ka[ks, :]) * (1.0 / SOFT_CAP))
        e = jnp.exp(SOFT_CAP * t) * s.ffb[a, 0:TILE, 0:win].astype(F32)
        pr = e * (1.0 / jnp.sum(e, axis=-1, keepdims=True))
        pr = pr.astype(BF)
        s.ps[i] = pr
        s.ts[i] = (1.0 - t * t).astype(BF)
        o = dot32(pr, s.va[ks, :])
        s.att[aligned(a * TILE, TILE), aligned(h * HD, HD)] = o.astype(BF)
        return carry

    lax.fori_loop(0, tiles * heads, attend, 0)

    weights_ready(1)
    s.ao[...] = dot32(s.att[...], s.wo[...])

    def second(rs):
        _, zed, g1 = norm_parts(s.ao[rs], s.gain_ref[1:2])
        h = s.tk[rs].astype(F32) + zed * g1
        s.h1[rs] = h
        _, zed, g1 = norm_parts(h, s.gain_ref[2:3])
        n = zed * g1
        s.xa[rs] = n.astype(BF)
        s.fit[:, rs] = permuted(n)

    per_rows(second)

    weights_ready(2)
    weights_ready(3)
    root = 0.7978845608028654

    def forward(i, carry):
        v, u = lax.div(i, 4), lax.rem(i, 4)
        us = aligned(u * TILE, TILE)
        gt = dot32(s.xa[...], s.wg[v, :, us])
        up = dot32(s.xa[...], s.wu[v, :, us])
        g2 = gt * gt
        th = jnp.tanh(root * gt * (1.0 + 0.044715 * g2))
        lift = 0.5 * (1.0 + th)
        act = gt * lift
        slope = lift + 0.5 * gt * (1.0 - th * th) * (root * (1.0 + 3.0 * 0.044715 * g2))
        s.ffb[v, :, us] = (act * up).astype(BF)
        s.ffb[2 + v, :, us] = (up * slope).astype(BF)
        s.ffb[4 + v, :, us] = act.astype(BF)
        return carry

    lax.fori_loop(0, 8, forward, 0)
    weights_ready(4)
    s.dn[...] = dot32(s.ffb[0], s.wd[:half_ff]) + dot32(s.ffb[1], s.wd[half_ff:])
    s.dg_ref[...] = jnp.zeros_like(s.dg_ref)

    def third(rs):
        dn = s.dn[rs]
        _, zed, g1 = norm_parts(dn, s.gain_ref[3:4])
        s.xa[rs] = (s.h1[rs] + zed * g1).astype(BF)
        dv, dg = norm_back(dn, s.gain_ref[3:4], s.ct[rs].astype(F32))
        s.dg_ref[3:4] += dg
        s.ddn[rs] = dv.astype(BF)
        s.ddnt[:, rs] = permuted(dv)

    cot_in.wait()
    per_rows(third)
    y_far = remote(s.xa, s.y_ref.at[out_rows], s.osend.at[0], s.orecv.at[0], partner)
    y_own = pltpu.make_async_copy(s.xa, s.y_ref.at[out_rows], s.oown.at[0])
    y_far.start()
    y_own.start()

    def part(m, u, width):
        return pl.ds(pl.multiple_of(offs[m] + u * width, 128), width)

    def slot(m, u):
        return lax.rem(u, 2) * 3 + m if m < 3 else (0, 2, 4, 5)[m - 3] + u

    def exchange(m, u, width):
        return remote(
            s.sb.at[slot(m, u), :, :, pl.ds(0, width)],
            s.gb.at[:, :, part(m, u, width)],
            s.csend.at[m, u],
            s.crecv.at[m, u],
            partner,
        )

    def give(m, u, width, value):
        if m < 3:

            @pl.when(u >= 2)
            def _():
                exchange(m, u - 2, width).wait_send()

        s.sb[slot(m, u), :, :, 0:width] = value.astype(BF).reshape(
            IN_COUNT, D // IN_COUNT, width
        )
        exchange(m, u, width).start()

    def keep(m, u, width, value):
        ps = part(m, u, width)
        exchange(m, u, width).wait_recv()
        total = value.reshape(IN_COUNT, D // IN_COUNT, width) + s.gb[:, :, ps].astype(F32)
        s.gb[:, :, ps] = total.astype(BF)

    def ffn_back(v, put):
        def run(u, carry):
            us = aligned(u * TILE, TILE)
            dh = dot_nt(s.ddn[...], s.wd[aligned((v * 4 + u) * TILE, TILE), :])
            dgt = (dh * s.ffb[2 + v, :, us].astype(F32)).astype(BF)
            dup = (dh * s.ffb[4 + v, :, us].astype(F32)).astype(BF)
            s.ffb[2 + v, :, us] = dgt
            s.ffb[4 + v, :, us] = dup
            put(0, u, TILE, dot32(s.ddnt[...], s.ffb[v, :, us]))
            put(1, u, TILE, dot32(s.fit[...], dgt))
            put(2, u, TILE, dot32(s.fit[...], dup))
            return carry

        lax.fori_loop(0, 4, run, 0)

    ffn_back(other, give)
    ffn_back(w, keep)
    s.dn[...] = (
        dot_nt(s.ffb[2], s.wg[0])
        + dot_nt(s.ffb[3], s.wg[1])
        + dot_nt(s.ffb[4], s.wu[0])
        + dot_nt(s.ffb[5], s.wu[1])
    )

    s.buffers_free()

    def fourth(rs):
        dv, dg = norm_back(s.h1[rs], s.gain_ref[2:3], s.dn[rs])
        s.dg_ref[2:3] += dg
        dh = s.ct[rs].astype(F32) + dv
        s.h1[rs] = dh
        dv, dg = norm_back(s.ao[rs], s.gain_ref[1:2], dh)
        s.dg_ref[1:2] += dg
        s.ddn[rs] = dv.astype(BF)
        s.ddnt[:, rs] = permuted(dv)

    per_rows(fourth)
    s.first_sends()
    for m in range(3):
        for u in (2, 3):
            exchange(m, u, TILE).wait_send()

    def out_back(v, put):
        def run(u, carry):
            hs = aligned((v * 2 + u) * HD, HD)
            s.datt[:, hs] = dot_nt(s.ddn[...], s.wo[hs, :]).astype(BF)
            put(3, u, HD, dot32(s.ddnt[...], s.att[:, hs]))
            return carry

        lax.fori_loop(0, 2, run, 0)

    out_back(other, give)
    out_back(w, keep)

    s.dka[...] = jnp.zeros_like(s.dka)
    s.dva[...] = jnp.zeros_like(s.dva)

    def attend_back(i, carry):
        a, h = lax.div(i, heads), lax.rem(i, heads)
        ks = pl.ds(pl.multiple_of(a * TILE, TILE), win)
        qr = aligned(a * TILE, TILE)
        hs = aligned(h * HD, HD)
        do = s.datt[qr, hs]
        pr = s.ps[i]
        s.dva[ks, :] += dot_tn(pr, do)
        dp = dot_nt(do, s.va[ks, :])
        pr = pr.astype(F32)
        inner = jnp.sum(pr * dp, axis=-1, keepdims=True)
        ds = (pr * (dp - inner) * s.ts[i].astype(F32)).astype(BF)
        s.dka[ks, :] += dot_tn(ds, s.qs[i])
        dq = dot32(ds, s.ka[ks, :])
        s.datt[qr, hs] = (turn_back(dq, s.cs[qr], s.sn[qr]) * HD ** (-0.5)).astype(BF)
        return carry

    lax.fori_loop(0, heads, attend_back, 0)
    s.plane_finish(0)
    lax.fori_loop(heads, tiles * heads, attend_back, 0)
    s.plane_finish(1)

    s.dks[0] = s.dka[0:WINDOW, :].astype(BF)
    s.dks[1] = s.dva[0:WINDOW, :].astype(BF)
    d_halo = [
        remote(s.dks.at[i], s.dkr.at[i], s.dsend.at[i], s.drecv.at[i], prev_id) for i in range(2)
    ]

    @pl.when(flat > 0)
    def _():
        for cp in d_halo:
            cp.start()

    def query_back(v, put):
        def run(u, carry):
            hs = aligned((v * 2 + u) * HD, HD)
            put(4, u, HD, dot32(s.xat[...], s.datt[:, hs]))
            return carry

        lax.fori_loop(0, 2, run, 0)

    query_back(other, give)
    s.dn[...] = dot_nt(s.datt[:, : HQ // 2], s.wq[0]) + dot_nt(s.datt[:, HQ // 2 :], s.wq[1])
    query_back(w, keep)
    s.plane_start(3)

    @pl.when(flat < n_dev - 1)
    def _():
        for cp in d_halo:
            cp.wait_recv()

    @pl.when(flat == n_dev - 1)
    def _():
        s.dkr[...] = jnp.zeros_like(s.dkr)

    dk = s.dka[tok:, :] + s.dkr[0].astype(F32)
    s.dkv[0] = turn_back(dk, s.cs[...], s.sn[...]).astype(BF)
    s.dkv[1] = (s.dva[tok:, :] + s.dkr[1].astype(F32)).astype(BF)
    kvw = HD // 2
    for i in range(2):
        give(5 + i, 0, kvw, dot32(s.xat[...], s.dkv[i, :, aligned(other * kvw, kvw)]))
    for i in range(2):
        keep(5 + i, 0, kvw, dot32(s.xat[...], s.dkv[i, :, aligned(w * kvw, kvw)]))
    s.plane_start(4)
    s.dn[...] += dot_nt(s.dkv[0], s.wkv_ref[0]) + dot_nt(s.dkv[1], s.wkv_ref[1])

    def fifth(rs):
        dv, dg = norm_back(s.tk[rs].astype(F32), s.gain_ref[0:1], s.dn[rs])
        s.dg_ref[0:1] += dg
        s.h1[rs] = s.h1[rs] + dv

    per_rows(fifth)
    x_far = remote(s.h1, s.x_ref.at[out_rows], s.osend.at[1], s.orecv.at[1], partner)
    x_own = pltpu.make_async_copy(s.h1, s.x_ref.at[out_rows], s.oown.at[1])
    x_far.start()
    x_own.start()

    def finish():
        for cp in w_far:
            cp.wait_send()

        @pl.when(flat < n_dev - 1)
        def _():
            for cp in halo:
                cp.wait_send()

        @pl.when(flat > 0)
        def _():
            for cp in d_halo:
                cp.wait_send()

        for m, count, width in ((3, 2, HD), (4, 2, HD), (5, 1, kvw), (6, 1, kvw)):
            for u in range(count):
                exchange(m, u, width).wait_send()
        y_own.wait()
        x_own.wait()
        y_far.wait()
        x_far.wait()

    return finish


LAYER_INPUTS = (
    "tok_ref",
    "cot_ref",
    "cosi_ref",
    "sini_ref",
    "mq_ref",
    "mkv_ref",
    "mgu_ref",
    "mo_ref",
    "md_ref",
    "ids_ref",
    "gain_ref",
    "wkv_ref",
    "cosb_ref",
    "sinb_ref",
    "wq_ref",
    "wo_ref",
    "wgu_ref",
    "wd_ref",
)
LAYER_OUTPUTS = ("y_ref", "x_ref", "sum_ref", "nm_ref", "ub", "gs_ref")
VMEM_BYTES = 63 << 20


def whole_kernel(ctx_count, wa_count, names, *refs):
    s = Refs()
    for name, ref in zip(names, refs):
        setattr(s, name, ref)
    c = lax.axis_index("ctx")
    w = lax.axis_index("wa")
    flat = c * wa_count + w
    n_dev = ctx_count * wa_count
    barrier = pltpu.get_barrier_semaphore()

    def greet(i, carry):
        other = lax.rem(flat + i, n_dev)
        pl.semaphore_signal(
            barrier,
            inc=1,
            device_id=(lax.div(other, wa_count), lax.rem(other, wa_count)),
            device_id_type=MESH,
        )
        return carry

    lax.fori_loop(1, n_dev, greet, 0)
    pl.semaphore_wait(barrier, n_dev - 1)
    tail = tail_phases(s, ctx_count, wa_count)
    finish = layer_phases(s, ctx_count, wa_count)
    tail()
    finish()


def rotation_tables(tok, n_dev):
    freq = ROPE_BASE ** (-2.0 * np.arange(HD // 2) / HD)
    inner = np.arange(tok)[:, None] * freq[None, :]
    base = (np.arange(n_dev) * tok)[:, None] * freq[None, :]
    return [jnp.asarray(f(a), F32) for a in (inner, base) for f in (np.cos, np.sin)]


def run_whole(
    tokens, cotangent, seq_ids, gains, wkv, moms, wq, wo, wgu, wd, ctx_count, wa_count
):
    block = tokens.shape[0]
    tok = block // wa_count
    n_dev = ctx_count * wa_count
    mom_query, mom_keyval, mom_out, mom_gateup, mom_down = moms
    cosi, sini, cosb, sinb = rotation_tables(tok, n_dev)
    scratch = layer_scratch(tok) | tail_scratch(ctx_count, wa_count)
    names = LAYER_INPUTS + LAYER_OUTPUTS + tuple(scratch)
    any_space = pl.BlockSpec(memory_space=pl.ANY)
    vmem = pl.BlockSpec(memory_space=pltpu.VMEM)
    cols = layout(wa_count)[2]
    shard = jax.ShapeDtypeStruct((D // ctx_count, cols), F32)
    return pl.pallas_call(
        partial(whole_kernel, ctx_count, wa_count, names),
        out_shape=(
            jax.ShapeDtypeStruct((block, D), BF),
            jax.ShapeDtypeStruct((block, D), F32),
            shard,
            shard,
            jax.ShapeDtypeStruct((-(-(D // ctx_count) // 16) * 16, cols), BF),
            jax.ShapeDtypeStruct((8, 128), F32),
        ),
        in_specs=[any_space] * 9 + [vmem] * 5 + [any_space] * 4,
        out_specs=(any_space, any_space, vmem, vmem, vmem, vmem),
        scratch_shapes=list(scratch.values()),
        compiler_params=pltpu.CompilerParams(
            collective_id=0, has_side_effects=True, vmem_limit_bytes=VMEM_BYTES
        ),
        name="whole",
    )(
        tokens,
        cotangent,
        cosi,
        sini,
        mom_query,
        mom_keyval,
        mom_gateup,
        mom_out.T,
        mom_down.T,
        seq_ids.reshape(wa_count, tok),
        gains,
        wkv,
        cosb,
        sinb,
        wq,
        wo,
        wgu,
        wd,
    )


def format_kernel(
    ctx_count,
    wa_count,
    sum_ref,
    nm_ref,
    ub_ref,
    gs_ref,
    first_ref,
    second_ref,
    y_ref,
    x_ref,
    *rest,
):
    outs, (sumv, nmv, ubv, gsv, fv, sv, yv, xv, sem) = rest[:21], rest[21:]
    rows = D // ctx_count
    halves, offs, _ = layout(wa_count)

    def copies(pairs, first):
        return [pltpu.make_async_copy(a, b, sem.at[first + i]) for i, (a, b) in enumerate(pairs)]

    def places(group):
        query, keyval, out, gateup, down = group
        return (down, gateup.at[0], gateup.at[1], out, query, keyval.at[0], keyval.at[1])

    fetched = copies(
        (
            (x_ref, xv),
            (y_ref, yv),
            (sum_ref, sumv),
            (nm_ref, nmv),
            (ub_ref, ubv),
            (gs_ref, gsv),
            (first_ref, fv),
            (second_ref, sv),
        ),
        0,
    )
    for cp in fetched:
        cp.start()
    stored = copies(((xv, outs[1]), (yv, outs[0])), 8)
    for src, group, first in ((sumv, outs[2:7], 10), (nmv, outs[8:13], 17)):
        stored += copies(
            [
                (src.at[:, pl.ds(offs[m], halves[m])], dst)
                for m, dst in enumerate(places(group))
            ],
            first,
        )
    starts = ((0, 1), (1, 2), (2, 9), (9, 16))
    for cp, (a, b) in zip(fetched[:4], starts):
        cp.wait()
        for out in stored[a:b]:
            out.start()
    for cp in fetched[4:]:
        cp.wait()
    for m, dst in enumerate(places(outs[13:18])):
        dst[...] = ubv[0:rows, offs[m] : offs[m] + halves[m]].astype(F32)
    g = gsv[0:4, 0:rows]
    first = ADAM_ONE * fv[...] + (1.0 - ADAM_ONE) * g
    second = ADAM_TWO * sv[...] + (1.0 - ADAM_TWO) * g * g
    outs[7][...] = g
    outs[18][...] = first
    outs[19][...] = second
    outs[20][...] = -GAIN_RATE * first / (jnp.sqrt(second) + ADAM_EPS)
    for cp in stored:
        cp.wait()


def run_format(sums, fresh, updates, gsum, gain_first, gain_second, y, x, ctx_count, wa_count):
    rows = D // ctx_count
    halves = layout(wa_count)[0]
    down, gate, _, out, query, key, _ = halves
    f = lambda *shape: jax.ShapeDtypeStruct(shape, F32)
    weights = [f(rows, query), f(2, rows, key), f(rows, out), f(2, rows, gate), f(rows, down)]
    any_space = pl.BlockSpec(memory_space=pl.ANY)
    vmem = pl.BlockSpec(memory_space=pltpu.VMEM)
    gain = f(4, rows)
    shapes = [jax.ShapeDtypeStruct(y.shape, y.dtype), jax.ShapeDtypeStruct(x.shape, x.dtype)]
    shapes += weights + [gain] + weights + weights + [gain] * 3
    outs = pl.pallas_call(
        partial(format_kernel, ctx_count, wa_count),
        out_shape=shapes,
        in_specs=[any_space] * 8,
        out_specs=[any_space] * 7 + [vmem] + [any_space] * 5 + [vmem] * 8,
        scratch_shapes=[
            *[
                pltpu.VMEM(a.shape, a.dtype)
                for a in (sums, fresh, updates, gsum, gain_first, gain_second, y, x)
            ],
            pltpu.SemaphoreType.DMA((24,)),
        ],
        compiler_params=pltpu.CompilerParams(vmem_limit_bytes=VMEM_BYTES),
        name="format",
    )(sums, fresh, updates, gsum, gain_first, gain_second, y, x)
    return tuple(o.T if i in (4, 6, 10, 12, 15, 17) else o for i, o in enumerate(outs))


def per_device(
    tokens,
    cotangent,
    seq_ids,
    w_query,
    w_keyval,
    w_out,
    w_gateup,
    w_down,
    norm_gains,
    mom_query,
    mom_keyval,
    mom_out,
    mom_gateup,
    mom_down,
    gain_first,
    gain_second,
):
    ctx_count = lax.axis_size("ctx")
    wa_count = lax.axis_size("wa")
    y, x, sums, fresh, updates, gsum = run_whole(
        tokens,
        cotangent,
        seq_ids,
        norm_gains,
        w_keyval,
        (mom_query, mom_keyval, mom_out, mom_gateup, mom_down),
        w_query,
        w_out,
        w_gateup,
        w_down,
        ctx_count,
        wa_count,
    )
    return tuple(
        run_format(
            sums, fresh, updates, gsum, gain_first, gain_second, y, x, ctx_count, wa_count
        )
    )


def solution(mesh):
    in_specs = (
        P("ctx", None),
        P("ctx", None),
        P("ctx"),
        P(None, "wa"),
        P(),
        P("wa", None),
        P(None, None, "wa"),
        P("wa", None),
        P(),
        P("ctx", "wa"),
        P(None, "ctx", "wa"),
        P("wa", "ctx"),
        P(None, "ctx", "wa"),
        P("wa", "ctx"),
        P(None, "ctx"),
        P(None, "ctx"),
    )
    out_specs = (
        P("ctx", None),
        P("ctx", None),
        P("ctx", "wa"),
        P(None, "ctx", "wa"),
        P("wa", "ctx"),
        P(None, "ctx", "wa"),
        P("wa", "ctx"),
        P(None, "ctx"),
        P("ctx", "wa"),
        P(None, "ctx", "wa"),
        P("wa", "ctx"),
        P(None, "ctx", "wa"),
        P("wa", "ctx"),
        P("ctx", "wa"),
        P(None, "ctx", "wa"),
        P("wa", "ctx"),
        P(None, "ctx", "wa"),
        P("wa", "ctx"),
        P(None, "ctx"),
        P(None, "ctx"),
        P(None, "ctx"),
    )
    return jax.shard_map(
        per_device, mesh=mesh, in_specs=in_specs, out_specs=out_specs, check_vma=False
    )
```

```python
from functools import partial
import math

import jax
import jax.numpy as jnp
import numpy as np
from jax import lax
from jax.experimental import pallas as pl
from jax.experimental.pallas import tpu as pltpu
from jax.sharding import PartitionSpec as P

D = 640
FF = 2048
HD = 256
WINDOW = 512
SOFT_CAP = 10
NS_STEPS = 5
HQ = 1024


EPS_NORM = 1e-06
ROPE_BASE = 10000.0
MOMENTUM = 0.95
ADAM_ONE = 0.9
ADAM_TWO = 0.95
ADAM_EPS = 1e-08
GAIN_RATE = 0.1
QUINTIC_A = 3.4445
QUINTIC_B = -4.775
QUINTIC_C = 2.0315
MATRIX_COUNT = 7
MUON_RATE = 0.2

MESH = pl.DeviceIdType.MESH
BF = jnp.bfloat16
F32 = jnp.float32
IN_COUNT = 4
NAMES = ("down", "gate", "up", "out", "query", "key", "value")
WIDTHS = (FF, FF, FF, HQ, HQ, HD, HD)
OWNERS = (7, 4, 8, 5, 11, 9, 10)
PARTS = (
    ((0, 0, 512),),
    ((0, 512, 512),),
    ((1, 0, 512),),
    ((1, 512, 512),),
    ((2, 0, 512),),
    ((2, 512, 512),),
    ((3, 0, 512),),
    ((4, 0, 512),),
    ((5, 0, 128), (6, 0, 128)),
)
TILE = 256


def layout(wa_count):
    halves = [w // wa_count for w in WIDTHS]
    offs = [sum(halves[:i]) for i in range(len(halves))]
    return halves, offs, sum(halves)


def dot32(a, b):
    return jnp.dot(a, b, preferred_element_type=F32)


def eye_mask(n):
    return (
        lax.broadcasted_iota(jnp.int32, (n, n), 0) == lax.broadcasted_iota(jnp.int32, (n, n), 1)
    )


def pad_rows(v, rows):
    if v.shape[0] == rows:
        return v
    return jnp.concatenate([v, jnp.zeros((rows - v.shape[0], v.shape[1]), v.dtype)], axis=0)


def split_into(v, hi, lo):
    top = v.astype(BF)
    hi[...] = top
    lo[...] = (v - top.astype(F32)).astype(BF)


SYM_TILES = ((0, 256), (256, 512), (512, 640))


def sym_tiles(out, block):
    for a, b in SYM_TILES:
        v = block(a, b)
        out[a:, a:b] = v
        if b < D:
            out[a:b, b:] = v[b - a :].T


def prod3(h1, l1, h2, l2):
    return lambda a, b: (
        dot32(h1[a:], h2[:, a:b]) + dot32(h1[a:], l2[:, a:b]) + dot32(l1[a:], h2[:, a:b])
    )


def tail_scratch(ctx_count, wa_count):
    v = pltpu.VMEM
    dma = pltpu.SemaphoreType.DMA
    n_in = IN_COUNT
    n_out = ctx_count // n_in
    rows = D // ctx_count
    rp = -(-rows // 16) * 16
    n_dev = ctx_count * wa_count
    n_ch = len(PARTS)
    cols = layout(wa_count)[2]
    return dict(
        mb=v((rp, cols), BF),
        early=v((6, D // n_in, 512), BF),
        xb=v((ctx_count, rp, FF), BF),
        am=v((D, D), F32),
        dg_ref=v((8, D), F32),
        dgs=v((ctx_count, 8, 128), F32),
        dgr=v((n_dev, 8, 128), F32),
        psend=dma((n_ch, 3)),
        precv=dma((n_ch, 3)),
        lsend=dma((n_ch, n_out - 1)),
        lrecv=dma((n_ch, n_out - 1)),
        gsend=dma((n_ch, 2)),
        grecv=dma,
        usend=dma((n_dev,)),
        urecv=dma((MATRIX_COUNT,)),
        gnsend=dma((n_dev,)),
        gnrecv=dma,
        msem=dma((MATRIX_COUNT,)),
        dfree=pltpu.SemaphoreType.REGULAR,
        pfree=pltpu.SemaphoreType.REGULAR,
        lfree=pltpu.SemaphoreType.REGULAR,
    )


def tail_phases(s, ctx_count, wa_count):
    c = lax.axis_index("ctx")
    w = lax.axis_index("wa")
    n_in = IN_COUNT
    n_out = ctx_count // n_in
    n_dev = ctx_count * wa_count
    p = lax.rem(c, n_in)
    z = lax.div(c, n_in)
    rows = D // ctx_count
    rp = s.xb.shape[1]
    block = D // n_in
    halves, offs, cols = layout(wa_count)
    chunks = [(offs[m[0][0]] + m[0][1], sum(i[2] for i in m)) for m in PARTS]
    me = c * wa_count + w
    per = ctx_count // 2

    near = (p + 1 - 2 * lax.rem(p, 2), p + 2 - 4 * lax.div(p, 2))
    across = 3 - p

    def plane_slot(ci, k):
        lanes = chunks[ci][1]
        if ci < 2:
            return s.early.at[ci * 3 + k]
        if ci < 4:
            return s.wd.at[pl.ds(((ci - 2) * 3 + k) * block, block), pl.ds(0, lanes)]
        i = (ci - 4) * 3 + k
        buf = (s.wg, s.wu)[i // 16]
        i = i % 16
        return buf.at[i // 8, pl.ds(i % 8 // 2 * block, block), pl.ds(i % 2 * 512, lanes)]

    def line_slot(base, ci, j):
        wid = chunks[ci][1]
        if ci < 8:
            start = ci % 4 // 2 * 256 + j * rp
            page, lane = base * 2 + ci // 4, ci % 2 * 512
        else:
            start, page, lane = j * rp, 4 + base, 0
        return s.ffb.at[page, pl.ds(pl.multiple_of(start, 16), rp), pl.ds(lane, wid)]

    def plane_copy(ci, k):
        off, wid = chunks[ci]
        first, second = near[ci % 2], near[1 - ci % 2]
        src, dst = ((first, first), (across, first), (second, second))[k]
        return pltpu.make_async_remote_copy(
            s.gb.at[src, :, pl.ds(off, wid)],
            plane_slot(ci, k),
            s.psend.at[ci, k],
            s.precv.at[ci, k],
            device_id=(z * n_in + dst, w),
            device_id_type=MESH,
        )

    def line_copy(ci, k):
        j = lax.rem(z + k, n_out)
        return pltpu.make_async_remote_copy(
            line_slot(0, ci, j),
            line_slot(1, ci, k - 1),
            s.lsend.at[ci, k - 1],
            s.lrecv.at[ci, k - 1],
            device_id=(j * n_in + p, w),
            device_id_type=MESH,
        )

    def tell_plane(sem):
        for q in near:
            pl.semaphore_signal(sem, inc=1, device_id=(z * n_in + q, w), device_id_type=MESH)

    def down_free():
        tell_plane(s.dfree)

    def buffers_free():
        tell_plane(s.pfree)
        for k in range(1, n_out):
            pl.semaphore_signal(
                s.lfree,
                inc=1,
                device_id=(lax.rem(z + k, n_out) * n_in + p, w),
                device_id_type=MESH,
            )

    def plane_start(ci):
        if ci == 2:
            pl.semaphore_wait(s.dfree, 2)
        if ci == 4:
            pl.semaphore_wait(s.pfree, 2)
        plane_copy(ci, 1).start()
        plane_copy(ci, 0).start()

    def plane_mid(ci):
        off, wid = chunks[ci]
        second = near[1 - ci % 2]
        plane_copy(ci, 1).wait_recv()

        def add(t, carry):
            cs = aligned(off + t * TILE, TILE)
            here = aligned(t * TILE, TILE)
            both = s.gb[second, :, cs].astype(F32) + plane_slot(ci, 1)[:, here].astype(F32)
            s.gb[second, :, cs] = both.astype(BF)
            return carry

        lax.fori_loop(0, wid // TILE, add, 0)
        plane_copy(ci, 2).start()

    def plane_finish(ci):
        off, wid = chunks[ci]
        plane_copy(ci, 0).wait_recv()
        plane_copy(ci, 2).wait_recv()

        def plane_sum(t, carry):
            cs = aligned(off + t * TILE, TILE)
            here = aligned(t * TILE, TILE)
            total = s.gb[p, :, cs].astype(F32)
            for k in (0, 2):
                total = total + plane_slot(ci, k)[:, here].astype(F32)
            for j in range(n_out):
                slab = total[j * rows : (j + 1) * rows]

                @pl.when(z == j)
                def _():
                    s.sum_ref[:, cs] = slab

                line_slot(0, ci, j)[:, here] = pad_rows(slab, rp).astype(BF)
            return carry

        lax.fori_loop(0, wid // TILE, plane_sum, 0)
        if ci == 0:
            pl.semaphore_wait(s.lfree, n_out - 1)
        for k in range(1, n_out):
            line_copy(ci, k).start()

    def gather_copy(ci, i, local):
        m, first, wid = PARTS[ci][i]
        src = s.mb.at[:, pl.ds(offs[m] + first, wid)]
        dst = s.xb.at[c, :, pl.ds(pl.multiple_of(w * halves[m] + first, 128), wid)]
        if local:
            return pltpu.make_async_copy(src, dst, s.grecv)
        return pltpu.make_async_remote_copy(
            src,
            dst,
            s.gsend.at[ci, i],
            s.grecv,
            device_id=(OWNERS[m], 0),
            device_id_type=MESH,
        )

    def line_finish(ci):
        off, wid = chunks[ci]
        for k in range(1, n_out):
            line_copy(ci, k).wait_recv()

        def line_sum(t, carry):
            cs = aligned(off + t * TILE, TILE)
            here = aligned(t * TILE, TILE)
            total = s.sum_ref[:, cs]
            for k in range(n_out - 1):
                total = total + line_slot(1, ci, k)[:, here][:rows].astype(F32)
            s.sum_ref[:, cs] = total
            fresh = MOMENTUM * s.nm_ref[:, cs] + total
            s.nm_ref[:, cs] = fresh
            s.mb[:, cs] = pad_rows(fresh, rp).astype(BF)
            return carry

        lax.fori_loop(0, wid // TILE, line_sum, 0)
        for i, piece in enumerate(PARTS[ci]):
            mine = me == OWNERS[piece[0]] * wa_count

            @pl.when(mine)
            def _():
                gather_copy(ci, i, True).start()

            @pl.when(jnp.logical_not(mine))
            def _():
                gather_copy(ci, i, False).start()

    s.down_free = down_free
    s.buffers_free = buffers_free
    s.plane_start = plane_start
    s.plane_mid = plane_mid
    s.plane_finish = plane_finish

    sources = (
        s.md_ref,
        s.mgu_ref.at[0],
        s.mgu_ref.at[1],
        s.mo_ref,
        s.mq_ref,
        s.mkv_ref.at[0],
        s.mkv_ref.at[1],
    )
    moms = [
        pltpu.make_async_copy(src, s.nm_ref.at[:, pl.ds(offs[m], halves[m])], s.msem.at[m])
        for m, src in enumerate(sources)
    ]
    for cp in moms:
        cp.start()

    def rest():
        for i in range(ctx_count):
            s.dgs[i, :, 0:rows] = s.dg_ref[:, i * rows : (i + 1) * rows]

        def gain_copy(t):
            i, v = lax.div(t, wa_count), lax.rem(t, wa_count)
            return pltpu.make_async_remote_copy(
                s.dgs.at[i],
                s.dgr.at[me],
                s.gnsend.at[t],
                s.gnrecv,
                device_id=(i, v),
                device_id_type=MESH,
            )

        def gain_send(t, carry):
            gain_copy(lax.rem(me + t, n_dev)).start()
            return carry

        def gain_sent(t, carry):
            gain_copy(lax.rem(me + t, n_dev)).wait_send()
            return carry

        for cp in moms:
            cp.wait()
        plane_mid(7)
        plane_mid(8)
        line_finish(0)
        line_finish(1)
        plane_finish(6)
        line_finish(2)
        line_finish(3)
        plane_finish(7)
        plane_finish(8)
        line_finish(4)
        line_finish(5)
        pltpu.make_async_copy(s.dgs.at[c], s.dgr.at[me], s.gnrecv).start()
        lax.fori_loop(1, n_dev, gain_send, 0)
        for ci in range(6, 9):
            line_finish(ci)
        for ci in range(len(chunks)):
            for k in range(3):
                plane_copy(ci, k).wait_send()
            for k in range(1, n_out):
                line_copy(ci, k).wait_send()
        solve()
        pltpu.make_async_copy(s.dgr, s.dgr, s.gnrecv).wait()
        s.gs_ref[...] = jnp.sum(s.dgr[...], axis=0)
        lax.fori_loop(1, n_dev, gain_sent, 0)
        updates_back()

    def owned_by(*which):
        hit = me == OWNERS[which[0]] * wa_count
        for m in which[1:]:
            hit = jnp.logical_or(hit, me == OWNERS[m] * wa_count)
        return hit

    def solve():
        is_owner = owned_by(*range(MATRIX_COUNT))
        is_small = owned_by(5, 6)
        is_wide = owned_by(0, 1, 2)
        tiles = jnp.where(is_small, HD // TILE, jnp.where(is_wide, FF // TILE, HQ // TILE))
        am, xf = s.am, s.dka.at[pl.ds(0, D)]
        ah = s.wd.at[pl.ds(0, D)]
        al = s.wd.at[pl.ds(D, D)]
        ph = s.wd.at[pl.ds(2 * D, D)]
        plo = s.wo.at[pl.ds(0, D)]
        qh = s.wu.at[0, :, pl.ds(0, D)]

        def tile_of(t):
            return s.wg.at[lax.div(t, 4), :, aligned(lax.rem(t, 4) * TILE, TILE)]

        for m in range(MATRIX_COUNT):

            @pl.when(me == OWNERS[m] * wa_count)
            def _(m=m):
                whole = s.xb.at[:, :, pl.ds(0, halves[m] * wa_count)]
                pltpu.make_async_copy(whole, whole, s.grecv).wait()

        @pl.when(is_owner)
        def _():
            am[...] = jnp.zeros_like(am)

            def gram(t, carry):
                cs = aligned(t * TILE, TILE)
                for i in range(ctx_count):
                    xf[i * rows : (i + 1) * rows, :] = s.xb[i, :, cs][:rows].astype(F32)
                x = xf[...].astype(BF)
                tile_of(t)[...] = x

                @pl.when(jnp.logical_not(is_small))
                def _():
                    for a, b in SYM_TILES:
                        am[a:, a:b] += dot_nt(x[a:], x[a:b])

                @pl.when(is_small)
                def _():
                    am[0:HD, 0:HD] = dot_tn(x, x)

                return carry

            lax.fori_loop(0, tiles, gram, 0)
            norm2 = jnp.sum(jnp.where(eye_mask(D), am[...], 0.0), keepdims=True)
            inv = 1.0 / (jnp.sqrt(norm2) + 1e-07)
            inv2 = inv * inv
            sym_tiles(am, lambda a, b: am[a:, a:b] * inv2)

            def shifted(a, b, square):
                rest = QUINTIC_B * am[a:, a:b] + QUINTIC_C * square
                top = rest[: b - a] + jnp.where(eye_mask(b - a), QUINTIC_A, 0.0)
                return jnp.concatenate([top, rest[b - a :]], axis=0) if b < D else top

            def poly():
                split_into(am[...], ah, al)
                square = prod3(ah, al, ah, al)
                sym_tiles(am, lambda a, b: shifted(a, b, square(a, b)))

            def advance():
                sym_tiles(am, prod3(ph, plo, ah, al))
                split_into(am[...], ah, al)
                sym_tiles(am, prod3(ah, al, ph, plo))

            def grow():
                sym_tiles(am, lambda a, b: dot32(ph[a:], qh[:, a:b]))
                qh[...] = am[...].astype(BF)

            poly()
            split_into(am[...], ph, plo)
            qh[...] = ph[...]
            advance()

            def sweep(i, carry):
                poly()
                split_into(am[...], ph, plo)
                grow()
                advance()
                return carry

            lax.fori_loop(0, NS_STEPS - 2, sweep, 0)
            ah[...] = am[...].astype(BF)
            sym_tiles(am, lambda a, b: shifted(a, b, dot32(ah[a:], ah[:, a:b])))
            ph[...] = am[...].astype(BF)
            grow()
            rates = [-MUON_RATE * 0.2 * math.sqrt(n) for n in (D, FF, HQ)]
            rate = jnp.where(is_small, rates[0], jnp.where(is_wide, rates[1], rates[2]))
            scale = rate * inv

            def put(v, lanes, value):
                for i in range(ctx_count):
                    s.ffb[v * 2 + i // per, i % per * rp : (i % per + 1) * rp, lanes] = pad_rows(
                        value[i * rows : (i + 1) * rows], rp
                    ).astype(BF)

            def back(v, t):
                @pl.when(jnp.logical_not(is_small))
                def _():
                    whole = v * jnp.where(is_wide, 4, 2) + t
                    xf[...] = dot32(qh[...], tile_of(whole)[...]) * scale
                    put(v, aligned(t * TILE, TILE), xf)

                @pl.when(is_small)
                def _():
                    xf[...] = dot32(tile_of(t)[...], s.wu[0, 0:HD, 0:HD]) * scale
                    for half in range(2):
                        lanes = slice(half * (HD // 2), (half + 1) * (HD // 2))
                        put(half, pl.ds(0, HD // 2), xf[:, lanes])

            for v in range(2):
                count = jnp.where(is_small, 1 - v, jnp.where(is_wide, 4, 2))

                def run(t, carry, v=v):
                    back(v, t)
                    return carry

                lax.fori_loop(0, count, run, 0)
                for m in range(MATRIX_COUNT):

                    @pl.when(me == OWNERS[m] * wa_count)
                    def _(m=m, v=v):
                        def send(i, carry):
                            there = lax.rem(c + i, ctx_count)
                            update_copy(m, there * wa_count + v, False).start()
                            return carry

                        if v == 0:
                            update_copy(m, c * wa_count, True).start()
                            lax.fori_loop(1, ctx_count, send, 0)
                        else:
                            lax.fori_loop(0, ctx_count, send, 0)

    def update_copy(m, t, local):
        i, v = lax.div(t, wa_count), lax.rem(t, wa_count)
        start = pl.multiple_of(lax.rem(i, per) * rp, 16)
        src = s.ffb.at[v * 2 + lax.div(i, per), pl.ds(start, rp), pl.ds(0, halves[m])]
        dst = s.ub.at[:, pl.ds(offs[m], halves[m])]
        if local:
            return pltpu.make_async_copy(src, dst, s.urecv.at[m])
        return pltpu.make_async_remote_copy(
            src, dst, s.usend.at[t], s.urecv.at[m], device_id=(i, v), device_id_type=MESH
        )

    def updates_back():
        for m in range(MATRIX_COUNT):
            piece = s.ub.at[:, pl.ds(offs[m], halves[m])]
            pltpu.make_async_copy(piece, piece, s.urecv.at[m]).wait()

        for m in range(MATRIX_COUNT):
            owner = OWNERS[m] * wa_count

            @pl.when(me != owner)
            def _(m=m):
                for ci, part in enumerate(PARTS):
                    for i, piece in enumerate(part):
                        if piece[0] == m:
                            gather_copy(ci, i, False).wait_send()

            @pl.when(me == owner)
            def _(m=m, owner=owner):
                def done(t, carry):
                    update_copy(m, lax.rem(owner + t, n_dev), False).wait_send()
                    return carry

                lax.fori_loop(1, n_dev, done, 0)

    return rest


class Refs:
    pass


def dot_nt(a, b):
    return lax.dot_general(a, b, (((1,), (1,)), ((), ())), preferred_element_type=F32)


def dot_tn(a, b):
    return lax.dot_general(a, b, (((0,), (0,)), ((), ())), preferred_element_type=F32)


def aligned(start, size):
    return pl.ds(pl.multiple_of(start, size), size)


def norm_parts(v, gain):
    r = lax.rsqrt(jnp.mean(v * v, axis=-1, keepdims=True) + EPS_NORM)
    return r, v * r, 1.0 + gain


def norm_back(v, gain, e):
    r, zed, g1 = norm_parts(v, gain)
    e1 = e * g1
    dv = r * (e1 - zed * jnp.mean(e1 * zed, axis=-1, keepdims=True))
    return dv, jnp.sum(e * zed, axis=0, keepdims=True)


def layer_scratch(tok):
    v = pltpu.VMEM
    dma = pltpu.SemaphoreType.DMA
    cols = sum(WIDTHS) // 2
    heads = HQ // HD
    tiles = tok // TILE
    win = WINDOW + TILE
    return dict(
        wq=v((2, D, HQ // 2), BF),
        wo=v((HQ, D), BF),
        wg=v((2, D, FF // 2), BF),
        wu=v((2, D, FF // 2), BF),
        wd=v((FF, D), BF),
        tk=v((tok, D), BF),
        ct=v((tok, D), BF),
        xa=v((tok, D), BF),
        xat=v((D, tok), BF),
        fit=v((D, tok), BF),
        ddn=v((tok, D), BF),
        ddnt=v((D, tok), BF),
        cs=v((tok, HD // 2), F32),
        sn=v((tok, HD // 2), F32),
        ka=v((WINDOW + tok, HD), BF),
        va=v((WINDOW + tok, HD), BF),
        idown=v((8, tok), jnp.int32),
        idprev=v((8, tok), jnp.int32),
        qs=v((tiles * heads, TILE, HD), BF),
        ps=v((tiles * heads, TILE, win), BF),
        ts=v((tiles * heads, TILE, win), BF),
        att=v((tok, HQ), BF),
        ao=v((tok, D), F32),
        h1=v((tok, D), F32),
        dn=v((tok, D), F32),
        ffb=v((6, tok, FF // 2), BF),
        datt=v((tok, HQ), BF),
        dka=v((WINDOW + tok, HD), F32),
        dva=v((WINDOW + tok, HD), F32),
        dks=v((2, tok, HD), BF),
        dkr=v((2, tok, HD), BF),
        dkv=v((2, tok, HD), BF),
        sb=v((6, IN_COUNT, D // IN_COUNT, TILE), BF),
        gb=v((IN_COUNT, D // IN_COUNT, cols), BF),
        wsend=dma((5,)),
        wrecv=dma((5,)),
        wown=dma((5,)),
        ksend=dma((3,)),
        krecv=dma((3,)),
        dsend=dma((2, 2)),
        drecv=dma((2, 2)),
        csend=dma((MATRIX_COUNT, 4)),
        crecv=dma((MATRIX_COUNT, 4)),
        osend=dma((2,)),
        orecv=dma((2,)),
        oown=dma((2,)),
        tsem=dma((4,)),
    )


def layer_phases(s, ctx_count, wa_count):
    c = lax.axis_index("ctx")
    w = lax.axis_index("wa")
    other = 1 - w
    flat = c * wa_count + w
    n_dev = ctx_count * wa_count
    tok = s.xa.shape[0]
    rows = D // ctx_count
    n_out = ctx_count // IN_COUNT
    heads = HQ // HD
    tiles = tok // TILE
    win = WINDOW + TILE
    half_ff = FF // 2
    halves, offs, cols = layout(wa_count)
    step = 128
    partner = (c, other)
    follow = jnp.minimum(flat + 1, n_dev - 1)
    ahead = jnp.maximum(flat - 1, 0)
    next_id = (lax.div(follow, wa_count), lax.rem(follow, wa_count))
    prev_id = (lax.div(ahead, wa_count), lax.rem(ahead, wa_count))
    order = [zz * IN_COUNT + pp for pp in range(IN_COUNT) for zz in range(n_out)]

    def remote(src, dst, send, recv, where):
        return pltpu.make_async_remote_copy(
            src, dst, send, recv, device_id=where, device_id_type=MESH
        )

    def permuted(v):
        t = v.astype(BF).astype(F32).T
        return jnp.concatenate([t[i * rows : (i + 1) * rows] for i in order], axis=0).astype(BF)

    def per_rows(body):
        def run(i, carry):
            body(aligned(i * step, step))
            return carry

        lax.fori_loop(0, tok // step, run, 0)

    out_rows = aligned(w * tok, tok)
    tok_in = pltpu.make_async_copy(s.tok_ref.at[out_rows], s.tk, s.tsem.at[0])
    cot_in = pltpu.make_async_copy(s.cot_ref.at[out_rows], s.ct, s.tsem.at[1])
    tables = [
        pltpu.make_async_copy(s.cosi_ref, s.cs, s.tsem.at[2]),
        pltpu.make_async_copy(s.sini_ref, s.sn, s.tsem.at[3]),
    ]
    tok_in.start()
    for cp in tables:
        cp.start()
    cot_in.start()

    wk_refs = (
        (s.wq_ref, s.wq.at[w]),
        (s.wo_ref, s.wo.at[aligned(w * (HQ // 2), HQ // 2)]),
        (s.wgu_ref.at[0], s.wg.at[w]),
        (s.wgu_ref.at[1], s.wu.at[w]),
        (s.wd_ref, s.wd.at[aligned(w * half_ff, half_ff)]),
    )
    w_far = [remote(a, b, s.wsend.at[i], s.wrecv.at[i], partner) for i, (a, b) in enumerate(wk_refs)]
    w_own = [pltpu.make_async_copy(a, b, s.wown.at[i]) for i, (a, b) in enumerate(wk_refs)]
    for far, own in zip(w_far, w_own):
        far.start()
        own.start()

    def weights_ready(i):
        w_own[i].wait()
        w_far[i].wait_recv()

    tok_in.wait()

    def first(rs):
        x = s.tk[rs].astype(F32)
        _, zed, g1 = norm_parts(x, s.gain_ref[0:1])
        s.xa[rs] = (zed * g1).astype(BF)

    per_rows(first)

    cb, sb_ = s.cosb_ref[pl.ds(flat, 1), :], s.sinb_ref[pl.ds(flat, 1), :]
    for cp in tables:
        cp.wait()
    cosi, sini = s.cs[...], s.sn[...]
    s.cs[...] = cb * cosi - sb_ * sini
    s.sn[...] = sb_ * cosi + cb * sini
    hh = HD // 2

    def turn(v, cosine, sine):
        a, b = v[:, :hh], v[:, hh:]
        return jnp.concatenate([a * cosine - b * sine, b * cosine + a * sine], axis=1)

    def turn_back(v, cosine, sine):
        a, b = v[:, :hh], v[:, hh:]
        return jnp.concatenate([a * cosine + b * sine, b * cosine - a * sine], axis=1)

    s.ka[WINDOW:, :] = turn(dot32(s.xa[...], s.wkv_ref[0]), s.cs[...], s.sn[...]).astype(BF)
    s.idown[...] = jnp.broadcast_to(s.ids_ref[pl.ds(w, 1), :], (8, tok))
    halo = [
        remote(src, dst, s.ksend.at[i], s.krecv.at[i], next_id)
        for i, (src, dst) in enumerate(
            (
                (s.ka.at[pl.ds(tok, WINDOW)], s.ka.at[pl.ds(0, WINDOW)]),
                (s.va.at[pl.ds(tok, WINDOW)], s.va.at[pl.ds(0, WINDOW)]),
                (s.idown, s.idprev),
            )
        )
    ]

    @pl.when(flat < n_dev - 1)
    def _():
        halo[2].start()
        halo[0].start()

    s.va[WINDOW:, :] = dot32(s.xa[...], s.wkv_ref[1]).astype(BF)

    @pl.when(flat < n_dev - 1)
    def _():
        halo[1].start()

    def flip(rs):
        s.xat[:, rs] = permuted(s.xa[rs])

    weights_ready(0)

    def project(h, carry):
        v, u = lax.div(h, heads // 2), lax.rem(h, heads // 2)
        q = dot32(s.xa[...], s.wq[v, :, aligned(u * HD, HD)])
        q = (turn(q, s.cs[...], s.sn[...]) * HD ** (-0.5)).astype(BF)
        for a in range(tiles):
            s.qs[a * heads + h] = q[a * TILE : (a + 1) * TILE]
        return carry

    lax.fori_loop(0, heads, project, 0)
    per_rows(flip)

    @pl.when(flat > 0)
    def _():
        for cp in halo:
            cp.wait_recv()

    @pl.when(flat == 0)
    def _():
        s.ka[0:WINDOW, :] = jnp.zeros((WINDOW, HD), BF)
        s.va[0:WINDOW, :] = jnp.zeros((WINDOW, HD), BF)
        s.idprev[...] = jnp.full((8, tok), -1, jnp.int32)

    row_ids = jnp.concatenate([s.idprev[0:1, :], s.idown[0:1, :]], axis=1)
    own_col = jnp.broadcast_to(s.idown[0:1, :], (128, tok)).T[:, 0:1]
    gap = lax.broadcasted_iota(jnp.int32, (TILE, win), 1) - lax.broadcasted_iota(
        jnp.int32, (TILE, win), 0
    )
    for a in range(tiles):
        same = own_col[a * TILE : (a + 1) * TILE] == row_ids[:, a * TILE : a * TILE + win]
        ok = jnp.logical_and(same, jnp.logical_and(gap > 0, gap <= WINDOW))
        s.ffb[a, 0:TILE, 0:win] = jnp.where(ok, 1.0, 0.0).astype(BF)

    def attend(i, carry):
        a, h = lax.div(i, heads), lax.rem(i, heads)
        ks = pl.ds(pl.multiple_of(a * TILE, TILE), win)
        t = jnp.tanh(dot_nt(s.qs[i], s.ka[ks, :]) * (1.0 / SOFT_CAP))
        e = jnp.exp(SOFT_CAP * t) * s.ffb[a, 0:TILE, 0:win].astype(F32)
        pr = e * (1.0 / jnp.sum(e, axis=-1, keepdims=True))
        pr = pr.astype(BF)
        s.ps[i] = pr
        s.ts[i] = (1.0 - t * t).astype(BF)
        o = dot32(pr, s.va[ks, :])
        s.att[aligned(a * TILE, TILE), aligned(h * HD, HD)] = o.astype(BF)
        return carry

    lax.fori_loop(0, tiles * heads, attend, 0)

    weights_ready(1)
    s.ao[...] = dot32(s.att[...], s.wo[...])

    def second(rs):
        _, zed, g1 = norm_parts(s.ao[rs], s.gain_ref[1:2])
        h = s.tk[rs].astype(F32) + zed * g1
        s.h1[rs] = h
        _, zed, g1 = norm_parts(h, s.gain_ref[2:3])
        n = zed * g1
        s.xa[rs] = n.astype(BF)
        s.fit[:, rs] = permuted(n)

    per_rows(second)

    weights_ready(2)
    weights_ready(3)
    root = 0.7978845608028654

    def forward(i, carry):
        v, u = lax.div(i, 4), lax.rem(i, 4)
        us = aligned(u * TILE, TILE)
        gt = dot32(s.xa[...], s.wg[v, :, us])
        up = dot32(s.xa[...], s.wu[v, :, us])
        g2 = gt * gt
        th = jnp.tanh(root * gt * (1.0 + 0.044715 * g2))
        lift = 0.5 * (1.0 + th)
        act = gt * lift
        slope = lift + 0.5 * gt * (1.0 - th * th) * (root * (1.0 + 3.0 * 0.044715 * g2))
        s.ffb[v, :, us] = (act * up).astype(BF)
        s.ffb[2 + v, :, us] = (up * slope).astype(BF)
        s.ffb[4 + v, :, us] = act.astype(BF)
        return carry

    lax.fori_loop(0, 8, forward, 0)
    weights_ready(4)
    s.dn[...] = dot32(s.ffb[0], s.wd[:half_ff]) + dot32(s.ffb[1], s.wd[half_ff:])
    s.dg_ref[...] = jnp.zeros_like(s.dg_ref)

    def third(rs):
        dn = s.dn[rs]
        _, zed, g1 = norm_parts(dn, s.gain_ref[3:4])
        s.xa[rs] = (s.h1[rs] + zed * g1).astype(BF)
        dv, dg = norm_back(dn, s.gain_ref[3:4], s.ct[rs].astype(F32))
        s.dg_ref[3:4] += dg
        s.ddn[rs] = dv.astype(BF)
        s.ddnt[:, rs] = permuted(dv)

    cot_in.wait()
    per_rows(third)
    y_far = remote(s.xa, s.y_ref.at[out_rows], s.osend.at[0], s.orecv.at[0], partner)
    y_own = pltpu.make_async_copy(s.xa, s.y_ref.at[out_rows], s.oown.at[0])
    y_far.start()
    y_own.start()

    def part(m, u, width):
        return pl.ds(pl.multiple_of(offs[m] + u * width, 128), width)

    def slot(m, u):
        return lax.rem(u, 2) * 3 + m if m < 3 else (0, 2, 4, 5)[m - 3] + u

    def exchange(m, u, width):
        return remote(
            s.sb.at[slot(m, u), :, :, pl.ds(0, width)],
            s.gb.at[:, :, part(m, u, width)],
            s.csend.at[m, u],
            s.crecv.at[m, u],
            partner,
        )

    def give(m, u, width, value):
        if m < 3:

            @pl.when(u >= 2)
            def _():
                exchange(m, u - 2, width).wait_send()

        s.sb[slot(m, u), :, :, 0:width] = value.astype(BF).reshape(
            IN_COUNT, D // IN_COUNT, width
        )
        exchange(m, u, width).start()

    def keep(m, u, width, value):
        ps = part(m, u, width)
        exchange(m, u, width).wait_recv()
        total = value.reshape(IN_COUNT, D // IN_COUNT, width) + s.gb[:, :, ps].astype(F32)
        s.gb[:, :, ps] = total.astype(BF)

    def down_back(v, put):
        def run(u, carry):
            put(0, u, TILE, dot32(s.ddnt[...], s.ffb[v, :, aligned(u * TILE, TILE)]))
            return carry

        lax.fori_loop(0, 4, run, 0)

    def gate_back(v, put):
        def run(u, carry):
            us = aligned(u * TILE, TILE)
            dh = dot_nt(s.ddn[...], s.wd[aligned((v * 4 + u) * TILE, TILE), :])
            dgt = (dh * s.ffb[2 + v, :, us].astype(F32)).astype(BF)
            dup = (dh * s.ffb[4 + v, :, us].astype(F32)).astype(BF)
            s.ffb[2 + v, :, us] = dgt
            s.ffb[4 + v, :, us] = dup
            put(1, u, TILE, dot32(s.fit[...], dgt))
            put(2, u, TILE, dot32(s.fit[...], dup))
            return carry

        lax.fori_loop(0, 4, run, 0)

    down_back(other, give)
    down_back(w, keep)
    s.plane_start(0)
    s.plane_start(1)
    gate_back(other, give)
    gate_back(w, keep)
    s.down_free()
    s.dn[...] = dot_nt(s.ffb[2], s.wg[0]) + dot_nt(s.ffb[3], s.wg[1])
    s.plane_mid(0)
    s.plane_mid(1)
    s.plane_start(2)
    s.plane_start(3)
    s.dn[...] += dot_nt(s.ffb[4], s.wu[0]) + dot_nt(s.ffb[5], s.wu[1])

    s.buffers_free()

    def fourth(rs):
        dv, dg = norm_back(s.h1[rs], s.gain_ref[2:3], s.dn[rs])
        s.dg_ref[2:3] += dg
        dh = s.ct[rs].astype(F32) + dv
        s.h1[rs] = dh
        dv, dg = norm_back(s.ao[rs], s.gain_ref[1:2], dh)
        s.dg_ref[1:2] += dg
        s.ddn[rs] = dv.astype(BF)
        s.ddnt[:, rs] = permuted(dv)

    per_rows(fourth)
    s.plane_start(4)
    s.plane_start(5)
    for m in range(3):
        for u in (2, 3):
            exchange(m, u, TILE).wait_send()

    def out_back(v, put):
        def run(u, carry):
            hs = aligned((v * 2 + u) * HD, HD)
            s.datt[:, hs] = dot_nt(s.ddn[...], s.wo[hs, :]).astype(BF)
            put(3, u, HD, dot32(s.ddnt[...], s.att[:, hs]))
            return carry

        lax.fori_loop(0, 2, run, 0)

    out_back(other, give)
    out_back(w, keep)
    s.plane_finish(0)
    s.plane_finish(1)

    s.dka[...] = jnp.zeros_like(s.dka)
    s.dva[...] = jnp.zeros_like(s.dva)

    def attend_back(i, carry):
        a, h = lax.div(i, heads), lax.rem(i, heads)
        ks = pl.ds(pl.multiple_of(a * TILE, TILE), win)
        qr = aligned(a * TILE, TILE)
        hs = aligned(h * HD, HD)
        do = s.datt[qr, hs]
        pr = s.ps[i]
        s.dva[ks, :] += dot_tn(pr, do)
        dp = dot_nt(do, s.va[ks, :])
        pr = pr.astype(F32)
        inner = jnp.sum(pr * dp, axis=-1, keepdims=True)
        ds = (pr * (dp - inner) * s.ts[i].astype(F32)).astype(BF)
        s.dka[ks, :] += dot_tn(ds, s.qs[i])
        dq = dot32(ds, s.ka[ks, :])
        s.datt[qr, hs] = (turn_back(dq, s.cs[qr], s.sn[qr]) * HD ** (-0.5)).astype(BF)
        return carry

    def d_part(i, half):
        rs = pl.ds(half * TILE, TILE)
        return remote(
            s.dks.at[i, rs], s.dkr.at[i, rs], s.dsend.at[i, half], s.drecv.at[i, half], prev_id
        )

    d_halo = [d_part(i, half) for half in range(2) for i in range(2)]

    def d_send(half):
        rs = slice(half * TILE, (half + 1) * TILE)
        s.dks[0, rs] = s.dka[rs].astype(BF)
        s.dks[1, rs] = s.dva[rs].astype(BF)

        @pl.when(flat > 0)
        def _():
            for cp in d_halo[half * 2 : half * 2 + 2]:
                cp.start()

    lax.fori_loop(0, heads, attend_back, 0)
    d_send(0)
    s.plane_mid(2)
    s.plane_mid(3)
    s.plane_start(6)
    lax.fori_loop(heads, tiles * heads, attend_back, 0)
    d_send(1)

    def query_back(v, put):
        def run(u, carry):
            hs = aligned((v * 2 + u) * HD, HD)
            put(4, u, HD, dot32(s.xat[...], s.datt[:, hs]))
            return carry

        lax.fori_loop(0, 2, run, 0)

    query_back(other, give)
    s.plane_mid(4)
    s.plane_mid(5)
    s.dn[...] = dot_nt(s.datt[:, : HQ // 2], s.wq[0]) + dot_nt(s.datt[:, HQ // 2 :], s.wq[1])
    query_back(w, keep)
    s.plane_start(7)
    s.plane_finish(2)
    s.plane_finish(3)

    @pl.when(flat < n_dev - 1)
    def _():
        for cp in d_halo:
            cp.wait_recv()

    @pl.when(flat == n_dev - 1)
    def _():
        s.dkr[...] = jnp.zeros_like(s.dkr)

    dk = s.dka[tok:, :] + s.dkr[0].astype(F32)
    s.dkv[0] = turn_back(dk, s.cs[...], s.sn[...]).astype(BF)
    s.dkv[1] = (s.dva[tok:, :] + s.dkr[1].astype(F32)).astype(BF)
    kvw = HD // 2
    for i in range(2):
        give(5 + i, 0, kvw, dot32(s.xat[...], s.dkv[i, :, aligned(other * kvw, kvw)]))
    for i in range(2):
        keep(5 + i, 0, kvw, dot32(s.xat[...], s.dkv[i, :, aligned(w * kvw, kvw)]))
    s.plane_start(8)
    s.plane_mid(6)
    s.plane_finish(4)
    s.plane_finish(5)
    s.dn[...] += dot_nt(s.dkv[0], s.wkv_ref[0]) + dot_nt(s.dkv[1], s.wkv_ref[1])

    def fifth(rs):
        dv, dg = norm_back(s.tk[rs].astype(F32), s.gain_ref[0:1], s.dn[rs])
        s.dg_ref[0:1] += dg
        s.h1[rs] = s.h1[rs] + dv

    per_rows(fifth)
    x_far = remote(s.h1, s.x_ref.at[out_rows], s.osend.at[1], s.orecv.at[1], partner)
    x_own = pltpu.make_async_copy(s.h1, s.x_ref.at[out_rows], s.oown.at[1])
    x_far.start()
    x_own.start()

    def finish():
        for cp in w_far:
            cp.wait_send()

        @pl.when(flat < n_dev - 1)
        def _():
            for cp in halo:
                cp.wait_send()

        @pl.when(flat > 0)
        def _():
            for cp in d_halo:
                cp.wait_send()

        for m, count, width in ((3, 2, HD), (4, 2, HD), (5, 1, kvw), (6, 1, kvw)):
            for u in range(count):
                exchange(m, u, width).wait_send()
        y_own.wait()
        x_own.wait()
        y_far.wait()
        x_far.wait()

    return finish


LAYER_INPUTS = (
    "tok_ref",
    "cot_ref",
    "cosi_ref",
    "sini_ref",
    "mq_ref",
    "mkv_ref",
    "mgu_ref",
    "mo_ref",
    "md_ref",
    "ids_ref",
    "gain_ref",
    "wkv_ref",
    "cosb_ref",
    "sinb_ref",
    "wq_ref",
    "wo_ref",
    "wgu_ref",
    "wd_ref",
)
LAYER_OUTPUTS = ("y_ref", "x_ref", "sum_ref", "nm_ref", "ub", "gs_ref")
VMEM_BYTES = 63 << 20


def whole_kernel(ctx_count, wa_count, names, *refs):
    s = Refs()
    for name, ref in zip(names, refs):
        setattr(s, name, ref)
    c = lax.axis_index("ctx")
    w = lax.axis_index("wa")
    flat = c * wa_count + w
    n_dev = ctx_count * wa_count
    barrier = pltpu.get_barrier_semaphore()

    def greet(i, carry):
        other = lax.rem(flat + i, n_dev)
        pl.semaphore_signal(
            barrier,
            inc=1,
            device_id=(lax.div(other, wa_count), lax.rem(other, wa_count)),
            device_id_type=MESH,
        )
        return carry

    lax.fori_loop(1, n_dev, greet, 0)
    pl.semaphore_wait(barrier, n_dev - 1)
    tail = tail_phases(s, ctx_count, wa_count)
    finish = layer_phases(s, ctx_count, wa_count)
    tail()
    finish()


def rotation_tables(tok, n_dev):
    freq = ROPE_BASE ** (-2.0 * np.arange(HD // 2) / HD)
    inner = np.arange(tok)[:, None] * freq[None, :]
    base = (np.arange(n_dev) * tok)[:, None] * freq[None, :]
    return [jnp.asarray(f(a), F32) for a in (inner, base) for f in (np.cos, np.sin)]


def run_whole(
    tokens, cotangent, seq_ids, gains, wkv, moms, wq, wo, wgu, wd, ctx_count, wa_count
):
    block = tokens.shape[0]
    tok = block // wa_count
    n_dev = ctx_count * wa_count
    mom_query, mom_keyval, mom_out, mom_gateup, mom_down = moms
    cosi, sini, cosb, sinb = rotation_tables(tok, n_dev)
    scratch = layer_scratch(tok) | tail_scratch(ctx_count, wa_count)
    names = LAYER_INPUTS + LAYER_OUTPUTS + tuple(scratch)
    any_space = pl.BlockSpec(memory_space=pl.ANY)
    vmem = pl.BlockSpec(memory_space=pltpu.VMEM)
    cols = layout(wa_count)[2]
    shard = jax.ShapeDtypeStruct((D // ctx_count, cols), F32)
    return pl.pallas_call(
        partial(whole_kernel, ctx_count, wa_count, names),
        out_shape=(
            jax.ShapeDtypeStruct((block, D), BF),
            jax.ShapeDtypeStruct((block, D), F32),
            shard,
            shard,
            jax.ShapeDtypeStruct((-(-(D // ctx_count) // 16) * 16, cols), BF),
            jax.ShapeDtypeStruct((8, 128), F32),
        ),
        in_specs=[any_space] * 9 + [vmem] * 5 + [any_space] * 4,
        out_specs=(any_space, any_space, vmem, vmem, vmem, vmem),
        scratch_shapes=list(scratch.values()),
        compiler_params=pltpu.CompilerParams(
            collective_id=0, has_side_effects=True, vmem_limit_bytes=VMEM_BYTES
        ),
        name="whole",
    )(
        tokens,
        cotangent,
        cosi,
        sini,
        mom_query,
        mom_keyval,
        mom_gateup,
        mom_out.T,
        mom_down.T,
        seq_ids.reshape(wa_count, tok),
        gains,
        wkv,
        cosb,
        sinb,
        wq,
        wo,
        wgu,
        wd,
    )


def format_kernel(
    ctx_count,
    wa_count,
    sum_ref,
    nm_ref,
    ub_ref,
    gs_ref,
    first_ref,
    second_ref,
    y_ref,
    x_ref,
    *rest,
):
    outs, (sumv, nmv, ubv, gsv, fv, sv, yv, xv, sem) = rest[:21], rest[21:]
    rows = D // ctx_count
    halves, offs, _ = layout(wa_count)

    def copies(pairs, first):
        return [pltpu.make_async_copy(a, b, sem.at[first + i]) for i, (a, b) in enumerate(pairs)]

    def places(group):
        query, keyval, out, gateup, down = group
        return (down, gateup.at[0], gateup.at[1], out, query, keyval.at[0], keyval.at[1])

    fetched = copies(
        (
            (x_ref, xv),
            (y_ref, yv),
            (sum_ref, sumv),
            (nm_ref, nmv),
            (ub_ref, ubv),
            (gs_ref, gsv),
            (first_ref, fv),
            (second_ref, sv),
        ),
        0,
    )
    for cp in fetched:
        cp.start()
    stored = copies(((xv, outs[1]), (yv, outs[0])), 8)
    for src, group, first in ((sumv, outs[2:7], 10), (nmv, outs[8:13], 17)):
        stored += copies(
            [
                (src.at[:, pl.ds(offs[m], halves[m])], dst)
                for m, dst in enumerate(places(group))
            ],
            first,
        )
    starts = ((0, 1), (1, 2), (2, 9), (9, 16))
    for cp, (a, b) in zip(fetched[:4], starts):
        cp.wait()
        for out in stored[a:b]:
            out.start()
    for cp in fetched[4:]:
        cp.wait()
    for m, dst in enumerate(places(outs[13:18])):
        dst[...] = ubv[0:rows, offs[m] : offs[m] + halves[m]].astype(F32)
    g = gsv[0:4, 0:rows]
    first = ADAM_ONE * fv[...] + (1.0 - ADAM_ONE) * g
    second = ADAM_TWO * sv[...] + (1.0 - ADAM_TWO) * g * g
    outs[7][...] = g
    outs[18][...] = first
    outs[19][...] = second
    outs[20][...] = -GAIN_RATE * first / (jnp.sqrt(second) + ADAM_EPS)
    for cp in stored:
        cp.wait()


def run_format(sums, fresh, updates, gsum, gain_first, gain_second, y, x, ctx_count, wa_count):
    rows = D // ctx_count
    halves = layout(wa_count)[0]
    down, gate, _, out, query, key, _ = halves
    f = lambda *shape: jax.ShapeDtypeStruct(shape, F32)
    weights = [f(rows, query), f(2, rows, key), f(rows, out), f(2, rows, gate), f(rows, down)]
    any_space = pl.BlockSpec(memory_space=pl.ANY)
    vmem = pl.BlockSpec(memory_space=pltpu.VMEM)
    gain = f(4, rows)
    shapes = [jax.ShapeDtypeStruct(y.shape, y.dtype), jax.ShapeDtypeStruct(x.shape, x.dtype)]
    shapes += weights + [gain] + weights + weights + [gain] * 3
    outs = pl.pallas_call(
        partial(format_kernel, ctx_count, wa_count),
        out_shape=shapes,
        in_specs=[any_space] * 8,
        out_specs=[any_space] * 7 + [vmem] + [any_space] * 5 + [vmem] * 8,
        scratch_shapes=[
            *[
                pltpu.VMEM(a.shape, a.dtype)
                for a in (sums, fresh, updates, gsum, gain_first, gain_second, y, x)
            ],
            pltpu.SemaphoreType.DMA((24,)),
        ],
        compiler_params=pltpu.CompilerParams(vmem_limit_bytes=VMEM_BYTES),
        name="format",
    )(sums, fresh, updates, gsum, gain_first, gain_second, y, x)
    return tuple(o.T if i in (4, 6, 10, 12, 15, 17) else o for i, o in enumerate(outs))


def per_device(
    tokens,
    cotangent,
    seq_ids,
    w_query,
    w_keyval,
    w_out,
    w_gateup,
    w_down,
    norm_gains,
    mom_query,
    mom_keyval,
    mom_out,
    mom_gateup,
    mom_down,
    gain_first,
    gain_second,
):
    ctx_count = lax.axis_size("ctx")
    wa_count = lax.axis_size("wa")
    y, x, sums, fresh, updates, gsum = run_whole(
        tokens,
        cotangent,
        seq_ids,
        norm_gains,
        w_keyval,
        (mom_query, mom_keyval, mom_out, mom_gateup, mom_down),
        w_query,
        w_out,
        w_gateup,
        w_down,
        ctx_count,
        wa_count,
    )
    return tuple(
        run_format(
            sums, fresh, updates, gsum, gain_first, gain_second, y, x, ctx_count, wa_count
        )
    )


def solution(mesh):
    in_specs = (
        P("ctx", None),
        P("ctx", None),
        P("ctx"),
        P(None, "wa"),
        P(),
        P("wa", None),
        P(None, None, "wa"),
        P("wa", None),
        P(),
        P("ctx", "wa"),
        P(None, "ctx", "wa"),
        P("wa", "ctx"),
        P(None, "ctx", "wa"),
        P("wa", "ctx"),
        P(None, "ctx"),
        P(None, "ctx"),
    )
    out_specs = (
        P("ctx", None),
        P("ctx", None),
        P("ctx", "wa"),
        P(None, "ctx", "wa"),
        P("wa", "ctx"),
        P(None, "ctx", "wa"),
        P("wa", "ctx"),
        P(None, "ctx"),
        P("ctx", "wa"),
        P(None, "ctx", "wa"),
        P("wa", "ctx"),
        P(None, "ctx", "wa"),
        P("wa", "ctx"),
        P("ctx", "wa"),
        P(None, "ctx", "wa"),
        P("wa", "ctx"),
        P(None, "ctx", "wa"),
        P("wa", "ctx"),
        P(None, "ctx"),
        P(None, "ctx"),
        P(None, "ctx"),
    )
    return jax.shard_map(
        per_device, mesh=mesh, in_specs=in_specs, out_specs=out_specs, check_vma=False
    )
```

```python
from functools import partial
import math

import jax
import jax.numpy as jnp
import numpy as np
from jax import lax
from jax.experimental import pallas as pl
from jax.experimental.pallas import tpu as pltpu
from jax.sharding import PartitionSpec as P

D = 640
FF = 2048
HD = 256
WINDOW = 512
SOFT_CAP = 10
NS_STEPS = 5
HQ = 1024


EPS_NORM = 1e-06
ROPE_BASE = 10000.0
MOMENTUM = 0.95
ADAM_ONE = 0.9
ADAM_TWO = 0.95
ADAM_EPS = 1e-08
GAIN_RATE = 0.1
QUINTIC_A = 3.4445
QUINTIC_B = -4.775
QUINTIC_C = 2.0315
MATRIX_COUNT = 7
MUON_RATE = 0.2

MESH = pl.DeviceIdType.MESH
BF = jnp.bfloat16
F32 = jnp.float32
IN_COUNT = 4
NAMES = ("down", "gate", "up", "out", "query", "key", "value")
WIDTHS = (FF, FF, FF, HQ, HQ, HD, HD)
OWNERS = (7, 4, 8, 5, 11, 9, 10)
PARTS = (
    ((0, 0, 512),),
    ((0, 512, 512),),
    ((1, 0, 512),),
    ((1, 512, 512),),
    ((2, 0, 512),),
    ((2, 512, 512),),
    ((3, 0, 512),),
    ((4, 0, 512),),
    ((5, 0, 128), (6, 0, 128)),
)
TILE = 256


def layout(wa_count):
    halves = [w // wa_count for w in WIDTHS]
    offs = [sum(halves[:i]) for i in range(len(halves))]
    return halves, offs, sum(halves)


def dot32(a, b):
    return jnp.dot(a, b, preferred_element_type=F32)


def eye_mask(n):
    return (
        lax.broadcasted_iota(jnp.int32, (n, n), 0) == lax.broadcasted_iota(jnp.int32, (n, n), 1)
    )


def pad_rows(v, rows):
    if v.shape[0] == rows:
        return v
    return jnp.concatenate([v, jnp.zeros((rows - v.shape[0], v.shape[1]), v.dtype)], axis=0)


def packed_rows(rows):
    return -(-2 * rows // 16) * 16


def pack(left, right, height):
    return pad_rows(jnp.concatenate([left, right], axis=0), height).astype(BF)


def unpack(block, rows):
    block = block.astype(F32)
    return block[:rows], block[rows : 2 * rows]


def split_into(v, hi, lo):
    top = v.astype(BF)
    hi[...] = top
    lo[...] = (v - top.astype(F32)).astype(BF)


SYM_TILES = ((0, 256), (256, 512), (512, 640))


def sym_tiles(out, block):
    for a, b in SYM_TILES:
        v = block(a, b)
        out[a:, a:b] = v
        if b < D:
            out[a:b, b:] = v[b - a :].T


def prod3(h1, l1, h2, l2):
    return lambda a, b: (
        dot32(h1[a:], h2[:, a:b]) + dot32(h1[a:], l2[:, a:b]) + dot32(l1[a:], h2[:, a:b])
    )


def tail_scratch(ctx_count, wa_count):
    v = pltpu.VMEM
    dma = pltpu.SemaphoreType.DMA
    n_in = IN_COUNT
    n_out = ctx_count // n_in
    rows = D // ctx_count
    rp = -(-rows // 16) * 16
    n_dev = ctx_count * wa_count
    n_ch = len(PARTS)
    hp = packed_rows(rows)
    cols = layout(wa_count)[2]
    return dict(
        mb=v((8, hp, 256), BF),
        mbk=v((2, rp, HD // 2), BF),
        early=v((6, D // n_in, 512), BF),
        xb=v((ctx_count, 4, hp, 256), BF),
        am=v((D, D), F32),
        dg_ref=v((8, D), F32),
        dgs=v((n_in, n_out, 8, 128), F32),
        dgc=v((n_in, n_out, 8, 128), F32),
        dgp=v((3, n_out, 8, 128), F32),
        dgo=v((n_out, 8, 128), F32),
        dgl=v((n_out - 1, 8, 128), F32),
        psend=dma((n_ch, 3)),
        precv=dma((n_ch, 3)),
        lsend=dma((n_ch, n_out - 1)),
        lrecv=dma((n_ch, n_out - 1)),
        gsend=dma((n_ch, 2)),
        grecv=dma,
        usend=dma((n_dev,)),
        urecv=dma((MATRIX_COUNT,)),
        gcsend=dma,
        gcrecv=dma,
        gpsend=dma((3,)),
        gprecv=dma((3,)),
        glsend=dma((n_out - 1,)),
        glrecv=dma((n_out - 1,)),
        msem=dma((MATRIX_COUNT,)),
        dfree=pltpu.SemaphoreType.REGULAR,
        pfree=pltpu.SemaphoreType.REGULAR,
        lfree=pltpu.SemaphoreType.REGULAR,
    )


def tail_phases(s, ctx_count, wa_count):
    c = lax.axis_index("ctx")
    w = lax.axis_index("wa")
    n_in = IN_COUNT
    n_out = ctx_count // n_in
    n_dev = ctx_count * wa_count
    p = lax.rem(c, n_in)
    z = lax.div(c, n_in)
    rows = D // ctx_count
    rp = s.mbk.shape[1]
    hp = packed_rows(rows)
    block = D // n_in
    halves, offs, cols = layout(wa_count)
    chunks = [(offs[m[0][0]] + m[0][1], sum(i[2] for i in m)) for m in PARTS]
    me = c * wa_count + w
    per = 512 // hp

    near = (p + 1 - 2 * lax.rem(p, 2), p + 2 - 4 * lax.div(p, 2))
    across = 3 - p

    def plane_slot(ci, k):
        lanes = chunks[ci][1]
        if ci < 2:
            return s.early.at[ci * 3 + k]
        if ci < 4:
            return s.wd.at[pl.ds(((ci - 2) * 3 + k) * block, block), pl.ds(0, lanes)]
        i = (ci - 4) * 3 + k
        buf = (s.wg, s.wu)[i // 16]
        i = i % 16
        return buf.at[i // 8, pl.ds(i % 8 // 2 * block, block), pl.ds(i % 2 * 512, lanes)]

    def line_slot(base, ci, j):
        half = chunks[ci][1] // 2
        page, lane = (base * 2 + ci // 4, ci % 4 * 256) if ci < 8 else (4 + base, 0)
        return s.ffb.at[page, pl.ds(pl.multiple_of(j * hp, 16), hp), pl.ds(lane, half)]

    def plane_copy(ci, k):
        off, wid = chunks[ci]
        first, second = near[ci % 2], near[1 - ci % 2]
        src, dst = ((first, first), (across, first), (second, second))[k]
        return pltpu.make_async_remote_copy(
            s.gb.at[src, :, pl.ds(off, wid)],
            plane_slot(ci, k),
            s.psend.at[ci, k],
            s.precv.at[ci, k],
            device_id=(z * n_in + dst, w),
            device_id_type=MESH,
        )

    def line_copy(ci, k):
        j = lax.rem(z + k, n_out)
        return pltpu.make_async_remote_copy(
            line_slot(0, ci, j),
            line_slot(1, ci, k - 1),
            s.lsend.at[ci, k - 1],
            s.lrecv.at[ci, k - 1],
            device_id=(j * n_in + p, w),
            device_id_type=MESH,
        )

    def tell_plane(sem):
        for q in near:
            pl.semaphore_signal(sem, inc=1, device_id=(z * n_in + q, w), device_id_type=MESH)

    def down_free():
        tell_plane(s.dfree)

    def buffers_free():
        tell_plane(s.pfree)
        for k in range(1, n_out):
            pl.semaphore_signal(
                s.lfree,
                inc=1,
                device_id=(lax.rem(z + k, n_out) * n_in + p, w),
                device_id_type=MESH,
            )

    def plane_start(ci):
        if ci == 2:
            pl.semaphore_wait(s.dfree, 2)
        if ci == 4:
            pl.semaphore_wait(s.pfree, 2)
        plane_copy(ci, 1).start()
        plane_copy(ci, 0).start()

    def plane_mid(ci):
        off, wid = chunks[ci]
        second = near[1 - ci % 2]
        plane_copy(ci, 1).wait_recv()

        def add(t, carry):
            cs = aligned(off + t * TILE, TILE)
            here = aligned(t * TILE, TILE)
            both = s.gb[second, :, cs].astype(F32) + plane_slot(ci, 1)[:, here].astype(F32)
            s.gb[second, :, cs] = both.astype(BF)
            return carry

        lax.fori_loop(0, wid // TILE, add, 0)
        plane_copy(ci, 2).start()

    def plane_finish(ci):
        off, wid = chunks[ci]
        plane_copy(ci, 0).wait_recv()
        plane_copy(ci, 2).wait_recv()

        half = wid // 2
        total = s.gb[p, :, off : off + wid].astype(F32)
        for k in (0, 2):
            total = total + plane_slot(ci, k)[...].astype(F32)
        for j in range(n_out):
            slab = total[j * rows : (j + 1) * rows]

            @pl.when(z == j)
            def _():
                s.sum_ref[:, off : off + wid] = slab

            line_slot(0, ci, j)[...] = pack(slab[:, :half], slab[:, half:], hp)
        if ci == 0:
            pl.semaphore_wait(s.lfree, n_out - 1)
        for k in range(1, n_out):
            line_copy(ci, k).start()

    def gather_copy(ci, i, local):
        m, first, wid = PARTS[ci][i]
        if ci < 8:
            src = s.mb.at[ci]
            dst = s.xb.at[c, w * (halves[m] // 512) + first // 512]
        else:
            src = s.mbk.at[i]
            dst = s.xb.at[c, w, pl.ds(0, rp), pl.ds(0, wid)]
        if local:
            return pltpu.make_async_copy(src, dst, s.grecv)
        return pltpu.make_async_remote_copy(
            src,
            dst,
            s.gsend.at[ci, i],
            s.grecv,
            device_id=(OWNERS[m], 0),
            device_id_type=MESH,
        )

    def line_finish(ci):
        off, wid = chunks[ci]
        half = wid // 2
        for k in range(1, n_out):
            line_copy(ci, k).wait_recv()
        sides = [s.sum_ref[:, off : off + half], s.sum_ref[:, off + half : off + wid]]
        for k in range(n_out - 1):
            for i, extra in enumerate(unpack(line_slot(1, ci, k)[...], rows)):
                sides[i] = sides[i] + extra
        for i in range(2):
            lanes = slice(off + i * half, off + (i + 1) * half)
            s.sum_ref[:, lanes] = sides[i]
            sides[i] = MOMENTUM * s.nm_ref[:, lanes] + sides[i]
            s.nm_ref[:, lanes] = sides[i]
        if ci < 8:
            s.mb[ci] = pack(sides[0], sides[1], hp)
        else:
            for i in range(2):
                s.mbk[i] = pad_rows(sides[i], rp).astype(BF)
        for i, piece in enumerate(PARTS[ci]):
            mine = me == OWNERS[piece[0]] * wa_count

            @pl.when(mine)
            def _():
                gather_copy(ci, i, True).start()

            @pl.when(jnp.logical_not(mine))
            def _():
                gather_copy(ci, i, False).start()

    s.down_free = down_free
    s.buffers_free = buffers_free
    s.plane_start = plane_start
    s.plane_mid = plane_mid
    s.plane_finish = plane_finish

    sources = (
        s.md_ref,
        s.mgu_ref.at[0],
        s.mgu_ref.at[1],
        s.mo_ref,
        s.mq_ref,
        s.mkv_ref.at[0],
        s.mkv_ref.at[1],
    )
    moms = [
        pltpu.make_async_copy(src, s.nm_ref.at[:, pl.ds(offs[m], halves[m])], s.msem.at[m])
        for m, src in enumerate(sources)
    ]
    for cp in moms:
        cp.start()

    def gain_core_copy():
        return pltpu.make_async_remote_copy(
            s.dgs, s.dgc, s.gcsend, s.gcrecv, device_id=(c, 1 - w), device_id_type=MESH
        )

    def gain_plane(k):
        src, dst = ((near[0], near[0]), (across, near[0]), (near[1], near[1]))[k]
        return pltpu.make_async_remote_copy(
            s.dgc.at[src],
            s.dgp.at[k],
            s.gpsend.at[k],
            s.gprecv.at[k],
            device_id=(z * n_in + dst, w),
            device_id_type=MESH,
        )

    def gain_line(k):
        j = lax.rem(z + k, n_out)
        return pltpu.make_async_remote_copy(
            s.dgo.at[j],
            s.dgl.at[k - 1],
            s.glsend.at[k - 1],
            s.glrecv.at[k - 1],
            device_id=(j * n_in + p, w),
            device_id_type=MESH,
        )

    def gains_core():
        for i in range(ctx_count):
            s.dgs[i % n_in, i // n_in, :, 0:rows] = s.dg_ref[:, i * rows : (i + 1) * rows]
        gain_core_copy().start()

    def gains_first():
        gain_core_copy().wait_recv()
        s.dgc[...] = s.dgc[...] + s.dgs[...]
        gain_plane(1).start()
        gain_plane(0).start()

    def gains_mid():
        gain_plane(1).wait_recv()
        s.dgc[near[1]] = s.dgc[near[1]] + s.dgp[1]
        gain_plane(2).start()

    def gains_line():
        gain_plane(0).wait_recv()
        gain_plane(2).wait_recv()
        s.dgo[...] = s.dgc[p] + s.dgp[0] + s.dgp[2]
        for k in range(1, n_out):
            gain_line(k).start()

    def gains_end():
        total = s.dgo[z]
        for k in range(1, n_out):
            gain_line(k).wait_recv()
            total = total + s.dgl[k - 1]
        s.gs_ref[...] = total
        gain_core_copy().wait_send()
        for k in range(3):
            gain_plane(k).wait_send()
        for k in range(1, n_out):
            gain_line(k).wait_send()

    s.gains_core = gains_core

    def rest():
        for cp in moms:
            cp.wait()
        plane_mid(7)
        plane_mid(8)
        line_finish(0)
        line_finish(1)
        plane_finish(6)
        line_finish(2)
        line_finish(3)
        plane_finish(7)
        plane_finish(8)
        gains_first()
        line_finish(4)
        line_finish(5)
        gains_mid()
        line_finish(6)
        line_finish(7)
        gains_line()
        line_finish(8)
        for ci in range(len(chunks)):
            for k in range(3):
                plane_copy(ci, k).wait_send()
            for k in range(1, n_out):
                line_copy(ci, k).wait_send()
        solve()
        gains_end()
        updates_back()

    def owned_by(*which):
        hit = me == OWNERS[which[0]] * wa_count
        for m in which[1:]:
            hit = jnp.logical_or(hit, me == OWNERS[m] * wa_count)
        return hit

    def solve():
        is_owner = owned_by(*range(MATRIX_COUNT))
        is_small = owned_by(5, 6)
        is_wide = owned_by(0, 1, 2)
        pairs = jnp.where(is_small, 0, jnp.where(is_wide, FF // 512, HQ // 512))
        am = s.am
        xfs = (s.dka.at[pl.ds(0, D)], s.dva.at[pl.ds(0, D)])
        ah = s.wd.at[pl.ds(0, D)]
        al = s.wd.at[pl.ds(D, D)]
        ph = s.wd.at[pl.ds(2 * D, D)]
        plo = s.wo.at[pl.ds(0, D)]
        qh = s.wu.at[0, :, pl.ds(0, D)]

        def tile_of(t):
            return s.wg.at[lax.div(t, 4), :, aligned(lax.rem(t, 4) * TILE, TILE)]

        for m in range(MATRIX_COUNT):

            @pl.when(me == OWNERS[m] * wa_count)
            def _(m=m):
                if m < 5:
                    whole = s.xb.at[:, pl.ds(0, halves[m] * wa_count // 512)]
                else:
                    whole = s.xb.at[:, pl.ds(0, 2), pl.ds(0, rp), pl.ds(0, halves[m])]
                pltpu.make_async_copy(whole, whole, s.grecv).wait()

        @pl.when(is_owner)
        def _():
            am[...] = jnp.zeros_like(am)

            def gram(q, carry):
                for i in range(ctx_count):
                    for xf, part in zip(xfs, unpack(s.xb[i, q], rows)):
                        xf[i * rows : (i + 1) * rows, :] = part
                for side in range(2):
                    x = xfs[side][...].astype(BF)
                    tile_of(2 * q + side)[...] = x
                    for a, b in SYM_TILES:
                        am[a:, a:b] += dot_nt(x[a:], x[a:b])
                return carry

            lax.fori_loop(0, pairs, gram, 0)

            @pl.when(is_small)
            def _():
                for i in range(ctx_count):
                    for v in range(2):
                        part = s.xb[i, v, 0:rp, 0 : HD // 2][...].astype(F32)[:rows]
                        lanes = slice(v * (HD // 2), (v + 1) * (HD // 2))
                        xfs[0][i * rows : (i + 1) * rows, lanes] = part
                x = xfs[0][...].astype(BF)
                tile_of(jnp.int32(0))[...] = x
                am[0:HD, 0:HD] = dot_tn(x, x)

            norm2 = jnp.sum(jnp.where(eye_mask(D), am[...], 0.0), keepdims=True)
            inv = 1.0 / (jnp.sqrt(norm2) + 1e-07)
            inv2 = inv * inv
            sym_tiles(am, lambda a, b: am[a:, a:b] * inv2)

            def shifted(a, b, square):
                rest = QUINTIC_B * am[a:, a:b] + QUINTIC_C * square
                top = rest[: b - a] + jnp.where(eye_mask(b - a), QUINTIC_A, 0.0)
                return jnp.concatenate([top, rest[b - a :]], axis=0) if b < D else top

            def poly():
                split_into(am[...], ah, al)
                square = prod3(ah, al, ah, al)
                sym_tiles(am, lambda a, b: shifted(a, b, square(a, b)))

            def advance():
                sym_tiles(am, prod3(ph, plo, ah, al))
                split_into(am[...], ah, al)
                sym_tiles(am, prod3(ah, al, ph, plo))

            def grow():
                sym_tiles(am, lambda a, b: dot32(ph[a:], qh[:, a:b]))
                qh[...] = am[...].astype(BF)

            poly()
            split_into(am[...], ph, plo)
            qh[...] = ph[...]
            advance()

            def sweep(i, carry):
                poly()
                split_into(am[...], ph, plo)
                grow()
                advance()
                return carry

            lax.fori_loop(0, NS_STEPS - 2, sweep, 0)
            ah[...] = am[...].astype(BF)
            sym_tiles(am, lambda a, b: shifted(a, b, dot32(ah[a:], ah[:, a:b])))
            ph[...] = am[...].astype(BF)
            grow()
            rates = [-MUON_RATE * 0.2 * math.sqrt(n) for n in (D, FF, HQ)]
            rate = jnp.where(is_small, rates[0], jnp.where(is_wide, rates[1], rates[2]))
            scale = rate * inv

            def place(i, height, lanes):
                return i // per, slice(i % per * hp, i % per * hp + height), lanes

            def back(q, carry):
                for side in range(2):
                    xfs[side][...] = dot32(qh[...], tile_of(2 * q + side)[...]) * scale
                for i in range(ctx_count):
                    rs = slice(i * rows, (i + 1) * rows)
                    s.ffb[place(i, hp, aligned(q * 256, 256))] = pack(xfs[0][rs], xfs[1][rs], hp)
                return carry

            @pl.when(is_small)
            def _():
                xfs[0][...] = dot32(tile_of(jnp.int32(0))[...], s.wu[0, 0:HD, 0:HD]) * scale
                for i in range(ctx_count):
                    rs = slice(i * rows, (i + 1) * rows)
                    both = pad_rows(xfs[0][rs], rp).astype(BF)
                    s.ffb[place(i, rp, slice(0, HD))] = both

            for v in range(2):
                lax.fori_loop(v * lax.div(pairs, 2), (v + 1) * lax.div(pairs, 2), back, 0)
                for m in range(MATRIX_COUNT):

                    @pl.when(me == OWNERS[m] * wa_count)
                    def _(m=m, v=v):
                        def send(i, carry):
                            there = lax.rem(c + i, ctx_count)
                            update_copy(m, there * wa_count + v, False).start()
                            return carry

                        if v == 0:
                            update_copy(m, c * wa_count, True).start()
                            lax.fori_loop(1, ctx_count, send, 0)
                        else:
                            lax.fori_loop(0, ctx_count, send, 0)

    def update_place(m):
        if m < 5:
            return s.ub.at[:, pl.ds(offs[m] // 2, halves[m] // 2)]
        return s.ubk.at[m - 5]

    def update_copy(m, t, local):
        i, v = lax.div(t, wa_count), lax.rem(t, wa_count)
        start = pl.multiple_of(lax.rem(i, per) * hp, 16)
        if m < 5:
            height, wid = hp, halves[m] // 2
        else:
            height, wid = rp, halves[m]
        lanes = pl.ds(pl.multiple_of(v * wid, 128), wid)
        src = s.ffb.at[lax.div(i, per), pl.ds(start, height), lanes]
        dst = update_place(m)
        if local:
            return pltpu.make_async_copy(src, dst, s.urecv.at[m])
        return pltpu.make_async_remote_copy(
            src, dst, s.usend.at[t], s.urecv.at[m], device_id=(i, v), device_id_type=MESH
        )

    def updates_back():
        for m in range(MATRIX_COUNT):
            piece = update_place(m)
            pltpu.make_async_copy(piece, piece, s.urecv.at[m]).wait()

        for m in range(MATRIX_COUNT):
            owner = OWNERS[m] * wa_count

            @pl.when(me != owner)
            def _(m=m):
                for ci, part in enumerate(PARTS):
                    for i, piece in enumerate(part):
                        if piece[0] == m:
                            gather_copy(ci, i, False).wait_send()

            @pl.when(me == owner)
            def _(m=m, owner=owner):
                def done(t, carry):
                    update_copy(m, lax.rem(owner + t, n_dev), False).wait_send()
                    return carry

                lax.fori_loop(1, n_dev, done, 0)

    return rest


class Refs:
    pass


def dot_nt(a, b):
    return lax.dot_general(a, b, (((1,), (1,)), ((), ())), preferred_element_type=F32)


def dot_tn(a, b):
    return lax.dot_general(a, b, (((0,), (0,)), ((), ())), preferred_element_type=F32)


def aligned(start, size):
    return pl.ds(pl.multiple_of(start, size), size)


def norm_parts(v, gain):
    r = lax.rsqrt(jnp.mean(v * v, axis=-1, keepdims=True) + EPS_NORM)
    return r, v * r, 1.0 + gain


def norm_back(v, gain, e):
    r, zed, g1 = norm_parts(v, gain)
    e1 = e * g1
    dv = r * (e1 - zed * jnp.mean(e1 * zed, axis=-1, keepdims=True))
    return dv, jnp.sum(e * zed, axis=0, keepdims=True)


def layer_scratch(tok):
    v = pltpu.VMEM
    dma = pltpu.SemaphoreType.DMA
    cols = sum(WIDTHS) // 2
    heads = HQ // HD
    tiles = tok // TILE
    win = WINDOW + TILE
    return dict(
        wq=v((2, D, HQ // 2), BF),
        wo=v((HQ, D), BF),
        wg=v((2, D, FF // 2), BF),
        wu=v((2, D, FF // 2), BF),
        wd=v((FF, D), BF),
        tk=v((tok, D), BF),
        ct=v((tok, D), BF),
        xa=v((tok, D), BF),
        xat=v((D, tok), BF),
        fit=v((D, tok), BF),
        ddn=v((tok, D), BF),
        ddnt=v((D, tok), BF),
        cs=v((tok, HD // 2), F32),
        sn=v((tok, HD // 2), F32),
        ka=v((WINDOW + tok, HD), BF),
        va=v((WINDOW + tok, HD), BF),
        idown=v((8, tok), jnp.int32),
        idprev=v((8, tok), jnp.int32),
        qs=v((tiles * heads, TILE, HD), BF),
        ps=v((tiles * heads, TILE, win), BF),
        ts=v((tiles * heads, TILE, win), BF),
        att=v((tok, HQ), BF),
        ao=v((tok, D), F32),
        h1=v((tok, D), F32),
        dn=v((tok, D), F32),
        ffb=v((6, tok, FF // 2), BF),
        datt=v((tok, HQ), BF),
        dka=v((WINDOW + tok, HD), F32),
        dva=v((WINDOW + tok, HD), F32),
        dks=v((2, tok, HD), BF),
        dkr=v((2, tok, HD), BF),
        dkv=v((2, tok, HD), BF),
        sb=v((6, IN_COUNT, D // IN_COUNT, TILE), BF),
        gb=v((IN_COUNT, D // IN_COUNT, cols), BF),
        wsend=dma((5,)),
        wrecv=dma((5,)),
        wown=dma((5,)),
        ksend=dma((3,)),
        krecv=dma((3,)),
        dsend=dma((2, 2)),
        drecv=dma((2, 2)),
        csend=dma((MATRIX_COUNT, 4)),
        crecv=dma((MATRIX_COUNT, 4)),
        osend=dma((2,)),
        orecv=dma((2,)),
        oown=dma((2,)),
        tsem=dma((4,)),
    )


def layer_phases(s, ctx_count, wa_count):
    c = lax.axis_index("ctx")
    w = lax.axis_index("wa")
    other = 1 - w
    flat = c * wa_count + w
    n_dev = ctx_count * wa_count
    tok = s.xa.shape[0]
    rows = D // ctx_count
    n_out = ctx_count // IN_COUNT
    heads = HQ // HD
    tiles = tok // TILE
    win = WINDOW + TILE
    half_ff = FF // 2
    halves, offs, cols = layout(wa_count)
    step = 128
    partner = (c, other)
    follow = jnp.minimum(flat + 1, n_dev - 1)
    ahead = jnp.maximum(flat - 1, 0)
    next_id = (lax.div(follow, wa_count), lax.rem(follow, wa_count))
    prev_id = (lax.div(ahead, wa_count), lax.rem(ahead, wa_count))
    order = [zz * IN_COUNT + pp for pp in range(IN_COUNT) for zz in range(n_out)]

    def remote(src, dst, send, recv, where):
        return pltpu.make_async_remote_copy(
            src, dst, send, recv, device_id=where, device_id_type=MESH
        )

    def permuted(v):
        t = v.astype(BF).astype(F32).T
        return jnp.concatenate([t[i * rows : (i + 1) * rows] for i in order], axis=0).astype(BF)

    def per_rows(body):
        def run(i, carry):
            body(aligned(i * step, step))
            return carry

        lax.fori_loop(0, tok // step, run, 0)

    out_rows = aligned(w * tok, tok)
    tok_in = pltpu.make_async_copy(s.tok_ref.at[out_rows], s.tk, s.tsem.at[0])
    cot_in = pltpu.make_async_copy(s.cot_ref.at[out_rows], s.ct, s.tsem.at[1])
    tables = [
        pltpu.make_async_copy(s.cosi_ref, s.cs, s.tsem.at[2]),
        pltpu.make_async_copy(s.sini_ref, s.sn, s.tsem.at[3]),
    ]
    tok_in.start()
    for cp in tables:
        cp.start()
    cot_in.start()

    wk_refs = (
        (s.wq_ref, s.wq.at[w]),
        (s.wo_ref, s.wo.at[aligned(w * (HQ // 2), HQ // 2)]),
        (s.wgu_ref.at[0], s.wg.at[w]),
        (s.wgu_ref.at[1], s.wu.at[w]),
        (s.wd_ref, s.wd.at[aligned(w * half_ff, half_ff)]),
    )
    w_far = [remote(a, b, s.wsend.at[i], s.wrecv.at[i], partner) for i, (a, b) in enumerate(wk_refs)]
    w_own = [pltpu.make_async_copy(a, b, s.wown.at[i]) for i, (a, b) in enumerate(wk_refs)]
    for far, own in zip(w_far, w_own):
        far.start()
        own.start()

    def weights_ready(i):
        w_own[i].wait()
        w_far[i].wait_recv()

    tok_in.wait()

    def first(rs):
        x = s.tk[rs].astype(F32)
        _, zed, g1 = norm_parts(x, s.gain_ref[0:1])
        s.xa[rs] = (zed * g1).astype(BF)

    per_rows(first)

    cb, sb_ = s.cosb_ref[pl.ds(flat, 1), :], s.sinb_ref[pl.ds(flat, 1), :]
    for cp in tables:
        cp.wait()
    cosi, sini = s.cs[...], s.sn[...]
    s.cs[...] = cb * cosi - sb_ * sini
    s.sn[...] = sb_ * cosi + cb * sini
    hh = HD // 2

    def turn(v, cosine, sine):
        a, b = v[:, :hh], v[:, hh:]
        return jnp.concatenate([a * cosine - b * sine, b * cosine + a * sine], axis=1)

    def turn_back(v, cosine, sine):
        a, b = v[:, :hh], v[:, hh:]
        return jnp.concatenate([a * cosine + b * sine, b * cosine - a * sine], axis=1)

    s.ka[WINDOW:, :] = turn(dot32(s.xa[...], s.wkv_ref[0]), s.cs[...], s.sn[...]).astype(BF)
    s.idown[...] = jnp.broadcast_to(s.ids_ref[pl.ds(w, 1), :], (8, tok))
    halo = [
        remote(src, dst, s.ksend.at[i], s.krecv.at[i], next_id)
        for i, (src, dst) in enumerate(
            (
                (s.ka.at[pl.ds(tok, WINDOW)], s.ka.at[pl.ds(0, WINDOW)]),
                (s.va.at[pl.ds(tok, WINDOW)], s.va.at[pl.ds(0, WINDOW)]),
                (s.idown, s.idprev),
            )
        )
    ]

    @pl.when(flat < n_dev - 1)
    def _():
        halo[2].start()
        halo[0].start()

    s.va[WINDOW:, :] = dot32(s.xa[...], s.wkv_ref[1]).astype(BF)

    @pl.when(flat < n_dev - 1)
    def _():
        halo[1].start()

    def flip(rs):
        s.xat[:, rs] = permuted(s.xa[rs])

    weights_ready(0)

    def project(h, carry):
        v, u = lax.div(h, heads // 2), lax.rem(h, heads // 2)
        q = dot32(s.xa[...], s.wq[v, :, aligned(u * HD, HD)])
        q = (turn(q, s.cs[...], s.sn[...]) * HD ** (-0.5)).astype(BF)
        for a in range(tiles):
            s.qs[a * heads + h] = q[a * TILE : (a + 1) * TILE]
        return carry

    lax.fori_loop(0, heads, project, 0)
    per_rows(flip)

    @pl.when(flat > 0)
    def _():
        for cp in halo:
            cp.wait_recv()

    @pl.when(flat == 0)
    def _():
        s.ka[0:WINDOW, :] = jnp.zeros((WINDOW, HD), BF)
        s.va[0:WINDOW, :] = jnp.zeros((WINDOW, HD), BF)
        s.idprev[...] = jnp.full((8, tok), -1, jnp.int32)

    row_ids = jnp.concatenate([s.idprev[0:1, :], s.idown[0:1, :]], axis=1)
    own_col = jnp.broadcast_to(s.idown[0:1, :], (128, tok)).T[:, 0:1]
    gap = lax.broadcasted_iota(jnp.int32, (TILE, win), 1) - lax.broadcasted_iota(
        jnp.int32, (TILE, win), 0
    )
    for a in range(tiles):
        same = own_col[a * TILE : (a + 1) * TILE] == row_ids[:, a * TILE : a * TILE + win]
        ok = jnp.logical_and(same, jnp.logical_and(gap > 0, gap <= WINDOW))
        s.ffb[a, 0:TILE, 0:win] = jnp.where(ok, 1.0, 0.0).astype(BF)

    def attend(i, carry):
        a, h = lax.div(i, heads), lax.rem(i, heads)
        ks = pl.ds(pl.multiple_of(a * TILE, TILE), win)
        t = jnp.tanh(dot_nt(s.qs[i], s.ka[ks, :]) * (1.0 / SOFT_CAP))
        e = jnp.exp(SOFT_CAP * t) * s.ffb[a, 0:TILE, 0:win].astype(F32)
        pr = e * (1.0 / jnp.sum(e, axis=-1, keepdims=True))
        pr = pr.astype(BF)
        s.ps[i] = pr
        s.ts[i] = (1.0 - t * t).astype(BF)
        o = dot32(pr, s.va[ks, :])
        s.att[aligned(a * TILE, TILE), aligned(h * HD, HD)] = o.astype(BF)
        return carry

    lax.fori_loop(0, tiles * heads, attend, 0)

    weights_ready(1)
    s.ao[...] = dot32(s.att[...], s.wo[...])

    def second(rs):
        _, zed, g1 = norm_parts(s.ao[rs], s.gain_ref[1:2])
        h = s.tk[rs].astype(F32) + zed * g1
        s.h1[rs] = h
        _, zed, g1 = norm_parts(h, s.gain_ref[2:3])
        n = zed * g1
        s.xa[rs] = n.astype(BF)
        s.fit[:, rs] = permuted(n)

    per_rows(second)

    weights_ready(2)
    weights_ready(3)
    root = 0.7978845608028654

    def forward(i, carry):
        v, u = lax.div(i, 4), lax.rem(i, 4)
        us = aligned(u * TILE, TILE)
        gt = dot32(s.xa[...], s.wg[v, :, us])
        up = dot32(s.xa[...], s.wu[v, :, us])
        g2 = gt * gt
        th = jnp.tanh(root * gt * (1.0 + 0.044715 * g2))
        lift = 0.5 * (1.0 + th)
        act = gt * lift
        slope = lift + 0.5 * gt * (1.0 - th * th) * (root * (1.0 + 3.0 * 0.044715 * g2))
        s.ffb[v, :, us] = (act * up).astype(BF)
        s.ffb[2 + v, :, us] = (up * slope).astype(BF)
        s.ffb[4 + v, :, us] = act.astype(BF)
        return carry

    lax.fori_loop(0, 8, forward, 0)
    weights_ready(4)
    s.dn[...] = dot32(s.ffb[0], s.wd[:half_ff]) + dot32(s.ffb[1], s.wd[half_ff:])
    s.dg_ref[...] = jnp.zeros_like(s.dg_ref)

    def third(rs):
        dn = s.dn[rs]
        _, zed, g1 = norm_parts(dn, s.gain_ref[3:4])
        s.xa[rs] = (s.h1[rs] + zed * g1).astype(BF)
        dv, dg = norm_back(dn, s.gain_ref[3:4], s.ct[rs].astype(F32))
        s.dg_ref[3:4] += dg
        s.ddn[rs] = dv.astype(BF)
        s.ddnt[:, rs] = permuted(dv)

    cot_in.wait()
    per_rows(third)
    y_far = remote(s.xa, s.y_ref.at[out_rows], s.osend.at[0], s.orecv.at[0], partner)
    y_own = pltpu.make_async_copy(s.xa, s.y_ref.at[out_rows], s.oown.at[0])
    y_far.start()
    y_own.start()

    def part(m, u, width):
        return pl.ds(pl.multiple_of(offs[m] + u * width, 128), width)

    def slot(m, u):
        return lax.rem(u, 2) * 3 + m if m < 3 else (0, 2, 4, 5)[m - 3] + u

    def exchange(m, u, width):
        return remote(
            s.sb.at[slot(m, u), :, :, pl.ds(0, width)],
            s.gb.at[:, :, part(m, u, width)],
            s.csend.at[m, u],
            s.crecv.at[m, u],
            partner,
        )

    def give(m, u, width, value):
        if m < 3:

            @pl.when(u >= 2)
            def _():
                exchange(m, u - 2, width).wait_send()

        s.sb[slot(m, u), :, :, 0:width] = value.astype(BF).reshape(
            IN_COUNT, D // IN_COUNT, width
        )
        exchange(m, u, width).start()

    def keep(m, u, width, value):
        ps = part(m, u, width)
        exchange(m, u, width).wait_recv()
        total = value.reshape(IN_COUNT, D // IN_COUNT, width) + s.gb[:, :, ps].astype(F32)
        s.gb[:, :, ps] = total.astype(BF)

    def down_back(v, put):
        def run(u, carry):
            put(0, u, TILE, dot32(s.ddnt[...], s.ffb[v, :, aligned(u * TILE, TILE)]))
            return carry

        lax.fori_loop(0, 4, run, 0)

    def gate_back(v, put):
        def run(u, carry):
            us = aligned(u * TILE, TILE)
            dh = dot_nt(s.ddn[...], s.wd[aligned((v * 4 + u) * TILE, TILE), :])
            dgt = (dh * s.ffb[2 + v, :, us].astype(F32)).astype(BF)
            dup = (dh * s.ffb[4 + v, :, us].astype(F32)).astype(BF)
            s.ffb[2 + v, :, us] = dgt
            s.ffb[4 + v, :, us] = dup
            put(1, u, TILE, dot32(s.fit[...], dgt))
            put(2, u, TILE, dot32(s.fit[...], dup))
            return carry

        lax.fori_loop(0, 4, run, 0)

    down_back(other, give)
    down_back(w, keep)
    s.plane_start(0)
    s.plane_start(1)
    gate_back(other, give)
    gate_back(w, keep)
    s.down_free()
    s.dn[...] = dot_nt(s.ffb[2], s.wg[0]) + dot_nt(s.ffb[3], s.wg[1])
    s.plane_mid(0)
    s.plane_mid(1)
    s.plane_start(2)
    s.plane_start(3)
    s.dn[...] += dot_nt(s.ffb[4], s.wu[0]) + dot_nt(s.ffb[5], s.wu[1])

    s.buffers_free()

    def fourth(rs):
        dv, dg = norm_back(s.h1[rs], s.gain_ref[2:3], s.dn[rs])
        s.dg_ref[2:3] += dg
        dh = s.ct[rs].astype(F32) + dv
        s.h1[rs] = dh
        dv, dg = norm_back(s.ao[rs], s.gain_ref[1:2], dh)
        s.dg_ref[1:2] += dg
        s.ddn[rs] = dv.astype(BF)
        s.ddnt[:, rs] = permuted(dv)

    per_rows(fourth)
    s.plane_start(4)
    s.plane_start(5)
    for m in range(3):
        for u in (2, 3):
            exchange(m, u, TILE).wait_send()

    def out_back(v, put):
        def run(u, carry):
            hs = aligned((v * 2 + u) * HD, HD)
            s.datt[:, hs] = dot_nt(s.ddn[...], s.wo[hs, :]).astype(BF)
            put(3, u, HD, dot32(s.ddnt[...], s.att[:, hs]))
            return carry

        lax.fori_loop(0, 2, run, 0)

    out_back(other, give)
    out_back(w, keep)
    s.plane_finish(0)
    s.plane_finish(1)

    s.dka[...] = jnp.zeros_like(s.dka)
    s.dva[...] = jnp.zeros_like(s.dva)

    def attend_back(i, carry):
        a, h = lax.div(i, heads), lax.rem(i, heads)
        ks = pl.ds(pl.multiple_of(a * TILE, TILE), win)
        qr = aligned(a * TILE, TILE)
        hs = aligned(h * HD, HD)
        do = s.datt[qr, hs]
        pr = s.ps[i]
        s.dva[ks, :] += dot_tn(pr, do)
        dp = dot_nt(do, s.va[ks, :])
        pr = pr.astype(F32)
        inner = jnp.sum(pr * dp, axis=-1, keepdims=True)
        ds = (pr * (dp - inner) * s.ts[i].astype(F32)).astype(BF)
        s.dka[ks, :] += dot_tn(ds, s.qs[i])
        dq = dot32(ds, s.ka[ks, :])
        s.datt[qr, hs] = (turn_back(dq, s.cs[qr], s.sn[qr]) * HD ** (-0.5)).astype(BF)
        return carry

    def d_part(i, half):
        rs = pl.ds(half * TILE, TILE)
        return remote(
            s.dks.at[i, rs], s.dkr.at[i, rs], s.dsend.at[i, half], s.drecv.at[i, half], prev_id
        )

    d_halo = [d_part(i, half) for half in range(2) for i in range(2)]

    def d_send(half):
        rs = slice(half * TILE, (half + 1) * TILE)
        s.dks[0, rs] = s.dka[rs].astype(BF)
        s.dks[1, rs] = s.dva[rs].astype(BF)

        @pl.when(flat > 0)
        def _():
            for cp in d_halo[half * 2 : half * 2 + 2]:
                cp.start()

    lax.fori_loop(0, heads, attend_back, 0)
    d_send(0)
    s.plane_mid(2)
    s.plane_mid(3)
    lax.fori_loop(heads, tiles * heads, attend_back, 0)
    d_send(1)
    s.plane_start(6)

    def query_back(v, put):
        def run(u, carry):
            hs = aligned((v * 2 + u) * HD, HD)
            put(4, u, HD, dot32(s.xat[...], s.datt[:, hs]))
            return carry

        lax.fori_loop(0, 2, run, 0)

    query_back(other, give)
    s.plane_mid(4)
    s.plane_mid(5)
    s.dn[...] = dot_nt(s.datt[:, : HQ // 2], s.wq[0]) + dot_nt(s.datt[:, HQ // 2 :], s.wq[1])
    query_back(w, keep)
    s.plane_start(7)
    s.plane_finish(2)
    s.plane_finish(3)

    @pl.when(flat < n_dev - 1)
    def _():
        for cp in d_halo:
            cp.wait_recv()

    @pl.when(flat == n_dev - 1)
    def _():
        s.dkr[...] = jnp.zeros_like(s.dkr)

    dk = s.dka[tok:, :] + s.dkr[0].astype(F32)
    s.dkv[0] = turn_back(dk, s.cs[...], s.sn[...]).astype(BF)
    s.dkv[1] = (s.dva[tok:, :] + s.dkr[1].astype(F32)).astype(BF)
    kvw = HD // 2
    for i in range(2):
        give(5 + i, 0, kvw, dot32(s.xat[...], s.dkv[i, :, aligned(other * kvw, kvw)]))
    for i in range(2):
        keep(5 + i, 0, kvw, dot32(s.xat[...], s.dkv[i, :, aligned(w * kvw, kvw)]))
    s.plane_start(8)
    s.plane_mid(6)
    s.plane_finish(4)
    s.plane_finish(5)
    s.dn[...] += dot_nt(s.dkv[0], s.wkv_ref[0]) + dot_nt(s.dkv[1], s.wkv_ref[1])

    def fifth(rs):
        dv, dg = norm_back(s.tk[rs].astype(F32), s.gain_ref[0:1], s.dn[rs])
        s.dg_ref[0:1] += dg
        s.h1[rs] = s.h1[rs] + dv

    per_rows(fifth)
    s.gains_core()
    x_far = remote(s.h1, s.x_ref.at[out_rows], s.osend.at[1], s.orecv.at[1], partner)
    x_own = pltpu.make_async_copy(s.h1, s.x_ref.at[out_rows], s.oown.at[1])
    x_far.start()
    x_own.start()

    def finish():
        for cp in w_far:
            cp.wait_send()

        @pl.when(flat < n_dev - 1)
        def _():
            for cp in halo:
                cp.wait_send()

        @pl.when(flat > 0)
        def _():
            for cp in d_halo:
                cp.wait_send()

        for m, count, width in ((3, 2, HD), (4, 2, HD), (5, 1, kvw), (6, 1, kvw)):
            for u in range(count):
                exchange(m, u, width).wait_send()
        y_own.wait()
        x_own.wait()
        y_far.wait()
        x_far.wait()

    return finish


LAYER_INPUTS = (
    "tok_ref",
    "cot_ref",
    "cosi_ref",
    "sini_ref",
    "mq_ref",
    "mkv_ref",
    "mgu_ref",
    "mo_ref",
    "md_ref",
    "ids_ref",
    "gain_ref",
    "wkv_ref",
    "cosb_ref",
    "sinb_ref",
    "wq_ref",
    "wo_ref",
    "wgu_ref",
    "wd_ref",
)
LAYER_OUTPUTS = ("y_ref", "x_ref", "sum_ref", "nm_ref", "ub", "ubk", "gs_ref")
VMEM_BYTES = 63 << 20


def whole_kernel(ctx_count, wa_count, names, *refs):
    s = Refs()
    for name, ref in zip(names, refs):
        setattr(s, name, ref)
    c = lax.axis_index("ctx")
    w = lax.axis_index("wa")
    flat = c * wa_count + w
    n_dev = ctx_count * wa_count
    barrier = pltpu.get_barrier_semaphore()

    def greet(i, carry):
        other = lax.rem(flat + i, n_dev)
        pl.semaphore_signal(
            barrier,
            inc=1,
            device_id=(lax.div(other, wa_count), lax.rem(other, wa_count)),
            device_id_type=MESH,
        )
        return carry

    lax.fori_loop(1, n_dev, greet, 0)
    pl.semaphore_wait(barrier, n_dev - 1)
    tail = tail_phases(s, ctx_count, wa_count)
    finish = layer_phases(s, ctx_count, wa_count)
    tail()
    finish()


def rotation_tables(tok, n_dev):
    freq = ROPE_BASE ** (-2.0 * np.arange(HD // 2) / HD)
    inner = np.arange(tok)[:, None] * freq[None, :]
    base = (np.arange(n_dev) * tok)[:, None] * freq[None, :]
    return [jnp.asarray(f(a), F32) for a in (inner, base) for f in (np.cos, np.sin)]


def run_whole(
    tokens, cotangent, seq_ids, gains, wkv, moms, wq, wo, wgu, wd, ctx_count, wa_count
):
    block = tokens.shape[0]
    tok = block // wa_count
    n_dev = ctx_count * wa_count
    mom_query, mom_keyval, mom_out, mom_gateup, mom_down = moms
    cosi, sini, cosb, sinb = rotation_tables(tok, n_dev)
    scratch = layer_scratch(tok) | tail_scratch(ctx_count, wa_count)
    names = LAYER_INPUTS + LAYER_OUTPUTS + tuple(scratch)
    any_space = pl.BlockSpec(memory_space=pl.ANY)
    vmem = pl.BlockSpec(memory_space=pltpu.VMEM)
    _, offs, cols = layout(wa_count)
    shard = jax.ShapeDtypeStruct((D // ctx_count, cols), F32)
    return pl.pallas_call(
        partial(whole_kernel, ctx_count, wa_count, names),
        out_shape=(
            jax.ShapeDtypeStruct((block, D), BF),
            jax.ShapeDtypeStruct((block, D), F32),
            shard,
            shard,
            jax.ShapeDtypeStruct((packed_rows(D // ctx_count), offs[5] // 2), BF),
            jax.ShapeDtypeStruct((2, -(-(D // ctx_count) // 16) * 16, HD // 2), BF),
            jax.ShapeDtypeStruct((8, 128), F32),
        ),
        in_specs=[any_space] * 9 + [vmem] * 5 + [any_space] * 4,
        out_specs=(any_space, any_space) + (vmem,) * 5,
        scratch_shapes=list(scratch.values()),
        compiler_params=pltpu.CompilerParams(
            collective_id=0, has_side_effects=True, vmem_limit_bytes=VMEM_BYTES
        ),
        name="whole",
    )(
        tokens,
        cotangent,
        cosi,
        sini,
        mom_query,
        mom_keyval,
        mom_gateup,
        mom_out.T,
        mom_down.T,
        seq_ids.reshape(wa_count, tok),
        gains,
        wkv,
        cosb,
        sinb,
        wq,
        wo,
        wgu,
        wd,
    )


def format_kernel(
    ctx_count,
    wa_count,
    sum_ref,
    nm_ref,
    ub_ref,
    ubk_ref,
    gs_ref,
    first_ref,
    second_ref,
    y_ref,
    x_ref,
    *rest,
):
    outs, (sumv, nmv, ubv, ubkv, gsv, fv, sv, yv, xv, sem) = rest[:21], rest[21:]
    rows = D // ctx_count
    halves, offs, _ = layout(wa_count)

    def copies(pairs, first):
        return [pltpu.make_async_copy(a, b, sem.at[first + i]) for i, (a, b) in enumerate(pairs)]

    def places(group):
        query, keyval, out, gateup, down = group
        return (down, gateup.at[0], gateup.at[1], out, query, keyval.at[0], keyval.at[1])

    fetched = copies(
        (
            (x_ref, xv),
            (y_ref, yv),
            (sum_ref, sumv),
            (nm_ref, nmv),
            (ub_ref, ubv),
            (ubk_ref, ubkv),
            (gs_ref, gsv),
            (first_ref, fv),
            (second_ref, sv),
        ),
        0,
    )
    for cp in fetched:
        cp.start()
    stored = copies(((xv, outs[1]), (yv, outs[0])), 9)
    for src, group, first in ((sumv, outs[2:7], 11), (nmv, outs[8:13], 18)):
        stored += copies(
            [
                (src.at[:, pl.ds(offs[m], halves[m])], dst)
                for m, dst in enumerate(places(group))
            ],
            first,
        )
    starts = ((0, 1), (1, 2), (2, 9), (9, 16))
    for cp, (a, b) in zip(fetched[:4], starts):
        cp.wait()
        for out in stored[a:b]:
            out.start()
    for cp in fetched[4:]:
        cp.wait()
    for m, dst in enumerate(places(outs[13:18])):
        if m < 5:
            for q in range(halves[m] // 512):
                at = offs[m] // 2 + q * 256
                for side, part in enumerate(unpack(ubv[:, at : at + 256], rows)):
                    dst[:, q * 512 + side * 256 : q * 512 + (side + 1) * 256] = part
        else:
            dst[...] = ubkv[m - 5].astype(F32)[:rows]
    g = gsv[0:4, 0:rows]
    first = ADAM_ONE * fv[...] + (1.0 - ADAM_ONE) * g
    second = ADAM_TWO * sv[...] + (1.0 - ADAM_TWO) * g * g
    outs[7][...] = g
    outs[18][...] = first
    outs[19][...] = second
    outs[20][...] = -GAIN_RATE * first / (jnp.sqrt(second) + ADAM_EPS)
    for cp in stored:
        cp.wait()


def run_format(sums, fresh, updates, small, gsum, gain_first, gain_second, y, x, ctx_count, wa_count):
    rows = D // ctx_count
    halves = layout(wa_count)[0]
    down, gate, _, out, query, key, _ = halves
    f = lambda *shape: jax.ShapeDtypeStruct(shape, F32)
    weights = [f(rows, query), f(2, rows, key), f(rows, out), f(2, rows, gate), f(rows, down)]
    any_space = pl.BlockSpec(memory_space=pl.ANY)
    vmem = pl.BlockSpec(memory_space=pltpu.VMEM)
    gain = f(4, rows)
    shapes = [jax.ShapeDtypeStruct(y.shape, y.dtype), jax.ShapeDtypeStruct(x.shape, x.dtype)]
    shapes += weights + [gain] + weights + weights + [gain] * 3
    outs = pl.pallas_call(
        partial(format_kernel, ctx_count, wa_count),
        out_shape=shapes,
        in_specs=[any_space] * 9,
        out_specs=[any_space] * 7 + [vmem] + [any_space] * 5 + [vmem] * 8,
        scratch_shapes=[
            *[
                pltpu.VMEM(a.shape, a.dtype)
                for a in (sums, fresh, updates, small, gsum, gain_first, gain_second, y, x)
            ],
            pltpu.SemaphoreType.DMA((25,)),
        ],
        compiler_params=pltpu.CompilerParams(vmem_limit_bytes=VMEM_BYTES),
        name="format",
    )(sums, fresh, updates, small, gsum, gain_first, gain_second, y, x)
    return tuple(o.T if i in (4, 6, 10, 12, 15, 17) else o for i, o in enumerate(outs))


def per_device(
    tokens,
    cotangent,
    seq_ids,
    w_query,
    w_keyval,
    w_out,
    w_gateup,
    w_down,
    norm_gains,
    mom_query,
    mom_keyval,
    mom_out,
    mom_gateup,
    mom_down,
    gain_first,
    gain_second,
):
    ctx_count = lax.axis_size("ctx")
    wa_count = lax.axis_size("wa")
    y, x, sums, fresh, updates, small, gsum = run_whole(
        tokens,
        cotangent,
        seq_ids,
        norm_gains,
        w_keyval,
        (mom_query, mom_keyval, mom_out, mom_gateup, mom_down),
        w_query,
        w_out,
        w_gateup,
        w_down,
        ctx_count,
        wa_count,
    )
    return tuple(
        run_format(
            sums, fresh, updates, small, gsum, gain_first, gain_second, y, x, ctx_count, wa_count
        )
    )


def solution(mesh):
    in_specs = (
        P("ctx", None),
        P("ctx", None),
        P("ctx"),
        P(None, "wa"),
        P(),
        P("wa", None),
        P(None, None, "wa"),
        P("wa", None),
        P(),
        P("ctx", "wa"),
        P(None, "ctx", "wa"),
        P("wa", "ctx"),
        P(None, "ctx", "wa"),
        P("wa", "ctx"),
        P(None, "ctx"),
        P(None, "ctx"),
    )
    out_specs = (
        P("ctx", None),
        P("ctx", None),
        P("ctx", "wa"),
        P(None, "ctx", "wa"),
        P("wa", "ctx"),
        P(None, "ctx", "wa"),
        P("wa", "ctx"),
        P(None, "ctx"),
        P("ctx", "wa"),
        P(None, "ctx", "wa"),
        P("wa", "ctx"),
        P(None, "ctx", "wa"),
        P("wa", "ctx"),
        P("ctx", "wa"),
        P(None, "ctx", "wa"),
        P("wa", "ctx"),
        P(None, "ctx", "wa"),
        P("wa", "ctx"),
        P(None, "ctx"),
        P(None, "ctx"),
        P(None, "ctx"),
    )
    return jax.shard_map(
        per_device, mesh=mesh, in_specs=in_specs, out_specs=out_specs, check_vma=False
    )
```

```python
from functools import partial
import math

import jax
import jax.numpy as jnp
import numpy as np
from jax import lax
from jax.experimental import pallas as pl
from jax.experimental.pallas import tpu as pltpu
from jax.sharding import PartitionSpec as P

D = 640
FF = 2048
HD = 256
WINDOW = 512
SOFT_CAP = 10
NS_STEPS = 5
HQ = 1024


EPS_NORM = 1e-06
ROPE_BASE = 10000.0
MOMENTUM = 0.95
ADAM_ONE = 0.9
ADAM_TWO = 0.95
ADAM_EPS = 1e-08
GAIN_RATE = 0.1
QUINTIC_A = 3.4445
QUINTIC_B = -4.775
QUINTIC_C = 2.0315
MATRIX_COUNT = 7
MUON_RATE = 0.2

MESH = pl.DeviceIdType.MESH
BF = jnp.bfloat16
F32 = jnp.float32
IN_COUNT = 4
NAMES = ("down", "gate", "up", "out", "query", "key", "value")
WIDTHS = (FF, FF, FF, HQ, HQ, HD, HD)
OWNERS = (7, 4, 8, 5, 11, 9, 10)
PARTS = (
    ((0, 0, 512),),
    ((0, 512, 512),),
    ((1, 0, 512),),
    ((1, 512, 512),),
    ((2, 0, 512),),
    ((2, 512, 512),),
    ((3, 0, 512),),
    ((4, 0, 512),),
    ((5, 0, 128), (6, 0, 128)),
)
TILE = 256


def layout(wa_count):
    halves = [w // wa_count for w in WIDTHS]
    offs = [sum(halves[:i]) for i in range(len(halves))]
    return halves, offs, sum(halves)


def dot32(a, b):
    return jnp.dot(a, b, preferred_element_type=F32)


def eye_mask(n):
    return (
        lax.broadcasted_iota(jnp.int32, (n, n), 0) == lax.broadcasted_iota(jnp.int32, (n, n), 1)
    )


def pad_rows(v, rows):
    if v.shape[0] == rows:
        return v
    return jnp.concatenate([v, jnp.zeros((rows - v.shape[0], v.shape[1]), v.dtype)], axis=0)


def packed_rows(rows):
    return -(-2 * rows // 16) * 16


def pack(left, right, height):
    return pad_rows(jnp.concatenate([left, right], axis=0), height).astype(BF)


def unpack(block, rows):
    block = block.astype(F32)
    return block[:rows], block[rows : 2 * rows]


def split_into(v, hi, lo):
    top = v.astype(BF)
    hi[...] = top
    lo[...] = (v - top.astype(F32)).astype(BF)


SYM_TILES = ((0, 256), (256, 512), (512, 640))


def sym_tiles(out, block):
    for a, b in SYM_TILES:
        v = block(a, b)
        out[a:, a:b] = v
        if b < D:
            out[a:b, b:] = v[b - a :].T


def prod3(h1, l1, h2, l2):
    return lambda a, b: (
        dot32(h1[a:], h2[:, a:b]) + dot32(h1[a:], l2[:, a:b]) + dot32(l1[a:], h2[:, a:b])
    )


def tail_scratch(ctx_count, wa_count):
    v = pltpu.VMEM
    dma = pltpu.SemaphoreType.DMA
    n_in = IN_COUNT
    n_out = ctx_count // n_in
    rows = D // ctx_count
    rp = -(-rows // 16) * 16
    n_dev = ctx_count * wa_count
    n_ch = len(PARTS)
    hp = packed_rows(rows)
    cols = layout(wa_count)[2]
    return dict(
        mb=v((8, hp, 256), BF),
        mbk=v((2, rp, HD // 2), BF),
        early=v((6, D // n_in, 512), BF),
        xb=v((ctx_count, 4, hp, 256), BF),
        am=v((D, D), F32),
        dg_ref=v((8, D), F32),
        dgs=v((n_in, n_out, 8, 128), F32),
        dgc=v((n_in, n_out, 8, 128), F32),
        dgp=v((3, n_out, 8, 128), F32),
        dgo=v((n_out, 8, 128), F32),
        dgl=v((n_out - 1, 8, 128), F32),
        psend=dma((n_ch, 3)),
        precv=dma((n_ch, 3)),
        lsend=dma((n_ch, n_out - 1)),
        lrecv=dma((n_ch, n_out - 1)),
        gsend=dma((n_ch, 2)),
        grecv=dma,
        usend=dma((n_dev,)),
        urecv=dma((MATRIX_COUNT,)),
        gcsend=dma,
        gcrecv=dma,
        gpsend=dma((3,)),
        gprecv=dma((3,)),
        glsend=dma((n_out - 1,)),
        glrecv=dma((n_out - 1,)),
        msem=dma((MATRIX_COUNT,)),
        dfree=pltpu.SemaphoreType.REGULAR,
        pfree=pltpu.SemaphoreType.REGULAR,
        lfree=pltpu.SemaphoreType.REGULAR,
    )


def tail_phases(s, ctx_count, wa_count):
    c = lax.axis_index("ctx")
    w = lax.axis_index("wa")
    n_in = IN_COUNT
    n_out = ctx_count // n_in
    n_dev = ctx_count * wa_count
    p = lax.rem(c, n_in)
    z = lax.div(c, n_in)
    rows = D // ctx_count
    rp = s.mbk.shape[1]
    hp = packed_rows(rows)
    block = D // n_in
    halves, offs, cols = layout(wa_count)
    chunks = [(offs[m[0][0]] + m[0][1], sum(i[2] for i in m)) for m in PARTS]
    me = c * wa_count + w
    per = 512 // hp

    near = (p + 1 - 2 * lax.rem(p, 2), p + 2 - 4 * lax.div(p, 2))
    across = 3 - p

    def plane_slot(ci, k):
        lanes = chunks[ci][1]
        if ci < 2:
            return s.early.at[ci * 3 + k]
        if ci < 4:
            return s.wd.at[pl.ds(((ci - 2) * 3 + k) * block, block), pl.ds(0, lanes)]
        i = (ci - 4) * 3 + k
        buf = (s.wg, s.wu)[i // 16]
        i = i % 16
        return buf.at[i // 8, pl.ds(i % 8 // 2 * block, block), pl.ds(i % 2 * 512, lanes)]

    def line_slot(base, ci, j):
        half = chunks[ci][1] // 2
        page, lane = (base * 2 + ci // 4, ci % 4 * 256) if ci < 8 else (4 + base, 0)
        return s.ffb.at[page, pl.ds(pl.multiple_of(j * hp, 16), hp), pl.ds(lane, half)]

    def plane_copy(ci, k):
        off, wid = chunks[ci]
        first, second = near[ci % 2], near[1 - ci % 2]
        src, dst = ((first, first), (across, first), (second, second))[k]
        return pltpu.make_async_remote_copy(
            s.gb.at[src, :, pl.ds(off, wid)],
            plane_slot(ci, k),
            s.psend.at[ci, k],
            s.precv.at[ci, k],
            device_id=(z * n_in + dst, w),
            device_id_type=MESH,
        )

    def line_copy(ci, k):
        j = lax.rem(z + k, n_out)
        return pltpu.make_async_remote_copy(
            line_slot(0, ci, j),
            line_slot(1, ci, k - 1),
            s.lsend.at[ci, k - 1],
            s.lrecv.at[ci, k - 1],
            device_id=(j * n_in + p, w),
            device_id_type=MESH,
        )

    def tell_plane(sem):
        for q in near:
            pl.semaphore_signal(sem, inc=1, device_id=(z * n_in + q, w), device_id_type=MESH)

    def down_free():
        tell_plane(s.dfree)

    def buffers_free():
        tell_plane(s.pfree)
        for k in range(1, n_out):
            pl.semaphore_signal(
                s.lfree,
                inc=1,
                device_id=(lax.rem(z + k, n_out) * n_in + p, w),
                device_id_type=MESH,
            )

    def plane_start(ci):
        if ci == 2:
            pl.semaphore_wait(s.dfree, 2)
        if ci == 4:
            pl.semaphore_wait(s.pfree, 2)
        plane_copy(ci, 1).start()
        plane_copy(ci, 0).start()

    def plane_mid(ci):
        off, wid = chunks[ci]
        second = near[1 - ci % 2]
        plane_copy(ci, 1).wait_recv()

        def add(t, carry):
            cs = aligned(off + t * TILE, TILE)
            here = aligned(t * TILE, TILE)
            both = s.gb[second, :, cs].astype(F32) + plane_slot(ci, 1)[:, here].astype(F32)
            s.gb[second, :, cs] = both.astype(BF)
            return carry

        lax.fori_loop(0, wid // TILE, add, 0)
        plane_copy(ci, 2).start()

    def plane_finish(ci):
        off, wid = chunks[ci]
        plane_copy(ci, 0).wait_recv()
        plane_copy(ci, 2).wait_recv()

        half = wid // 2
        total = s.gb[p, :, off : off + wid].astype(F32)
        for k in (0, 2):
            total = total + plane_slot(ci, k)[...].astype(F32)
        for j in range(n_out):
            slab = total[j * rows : (j + 1) * rows]

            @pl.when(z == j)
            def _():
                s.sum_ref[:, off : off + wid] = slab

            line_slot(0, ci, j)[...] = pack(slab[:, :half], slab[:, half:], hp)
        if ci == 0:
            pl.semaphore_wait(s.lfree, n_out - 1)
        for k in range(1, n_out):
            line_copy(ci, k).start()

    def gather_copy(ci, i, local):
        m, first, wid = PARTS[ci][i]
        if ci < 8:
            src = s.mb.at[ci]
            dst = s.xb.at[c, w * (halves[m] // 512) + first // 512]
        else:
            src = s.mbk.at[i]
            dst = s.xb.at[c, w, pl.ds(0, rp), pl.ds(0, wid)]
        if local:
            return pltpu.make_async_copy(src, dst, s.grecv)
        return pltpu.make_async_remote_copy(
            src,
            dst,
            s.gsend.at[ci, i],
            s.grecv,
            device_id=(OWNERS[m], 0),
            device_id_type=MESH,
        )

    def line_finish(ci):
        off, wid = chunks[ci]
        half = wid // 2
        for k in range(1, n_out):
            line_copy(ci, k).wait_recv()
        sides = [s.sum_ref[:, off : off + half], s.sum_ref[:, off + half : off + wid]]
        for k in range(n_out - 1):
            for i, extra in enumerate(unpack(line_slot(1, ci, k)[...], rows)):
                sides[i] = sides[i] + extra
        for i in range(2):
            lanes = slice(off + i * half, off + (i + 1) * half)
            s.sum_ref[:, lanes] = sides[i]
            sides[i] = MOMENTUM * s.nm_ref[:, lanes] + sides[i]
            s.nm_ref[:, lanes] = sides[i]
        if ci < 8:
            s.mb[ci] = pack(sides[0], sides[1], hp)
        else:
            for i in range(2):
                s.mbk[i] = pad_rows(sides[i], rp).astype(BF)
        for i, piece in enumerate(PARTS[ci]):
            mine = me == OWNERS[piece[0]] * wa_count

            @pl.when(mine)
            def _():
                gather_copy(ci, i, True).start()

            @pl.when(jnp.logical_not(mine))
            def _():
                gather_copy(ci, i, False).start()

    s.down_free = down_free
    s.buffers_free = buffers_free
    s.plane_start = plane_start
    s.plane_mid = plane_mid
    s.plane_finish = plane_finish

    sources = (
        s.md_ref,
        s.mgu_ref.at[0],
        s.mgu_ref.at[1],
        s.mo_ref,
        s.mq_ref,
        s.mkv_ref.at[0],
        s.mkv_ref.at[1],
    )
    moms = [
        pltpu.make_async_copy(src, s.nm_ref.at[:, pl.ds(offs[m], halves[m])], s.msem.at[m])
        for m, src in enumerate(sources)
    ]
    for cp in moms:
        cp.start()

    def gain_core_copy():
        return pltpu.make_async_remote_copy(
            s.dgs, s.dgc, s.gcsend, s.gcrecv, device_id=(c, 1 - w), device_id_type=MESH
        )

    def gain_plane(k):
        src, dst = ((near[0], near[0]), (across, near[0]), (near[1], near[1]))[k]
        return pltpu.make_async_remote_copy(
            s.dgc.at[src],
            s.dgp.at[k],
            s.gpsend.at[k],
            s.gprecv.at[k],
            device_id=(z * n_in + dst, w),
            device_id_type=MESH,
        )

    def gain_line(k):
        j = lax.rem(z + k, n_out)
        return pltpu.make_async_remote_copy(
            s.dgo.at[j],
            s.dgl.at[k - 1],
            s.glsend.at[k - 1],
            s.glrecv.at[k - 1],
            device_id=(j * n_in + p, w),
            device_id_type=MESH,
        )

    def gains_core():
        for i in range(ctx_count):
            s.dgs[i % n_in, i // n_in, :, 0:rows] = s.dg_ref[:, i * rows : (i + 1) * rows]
        gain_core_copy().start()

    def gains_first():
        gain_core_copy().wait_recv()
        s.dgc[...] = s.dgc[...] + s.dgs[...]
        gain_plane(1).start()
        gain_plane(0).start()

    def gains_mid():
        gain_plane(1).wait_recv()
        s.dgc[near[1]] = s.dgc[near[1]] + s.dgp[1]
        gain_plane(2).start()

    def gains_line():
        gain_plane(0).wait_recv()
        gain_plane(2).wait_recv()
        s.dgo[...] = s.dgc[p] + s.dgp[0] + s.dgp[2]
        for k in range(1, n_out):
            gain_line(k).start()

    def gains_end():
        total = s.dgo[z]
        for k in range(1, n_out):
            gain_line(k).wait_recv()
            total = total + s.dgl[k - 1]
        s.gs_ref[...] = total
        gain_core_copy().wait_send()
        for k in range(3):
            gain_plane(k).wait_send()
        for k in range(1, n_out):
            gain_line(k).wait_send()

    s.gains_core = gains_core

    def rest():
        for cp in moms:
            cp.wait()
        plane_mid(7)
        plane_mid(8)
        line_finish(0)
        line_finish(1)
        plane_finish(6)
        line_finish(2)
        line_finish(3)
        plane_finish(7)
        plane_finish(8)
        gains_first()
        line_finish(4)
        line_finish(5)
        gains_mid()
        line_finish(6)
        line_finish(7)
        gains_line()
        line_finish(8)
        for ci in range(len(chunks)):
            for k in range(3):
                plane_copy(ci, k).wait_send()
            for k in range(1, n_out):
                line_copy(ci, k).wait_send()
        solve()
        gains_end()
        updates_back()

    def owned_by(*which):
        hit = me == OWNERS[which[0]] * wa_count
        for m in which[1:]:
            hit = jnp.logical_or(hit, me == OWNERS[m] * wa_count)
        return hit

    def solve():
        is_owner = owned_by(*range(MATRIX_COUNT))
        is_small = owned_by(5, 6)
        is_wide = owned_by(0, 1, 2)
        pairs = jnp.where(is_small, 0, jnp.where(is_wide, FF // 512, HQ // 512))
        am = s.am
        xfs = (s.dka.at[pl.ds(0, D)], s.dva.at[pl.ds(0, D)])
        ah = s.wd.at[pl.ds(0, D)]
        al = s.wd.at[pl.ds(D, D)]
        ph = s.wd.at[pl.ds(2 * D, D)]
        plo = s.wo.at[pl.ds(0, D)]
        qh = s.wu.at[0, :, pl.ds(0, D)]

        def tile_of(t):
            return s.wg.at[lax.div(t, 4), :, aligned(lax.rem(t, 4) * TILE, TILE)]

        for m in range(MATRIX_COUNT):

            @pl.when(me == OWNERS[m] * wa_count)
            def _(m=m):
                if m < 5:
                    whole = s.xb.at[:, pl.ds(0, halves[m] * wa_count // 512)]
                else:
                    whole = s.xb.at[:, pl.ds(0, 2), pl.ds(0, rp), pl.ds(0, halves[m])]
                pltpu.make_async_copy(whole, whole, s.grecv).wait()

        @pl.when(is_owner)
        def _():
            am[...] = jnp.zeros_like(am)

            def gram(q, carry):
                for i in range(ctx_count):
                    for xf, part in zip(xfs, unpack(s.xb[i, q], rows)):
                        xf[i * rows : (i + 1) * rows, :] = part
                for side in range(2):
                    x = xfs[side][...].astype(BF)
                    tile_of(2 * q + side)[...] = x
                    for a, b in SYM_TILES:
                        am[a:, a:b] += dot_nt(x[a:], x[a:b])
                return carry

            lax.fori_loop(0, pairs, gram, 0)

            @pl.when(is_small)
            def _():
                for i in range(ctx_count):
                    for v in range(2):
                        part = s.xb[i, v, 0:rp, 0 : HD // 2][...].astype(F32)[:rows]
                        lanes = slice(v * (HD // 2), (v + 1) * (HD // 2))
                        xfs[0][i * rows : (i + 1) * rows, lanes] = part
                x = xfs[0][...].astype(BF)
                tile_of(jnp.int32(0))[...] = x
                am[0:HD, 0:HD] = dot_tn(x, x)

            norm2 = jnp.sum(jnp.where(eye_mask(D), am[...], 0.0), keepdims=True)
            inv = 1.0 / (jnp.sqrt(norm2) + 1e-07)
            inv2 = inv * inv
            sym_tiles(am, lambda a, b: am[a:, a:b] * inv2)

            def shifted(a, b, square):
                rest = QUINTIC_B * am[a:, a:b] + QUINTIC_C * square
                top = rest[: b - a] + jnp.where(eye_mask(b - a), QUINTIC_A, 0.0)
                return jnp.concatenate([top, rest[b - a :]], axis=0) if b < D else top

            def poly():
                split_into(am[...], ah, al)
                square = prod3(ah, al, ah, al)
                sym_tiles(am, lambda a, b: shifted(a, b, square(a, b)))

            def advance():
                sym_tiles(am, prod3(ph, plo, ah, al))
                split_into(am[...], ah, al)
                sym_tiles(am, prod3(ah, al, ph, plo))

            def grow():
                sym_tiles(am, lambda a, b: dot32(ph[a:], qh[:, a:b]))
                qh[...] = am[...].astype(BF)

            poly()
            split_into(am[...], ph, plo)
            qh[...] = ph[...]
            advance()

            def sweep(i, carry):
                poly()
                split_into(am[...], ph, plo)
                grow()
                advance()
                return carry

            lax.fori_loop(0, NS_STEPS - 2, sweep, 0)
            ah[...] = am[...].astype(BF)
            sym_tiles(am, lambda a, b: shifted(a, b, dot32(ah[a:], ah[:, a:b])))
            ph[...] = am[...].astype(BF)
            grow()
            rates = [-MUON_RATE * 0.2 * math.sqrt(n) for n in (D, FF, HQ)]
            rate = jnp.where(is_small, rates[0], jnp.where(is_wide, rates[1], rates[2]))
            scale = rate * inv

            def place(i, height, lanes):
                return i // per, slice(i % per * hp, i % per * hp + height), lanes

            def back(q, carry):
                for side in range(2):
                    xfs[side][...] = dot32(qh[...], tile_of(2 * q + side)[...]) * scale
                for i in range(ctx_count):
                    rs = slice(i * rows, (i + 1) * rows)
                    s.ffb[place(i, hp, aligned(q * 256, 256))] = pack(xfs[0][rs], xfs[1][rs], hp)
                return carry

            @pl.when(is_small)
            def _():
                xfs[0][...] = dot32(tile_of(jnp.int32(0))[...], s.wu[0, 0:HD, 0:HD]) * scale
                for i in range(ctx_count):
                    rs = slice(i * rows, (i + 1) * rows)
                    both = pad_rows(xfs[0][rs], rp).astype(BF)
                    s.ffb[place(i, rp, slice(0, HD))] = both

            for v in range(2):
                lax.fori_loop(v * lax.div(pairs, 2), (v + 1) * lax.div(pairs, 2), back, 0)
                for m in range(MATRIX_COUNT):

                    @pl.when(me == OWNERS[m] * wa_count)
                    def _(m=m, v=v):
                        def send(i, carry):
                            there = lax.rem(c + i, ctx_count)
                            update_copy(m, there * wa_count + v, False).start()
                            return carry

                        if v == 0:
                            update_copy(m, c * wa_count, True).start()
                            lax.fori_loop(1, ctx_count, send, 0)
                        else:
                            lax.fori_loop(0, ctx_count, send, 0)

    def update_place(m):
        if m < 5:
            return s.ub.at[:, pl.ds(offs[m] // 2, halves[m] // 2)]
        return s.ubk.at[m - 5]

    def update_copy(m, t, local):
        i, v = lax.div(t, wa_count), lax.rem(t, wa_count)
        start = pl.multiple_of(lax.rem(i, per) * hp, 16)
        if m < 5:
            height, wid = hp, halves[m] // 2
        else:
            height, wid = rp, halves[m]
        lanes = pl.ds(pl.multiple_of(v * wid, 128), wid)
        src = s.ffb.at[lax.div(i, per), pl.ds(start, height), lanes]
        dst = update_place(m)
        if local:
            return pltpu.make_async_copy(src, dst, s.urecv.at[m])
        return pltpu.make_async_remote_copy(
            src, dst, s.usend.at[t], s.urecv.at[m], device_id=(i, v), device_id_type=MESH
        )

    def updates_back():
        for m in range(MATRIX_COUNT):
            piece = update_place(m)
            pltpu.make_async_copy(piece, piece, s.urecv.at[m]).wait()

        for m in range(MATRIX_COUNT):
            owner = OWNERS[m] * wa_count

            @pl.when(me != owner)
            def _(m=m):
                for ci, part in enumerate(PARTS):
                    for i, piece in enumerate(part):
                        if piece[0] == m:
                            gather_copy(ci, i, False).wait_send()

            @pl.when(me == owner)
            def _(m=m, owner=owner):
                def done(t, carry):
                    update_copy(m, lax.rem(owner + t, n_dev), False).wait_send()
                    return carry

                lax.fori_loop(1, n_dev, done, 0)

    return rest


class Refs:
    pass


def dot_nt(a, b):
    return lax.dot_general(a, b, (((1,), (1,)), ((), ())), preferred_element_type=F32)


def dot_tn(a, b):
    return lax.dot_general(a, b, (((0,), (0,)), ((), ())), preferred_element_type=F32)


def aligned(start, size):
    return pl.ds(pl.multiple_of(start, size), size)


def norm_parts(v, gain):
    r = lax.rsqrt(jnp.mean(v * v, axis=-1, keepdims=True) + EPS_NORM)
    return r, v * r, 1.0 + gain


def norm_back(v, gain, e):
    r, zed, g1 = norm_parts(v, gain)
    e1 = e * g1
    dv = r * (e1 - zed * jnp.mean(e1 * zed, axis=-1, keepdims=True))
    return dv, jnp.sum(e * zed, axis=0, keepdims=True)


def layer_scratch(tok):
    v = pltpu.VMEM
    dma = pltpu.SemaphoreType.DMA
    cols = sum(WIDTHS) // 2
    heads = HQ // HD
    tiles = tok // TILE
    win = WINDOW + TILE
    return dict(
        wq=v((2, D, HQ // 2), BF),
        wo=v((HQ, D), BF),
        wg=v((2, D, FF // 2), BF),
        wu=v((2, D, FF // 2), BF),
        wd=v((FF, D), BF),
        tk=v((tok, D), BF),
        ct=v((tok, D), BF),
        xa=v((tok, D), BF),
        xat=v((D, tok), BF),
        fit=v((D, tok), BF),
        ddn=v((tok, D), BF),
        ddnt=v((D, tok), BF),
        cs=v((tok, HD // 2), F32),
        sn=v((tok, HD // 2), F32),
        ka=v((WINDOW + tok, HD), BF),
        va=v((WINDOW + tok, HD), BF),
        idown=v((8, tok), jnp.int32),
        idprev=v((8, tok), jnp.int32),
        qs=v((tiles * heads, TILE, HD), BF),
        ps=v((tiles * heads, TILE, win), BF),
        ts=v((tiles * heads, TILE, win), BF),
        att=v((tok, HQ), BF),
        ao=v((tok, D), F32),
        h1=v((tok, D), F32),
        dn=v((tok, D), F32),
        ffb=v((6, tok, FF // 2), BF),
        datt=v((tok, HQ), BF),
        dka=v((WINDOW + tok, HD), F32),
        dva=v((WINDOW + tok, HD), F32),
        dks=v((2, tok, HD), BF),
        dkr=v((2, tok, HD), BF),
        dkv=v((2, tok, HD), BF),
        sb=v((6, IN_COUNT, D // IN_COUNT, TILE), BF),
        gb=v((IN_COUNT, D // IN_COUNT, cols), BF),
        wsend=dma((5,)),
        wrecv=dma((5,)),
        wown=dma((5,)),
        ksend=dma((3,)),
        krecv=dma((3,)),
        dsend=dma((2, 2)),
        drecv=dma((2, 2)),
        csend=dma((MATRIX_COUNT, 4)),
        crecv=dma((MATRIX_COUNT, 4)),
        osend=dma((2,)),
        orecv=dma((2,)),
        oown=dma((2,)),
        tsem=dma((4,)),
    )


def layer_phases(s, ctx_count, wa_count):
    c = lax.axis_index("ctx")
    w = lax.axis_index("wa")
    other = 1 - w
    flat = c * wa_count + w
    n_dev = ctx_count * wa_count
    tok = s.xa.shape[0]
    rows = D // ctx_count
    n_out = ctx_count // IN_COUNT
    heads = HQ // HD
    tiles = tok // TILE
    win = WINDOW + TILE
    half_ff = FF // 2
    halves, offs, cols = layout(wa_count)
    step = 128
    partner = (c, other)
    follow = jnp.minimum(flat + 1, n_dev - 1)
    ahead = jnp.maximum(flat - 1, 0)
    next_id = (lax.div(follow, wa_count), lax.rem(follow, wa_count))
    prev_id = (lax.div(ahead, wa_count), lax.rem(ahead, wa_count))
    order = [zz * IN_COUNT + pp for pp in range(IN_COUNT) for zz in range(n_out)]

    def remote(src, dst, send, recv, where):
        return pltpu.make_async_remote_copy(
            src, dst, send, recv, device_id=where, device_id_type=MESH
        )

    def permuted(v):
        t = v.astype(BF).astype(F32).T
        return jnp.concatenate([t[i * rows : (i + 1) * rows] for i in order], axis=0).astype(BF)

    def per_rows(body):
        def run(i, carry):
            body(aligned(i * step, step))
            return carry

        lax.fori_loop(0, tok // step, run, 0)

    out_rows = aligned(w * tok, tok)
    tok_in = pltpu.make_async_copy(s.tok_ref.at[out_rows], s.tk, s.tsem.at[0])
    cot_in = pltpu.make_async_copy(s.cot_ref.at[out_rows], s.ct, s.tsem.at[1])
    tables = [
        pltpu.make_async_copy(s.cosi_ref, s.cs, s.tsem.at[2]),
        pltpu.make_async_copy(s.sini_ref, s.sn, s.tsem.at[3]),
    ]
    tok_in.start()
    for cp in tables:
        cp.start()
    cot_in.start()

    wk_refs = (
        (s.wq_ref, s.wq.at[w]),
        (s.wo_ref, s.wo.at[aligned(w * (HQ // 2), HQ // 2)]),
        (s.wgu_ref.at[0], s.wg.at[w]),
        (s.wgu_ref.at[1], s.wu.at[w]),
        (s.wd_ref, s.wd.at[aligned(w * half_ff, half_ff)]),
    )
    w_far = [remote(a, b, s.wsend.at[i], s.wrecv.at[i], partner) for i, (a, b) in enumerate(wk_refs)]
    w_own = [pltpu.make_async_copy(a, b, s.wown.at[i]) for i, (a, b) in enumerate(wk_refs)]

    def weights_start(first, last):
        for i in range(first, last):
            w_far[i].start()
            w_own[i].start()

    weights_start(0, 1)

    def weights_ready(i):
        w_own[i].wait()
        w_far[i].wait_recv()

    tok_in.wait()

    def first(rs):
        x = s.tk[rs].astype(F32)
        _, zed, g1 = norm_parts(x, s.gain_ref[0:1])
        s.xa[rs] = (zed * g1).astype(BF)

    per_rows(first)

    cb, sb_ = s.cosb_ref[pl.ds(flat, 1), :], s.sinb_ref[pl.ds(flat, 1), :]
    for cp in tables:
        cp.wait()
    cosi, sini = s.cs[...], s.sn[...]
    s.cs[...] = cb * cosi - sb_ * sini
    s.sn[...] = sb_ * cosi + cb * sini
    hh = HD // 2

    def turn(v, cosine, sine):
        a, b = v[:, :hh], v[:, hh:]
        return jnp.concatenate([a * cosine - b * sine, b * cosine + a * sine], axis=1)

    def turn_back(v, cosine, sine):
        a, b = v[:, :hh], v[:, hh:]
        return jnp.concatenate([a * cosine + b * sine, b * cosine - a * sine], axis=1)

    s.ka[WINDOW:, :] = turn(dot32(s.xa[...], s.wkv_ref[0]), s.cs[...], s.sn[...]).astype(BF)
    s.idown[...] = jnp.broadcast_to(s.ids_ref[:, aligned(w * tok, tok)], (8, tok))
    halo = [
        remote(src, dst, s.ksend.at[i], s.krecv.at[i], next_id)
        for i, (src, dst) in enumerate(
            (
                (s.ka.at[pl.ds(tok, WINDOW)], s.ka.at[pl.ds(0, WINDOW)]),
                (s.va.at[pl.ds(tok, WINDOW)], s.va.at[pl.ds(0, WINDOW)]),
                (s.idown, s.idprev),
            )
        )
    ]

    @pl.when(flat < n_dev - 1)
    def _():
        halo[2].start()
        halo[0].start()

    s.va[WINDOW:, :] = dot32(s.xa[...], s.wkv_ref[1]).astype(BF)

    @pl.when(flat < n_dev - 1)
    def _():
        halo[1].start()

    weights_start(1, 5)

    def flip(rs):
        s.xat[:, rs] = permuted(s.xa[rs])

    weights_ready(0)

    def project(h, carry):
        v, u = lax.div(h, heads // 2), lax.rem(h, heads // 2)
        q = dot32(s.xa[...], s.wq[v, :, aligned(u * HD, HD)])
        q = (turn(q, s.cs[...], s.sn[...]) * HD ** (-0.5)).astype(BF)
        for a in range(tiles):
            s.qs[a * heads + h] = q[a * TILE : (a + 1) * TILE]
        return carry

    lax.fori_loop(0, heads, project, 0)
    per_rows(flip)

    @pl.when(flat > 0)
    def _():
        for cp in halo:
            cp.wait_recv()

    @pl.when(flat == 0)
    def _():
        s.ka[0:WINDOW, :] = jnp.zeros((WINDOW, HD), BF)
        s.va[0:WINDOW, :] = jnp.zeros((WINDOW, HD), BF)
        s.idprev[...] = jnp.full((8, tok), -1, jnp.int32)

    row_ids = jnp.concatenate([s.idprev[0:1, :], s.idown[0:1, :]], axis=1)
    own_col = jnp.broadcast_to(s.idown[0:1, :], (128, tok)).T[:, 0:1]
    gap = lax.broadcasted_iota(jnp.int32, (TILE, win), 1) - lax.broadcasted_iota(
        jnp.int32, (TILE, win), 0
    )
    for a in range(tiles):
        same = own_col[a * TILE : (a + 1) * TILE] == row_ids[:, a * TILE : a * TILE + win]
        ok = jnp.logical_and(same, jnp.logical_and(gap > 0, gap <= WINDOW))
        s.ffb[a, 0:TILE, 0:win] = jnp.where(ok, 1.0, 0.0).astype(BF)

    def attend(i, carry):
        a, h = lax.div(i, heads), lax.rem(i, heads)
        ks = pl.ds(pl.multiple_of(a * TILE, TILE), win)
        t = jnp.tanh(dot_nt(s.qs[i], s.ka[ks, :]) * (1.0 / SOFT_CAP))
        e = jnp.exp(SOFT_CAP * t) * s.ffb[a, 0:TILE, 0:win].astype(F32)
        pr = e * (1.0 / jnp.sum(e, axis=-1, keepdims=True))
        pr = pr.astype(BF)
        s.ps[i] = pr
        s.ts[i] = (1.0 - t * t).astype(BF)
        o = dot32(pr, s.va[ks, :])
        s.att[aligned(a * TILE, TILE), aligned(h * HD, HD)] = o.astype(BF)
        return carry

    lax.fori_loop(0, tiles * heads, attend, 0)

    weights_ready(1)
    s.ao[...] = dot32(s.att[...], s.wo[...])

    def second(rs):
        _, zed, g1 = norm_parts(s.ao[rs], s.gain_ref[1:2])
        h = s.tk[rs].astype(F32) + zed * g1
        s.h1[rs] = h
        _, zed, g1 = norm_parts(h, s.gain_ref[2:3])
        n = zed * g1
        s.xa[rs] = n.astype(BF)
        s.fit[:, rs] = permuted(n)

    per_rows(second)

    weights_ready(2)
    weights_ready(3)
    root = 0.7978845608028654

    def forward(i, carry):
        v, u = lax.div(i, 4), lax.rem(i, 4)
        us = aligned(u * TILE, TILE)
        gt = dot32(s.xa[...], s.wg[v, :, us])
        up = dot32(s.xa[...], s.wu[v, :, us])
        g2 = gt * gt
        th = jnp.tanh(root * gt * (1.0 + 0.044715 * g2))
        lift = 0.5 * (1.0 + th)
        act = gt * lift
        slope = lift + 0.5 * gt * (1.0 - th * th) * (root * (1.0 + 3.0 * 0.044715 * g2))
        s.ffb[v, :, us] = (act * up).astype(BF)
        s.ffb[2 + v, :, us] = (up * slope).astype(BF)
        s.ffb[4 + v, :, us] = act.astype(BF)
        return carry

    lax.fori_loop(0, 8, forward, 0)
    weights_ready(4)
    s.dn[...] = dot32(s.ffb[0], s.wd[:half_ff]) + dot32(s.ffb[1], s.wd[half_ff:])
    s.dg_ref[...] = jnp.zeros_like(s.dg_ref)

    def third(rs):
        dn = s.dn[rs]
        _, zed, g1 = norm_parts(dn, s.gain_ref[3:4])
        s.xa[rs] = (s.h1[rs] + zed * g1).astype(BF)
        dv, dg = norm_back(dn, s.gain_ref[3:4], s.ct[rs].astype(F32))
        s.dg_ref[3:4] += dg
        s.ddn[rs] = dv.astype(BF)
        s.ddnt[:, rs] = permuted(dv)

    cot_in.wait()
    per_rows(third)
    y_far = remote(s.xa, s.y_ref.at[out_rows], s.osend.at[0], s.orecv.at[0], partner)
    y_own = pltpu.make_async_copy(s.xa, s.y_ref.at[out_rows], s.oown.at[0])
    y_far.start()
    y_own.start()

    def part(m, u, width):
        return pl.ds(pl.multiple_of(offs[m] + u * width, 128), width)

    def slot(m, u):
        return lax.rem(u, 2) * 3 + m if m < 3 else (0, 2, 4, 5)[m - 3] + u

    def exchange(m, u, width):
        return remote(
            s.sb.at[slot(m, u), :, :, pl.ds(0, width)],
            s.gb.at[:, :, part(m, u, width)],
            s.csend.at[m, u],
            s.crecv.at[m, u],
            partner,
        )

    def give(m, u, width, value):
        if m < 3:

            @pl.when(u >= 2)
            def _():
                exchange(m, u - 2, width).wait_send()

        s.sb[slot(m, u), :, :, 0:width] = value.astype(BF).reshape(
            IN_COUNT, D // IN_COUNT, width
        )
        exchange(m, u, width).start()

    def keep(m, u, width, value):
        ps = part(m, u, width)
        exchange(m, u, width).wait_recv()
        total = value.reshape(IN_COUNT, D // IN_COUNT, width) + s.gb[:, :, ps].astype(F32)
        s.gb[:, :, ps] = total.astype(BF)

    def down_back(v, put):
        def run(u, carry):
            put(0, u, TILE, dot32(s.ddnt[...], s.ffb[v, :, aligned(u * TILE, TILE)]))
            return carry

        lax.fori_loop(0, 4, run, 0)

    def gate_back(v, put):
        def run(u, carry):
            us = aligned(u * TILE, TILE)
            dh = dot_nt(s.ddn[...], s.wd[aligned((v * 4 + u) * TILE, TILE), :])
            dgt = (dh * s.ffb[2 + v, :, us].astype(F32)).astype(BF)
            dup = (dh * s.ffb[4 + v, :, us].astype(F32)).astype(BF)
            s.ffb[2 + v, :, us] = dgt
            s.ffb[4 + v, :, us] = dup
            put(1, u, TILE, dot32(s.fit[...], dgt))
            return carry

        lax.fori_loop(0, 4, run, 0)

    def up_back(v, put):
        def run(u, carry):
            put(2, u, TILE, dot32(s.fit[...], s.ffb[4 + v, :, aligned(u * TILE, TILE)]))
            return carry

        lax.fori_loop(0, 4, run, 0)

    down_back(other, give)
    down_back(w, keep)
    s.plane_start(0)
    s.plane_start(1)
    gate_back(other, give)
    gate_back(w, keep)
    s.down_free()
    up_back(other, give)
    s.plane_start(2)
    s.plane_start(3)
    up_back(w, keep)
    s.plane_mid(0)
    s.plane_mid(1)
    s.dn[...] = dot_nt(s.ffb[2], s.wg[0]) + dot_nt(s.ffb[3], s.wg[1])
    s.dn[...] += dot_nt(s.ffb[4], s.wu[0]) + dot_nt(s.ffb[5], s.wu[1])

    s.buffers_free()

    def fourth(rs):
        dv, dg = norm_back(s.h1[rs], s.gain_ref[2:3], s.dn[rs])
        s.dg_ref[2:3] += dg
        dh = s.ct[rs].astype(F32) + dv
        s.h1[rs] = dh
        dv, dg = norm_back(s.ao[rs], s.gain_ref[1:2], dh)
        s.dg_ref[1:2] += dg
        s.ddn[rs] = dv.astype(BF)
        s.ddnt[:, rs] = permuted(dv)

    per_rows(fourth)
    s.plane_start(4)
    s.plane_start(5)
    for m in range(3):
        for u in (2, 3):
            exchange(m, u, TILE).wait_send()

    def out_back(v, put):
        def run(u, carry):
            hs = aligned((v * 2 + u) * HD, HD)
            s.datt[:, hs] = dot_nt(s.ddn[...], s.wo[hs, :]).astype(BF)
            put(3, u, HD, dot32(s.ddnt[...], s.att[:, hs]))
            return carry

        lax.fori_loop(0, 2, run, 0)

    out_back(other, give)
    out_back(w, keep)
    s.plane_finish(0)
    s.plane_finish(1)

    s.dka[...] = jnp.zeros_like(s.dka)
    s.dva[...] = jnp.zeros_like(s.dva)

    def attend_back(i, carry):
        a, h = lax.div(i, heads), lax.rem(i, heads)
        ks = pl.ds(pl.multiple_of(a * TILE, TILE), win)
        qr = aligned(a * TILE, TILE)
        hs = aligned(h * HD, HD)
        do = s.datt[qr, hs]
        pr = s.ps[i]
        s.dva[ks, :] += dot_tn(pr, do)
        dp = dot_nt(do, s.va[ks, :])
        pr = pr.astype(F32)
        inner = jnp.sum(pr * dp, axis=-1, keepdims=True)
        ds = (pr * (dp - inner) * s.ts[i].astype(F32)).astype(BF)
        s.dka[ks, :] += dot_tn(ds, s.qs[i])
        dq = dot32(ds, s.ka[ks, :])
        s.datt[qr, hs] = (turn_back(dq, s.cs[qr], s.sn[qr]) * HD ** (-0.5)).astype(BF)
        return carry

    def d_part(i, half):
        rs = pl.ds(half * TILE, TILE)
        return remote(
            s.dks.at[i, rs], s.dkr.at[i, rs], s.dsend.at[i, half], s.drecv.at[i, half], prev_id
        )

    d_halo = [d_part(i, half) for half in range(2) for i in range(2)]

    def d_send(half):
        rs = slice(half * TILE, (half + 1) * TILE)
        s.dks[0, rs] = s.dka[rs].astype(BF)
        s.dks[1, rs] = s.dva[rs].astype(BF)

        @pl.when(flat > 0)
        def _():
            for cp in d_halo[half * 2 : half * 2 + 2]:
                cp.start()

    lax.fori_loop(0, heads, attend_back, 0)
    d_send(0)
    s.plane_mid(2)
    s.plane_mid(3)
    lax.fori_loop(heads, tiles * heads, attend_back, 0)
    d_send(1)
    s.plane_start(6)

    def query_back(v, put):
        def run(u, carry):
            hs = aligned((v * 2 + u) * HD, HD)
            put(4, u, HD, dot32(s.xat[...], s.datt[:, hs]))
            return carry

        lax.fori_loop(0, 2, run, 0)

    query_back(other, give)
    s.plane_mid(4)
    s.plane_mid(5)
    s.dn[...] = dot_nt(s.datt[:, : HQ // 2], s.wq[0]) + dot_nt(s.datt[:, HQ // 2 :], s.wq[1])
    query_back(w, keep)
    s.plane_start(7)
    s.plane_finish(2)
    s.plane_finish(3)

    @pl.when(flat < n_dev - 1)
    def _():
        for cp in d_halo:
            cp.wait_recv()

    @pl.when(flat == n_dev - 1)
    def _():
        s.dkr[...] = jnp.zeros_like(s.dkr)

    dk = s.dka[tok:, :] + s.dkr[0].astype(F32)
    s.dkv[0] = turn_back(dk, s.cs[...], s.sn[...]).astype(BF)
    s.dkv[1] = (s.dva[tok:, :] + s.dkr[1].astype(F32)).astype(BF)
    kvw = HD // 2
    for i in range(2):
        give(5 + i, 0, kvw, dot32(s.xat[...], s.dkv[i, :, aligned(other * kvw, kvw)]))
    for i in range(2):
        keep(5 + i, 0, kvw, dot32(s.xat[...], s.dkv[i, :, aligned(w * kvw, kvw)]))
    s.plane_start(8)
    s.plane_mid(6)
    s.plane_finish(4)
    s.plane_finish(5)
    s.dn[...] += dot_nt(s.dkv[0], s.wkv_ref[0]) + dot_nt(s.dkv[1], s.wkv_ref[1])

    def fifth(rs):
        dv, dg = norm_back(s.tk[rs].astype(F32), s.gain_ref[0:1], s.dn[rs])
        s.dg_ref[0:1] += dg
        s.h1[rs] = s.h1[rs] + dv

    per_rows(fifth)
    s.gains_core()
    x_far = remote(s.h1, s.x_ref.at[out_rows], s.osend.at[1], s.orecv.at[1], partner)
    x_own = pltpu.make_async_copy(s.h1, s.x_ref.at[out_rows], s.oown.at[1])
    x_far.start()
    x_own.start()

    def finish():
        for cp in w_far:
            cp.wait_send()

        @pl.when(flat < n_dev - 1)
        def _():
            for cp in halo:
                cp.wait_send()

        @pl.when(flat > 0)
        def _():
            for cp in d_halo:
                cp.wait_send()

        for m, count, width in ((3, 2, HD), (4, 2, HD), (5, 1, kvw), (6, 1, kvw)):
            for u in range(count):
                exchange(m, u, width).wait_send()
        y_own.wait()
        x_own.wait()
        y_far.wait()
        x_far.wait()

    return finish


LAYER_INPUTS = (
    "tok_ref",
    "cot_ref",
    "cosi_ref",
    "sini_ref",
    "mq_ref",
    "mkv_ref",
    "mgu_ref",
    "mo_ref",
    "md_ref",
    "ids_ref",
    "gain_ref",
    "wkv_ref",
    "cosb_ref",
    "sinb_ref",
    "wq_ref",
    "wo_ref",
    "wgu_ref",
    "wd_ref",
)
LAYER_OUTPUTS = ("y_ref", "x_ref", "sum_ref", "nm_ref", "ub", "ubk", "gs_ref")
VMEM_BYTES = 63 << 20


def whole_kernel(ctx_count, wa_count, names, *refs):
    s = Refs()
    for name, ref in zip(names, refs):
        setattr(s, name, ref)
    c = lax.axis_index("ctx")
    w = lax.axis_index("wa")
    flat = c * wa_count + w
    n_dev = ctx_count * wa_count
    barrier = pltpu.get_barrier_semaphore()

    def greet(i, carry):
        other = lax.rem(flat + i, n_dev)
        pl.semaphore_signal(
            barrier,
            inc=1,
            device_id=(lax.div(other, wa_count), lax.rem(other, wa_count)),
            device_id_type=MESH,
        )
        return carry

    lax.fori_loop(1, n_dev, greet, 0)
    pl.semaphore_wait(barrier, n_dev - 1)
    tail = tail_phases(s, ctx_count, wa_count)
    finish = layer_phases(s, ctx_count, wa_count)
    tail()
    finish()


def rotation_tables(tok, n_dev):
    freq = ROPE_BASE ** (-2.0 * np.arange(HD // 2) / HD)
    inner = np.arange(tok)[:, None] * freq[None, :]
    base = (np.arange(n_dev) * tok)[:, None] * freq[None, :]
    return [jnp.asarray(f(a), F32) for a in (inner, base) for f in (np.cos, np.sin)]


def run_whole(
    tokens, cotangent, seq_ids, gains, wkv, moms, wq, wo, wgu, wd, ctx_count, wa_count
):
    block = tokens.shape[0]
    tok = block // wa_count
    n_dev = ctx_count * wa_count
    mom_query, mom_keyval, mom_out, mom_gateup, mom_down = moms
    cosi, sini, cosb, sinb = rotation_tables(tok, n_dev)
    scratch = layer_scratch(tok) | tail_scratch(ctx_count, wa_count)
    names = LAYER_INPUTS + LAYER_OUTPUTS + tuple(scratch)
    any_space = pl.BlockSpec(memory_space=pl.ANY)
    vmem = pl.BlockSpec(memory_space=pltpu.VMEM)
    _, offs, cols = layout(wa_count)
    shard = jax.ShapeDtypeStruct((D // ctx_count, cols), F32)
    return pl.pallas_call(
        partial(whole_kernel, ctx_count, wa_count, names),
        out_shape=(
            jax.ShapeDtypeStruct((block, D), BF),
            jax.ShapeDtypeStruct((block, D), F32),
            shard,
            shard,
            jax.ShapeDtypeStruct((packed_rows(D // ctx_count), offs[5] // 2), BF),
            jax.ShapeDtypeStruct((2, -(-(D // ctx_count) // 16) * 16, HD // 2), BF),
            jax.ShapeDtypeStruct((8, 128), F32),
        ),
        in_specs=[any_space] * 9 + [vmem] * 5 + [any_space] * 4,
        out_specs=(any_space, any_space) + (vmem,) * 5,
        scratch_shapes=list(scratch.values()),
        compiler_params=pltpu.CompilerParams(
            collective_id=0, has_side_effects=True, vmem_limit_bytes=VMEM_BYTES
        ),
        name="whole",
    )(
        tokens,
        cotangent,
        cosi,
        sini,
        mom_query,
        mom_keyval,
        mom_gateup,
        mom_out.T,
        mom_down.T,
        seq_ids[None],
        gains,
        wkv,
        cosb,
        sinb,
        wq,
        wo,
        wgu,
        wd,
    )


def format_kernel(
    ctx_count,
    wa_count,
    sum_ref,
    nm_ref,
    ub_ref,
    ubk_ref,
    gs_ref,
    first_ref,
    second_ref,
    y_ref,
    x_ref,
    *rest,
):
    outs, (sumv, nmv, ubv, ubkv, gsv, fv, sv, yv, xv, sem) = rest[:21], rest[21:]
    rows = D // ctx_count
    halves, offs, _ = layout(wa_count)

    def copies(pairs, first):
        return [pltpu.make_async_copy(a, b, sem.at[first + i]) for i, (a, b) in enumerate(pairs)]

    def places(group):
        query, keyval, out, gateup, down = group
        return (down, gateup.at[0], gateup.at[1], out, query, keyval.at[0], keyval.at[1])

    fetched = copies(
        (
            (x_ref, xv),
            (y_ref, yv),
            (sum_ref, sumv),
            (nm_ref, nmv),
            (ub_ref, ubv),
            (ubk_ref, ubkv),
            (gs_ref, gsv),
            (first_ref, fv),
            (second_ref, sv),
        ),
        0,
    )
    for cp in fetched:
        cp.start()
    stored = copies(((xv, outs[1]), (yv, outs[0])), 9)
    for src, group, first in ((sumv, outs[2:7], 11), (nmv, outs[8:13], 18)):
        stored += copies(
            [
                (src.at[:, pl.ds(offs[m], halves[m])], dst)
                for m, dst in enumerate(places(group))
            ],
            first,
        )
    starts = ((0, 1), (1, 2), (2, 9), (9, 16))
    for cp, (a, b) in zip(fetched[:4], starts):
        cp.wait()
        for out in stored[a:b]:
            out.start()
    for cp in fetched[4:]:
        cp.wait()
    for m, dst in enumerate(places(outs[13:18])):
        if m < 5:
            for q in range(halves[m] // 512):
                at = offs[m] // 2 + q * 256
                for side, part in enumerate(unpack(ubv[:, at : at + 256], rows)):
                    dst[:, q * 512 + side * 256 : q * 512 + (side + 1) * 256] = part
        else:
            dst[...] = ubkv[m - 5].astype(F32)[:rows]
    g = gsv[0:4, 0:rows]
    first = ADAM_ONE * fv[...] + (1.0 - ADAM_ONE) * g
    second = ADAM_TWO * sv[...] + (1.0 - ADAM_TWO) * g * g
    outs[7][...] = g
    outs[18][...] = first
    outs[19][...] = second
    outs[20][...] = -GAIN_RATE * first / (jnp.sqrt(second) + ADAM_EPS)
    for cp in stored:
        cp.wait()


def run_format(sums, fresh, updates, small, gsum, gain_first, gain_second, y, x, ctx_count, wa_count):
    rows = D // ctx_count
    halves = layout(wa_count)[0]
    down, gate, _, out, query, key, _ = halves
    f = lambda *shape: jax.ShapeDtypeStruct(shape, F32)
    weights = [f(rows, query), f(2, rows, key), f(rows, out), f(2, rows, gate), f(rows, down)]
    any_space = pl.BlockSpec(memory_space=pl.ANY)
    vmem = pl.BlockSpec(memory_space=pltpu.VMEM)
    gain = f(4, rows)
    shapes = [jax.ShapeDtypeStruct(y.shape, y.dtype), jax.ShapeDtypeStruct(x.shape, x.dtype)]
    shapes += weights + [gain] + weights + weights + [gain] * 3
    outs = pl.pallas_call(
        partial(format_kernel, ctx_count, wa_count),
        out_shape=shapes,
        in_specs=[any_space] * 9,
        out_specs=[any_space] * 7 + [vmem] + [any_space] * 5 + [vmem] * 8,
        scratch_shapes=[
            *[
                pltpu.VMEM(a.shape, a.dtype)
                for a in (sums, fresh, updates, small, gsum, gain_first, gain_second, y, x)
            ],
            pltpu.SemaphoreType.DMA((25,)),
        ],
        compiler_params=pltpu.CompilerParams(vmem_limit_bytes=VMEM_BYTES),
        name="format",
    )(sums, fresh, updates, small, gsum, gain_first, gain_second, y, x)
    return tuple(o.T if i in (4, 6, 10, 12, 15, 17) else o for i, o in enumerate(outs))


def per_device(
    tokens,
    cotangent,
    seq_ids,
    w_query,
    w_keyval,
    w_out,
    w_gateup,
    w_down,
    norm_gains,
    mom_query,
    mom_keyval,
    mom_out,
    mom_gateup,
    mom_down,
    gain_first,
    gain_second,
):
    ctx_count = lax.axis_size("ctx")
    wa_count = lax.axis_size("wa")
    y, x, sums, fresh, updates, small, gsum = run_whole(
        tokens,
        cotangent,
        seq_ids,
        norm_gains,
        w_keyval,
        (mom_query, mom_keyval, mom_out, mom_gateup, mom_down),
        w_query,
        w_out,
        w_gateup,
        w_down,
        ctx_count,
        wa_count,
    )
    return tuple(
        run_format(
            sums, fresh, updates, small, gsum, gain_first, gain_second, y, x, ctx_count, wa_count
        )
    )


def solution(mesh):
    in_specs = (
        P("ctx", None),
        P("ctx", None),
        P("ctx"),
        P(None, "wa"),
        P(),
        P("wa", None),
        P(None, None, "wa"),
        P("wa", None),
        P(),
        P("ctx", "wa"),
        P(None, "ctx", "wa"),
        P("wa", "ctx"),
        P(None, "ctx", "wa"),
        P("wa", "ctx"),
        P(None, "ctx"),
        P(None, "ctx"),
    )
    out_specs = (
        P("ctx", None),
        P("ctx", None),
        P("ctx", "wa"),
        P(None, "ctx", "wa"),
        P("wa", "ctx"),
        P(None, "ctx", "wa"),
        P("wa", "ctx"),
        P(None, "ctx"),
        P("ctx", "wa"),
        P(None, "ctx", "wa"),
        P("wa", "ctx"),
        P(None, "ctx", "wa"),
        P("wa", "ctx"),
        P("ctx", "wa"),
        P(None, "ctx", "wa"),
        P("wa", "ctx"),
        P(None, "ctx", "wa"),
        P("wa", "ctx"),
        P(None, "ctx"),
        P(None, "ctx"),
        P(None, "ctx"),
    )
    return jax.shard_map(
        per_device, mesh=mesh, in_specs=in_specs, out_specs=out_specs, check_vma=False
    )
```

```python
from functools import partial
import math

import jax
import jax.numpy as jnp
import numpy as np
from jax import lax
from jax.experimental import pallas as pl
from jax.experimental.pallas import tpu as pltpu
from jax.sharding import PartitionSpec as P

D = 640
FF = 2048
HD = 256
WINDOW = 512
SOFT_CAP = 10
NS_STEPS = 5
HQ = 1024


EPS_NORM = 1e-06
ROPE_BASE = 10000.0
MOMENTUM = 0.95
ADAM_ONE = 0.9
ADAM_TWO = 0.95
ADAM_EPS = 1e-08
GAIN_RATE = 0.1
QUINTIC_A = 3.4445
QUINTIC_B = -4.775
QUINTIC_C = 2.0315
MATRIX_COUNT = 7
MUON_RATE = 0.2

MESH = pl.DeviceIdType.MESH
BF = jnp.bfloat16
F32 = jnp.float32
IN_COUNT = 4
NAMES = ("down", "gate", "up", "out", "query", "key", "value")
WIDTHS = (FF, FF, FF, HQ, HQ, HD, HD)
OWNERS = (7, 4, 9, 6, 10, 8, 11)
PARTS = (
    ((0, 0, 512),),
    ((0, 512, 512),),
    ((1, 0, 512),),
    ((1, 512, 512),),
    ((2, 0, 512),),
    ((2, 512, 512),),
    ((3, 0, 512),),
    ((4, 0, 512),),
    ((5, 0, 128), (6, 0, 128)),
)
TILE = 256


def layout(wa_count):
    halves = [w // wa_count for w in WIDTHS]
    offs = [sum(halves[:i]) for i in range(len(halves))]
    return halves, offs, sum(halves)


def dot32(a, b):
    return jnp.dot(a, b, preferred_element_type=F32)


def eye_mask(n):
    return (
        lax.broadcasted_iota(jnp.int32, (n, n), 0) == lax.broadcasted_iota(jnp.int32, (n, n), 1)
    )


def pad_rows(v, rows):
    if v.shape[0] == rows:
        return v
    return jnp.concatenate([v, jnp.zeros((rows - v.shape[0], v.shape[1]), v.dtype)], axis=0)


def packed_rows(rows):
    return -(-2 * rows // 16) * 16


def pack(left, right, height):
    return pad_rows(jnp.concatenate([left, right], axis=0), height).astype(BF)


def unpack(block, rows):
    block = block.astype(F32)
    return block[:rows], block[rows : 2 * rows]


def split_into(v, hi, lo):
    top = v.astype(BF)
    hi[...] = top
    lo[...] = (v - top.astype(F32)).astype(BF)


SYM_TILES = ((0, 256), (256, 512), (512, 640))


def sym_tiles(out, block):
    for a, b in SYM_TILES:
        v = block(a, b)
        out[a:, a:b] = v
        if b < D:
            out[a:b, b:] = v[b - a :].T


def prod3(h1, l1, h2, l2):
    return lambda a, b: (
        dot32(h1[a:], h2[:, a:b]) + dot32(h1[a:], l2[:, a:b]) + dot32(l1[a:], h2[:, a:b])
    )


def tail_scratch(ctx_count, wa_count):
    v = pltpu.VMEM
    dma = pltpu.SemaphoreType.DMA
    n_in = IN_COUNT
    n_out = ctx_count // n_in
    rows = D // ctx_count
    rp = -(-rows // 16) * 16
    n_dev = ctx_count * wa_count
    n_ch = len(PARTS)
    hp = packed_rows(rows)
    cols = layout(wa_count)[2]
    return dict(
        mb=v((8, hp, 256), BF),
        mbk=v((2, rp, HD // 2), BF),
        early=v((6, D // n_in, 512), BF),
        xb=v((ctx_count, 4, hp, 256), BF),
        am=v((D, D), F32),
        dg_ref=v((8, D), F32),
        dgs=v((n_in, n_out, 8, 128), F32),
        dgc=v((n_in, n_out, 8, 128), F32),
        dgp=v((3, n_out, 8, 128), F32),
        dgo=v((n_out, 8, 128), F32),
        dgl=v((n_out - 1, 8, 128), F32),
        psend=dma((n_ch, 3)),
        precv=dma((n_ch, 3)),
        lsend=dma((n_ch, n_out - 1)),
        lrecv=dma((n_ch, n_out - 1)),
        gsend=dma((n_ch, 2)),
        grecv=dma,
        usend=dma((n_dev,)),
        urecv=dma((MATRIX_COUNT,)),
        gcsend=dma,
        gcrecv=dma,
        gpsend=dma((3,)),
        gprecv=dma((3,)),
        glsend=dma((n_out - 1,)),
        glrecv=dma((n_out - 1,)),
        msem=dma((MATRIX_COUNT,)),
        dfree=pltpu.SemaphoreType.REGULAR,
        pfree=pltpu.SemaphoreType.REGULAR,
        lfree=pltpu.SemaphoreType.REGULAR,
    )


def tail_phases(s, ctx_count, wa_count):
    c = lax.axis_index("ctx")
    w = lax.axis_index("wa")
    n_in = IN_COUNT
    n_out = ctx_count // n_in
    n_dev = ctx_count * wa_count
    p = lax.rem(c, n_in)
    z = lax.div(c, n_in)
    rows = D // ctx_count
    rp = s.mbk.shape[1]
    hp = packed_rows(rows)
    block = D // n_in
    halves, offs, cols = layout(wa_count)
    chunks = [(offs[m[0][0]] + m[0][1], sum(i[2] for i in m)) for m in PARTS]
    me = c * wa_count + w
    per = 512 // hp

    near = (p + 1 - 2 * lax.rem(p, 2), p + 2 - 4 * lax.div(p, 2))
    across = 3 - p

    def plane_slot(ci, k):
        lanes = chunks[ci][1]
        if ci < 2:
            return s.early.at[ci * 3 + k]
        if ci < 4:
            return s.wd.at[pl.ds(((ci - 2) * 3 + k) * block, block), pl.ds(0, lanes)]
        i = (ci - 4) * 3 + k
        buf = (s.wg, s.wu)[i // 16]
        i = i % 16
        return buf.at[i // 8, pl.ds(i % 8 // 2 * block, block), pl.ds(i % 2 * 512, lanes)]

    def line_slot(base, ci, j):
        half = chunks[ci][1] // 2
        page, lane = (base * 2 + ci // 4, ci % 4 * 256) if ci < 8 else (4 + base, 0)
        return s.ffb.at[page, pl.ds(pl.multiple_of(j * hp, 16), hp), pl.ds(lane, half)]

    def plane_copy(ci, k):
        off, wid = chunks[ci]
        first, second = near[ci % 2], near[1 - ci % 2]
        src, dst = ((first, first), (across, first), (second, second))[k]
        return pltpu.make_async_remote_copy(
            s.gb.at[src, :, pl.ds(off, wid)],
            plane_slot(ci, k),
            s.psend.at[ci, k],
            s.precv.at[ci, k],
            device_id=(z * n_in + dst, w),
            device_id_type=MESH,
        )

    def line_copy(ci, k):
        j = lax.rem(z + k, n_out)
        return pltpu.make_async_remote_copy(
            line_slot(0, ci, j),
            line_slot(1, ci, k - 1),
            s.lsend.at[ci, k - 1],
            s.lrecv.at[ci, k - 1],
            device_id=(j * n_in + p, w),
            device_id_type=MESH,
        )

    def tell_plane(sem):
        for q in near:
            pl.semaphore_signal(sem, inc=1, device_id=(z * n_in + q, w), device_id_type=MESH)

    def down_free():
        tell_plane(s.dfree)

    def buffers_free():
        tell_plane(s.pfree)
        for k in range(1, n_out):
            pl.semaphore_signal(
                s.lfree,
                inc=1,
                device_id=(lax.rem(z + k, n_out) * n_in + p, w),
                device_id_type=MESH,
            )

    def plane_start(ci):
        if ci == 2:
            pl.semaphore_wait(s.dfree, 2)
        if ci == 4:
            pl.semaphore_wait(s.pfree, 2)
        plane_copy(ci, 1).start()
        plane_copy(ci, 0).start()

    def plane_mid(ci):
        off, wid = chunks[ci]
        second = near[1 - ci % 2]
        plane_copy(ci, 1).wait_recv()

        def add(t, carry):
            cs = aligned(off + t * TILE, TILE)
            here = aligned(t * TILE, TILE)
            both = s.gb[second, :, cs].astype(F32) + plane_slot(ci, 1)[:, here].astype(F32)
            s.gb[second, :, cs] = both.astype(BF)
            return carry

        lax.fori_loop(0, wid // TILE, add, 0)
        plane_copy(ci, 2).start()

    def plane_finish(ci):
        off, wid = chunks[ci]
        plane_copy(ci, 0).wait_recv()
        plane_copy(ci, 2).wait_recv()

        half = wid // 2
        total = s.gb[p, :, off : off + wid].astype(F32)
        for k in (0, 2):
            total = total + plane_slot(ci, k)[...].astype(F32)
        for j in range(n_out):
            slab = total[j * rows : (j + 1) * rows]

            @pl.when(z == j)
            def _():
                s.sum_ref[:, off : off + wid] = slab

            line_slot(0, ci, j)[...] = pack(slab[:, :half], slab[:, half:], hp)
        if ci == 0:
            pl.semaphore_wait(s.lfree, n_out - 1)
        for k in range(1, n_out):
            line_copy(ci, k).start()

    def gather_copy(ci, i, local):
        m, first, wid = PARTS[ci][i]
        if ci < 8:
            src = s.mb.at[ci]
            dst = s.xb.at[c, w * (halves[m] // 512) + first // 512]
        else:
            src = s.mbk.at[i]
            dst = s.xb.at[c, w, pl.ds(0, rp), pl.ds(0, wid)]
        if local:
            return pltpu.make_async_copy(src, dst, s.grecv)
        return pltpu.make_async_remote_copy(
            src,
            dst,
            s.gsend.at[ci, i],
            s.grecv,
            device_id=(OWNERS[m], 0),
            device_id_type=MESH,
        )

    def line_finish(ci):
        off, wid = chunks[ci]
        half = wid // 2
        for k in range(1, n_out):
            line_copy(ci, k).wait_recv()
        sides = [s.sum_ref[:, off : off + half], s.sum_ref[:, off + half : off + wid]]
        for k in range(n_out - 1):
            for i, extra in enumerate(unpack(line_slot(1, ci, k)[...], rows)):
                sides[i] = sides[i] + extra
        for i in range(2):
            lanes = slice(off + i * half, off + (i + 1) * half)
            s.sum_ref[:, lanes] = sides[i]
            sides[i] = MOMENTUM * s.nm_ref[:, lanes] + sides[i]
            s.nm_ref[:, lanes] = sides[i]
        if ci < 8:
            s.mb[ci] = pack(sides[0], sides[1], hp)
        else:
            for i in range(2):
                s.mbk[i] = pad_rows(sides[i], rp).astype(BF)
        for i, piece in enumerate(PARTS[ci]):
            mine = me == OWNERS[piece[0]] * wa_count

            @pl.when(mine)
            def _():
                gather_copy(ci, i, True).start()

            @pl.when(jnp.logical_not(mine))
            def _():
                gather_copy(ci, i, False).start()

    s.down_free = down_free
    s.buffers_free = buffers_free
    s.plane_start = plane_start
    s.plane_mid = plane_mid
    s.plane_finish = plane_finish

    sources = (
        s.md_ref,
        s.mgu_ref.at[0],
        s.mgu_ref.at[1],
        s.mo_ref,
        s.mq_ref,
        s.mkv_ref.at[0],
        s.mkv_ref.at[1],
    )
    moms = [
        pltpu.make_async_copy(src, s.nm_ref.at[:, pl.ds(offs[m], halves[m])], s.msem.at[m])
        for m, src in enumerate(sources)
    ]
    for cp in moms:
        cp.start()

    def gain_core_copy():
        return pltpu.make_async_remote_copy(
            s.dgs, s.dgc, s.gcsend, s.gcrecv, device_id=(c, 1 - w), device_id_type=MESH
        )

    def gain_plane(k):
        src, dst = ((near[0], near[0]), (across, near[0]), (near[1], near[1]))[k]
        return pltpu.make_async_remote_copy(
            s.dgc.at[src],
            s.dgp.at[k],
            s.gpsend.at[k],
            s.gprecv.at[k],
            device_id=(z * n_in + dst, w),
            device_id_type=MESH,
        )

    def gain_line(k):
        j = lax.rem(z + k, n_out)
        return pltpu.make_async_remote_copy(
            s.dgo.at[j],
            s.dgl.at[k - 1],
            s.glsend.at[k - 1],
            s.glrecv.at[k - 1],
            device_id=(j * n_in + p, w),
            device_id_type=MESH,
        )

    def gains_core():
        for i in range(ctx_count):
            s.dgs[i % n_in, i // n_in, :, 0:rows] = s.dg_ref[:, i * rows : (i + 1) * rows]
        gain_core_copy().start()

    def gains_first():
        gain_core_copy().wait_recv()
        s.dgc[...] = s.dgc[...] + s.dgs[...]
        gain_plane(1).start()
        gain_plane(0).start()

    def gains_mid():
        gain_plane(1).wait_recv()
        s.dgc[near[1]] = s.dgc[near[1]] + s.dgp[1]
        gain_plane(2).start()

    def gains_line():
        gain_plane(0).wait_recv()
        gain_plane(2).wait_recv()
        s.dgo[...] = s.dgc[p] + s.dgp[0] + s.dgp[2]
        for k in range(1, n_out):
            gain_line(k).start()

    def gains_end():
        total = s.dgo[z]
        for k in range(1, n_out):
            gain_line(k).wait_recv()
            total = total + s.dgl[k - 1]
        s.gs_ref[...] = total
        gain_core_copy().wait_send()
        for k in range(3):
            gain_plane(k).wait_send()
        for k in range(1, n_out):
            gain_line(k).wait_send()

    s.gains_core = gains_core

    def rest():
        for cp in moms:
            cp.wait()
        plane_mid(7)
        plane_mid(8)
        plane_finish(6)
        line_finish(0)
        line_finish(1)
        line_finish(2)
        line_finish(3)
        plane_finish(7)
        plane_finish(8)
        gains_first()
        line_finish(4)
        line_finish(5)
        gains_mid()
        line_finish(6)
        line_finish(7)
        gains_line()
        line_finish(8)
        for ci in range(len(chunks)):
            for k in range(3):
                plane_copy(ci, k).wait_send()
            for k in range(1, n_out):
                line_copy(ci, k).wait_send()
        solve()
        gains_end()
        updates_back()

    def owned_by(*which):
        hit = me == OWNERS[which[0]] * wa_count
        for m in which[1:]:
            hit = jnp.logical_or(hit, me == OWNERS[m] * wa_count)
        return hit

    def solve():
        is_owner = owned_by(*range(MATRIX_COUNT))
        is_small = owned_by(5, 6)
        is_wide = owned_by(0, 1, 2)
        pairs = jnp.where(is_small, 0, jnp.where(is_wide, FF // 512, HQ // 512))
        am = s.am
        xfs = (s.dka.at[pl.ds(0, D)], s.dva.at[pl.ds(0, D)])
        ah = s.wd.at[pl.ds(0, D)]
        al = s.wd.at[pl.ds(D, D)]
        ph = s.wd.at[pl.ds(2 * D, D)]
        plo = s.wo.at[pl.ds(0, D)]
        qh = s.wu.at[0, :, pl.ds(0, D)]

        def tile_of(t):
            return s.wg.at[lax.div(t, 4), :, aligned(lax.rem(t, 4) * TILE, TILE)]

        for m in range(MATRIX_COUNT):

            @pl.when(me == OWNERS[m] * wa_count)
            def _(m=m):
                if m < 5:
                    whole = s.xb.at[:, pl.ds(0, halves[m] * wa_count // 512)]
                else:
                    whole = s.xb.at[:, pl.ds(0, 2), pl.ds(0, rp), pl.ds(0, halves[m])]
                pltpu.make_async_copy(whole, whole, s.grecv).wait()

        @pl.when(is_owner)
        def _():
            am[...] = jnp.zeros_like(am)

            def gram(q, carry):
                for i in range(ctx_count):
                    for xf, part in zip(xfs, unpack(s.xb[i, q], rows)):
                        xf[i * rows : (i + 1) * rows, :] = part
                for side in range(2):
                    x = xfs[side][...].astype(BF)
                    tile_of(2 * q + side)[...] = x
                    for a, b in SYM_TILES:
                        am[a:, a:b] += dot_nt(x[a:], x[a:b])
                return carry

            lax.fori_loop(0, pairs, gram, 0)

            @pl.when(is_small)
            def _():
                for i in range(ctx_count):
                    for v in range(2):
                        part = s.xb[i, v, 0:rp, 0 : HD // 2][...].astype(F32)[:rows]
                        lanes = slice(v * (HD // 2), (v + 1) * (HD // 2))
                        xfs[0][i * rows : (i + 1) * rows, lanes] = part
                x = xfs[0][...].astype(BF)
                tile_of(jnp.int32(0))[...] = x
                am[0:HD, 0:HD] = dot_tn(x, x)

            norm2 = jnp.sum(jnp.where(eye_mask(D), am[...], 0.0), keepdims=True)
            inv = 1.0 / (jnp.sqrt(norm2) + 1e-07)
            inv2 = inv * inv
            sym_tiles(am, lambda a, b: am[a:, a:b] * inv2)

            def shifted(a, b, square):
                rest = QUINTIC_B * am[a:, a:b] + QUINTIC_C * square
                top = rest[: b - a] + jnp.where(eye_mask(b - a), QUINTIC_A, 0.0)
                return jnp.concatenate([top, rest[b - a :]], axis=0) if b < D else top

            def poly():
                split_into(am[...], ah, al)
                square = prod3(ah, al, ah, al)
                sym_tiles(am, lambda a, b: shifted(a, b, square(a, b)))

            def advance():
                sym_tiles(am, prod3(ph, plo, ah, al))
                split_into(am[...], ah, al)
                sym_tiles(am, prod3(ah, al, ph, plo))

            def grow():
                sym_tiles(am, lambda a, b: dot32(ph[a:], qh[:, a:b]))
                qh[...] = am[...].astype(BF)

            poly()
            split_into(am[...], ph, plo)
            qh[...] = ph[...]
            advance()

            def sweep(i, carry):
                poly()
                split_into(am[...], ph, plo)
                grow()
                advance()
                return carry

            lax.fori_loop(0, NS_STEPS - 2, sweep, 0)
            ah[...] = am[...].astype(BF)
            sym_tiles(am, lambda a, b: shifted(a, b, dot32(ah[a:], ah[:, a:b])))
            ph[...] = am[...].astype(BF)
            grow()
            rates = [-MUON_RATE * 0.2 * math.sqrt(n) for n in (D, FF, HQ)]
            rate = jnp.where(is_small, rates[0], jnp.where(is_wide, rates[1], rates[2]))
            scale = rate * inv

            def place(i, height, lanes):
                return i // per, slice(i % per * hp, i % per * hp + height), lanes

            def back(q, carry):
                for side in range(2):
                    xfs[side][...] = dot32(qh[...], tile_of(2 * q + side)[...]) * scale
                for i in range(ctx_count):
                    rs = slice(i * rows, (i + 1) * rows)
                    s.ffb[place(i, hp, aligned(q * 256, 256))] = pack(xfs[0][rs], xfs[1][rs], hp)
                return carry

            @pl.when(is_small)
            def _():
                xfs[0][...] = dot32(tile_of(jnp.int32(0))[...], s.wu[0, 0:HD, 0:HD]) * scale
                for i in range(ctx_count):
                    rs = slice(i * rows, (i + 1) * rows)
                    both = pad_rows(xfs[0][rs], rp).astype(BF)
                    s.ffb[place(i, rp, slice(0, HD))] = both

            for v in range(2):
                lax.fori_loop(v * lax.div(pairs, 2), (v + 1) * lax.div(pairs, 2), back, 0)
                for m in range(MATRIX_COUNT):

                    @pl.when(me == OWNERS[m] * wa_count)
                    def _(m=m, v=v):
                        def send(i, carry):
                            there = lax.rem(c + i, ctx_count)
                            update_copy(m, there * wa_count + v, False).start()
                            return carry

                        if v == 0:
                            update_copy(m, c * wa_count, True).start()
                            lax.fori_loop(1, ctx_count, send, 0)
                        else:
                            lax.fori_loop(0, ctx_count, send, 0)

    def update_place(m):
        if m < 5:
            return s.ub.at[:, pl.ds(offs[m] // 2, halves[m] // 2)]
        return s.ubk.at[m - 5]

    def update_copy(m, t, local):
        i, v = lax.div(t, wa_count), lax.rem(t, wa_count)
        start = pl.multiple_of(lax.rem(i, per) * hp, 16)
        if m < 5:
            height, wid = hp, halves[m] // 2
        else:
            height, wid = rp, halves[m]
        lanes = pl.ds(pl.multiple_of(v * wid, 128), wid)
        src = s.ffb.at[lax.div(i, per), pl.ds(start, height), lanes]
        dst = update_place(m)
        if local:
            return pltpu.make_async_copy(src, dst, s.urecv.at[m])
        return pltpu.make_async_remote_copy(
            src, dst, s.usend.at[t], s.urecv.at[m], device_id=(i, v), device_id_type=MESH
        )

    def updates_back():
        for m in range(MATRIX_COUNT):
            piece = update_place(m)
            pltpu.make_async_copy(piece, piece, s.urecv.at[m]).wait()

        for m in range(MATRIX_COUNT):
            owner = OWNERS[m] * wa_count

            @pl.when(me != owner)
            def _(m=m):
                for ci, part in enumerate(PARTS):
                    for i, piece in enumerate(part):
                        if piece[0] == m:
                            gather_copy(ci, i, False).wait_send()

            @pl.when(me == owner)
            def _(m=m, owner=owner):
                def done(t, carry):
                    update_copy(m, lax.rem(owner + t, n_dev), False).wait_send()
                    return carry

                lax.fori_loop(1, n_dev, done, 0)

    return rest


class Refs:
    pass


def dot_nt(a, b):
    return lax.dot_general(a, b, (((1,), (1,)), ((), ())), preferred_element_type=F32)


def dot_tn(a, b):
    return lax.dot_general(a, b, (((0,), (0,)), ((), ())), preferred_element_type=F32)


def aligned(start, size):
    return pl.ds(pl.multiple_of(start, size), size)


def norm_parts(v, gain):
    r = lax.rsqrt(jnp.mean(v * v, axis=-1, keepdims=True) + EPS_NORM)
    return r, v * r, 1.0 + gain


def norm_back(v, gain, e):
    r, zed, g1 = norm_parts(v, gain)
    e1 = e * g1
    dv = r * (e1 - zed * jnp.mean(e1 * zed, axis=-1, keepdims=True))
    return dv, jnp.sum(e * zed, axis=0, keepdims=True)


def layer_scratch(tok):
    v = pltpu.VMEM
    dma = pltpu.SemaphoreType.DMA
    cols = sum(WIDTHS) // 2
    heads = HQ // HD
    tiles = tok // TILE
    win = WINDOW + TILE
    return dict(
        wq=v((2, D, HQ // 2), BF),
        wo=v((HQ, D), BF),
        wg=v((2, D, FF // 2), BF),
        wu=v((2, D, FF // 2), BF),
        wd=v((FF, D), BF),
        tk=v((tok, D), BF),
        ct=v((tok, D), BF),
        xa=v((tok, D), BF),
        xat=v((D, tok), BF),
        fit=v((D, tok), BF),
        ddn=v((tok, D), BF),
        ddnt=v((D, tok), BF),
        cs=v((tok, HD // 2), F32),
        sn=v((tok, HD // 2), F32),
        ka=v((WINDOW + tok, HD), BF),
        va=v((WINDOW + tok, HD), BF),
        idown=v((8, tok), jnp.int32),
        idprev=v((8, tok), jnp.int32),
        qs=v((tiles * heads, TILE, HD), BF),
        ps=v((tiles * heads, TILE, win), BF),
        ts=v((tiles * heads, TILE, win), BF),
        att=v((tok, HQ), BF),
        ao=v((tok, D), F32),
        h1=v((tok, D), F32),
        dn=v((tok, D), F32),
        ffb=v((6, tok, FF // 2), BF),
        datt=v((tok, HQ), BF),
        dka=v((WINDOW + tok, HD), F32),
        dva=v((WINDOW + tok, HD), F32),
        dks=v((2, tok, HD), BF),
        dkr=v((2, tok, HD), BF),
        dkv=v((2, tok, HD), BF),
        sb=v((6, IN_COUNT, D // IN_COUNT, TILE), BF),
        gb=v((IN_COUNT, D // IN_COUNT, cols), BF),
        wsend=dma((5,)),
        wrecv=dma((5,)),
        wown=dma((5,)),
        ksend=dma((3,)),
        krecv=dma((3,)),
        dsend=dma((2, 2)),
        drecv=dma((2, 2)),
        csend=dma((MATRIX_COUNT, 4)),
        crecv=dma((MATRIX_COUNT, 4)),
        osend=dma((2,)),
        orecv=dma((2,)),
        oown=dma((2,)),
        tsem=dma((4,)),
    )


def layer_phases(s, ctx_count, wa_count):
    c = lax.axis_index("ctx")
    w = lax.axis_index("wa")
    other = 1 - w
    flat = c * wa_count + w
    n_dev = ctx_count * wa_count
    tok = s.xa.shape[0]
    rows = D // ctx_count
    n_out = ctx_count // IN_COUNT
    heads = HQ // HD
    tiles = tok // TILE
    win = WINDOW + TILE
    half_ff = FF // 2
    halves, offs, cols = layout(wa_count)
    step = 128
    partner = (c, other)
    follow = jnp.minimum(flat + 1, n_dev - 1)
    ahead = jnp.maximum(flat - 1, 0)
    next_id = (lax.div(follow, wa_count), lax.rem(follow, wa_count))
    prev_id = (lax.div(ahead, wa_count), lax.rem(ahead, wa_count))
    order = [zz * IN_COUNT + pp for pp in range(IN_COUNT) for zz in range(n_out)]

    def remote(src, dst, send, recv, where):
        return pltpu.make_async_remote_copy(
            src, dst, send, recv, device_id=where, device_id_type=MESH
        )

    def permuted(v):
        t = v.astype(BF).astype(F32).T
        return jnp.concatenate([t[i * rows : (i + 1) * rows] for i in order], axis=0).astype(BF)

    def per_rows(body):
        def run(i, carry):
            body(aligned(i * step, step))
            return carry

        lax.fori_loop(0, tok // step, run, 0)

    out_rows = aligned(w * tok, tok)
    tok_in = pltpu.make_async_copy(s.tok_ref.at[out_rows], s.tk, s.tsem.at[0])
    cot_in = pltpu.make_async_copy(s.cot_ref.at[out_rows], s.ct, s.tsem.at[1])
    tables = [
        pltpu.make_async_copy(s.cosi_ref, s.cs, s.tsem.at[2]),
        pltpu.make_async_copy(s.sini_ref, s.sn, s.tsem.at[3]),
    ]
    tok_in.start()
    for cp in tables:
        cp.start()
    cot_in.start()

    wk_refs = (
        (s.wq_ref, s.wq.at[w]),
        (s.wo_ref, s.wo.at[aligned(w * (HQ // 2), HQ // 2)]),
        (s.wgu_ref.at[0], s.wg.at[w]),
        (s.wgu_ref.at[1], s.wu.at[w]),
        (s.wd_ref, s.wd.at[aligned(w * half_ff, half_ff)]),
    )
    w_far = [remote(a, b, s.wsend.at[i], s.wrecv.at[i], partner) for i, (a, b) in enumerate(wk_refs)]
    w_own = [pltpu.make_async_copy(a, b, s.wown.at[i]) for i, (a, b) in enumerate(wk_refs)]

    def weights_start(first, last):
        for i in range(first, last):
            w_far[i].start()
            w_own[i].start()

    weights_start(0, 1)

    def weights_ready(i):
        w_own[i].wait()
        w_far[i].wait_recv()

    tok_in.wait()

    def first(rs):
        x = s.tk[rs].astype(F32)
        _, zed, g1 = norm_parts(x, s.gain_ref[0:1])
        s.xa[rs] = (zed * g1).astype(BF)

    per_rows(first)

    cb, sb_ = s.cosb_ref[pl.ds(flat, 1), :], s.sinb_ref[pl.ds(flat, 1), :]
    for cp in tables:
        cp.wait()
    cosi, sini = s.cs[...], s.sn[...]
    s.cs[...] = cb * cosi - sb_ * sini
    s.sn[...] = sb_ * cosi + cb * sini
    hh = HD // 2

    def turn(v, cosine, sine):
        a, b = v[:, :hh], v[:, hh:]
        return jnp.concatenate([a * cosine - b * sine, b * cosine + a * sine], axis=1)

    def turn_back(v, cosine, sine):
        a, b = v[:, :hh], v[:, hh:]
        return jnp.concatenate([a * cosine + b * sine, b * cosine - a * sine], axis=1)

    s.ka[WINDOW:, :] = turn(dot32(s.xa[...], s.wkv_ref[0]), s.cs[...], s.sn[...]).astype(BF)
    s.idown[...] = jnp.broadcast_to(s.ids_ref[:, aligned(w * tok, tok)], (8, tok))
    halo = [
        remote(src, dst, s.ksend.at[i], s.krecv.at[i], next_id)
        for i, (src, dst) in enumerate(
            (
                (s.ka.at[pl.ds(tok, WINDOW)], s.ka.at[pl.ds(0, WINDOW)]),
                (s.va.at[pl.ds(tok, WINDOW)], s.va.at[pl.ds(0, WINDOW)]),
                (s.idown, s.idprev),
            )
        )
    ]

    @pl.when(flat < n_dev - 1)
    def _():
        halo[2].start()
        halo[0].start()

    s.va[WINDOW:, :] = dot32(s.xa[...], s.wkv_ref[1]).astype(BF)

    @pl.when(flat < n_dev - 1)
    def _():
        halo[1].start()

    weights_start(1, 5)

    def flip(rs):
        s.xat[:, rs] = permuted(s.xa[rs])

    weights_ready(0)

    def project(h, carry):
        v, u = lax.div(h, heads // 2), lax.rem(h, heads // 2)
        q = dot32(s.xa[...], s.wq[v, :, aligned(u * HD, HD)])
        q = (turn(q, s.cs[...], s.sn[...]) * HD ** (-0.5)).astype(BF)
        for a in range(tiles):
            s.qs[a * heads + h] = q[a * TILE : (a + 1) * TILE]
        return carry

    lax.fori_loop(0, heads, project, 0)
    per_rows(flip)

    @pl.when(flat > 0)
    def _():
        halo[2].wait_recv()

    @pl.when(flat == 0)
    def _():
        s.idprev[...] = jnp.full((8, tok), -1, jnp.int32)

    row_ids = jnp.concatenate([s.idprev[0:1, :], s.idown[0:1, :]], axis=1)
    own_col = jnp.broadcast_to(s.idown[0:1, :], (128, tok)).T[:, 0:1]
    gap = lax.broadcasted_iota(jnp.int32, (TILE, win), 1) - lax.broadcasted_iota(
        jnp.int32, (TILE, win), 0
    )
    for a in range(tiles):
        same = own_col[a * TILE : (a + 1) * TILE] == row_ids[:, a * TILE : a * TILE + win]
        ok = jnp.logical_and(same, jnp.logical_and(gap > 0, gap <= WINDOW))
        s.ffb[a, 0:TILE, 0:win] = jnp.where(ok, 1.0, 0.0).astype(BF)

    @pl.when(flat > 0)
    def _():
        halo[0].wait_recv()
        halo[1].wait_recv()

    @pl.when(flat == 0)
    def _():
        s.ka[0:WINDOW, :] = jnp.zeros((WINDOW, HD), BF)
        s.va[0:WINDOW, :] = jnp.zeros((WINDOW, HD), BF)

    def attend(i, carry):
        a, h = lax.div(i, heads), lax.rem(i, heads)
        ks = pl.ds(pl.multiple_of(a * TILE, TILE), win)
        t = jnp.tanh(dot_nt(s.qs[i], s.ka[ks, :]) * (1.0 / SOFT_CAP))
        e = jnp.exp(SOFT_CAP * t) * s.ffb[a, 0:TILE, 0:win].astype(F32)
        pr = e * (1.0 / jnp.sum(e, axis=-1, keepdims=True))
        pr = pr.astype(BF)
        s.ps[i] = pr
        s.ts[i] = (1.0 - t * t).astype(BF)
        o = dot32(pr, s.va[ks, :])
        s.att[aligned(a * TILE, TILE), aligned(h * HD, HD)] = o.astype(BF)
        return carry

    lax.fori_loop(0, tiles * heads, attend, 0)

    weights_ready(1)
    s.ao[...] = dot32(s.att[...], s.wo[...])

    def second(rs):
        _, zed, g1 = norm_parts(s.ao[rs], s.gain_ref[1:2])
        h = s.tk[rs].astype(F32) + zed * g1
        s.h1[rs] = h
        _, zed, g1 = norm_parts(h, s.gain_ref[2:3])
        n = zed * g1
        s.xa[rs] = n.astype(BF)
        s.fit[:, rs] = permuted(n)

    per_rows(second)

    weights_ready(2)
    weights_ready(3)
    root = 0.7978845608028654

    def forward(i, carry):
        v, u = lax.div(i, 4), lax.rem(i, 4)
        us = aligned(u * TILE, TILE)
        gt = dot32(s.xa[...], s.wg[v, :, us])
        up = dot32(s.xa[...], s.wu[v, :, us])
        g2 = gt * gt
        th = jnp.tanh(root * gt * (1.0 + 0.044715 * g2))
        lift = 0.5 * (1.0 + th)
        act = gt * lift
        slope = lift + 0.5 * gt * (1.0 - th * th) * (root * (1.0 + 3.0 * 0.044715 * g2))
        s.ffb[v, :, us] = (act * up).astype(BF)
        s.ffb[2 + v, :, us] = (up * slope).astype(BF)
        s.ffb[4 + v, :, us] = act.astype(BF)
        return carry

    lax.fori_loop(0, 8, forward, 0)
    weights_ready(4)
    s.dn[...] = dot32(s.ffb[0], s.wd[:half_ff]) + dot32(s.ffb[1], s.wd[half_ff:])
    s.dg_ref[...] = jnp.zeros_like(s.dg_ref)

    def third(rs):
        dn = s.dn[rs]
        _, zed, g1 = norm_parts(dn, s.gain_ref[3:4])
        s.xa[rs] = (s.h1[rs] + zed * g1).astype(BF)
        dv, dg = norm_back(dn, s.gain_ref[3:4], s.ct[rs].astype(F32))
        s.dg_ref[3:4] += dg
        s.ddn[rs] = dv.astype(BF)
        s.ddnt[:, rs] = permuted(dv)

    cot_in.wait()
    per_rows(third)
    y_far = remote(s.xa, s.y_ref.at[out_rows], s.osend.at[0], s.orecv.at[0], partner)
    y_own = pltpu.make_async_copy(s.xa, s.y_ref.at[out_rows], s.oown.at[0])
    y_far.start()
    y_own.start()

    def part(m, u, width):
        return pl.ds(pl.multiple_of(offs[m] + u * width, 128), width)

    def slot(m, u):
        return lax.rem(u, 2) * 3 + m if m < 3 else (0, 2, 4, 5)[m - 3] + u

    def exchange(m, u, width):
        return remote(
            s.sb.at[slot(m, u), :, :, pl.ds(0, width)],
            s.gb.at[:, :, part(m, u, width)],
            s.csend.at[m, u],
            s.crecv.at[m, u],
            partner,
        )

    def give(m, u, width, value):
        if m < 3:

            @pl.when(u >= 2)
            def _():
                exchange(m, u - 2, width).wait_send()

        s.sb[slot(m, u), :, :, 0:width] = value.astype(BF).reshape(
            IN_COUNT, D // IN_COUNT, width
        )
        exchange(m, u, width).start()

    def keep(m, u, width, value):
        ps = part(m, u, width)
        exchange(m, u, width).wait_recv()
        total = value.reshape(IN_COUNT, D // IN_COUNT, width) + s.gb[:, :, ps].astype(F32)
        s.gb[:, :, ps] = total.astype(BF)

    def down_back(v, put):
        def run(u, carry):
            put(0, u, TILE, dot32(s.ddnt[...], s.ffb[v, :, aligned(u * TILE, TILE)]))
            return carry

        lax.fori_loop(0, 4, run, 0)

    def gate_back(v, put):
        def run(u, carry):
            us = aligned(u * TILE, TILE)
            dh = dot_nt(s.ddn[...], s.wd[aligned((v * 4 + u) * TILE, TILE), :])
            dgt = (dh * s.ffb[2 + v, :, us].astype(F32)).astype(BF)
            dup = (dh * s.ffb[4 + v, :, us].astype(F32)).astype(BF)
            s.ffb[2 + v, :, us] = dgt
            s.ffb[4 + v, :, us] = dup
            put(1, u, TILE, dot32(s.fit[...], dgt))
            return carry

        lax.fori_loop(0, 4, run, 0)

    def up_back(v, put):
        def run(u, carry):
            put(2, u, TILE, dot32(s.fit[...], s.ffb[4 + v, :, aligned(u * TILE, TILE)]))
            return carry

        lax.fori_loop(0, 4, run, 0)

    down_back(other, give)
    down_back(w, keep)
    s.plane_start(0)
    s.plane_start(1)
    gate_back(other, give)
    gate_back(w, keep)
    s.down_free()
    up_back(other, give)
    s.plane_start(2)
    s.plane_start(3)
    up_back(w, keep)
    s.plane_mid(0)
    s.plane_mid(1)
    s.dn[...] = dot_nt(s.ffb[2], s.wg[0]) + dot_nt(s.ffb[3], s.wg[1])
    s.dn[...] += dot_nt(s.ffb[4], s.wu[0]) + dot_nt(s.ffb[5], s.wu[1])

    s.buffers_free()

    def fourth(rs):
        dv, dg = norm_back(s.h1[rs], s.gain_ref[2:3], s.dn[rs])
        s.dg_ref[2:3] += dg
        dh = s.ct[rs].astype(F32) + dv
        s.h1[rs] = dh
        dv, dg = norm_back(s.ao[rs], s.gain_ref[1:2], dh)
        s.dg_ref[1:2] += dg
        s.ddn[rs] = dv.astype(BF)
        s.ddnt[:, rs] = permuted(dv)

    per_rows(fourth)
    s.plane_start(4)
    s.plane_start(5)
    for m in range(3):
        for u in (2, 3):
            exchange(m, u, TILE).wait_send()

    def out_back(v, put):
        def run(u, carry):
            hs = aligned((v * 2 + u) * HD, HD)
            s.datt[:, hs] = dot_nt(s.ddn[...], s.wo[hs, :]).astype(BF)
            put(3, u, HD, dot32(s.ddnt[...], s.att[:, hs]))
            return carry

        lax.fori_loop(0, 2, run, 0)

    out_back(other, give)
    out_back(w, keep)
    s.plane_finish(0)
    s.plane_finish(1)

    s.dka[...] = jnp.zeros_like(s.dka)
    s.dva[...] = jnp.zeros_like(s.dva)

    def attend_back(i, carry):
        a, h = lax.div(i, heads), lax.rem(i, heads)
        ks = pl.ds(pl.multiple_of(a * TILE, TILE), win)
        qr = aligned(a * TILE, TILE)
        hs = aligned(h * HD, HD)
        do = s.datt[qr, hs]
        pr = s.ps[i]
        s.dva[ks, :] += dot_tn(pr, do)
        dp = dot_nt(do, s.va[ks, :])
        pr = pr.astype(F32)
        inner = jnp.sum(pr * dp, axis=-1, keepdims=True)
        ds = (pr * (dp - inner) * s.ts[i].astype(F32)).astype(BF)
        s.dka[ks, :] += dot_tn(ds, s.qs[i])
        dq = dot32(ds, s.ka[ks, :])
        s.datt[qr, hs] = (turn_back(dq, s.cs[qr], s.sn[qr]) * HD ** (-0.5)).astype(BF)
        return carry

    def d_part(i, half):
        rs = pl.ds(half * TILE, TILE)
        return remote(
            s.dks.at[i, rs], s.dkr.at[i, rs], s.dsend.at[i, half], s.drecv.at[i, half], prev_id
        )

    d_halo = [d_part(i, half) for half in range(2) for i in range(2)]

    def d_send(half):
        rs = slice(half * TILE, (half + 1) * TILE)
        s.dks[0, rs] = s.dka[rs].astype(BF)
        s.dks[1, rs] = s.dva[rs].astype(BF)

        @pl.when(flat > 0)
        def _():
            for cp in d_halo[half * 2 : half * 2 + 2]:
                cp.start()

    lax.fori_loop(0, heads, attend_back, 0)
    d_send(0)
    s.plane_mid(2)
    s.plane_mid(3)
    lax.fori_loop(heads, tiles * heads, attend_back, 0)
    d_send(1)
    s.plane_start(6)

    def query_back(v, put):
        def run(u, carry):
            hs = aligned((v * 2 + u) * HD, HD)
            put(4, u, HD, dot32(s.xat[...], s.datt[:, hs]))
            return carry

        lax.fori_loop(0, 2, run, 0)

    query_back(other, give)
    s.plane_mid(4)
    s.plane_mid(5)
    s.dn[...] = dot_nt(s.datt[:, : HQ // 2], s.wq[0]) + dot_nt(s.datt[:, HQ // 2 :], s.wq[1])
    query_back(w, keep)
    s.plane_start(7)
    s.plane_finish(2)
    s.plane_finish(3)

    @pl.when(flat < n_dev - 1)
    def _():
        for cp in d_halo:
            cp.wait_recv()

    @pl.when(flat == n_dev - 1)
    def _():
        s.dkr[...] = jnp.zeros_like(s.dkr)

    dk = s.dka[tok:, :] + s.dkr[0].astype(F32)
    s.dkv[0] = turn_back(dk, s.cs[...], s.sn[...]).astype(BF)
    s.dkv[1] = (s.dva[tok:, :] + s.dkr[1].astype(F32)).astype(BF)
    kvw = HD // 2
    for i in range(2):
        give(5 + i, 0, kvw, dot32(s.xat[...], s.dkv[i, :, aligned(other * kvw, kvw)]))
    for i in range(2):
        keep(5 + i, 0, kvw, dot32(s.xat[...], s.dkv[i, :, aligned(w * kvw, kvw)]))
    s.plane_start(8)
    s.plane_mid(6)
    s.plane_finish(4)
    s.plane_finish(5)
    s.dn[...] += dot_nt(s.dkv[0], s.wkv_ref[0]) + dot_nt(s.dkv[1], s.wkv_ref[1])

    def fifth(rs):
        dv, dg = norm_back(s.tk[rs].astype(F32), s.gain_ref[0:1], s.dn[rs])
        s.dg_ref[0:1] += dg
        s.h1[rs] = s.h1[rs] + dv

    per_rows(fifth)
    s.gains_core()
    x_far = remote(s.h1, s.x_ref.at[out_rows], s.osend.at[1], s.orecv.at[1], partner)
    x_own = pltpu.make_async_copy(s.h1, s.x_ref.at[out_rows], s.oown.at[1])
    x_far.start()
    x_own.start()

    def finish():
        for cp in w_far:
            cp.wait_send()

        @pl.when(flat < n_dev - 1)
        def _():
            for cp in halo:
                cp.wait_send()

        @pl.when(flat > 0)
        def _():
            for cp in d_halo:
                cp.wait_send()

        for m, count, width in ((3, 2, HD), (4, 2, HD), (5, 1, kvw), (6, 1, kvw)):
            for u in range(count):
                exchange(m, u, width).wait_send()
        y_own.wait()
        x_own.wait()
        y_far.wait()
        x_far.wait()

    return finish


LAYER_INPUTS = (
    "tok_ref",
    "cot_ref",
    "cosi_ref",
    "sini_ref",
    "mq_ref",
    "mkv_ref",
    "mgu_ref",
    "mo_ref",
    "md_ref",
    "ids_ref",
    "gain_ref",
    "wkv_ref",
    "cosb_ref",
    "sinb_ref",
    "wq_ref",
    "wo_ref",
    "wgu_ref",
    "wd_ref",
)
LAYER_OUTPUTS = ("y_ref", "x_ref", "sum_ref", "nm_ref", "ub", "ubk", "gs_ref")
VMEM_BYTES = 63 << 20


def whole_kernel(ctx_count, wa_count, names, *refs):
    s = Refs()
    for name, ref in zip(names, refs):
        setattr(s, name, ref)
    c = lax.axis_index("ctx")
    w = lax.axis_index("wa")
    flat = c * wa_count + w
    n_dev = ctx_count * wa_count
    barrier = pltpu.get_barrier_semaphore()

    def greet(i, carry):
        other = lax.rem(flat + i, n_dev)
        pl.semaphore_signal(
            barrier,
            inc=1,
            device_id=(lax.div(other, wa_count), lax.rem(other, wa_count)),
            device_id_type=MESH,
        )
        return carry

    lax.fori_loop(1, n_dev, greet, 0)
    pl.semaphore_wait(barrier, n_dev - 1)
    tail = tail_phases(s, ctx_count, wa_count)
    finish = layer_phases(s, ctx_count, wa_count)
    tail()
    finish()


def rotation_tables(tok, n_dev):
    freq = ROPE_BASE ** (-2.0 * np.arange(HD // 2) / HD)
    inner = np.arange(tok)[:, None] * freq[None, :]
    base = (np.arange(n_dev) * tok)[:, None] * freq[None, :]
    return [jnp.asarray(f(a), F32) for a in (inner, base) for f in (np.cos, np.sin)]


def run_whole(
    tokens, cotangent, seq_ids, gains, wkv, moms, wq, wo, wgu, wd, ctx_count, wa_count
):
    block = tokens.shape[0]
    tok = block // wa_count
    n_dev = ctx_count * wa_count
    mom_query, mom_keyval, mom_out, mom_gateup, mom_down = moms
    cosi, sini, cosb, sinb = rotation_tables(tok, n_dev)
    scratch = layer_scratch(tok) | tail_scratch(ctx_count, wa_count)
    names = LAYER_INPUTS + LAYER_OUTPUTS + tuple(scratch)
    any_space = pl.BlockSpec(memory_space=pl.ANY)
    vmem = pl.BlockSpec(memory_space=pltpu.VMEM)
    _, offs, cols = layout(wa_count)
    shard = jax.ShapeDtypeStruct((D // ctx_count, cols), F32)
    return pl.pallas_call(
        partial(whole_kernel, ctx_count, wa_count, names),
        out_shape=(
            jax.ShapeDtypeStruct((block, D), BF),
            jax.ShapeDtypeStruct((block, D), F32),
            shard,
            shard,
            jax.ShapeDtypeStruct((packed_rows(D // ctx_count), offs[5] // 2), BF),
            jax.ShapeDtypeStruct((2, -(-(D // ctx_count) // 16) * 16, HD // 2), BF),
            jax.ShapeDtypeStruct((8, 128), F32),
        ),
        in_specs=[any_space] * 9 + [vmem] * 5 + [any_space] * 4,
        out_specs=(any_space, any_space) + (vmem,) * 5,
        scratch_shapes=list(scratch.values()),
        compiler_params=pltpu.CompilerParams(
            collective_id=0, has_side_effects=True, vmem_limit_bytes=VMEM_BYTES
        ),
        name="whole",
    )(
        tokens,
        cotangent,
        cosi,
        sini,
        mom_query,
        mom_keyval,
        mom_gateup,
        mom_out.T,
        mom_down.T,
        seq_ids[None],
        gains,
        wkv,
        cosb,
        sinb,
        wq,
        wo,
        wgu,
        wd,
    )


def format_kernel(
    ctx_count,
    wa_count,
    sum_ref,
    nm_ref,
    ub_ref,
    ubk_ref,
    gs_ref,
    first_ref,
    second_ref,
    y_ref,
    x_ref,
    *rest,
):
    outs, (sumv, nmv, ubv, ubkv, gsv, fv, sv, yv, xv, sem) = rest[:21], rest[21:]
    rows = D // ctx_count
    halves, offs, _ = layout(wa_count)

    def copies(pairs, first):
        return [pltpu.make_async_copy(a, b, sem.at[first + i]) for i, (a, b) in enumerate(pairs)]

    def places(group):
        query, keyval, out, gateup, down = group
        return (down, gateup.at[0], gateup.at[1], out, query, keyval.at[0], keyval.at[1])

    fetched = copies(
        (
            (x_ref, xv),
            (y_ref, yv),
            (sum_ref, sumv),
            (nm_ref, nmv),
            (ub_ref, ubv),
            (ubk_ref, ubkv),
            (gs_ref, gsv),
            (first_ref, fv),
            (second_ref, sv),
        ),
        0,
    )
    for cp in fetched:
        cp.start()
    stored = copies(((xv, outs[1]), (yv, outs[0])), 9)
    for src, group, first in ((sumv, outs[2:7], 11), (nmv, outs[8:13], 18)):
        stored += copies(
            [
                (src.at[:, pl.ds(offs[m], halves[m])], dst)
                for m, dst in enumerate(places(group))
            ],
            first,
        )
    starts = ((0, 1), (1, 2), (2, 9), (9, 16))
    for cp, (a, b) in zip(fetched[:4], starts):
        cp.wait()
        for out in stored[a:b]:
            out.start()
    for cp in fetched[4:]:
        cp.wait()
    for m, dst in enumerate(places(outs[13:18])):
        if m < 5:
            for q in range(halves[m] // 512):
                at = offs[m] // 2 + q * 256
                for side, part in enumerate(unpack(ubv[:, at : at + 256], rows)):
                    dst[:, q * 512 + side * 256 : q * 512 + (side + 1) * 256] = part
        else:
            dst[...] = ubkv[m - 5].astype(F32)[:rows]
    g = gsv[0:4, 0:rows]
    first = ADAM_ONE * fv[...] + (1.0 - ADAM_ONE) * g
    second = ADAM_TWO * sv[...] + (1.0 - ADAM_TWO) * g * g
    outs[7][...] = g
    outs[18][...] = first
    outs[19][...] = second
    outs[20][...] = -GAIN_RATE * first / (jnp.sqrt(second) + ADAM_EPS)
    for cp in stored:
        cp.wait()


def run_format(sums, fresh, updates, small, gsum, gain_first, gain_second, y, x, ctx_count, wa_count):
    rows = D // ctx_count
    halves = layout(wa_count)[0]
    down, gate, _, out, query, key, _ = halves
    f = lambda *shape: jax.ShapeDtypeStruct(shape, F32)
    weights = [f(rows, query), f(2, rows, key), f(rows, out), f(2, rows, gate), f(rows, down)]
    any_space = pl.BlockSpec(memory_space=pl.ANY)
    vmem = pl.BlockSpec(memory_space=pltpu.VMEM)
    gain = f(4, rows)
    shapes = [jax.ShapeDtypeStruct(y.shape, y.dtype), jax.ShapeDtypeStruct(x.shape, x.dtype)]
    shapes += weights + [gain] + weights + weights + [gain] * 3
    outs = pl.pallas_call(
        partial(format_kernel, ctx_count, wa_count),
        out_shape=shapes,
        in_specs=[any_space] * 9,
        out_specs=[any_space] * 7 + [vmem] + [any_space] * 5 + [vmem] * 8,
        scratch_shapes=[
            *[
                pltpu.VMEM(a.shape, a.dtype)
                for a in (sums, fresh, updates, small, gsum, gain_first, gain_second, y, x)
            ],
            pltpu.SemaphoreType.DMA((25,)),
        ],
        compiler_params=pltpu.CompilerParams(vmem_limit_bytes=VMEM_BYTES),
        name="format",
    )(sums, fresh, updates, small, gsum, gain_first, gain_second, y, x)
    return tuple(o.T if i in (4, 6, 10, 12, 15, 17) else o for i, o in enumerate(outs))


def per_device(
    tokens,
    cotangent,
    seq_ids,
    w_query,
    w_keyval,
    w_out,
    w_gateup,
    w_down,
    norm_gains,
    mom_query,
    mom_keyval,
    mom_out,
    mom_gateup,
    mom_down,
    gain_first,
    gain_second,
):
    ctx_count = lax.axis_size("ctx")
    wa_count = lax.axis_size("wa")
    y, x, sums, fresh, updates, small, gsum = run_whole(
        tokens,
        cotangent,
        seq_ids,
        norm_gains,
        w_keyval,
        (mom_query, mom_keyval, mom_out, mom_gateup, mom_down),
        w_query,
        w_out,
        w_gateup,
        w_down,
        ctx_count,
        wa_count,
    )
    return tuple(
        run_format(
            sums, fresh, updates, small, gsum, gain_first, gain_second, y, x, ctx_count, wa_count
        )
    )


def solution(mesh):
    in_specs = (
        P("ctx", None),
        P("ctx", None),
        P("ctx"),
        P(None, "wa"),
        P(),
        P("wa", None),
        P(None, None, "wa"),
        P("wa", None),
        P(),
        P("ctx", "wa"),
        P(None, "ctx", "wa"),
        P("wa", "ctx"),
        P(None, "ctx", "wa"),
        P("wa", "ctx"),
        P(None, "ctx"),
        P(None, "ctx"),
    )
    out_specs = (
        P("ctx", None),
        P("ctx", None),
        P("ctx", "wa"),
        P(None, "ctx", "wa"),
        P("wa", "ctx"),
        P(None, "ctx", "wa"),
        P("wa", "ctx"),
        P(None, "ctx"),
        P("ctx", "wa"),
        P(None, "ctx", "wa"),
        P("wa", "ctx"),
        P(None, "ctx", "wa"),
        P("wa", "ctx"),
        P("ctx", "wa"),
        P(None, "ctx", "wa"),
        P("wa", "ctx"),
        P(None, "ctx", "wa"),
        P("wa", "ctx"),
        P(None, "ctx"),
        P(None, "ctx"),
        P(None, "ctx"),
    )
    return jax.shard_map(
        per_device, mesh=mesh, in_specs=in_specs, out_specs=out_specs, check_vma=False
    )
```

```python
from functools import partial
import math

import jax
import jax.numpy as jnp
import numpy as np
from jax import lax
from jax.experimental import pallas as pl
from jax.experimental.pallas import tpu as pltpu
from jax.sharding import PartitionSpec as P

D = 640
FF = 2048
HD = 256
WINDOW = 512
SOFT_CAP = 10
NS_STEPS = 5
HQ = 1024


EPS_NORM = 1e-06
ROPE_BASE = 10000.0
MOMENTUM = 0.95
ADAM_ONE = 0.9
ADAM_TWO = 0.95
ADAM_EPS = 1e-08
GAIN_RATE = 0.1
QUINTIC_A = 3.4445
QUINTIC_B = -4.775
QUINTIC_C = 2.0315
MATRIX_COUNT = 7
MUON_RATE = 0.2

MESH = pl.DeviceIdType.MESH
BF = jnp.bfloat16
F32 = jnp.float32
IN_COUNT = 4
NAMES = ("down", "gate", "up", "out", "query", "key", "value")
WIDTHS = (FF, FF, FF, HQ, HQ, HD, HD)
OWNERS = (7, 4, 9, 6, 10, 8, 11)
PARTS = (
    ((0, 0, 512),),
    ((0, 512, 512),),
    ((1, 0, 512),),
    ((1, 512, 512),),
    ((2, 0, 512),),
    ((2, 512, 512),),
    ((3, 0, 512),),
    ((4, 0, 512),),
    ((5, 0, 128), (6, 0, 128)),
)
TILE = 256


def layout(wa_count):
    halves = [w // wa_count for w in WIDTHS]
    offs = [sum(halves[:i]) for i in range(len(halves))]
    return halves, offs, sum(halves)


def dot32(a, b):
    return jnp.dot(a, b, preferred_element_type=F32)


def eye_mask(n):
    return (
        lax.broadcasted_iota(jnp.int32, (n, n), 0) == lax.broadcasted_iota(jnp.int32, (n, n), 1)
    )


def pad_rows(v, rows):
    if v.shape[0] == rows:
        return v
    return jnp.concatenate([v, jnp.zeros((rows - v.shape[0], v.shape[1]), v.dtype)], axis=0)


def packed_rows(rows):
    return -(-2 * rows // 16) * 16


def pack(left, right, height):
    return pad_rows(jnp.concatenate([left, right], axis=0), height).astype(BF)


def unpack(block, rows):
    block = block.astype(F32)
    return block[:rows], block[rows : 2 * rows]


def split_into(v, hi, lo):
    top = v.astype(BF)
    hi[...] = top
    lo[...] = (v - top.astype(F32)).astype(BF)


SYM_TILES = ((0, 256), (256, 512), (512, 640))


def sym_tiles(out, block):
    for a, b in SYM_TILES:
        v = block(a, b)
        out[a:, a:b] = v
        if b < D:
            out[a:b, b:] = v[b - a :].T


def prod3(h1, l1, h2, l2):
    return lambda a, b: (
        dot32(h1[a:], h2[:, a:b]) + dot32(h1[a:], l2[:, a:b]) + dot32(l1[a:], h2[:, a:b])
    )


def tail_scratch(ctx_count, wa_count):
    v = pltpu.VMEM
    dma = pltpu.SemaphoreType.DMA
    n_in = IN_COUNT
    n_out = ctx_count // n_in
    rows = D // ctx_count
    rp = -(-rows // 16) * 16
    n_dev = ctx_count * wa_count
    n_ch = len(PARTS)
    hp = packed_rows(rows)
    cols = layout(wa_count)[2]
    return dict(
        mb=v((8, hp, 256), BF),
        mbk=v((2, rp, HD // 2), BF),
        early=v((6, D // n_in, 512), BF),
        xb=v((ctx_count, 4, hp, 256), BF),
        am=v((D, D), F32),
        dg_ref=v((8, D), F32),
        dgs=v((n_in, n_out, 8, 128), F32),
        dgc=v((n_in, n_out, 8, 128), F32),
        dgp=v((3, n_out, 8, 128), F32),
        dgo=v((n_out, 8, 128), F32),
        dgl=v((n_out - 1, 8, 128), F32),
        psend=dma((n_ch, 3)),
        precv=dma((n_ch, 3)),
        lsend=dma((n_ch, n_out - 1)),
        lrecv=dma((n_ch, n_out - 1)),
        gsend=dma((n_ch, 2)),
        grecv=dma,
        usend=dma((n_dev,)),
        urecv=dma((MATRIX_COUNT,)),
        gcsend=dma,
        gcrecv=dma,
        gpsend=dma((3,)),
        gprecv=dma((3,)),
        glsend=dma((n_out - 1,)),
        glrecv=dma((n_out - 1,)),
        msem=dma((MATRIX_COUNT,)),
        dfree=pltpu.SemaphoreType.REGULAR,
        pfree=pltpu.SemaphoreType.REGULAR,
        lfree=pltpu.SemaphoreType.REGULAR,
    )


def tail_phases(s, ctx_count, wa_count):
    c = lax.axis_index("ctx")
    w = lax.axis_index("wa")
    n_in = IN_COUNT
    n_out = ctx_count // n_in
    n_dev = ctx_count * wa_count
    p = lax.rem(c, n_in)
    z = lax.div(c, n_in)
    rows = D // ctx_count
    rp = s.mbk.shape[1]
    hp = packed_rows(rows)
    block = D // n_in
    halves, offs, cols = layout(wa_count)
    chunks = [(offs[m[0][0]] + m[0][1], sum(i[2] for i in m)) for m in PARTS]
    me = c * wa_count + w
    per = 512 // hp

    near = (p + 1 - 2 * lax.rem(p, 2), p + 2 - 4 * lax.div(p, 2))
    across = 3 - p

    def plane_slot(ci, k):
        lanes = chunks[ci][1]
        if ci < 2:
            return s.early.at[ci * 3 + k]
        if ci < 4:
            return s.wd.at[pl.ds(((ci - 2) * 3 + k) * block, block), pl.ds(0, lanes)]
        i = (ci - 4) * 3 + k
        buf = (s.wg, s.wu)[i // 16]
        i = i % 16
        return buf.at[i // 8, pl.ds(i % 8 // 2 * block, block), pl.ds(i % 2 * 512, lanes)]

    def line_slot(base, ci, j):
        half = chunks[ci][1] // 2
        page, lane = (base * 2 + ci // 4, ci % 4 * 256) if ci < 8 else (4 + base, 0)
        return s.ffb.at[page, pl.ds(pl.multiple_of(j * hp, 16), hp), pl.ds(lane, half)]

    def plane_copy(ci, k):
        off, wid = chunks[ci]
        first, second = near[ci % 2], near[1 - ci % 2]
        src, dst = ((first, first), (across, first), (second, second))[k]
        return pltpu.make_async_remote_copy(
            s.gb.at[src, :, pl.ds(off, wid)],
            plane_slot(ci, k),
            s.psend.at[ci, k],
            s.precv.at[ci, k],
            device_id=(z * n_in + dst, w),
            device_id_type=MESH,
        )

    def line_copy(ci, k):
        j = lax.rem(z + k, n_out)
        return pltpu.make_async_remote_copy(
            line_slot(0, ci, j),
            line_slot(1, ci, k - 1),
            s.lsend.at[ci, k - 1],
            s.lrecv.at[ci, k - 1],
            device_id=(j * n_in + p, w),
            device_id_type=MESH,
        )

    def tell_plane(sem):
        for q in near:
            pl.semaphore_signal(sem, inc=1, device_id=(z * n_in + q, w), device_id_type=MESH)

    def down_free():
        tell_plane(s.dfree)

    def buffers_free():
        tell_plane(s.pfree)
        for k in range(1, n_out):
            pl.semaphore_signal(
                s.lfree,
                inc=1,
                device_id=(lax.rem(z + k, n_out) * n_in + p, w),
                device_id_type=MESH,
            )

    def plane_start(ci):
        if ci == 2:
            pl.semaphore_wait(s.dfree, 2)
        if ci == 4:
            pl.semaphore_wait(s.pfree, 2)
        plane_copy(ci, 1).start()
        plane_copy(ci, 0).start()

    def plane_mid(ci):
        off, wid = chunks[ci]
        second = near[1 - ci % 2]
        plane_copy(ci, 1).wait_recv()

        def add(t, carry):
            cs = aligned(off + t * TILE, TILE)
            here = aligned(t * TILE, TILE)
            both = s.gb[second, :, cs].astype(F32) + plane_slot(ci, 1)[:, here].astype(F32)
            s.gb[second, :, cs] = both.astype(BF)
            return carry

        lax.fori_loop(0, wid // TILE, add, 0)
        plane_copy(ci, 2).start()

    def plane_finish(ci):
        off, wid = chunks[ci]
        plane_copy(ci, 0).wait_recv()
        plane_copy(ci, 2).wait_recv()

        half = wid // 2
        total = s.gb[p, :, off : off + wid].astype(F32)
        for k in (0, 2):
            total = total + plane_slot(ci, k)[...].astype(F32)
        for j in range(n_out):
            slab = total[j * rows : (j + 1) * rows]

            @pl.when(z == j)
            def _():
                s.sum_ref[:, off : off + wid] = slab

            line_slot(0, ci, j)[...] = pack(slab[:, :half], slab[:, half:], hp)
        if ci == 0:
            pl.semaphore_wait(s.lfree, n_out - 1)
        for k in range(1, n_out):
            line_copy(ci, k).start()

    def gather_copy(ci, i, local):
        m, first, wid = PARTS[ci][i]
        if ci < 8:
            src = s.mb.at[ci]
            dst = s.xb.at[c, w * (halves[m] // 512) + first // 512]
        else:
            src = s.mbk.at[i]
            dst = s.xb.at[c, w, pl.ds(0, rp), pl.ds(0, wid)]
        if local:
            return pltpu.make_async_copy(src, dst, s.grecv)
        return pltpu.make_async_remote_copy(
            src,
            dst,
            s.gsend.at[ci, i],
            s.grecv,
            device_id=(OWNERS[m], 0),
            device_id_type=MESH,
        )

    def line_finish(ci):
        off, wid = chunks[ci]
        half = wid // 2
        for k in range(1, n_out):
            line_copy(ci, k).wait_recv()
        sides = [s.sum_ref[:, off : off + half], s.sum_ref[:, off + half : off + wid]]
        for k in range(n_out - 1):
            for i, extra in enumerate(unpack(line_slot(1, ci, k)[...], rows)):
                sides[i] = sides[i] + extra
        for i in range(2):
            lanes = slice(off + i * half, off + (i + 1) * half)
            s.sum_ref[:, lanes] = sides[i]
            sides[i] = MOMENTUM * s.nm_ref[:, lanes] + sides[i]
            s.nm_ref[:, lanes] = sides[i]
        if ci < 8:
            s.mb[ci] = pack(sides[0], sides[1], hp)
        else:
            for i in range(2):
                s.mbk[i] = pad_rows(sides[i], rp).astype(BF)
        for i, piece in enumerate(PARTS[ci]):
            mine = me == OWNERS[piece[0]] * wa_count

            @pl.when(mine)
            def _():
                gather_copy(ci, i, True).start()

            @pl.when(jnp.logical_not(mine))
            def _():
                gather_copy(ci, i, False).start()

    s.down_free = down_free
    s.buffers_free = buffers_free
    s.plane_start = plane_start
    s.plane_mid = plane_mid
    s.plane_finish = plane_finish

    sources = (
        s.md_ref,
        s.mgu_ref.at[0],
        s.mgu_ref.at[1],
        s.mo_ref,
        s.mq_ref,
        s.mkv_ref.at[0],
        s.mkv_ref.at[1],
    )
    moms = [
        pltpu.make_async_copy(src, s.nm_ref.at[:, pl.ds(offs[m], halves[m])], s.msem.at[m])
        for m, src in enumerate(sources)
    ]
    for cp in moms:
        cp.start()

    def gain_core_copy():
        return pltpu.make_async_remote_copy(
            s.dgs, s.dgc, s.gcsend, s.gcrecv, device_id=(c, 1 - w), device_id_type=MESH
        )

    def gain_plane(k):
        src, dst = ((near[0], near[0]), (across, near[0]), (near[1], near[1]))[k]
        return pltpu.make_async_remote_copy(
            s.dgc.at[src],
            s.dgp.at[k],
            s.gpsend.at[k],
            s.gprecv.at[k],
            device_id=(z * n_in + dst, w),
            device_id_type=MESH,
        )

    def gain_line(k):
        j = lax.rem(z + k, n_out)
        return pltpu.make_async_remote_copy(
            s.dgo.at[j],
            s.dgl.at[k - 1],
            s.glsend.at[k - 1],
            s.glrecv.at[k - 1],
            device_id=(j * n_in + p, w),
            device_id_type=MESH,
        )

    def gains_core():
        for i in range(ctx_count):
            s.dgs[i % n_in, i // n_in, :, 0:rows] = s.dg_ref[:, i * rows : (i + 1) * rows]
        gain_core_copy().start()

    def gains_first():
        gain_core_copy().wait_recv()
        s.dgc[...] = s.dgc[...] + s.dgs[...]
        gain_plane(1).start()
        gain_plane(0).start()

    def gains_mid():
        gain_plane(1).wait_recv()
        s.dgc[near[1]] = s.dgc[near[1]] + s.dgp[1]
        gain_plane(2).start()

    def gains_line():
        gain_plane(0).wait_recv()
        gain_plane(2).wait_recv()
        s.dgo[...] = s.dgc[p] + s.dgp[0] + s.dgp[2]
        for k in range(1, n_out):
            gain_line(k).start()

    def gains_end():
        total = s.dgo[z]
        for k in range(1, n_out):
            gain_line(k).wait_recv()
            total = total + s.dgl[k - 1]
        s.gs_ref[...] = total
        gain_core_copy().wait_send()
        for k in range(3):
            gain_plane(k).wait_send()
        for k in range(1, n_out):
            gain_line(k).wait_send()

    s.gains_core = gains_core

    def rest():
        for cp in moms:
            cp.wait()
        plane_mid(7)
        plane_mid(8)
        plane_finish(6)
        line_finish(0)
        line_finish(1)
        line_finish(2)
        line_finish(3)
        plane_finish(7)
        plane_finish(8)
        gains_first()
        line_finish(4)
        line_finish(5)
        gains_mid()
        line_finish(6)
        line_finish(7)
        gains_line()
        line_finish(8)
        for ci in range(len(chunks)):
            for k in range(3):
                plane_copy(ci, k).wait_send()
            for k in range(1, n_out):
                line_copy(ci, k).wait_send()
        solve()
        gains_end()
        updates_back()

    def owned_by(*which):
        hit = me == OWNERS[which[0]] * wa_count
        for m in which[1:]:
            hit = jnp.logical_or(hit, me == OWNERS[m] * wa_count)
        return hit

    def solve():
        is_owner = owned_by(*range(MATRIX_COUNT))
        is_small = owned_by(5, 6)
        is_wide = owned_by(0, 1, 2)
        pairs = jnp.where(is_small, 0, jnp.where(is_wide, FF // 512, HQ // 512))
        am = s.am
        xfs = (s.dka.at[pl.ds(0, D)], s.dva.at[pl.ds(0, D)])
        ah = s.wd.at[pl.ds(0, D)]
        al = s.wd.at[pl.ds(D, D)]
        ph = s.wd.at[pl.ds(2 * D, D)]
        plo = s.wo.at[pl.ds(0, D)]
        qh = s.wu.at[0, :, pl.ds(0, D)]

        def tile_of(t):
            return s.wg.at[lax.div(t, 4), :, aligned(lax.rem(t, 4) * TILE, TILE)]

        for m in range(MATRIX_COUNT):

            @pl.when(me == OWNERS[m] * wa_count)
            def _(m=m):
                if m < 5:
                    whole = s.xb.at[:, pl.ds(0, halves[m] * wa_count // 512)]
                else:
                    whole = s.xb.at[:, pl.ds(0, 2), pl.ds(0, rp), pl.ds(0, halves[m])]
                pltpu.make_async_copy(whole, whole, s.grecv).wait()

        @pl.when(is_owner)
        def _():
            am[...] = jnp.zeros_like(am)

            def gram(q, carry):
                for i in range(ctx_count):
                    for xf, part in zip(xfs, unpack(s.xb[i, q], rows)):
                        xf[i * rows : (i + 1) * rows, :] = part
                for side in range(2):
                    x = xfs[side][...].astype(BF)
                    tile_of(2 * q + side)[...] = x
                    for a, b in SYM_TILES:
                        am[a:, a:b] += dot_nt(x[a:], x[a:b])
                return carry

            lax.fori_loop(0, pairs, gram, 0)

            @pl.when(is_small)
            def _():
                for i in range(ctx_count):
                    for v in range(2):
                        part = s.xb[i, v, 0:rp, 0 : HD // 2][...].astype(F32)[:rows]
                        lanes = slice(v * (HD // 2), (v + 1) * (HD // 2))
                        xfs[0][i * rows : (i + 1) * rows, lanes] = part
                x = xfs[0][...].astype(BF)
                tile_of(jnp.int32(0))[...] = x
                am[0:HD, 0:HD] = dot_tn(x, x)

            norm2 = jnp.sum(jnp.where(eye_mask(D), am[...], 0.0), keepdims=True)
            inv = 1.0 / (jnp.sqrt(norm2) + 1e-07)
            inv2 = inv * inv
            sym_tiles(am, lambda a, b: am[a:, a:b] * inv2)

            def shifted(a, b, square):
                rest = QUINTIC_B * am[a:, a:b] + QUINTIC_C * square
                top = rest[: b - a] + jnp.where(eye_mask(b - a), QUINTIC_A, 0.0)
                return jnp.concatenate([top, rest[b - a :]], axis=0) if b < D else top

            def poly():
                split_into(am[...], ah, al)
                square = prod3(ah, al, ah, al)
                sym_tiles(am, lambda a, b: shifted(a, b, square(a, b)))

            def advance():
                sym_tiles(am, prod3(ph, plo, ah, al))
                split_into(am[...], ah, al)
                sym_tiles(am, prod3(ah, al, ph, plo))

            def grow():
                sym_tiles(am, lambda a, b: dot32(ph[a:], qh[:, a:b]))
                qh[...] = am[...].astype(BF)

            poly()
            split_into(am[...], ph, plo)
            qh[...] = ph[...]
            advance()

            def sweep(i, carry):
                poly()
                split_into(am[...], ph, plo)
                grow()
                advance()
                return carry

            lax.fori_loop(0, NS_STEPS - 2, sweep, 0)
            ah[...] = am[...].astype(BF)
            sym_tiles(am, lambda a, b: shifted(a, b, dot32(ah[a:], ah[:, a:b])))
            ph[...] = am[...].astype(BF)
            grow()
            rates = [-MUON_RATE * 0.2 * math.sqrt(n) for n in (D, FF, HQ)]
            rate = jnp.where(is_small, rates[0], jnp.where(is_wide, rates[1], rates[2]))
            scale = rate * inv

            def place(i, height, lanes):
                return i // per, slice(i % per * hp, i % per * hp + height), lanes

            def back(q, carry):
                for side in range(2):
                    xfs[side][...] = dot32(qh[...], tile_of(2 * q + side)[...]) * scale
                for i in range(ctx_count):
                    rs = slice(i * rows, (i + 1) * rows)
                    s.ffb[place(i, hp, aligned(q * 256, 256))] = pack(xfs[0][rs], xfs[1][rs], hp)
                return carry

            @pl.when(is_small)
            def _():
                xfs[0][...] = dot32(tile_of(jnp.int32(0))[...], s.wu[0, 0:HD, 0:HD]) * scale
                for i in range(ctx_count):
                    rs = slice(i * rows, (i + 1) * rows)
                    both = pad_rows(xfs[0][rs], rp).astype(BF)
                    s.ffb[place(i, rp, slice(0, HD))] = both

            for v in range(2):
                lax.fori_loop(v * lax.div(pairs, 2), (v + 1) * lax.div(pairs, 2), back, 0)
                for m in range(MATRIX_COUNT):

                    @pl.when(me == OWNERS[m] * wa_count)
                    def _(m=m, v=v):
                        def send(i, carry):
                            there = lax.rem(c + i, ctx_count)
                            update_copy(m, there * wa_count + v, False).start()
                            return carry

                        if v == 0:
                            update_copy(m, c * wa_count, True).start()
                            lax.fori_loop(1, ctx_count, send, 0)
                        else:
                            lax.fori_loop(0, ctx_count, send, 0)

    def update_place(m):
        if m < 5:
            return s.ub.at[:, pl.ds(offs[m] // 2, halves[m] // 2)]
        return s.ubk.at[m - 5]

    def update_copy(m, t, local):
        i, v = lax.div(t, wa_count), lax.rem(t, wa_count)
        start = pl.multiple_of(lax.rem(i, per) * hp, 16)
        if m < 5:
            height, wid = hp, halves[m] // 2
        else:
            height, wid = rp, halves[m]
        lanes = pl.ds(pl.multiple_of(v * wid, 128), wid)
        src = s.ffb.at[lax.div(i, per), pl.ds(start, height), lanes]
        dst = update_place(m)
        if local:
            return pltpu.make_async_copy(src, dst, s.urecv.at[m])
        return pltpu.make_async_remote_copy(
            src, dst, s.usend.at[t], s.urecv.at[m], device_id=(i, v), device_id_type=MESH
        )

    def updates_back():
        for m in range(MATRIX_COUNT):
            piece = update_place(m)
            pltpu.make_async_copy(piece, piece, s.urecv.at[m]).wait()

        for m in range(MATRIX_COUNT):
            owner = OWNERS[m] * wa_count

            @pl.when(me != owner)
            def _(m=m):
                for ci, part in enumerate(PARTS):
                    for i, piece in enumerate(part):
                        if piece[0] == m:
                            gather_copy(ci, i, False).wait_send()

            @pl.when(me == owner)
            def _(m=m, owner=owner):
                def done(t, carry):
                    update_copy(m, lax.rem(owner + t, n_dev), False).wait_send()
                    return carry

                lax.fori_loop(1, n_dev, done, 0)

    return rest


class Refs:
    pass


def dot_nt(a, b):
    return lax.dot_general(a, b, (((1,), (1,)), ((), ())), preferred_element_type=F32)


def dot_tn(a, b):
    return lax.dot_general(a, b, (((0,), (0,)), ((), ())), preferred_element_type=F32)


def aligned(start, size):
    return pl.ds(pl.multiple_of(start, size), size)


def norm_parts(v, gain):
    r = lax.rsqrt(jnp.mean(v * v, axis=-1, keepdims=True) + EPS_NORM)
    return r, v * r, 1.0 + gain


def norm_back(v, gain, e):
    r, zed, g1 = norm_parts(v, gain)
    e1 = e * g1
    dv = r * (e1 - zed * jnp.mean(e1 * zed, axis=-1, keepdims=True))
    return dv, jnp.sum(e * zed, axis=0, keepdims=True)


def layer_scratch(tok):
    v = pltpu.VMEM
    dma = pltpu.SemaphoreType.DMA
    cols = sum(WIDTHS) // 2
    heads = HQ // HD
    tiles = tok // TILE
    win = WINDOW + TILE
    return dict(
        wq=v((2, D, HQ // 2), BF),
        wo=v((HQ, D), BF),
        wg=v((2, D, FF // 2), BF),
        wu=v((2, D, FF // 2), BF),
        wd=v((FF, D), BF),
        tk=v((tok, D), BF),
        ct=v((tok, D), BF),
        xa=v((tok, D), BF),
        xat=v((D, tok), BF),
        fit=v((D, tok), BF),
        ddn=v((tok, D), BF),
        ddnt=v((D, tok), BF),
        cs=v((tok, HD // 2), F32),
        sn=v((tok, HD // 2), F32),
        ka=v((WINDOW + tok, HD), BF),
        va=v((WINDOW + tok, HD), BF),
        idown=v((8, tok), jnp.int32),
        idprev=v((8, tok), jnp.int32),
        qs=v((tiles * heads, TILE, HD), BF),
        ps=v((tiles * heads, TILE, win), BF),
        ts=v((tiles * heads, TILE, win), BF),
        att=v((tok, HQ), BF),
        ao=v((tok, D), F32),
        h1=v((tok, D), F32),
        dn=v((tok, D), F32),
        ffb=v((6, tok, FF // 2), BF),
        datt=v((tok, HQ), BF),
        dka=v((WINDOW + tok, HD), F32),
        dva=v((WINDOW + tok, HD), F32),
        dks=v((2, tok, HD), BF),
        dkr=v((2, tok, HD), BF),
        dkv=v((2, tok, HD), BF),
        sb=v((6, IN_COUNT, D // IN_COUNT, TILE), BF),
        gb=v((IN_COUNT, D // IN_COUNT, cols), BF),
        wsend=dma((5,)),
        wrecv=dma((5,)),
        wown=dma((5,)),
        ksend=dma((3,)),
        krecv=dma((3,)),
        dsend=dma((2, 2)),
        drecv=dma((2, 2)),
        csend=dma((MATRIX_COUNT, 4)),
        crecv=dma((MATRIX_COUNT, 4)),
        osend=dma((2,)),
        orecv=dma((2,)),
        oown=dma((2,)),
        tsem=dma((4,)),
    )


def layer_phases(s, ctx_count, wa_count):
    c = lax.axis_index("ctx")
    w = lax.axis_index("wa")
    other = 1 - w
    flat = c * wa_count + w
    n_dev = ctx_count * wa_count
    tok = s.xa.shape[0]
    rows = D // ctx_count
    n_out = ctx_count // IN_COUNT
    heads = HQ // HD
    tiles = tok // TILE
    win = WINDOW + TILE
    half_ff = FF // 2
    halves, offs, cols = layout(wa_count)
    step = 128
    partner = (c, other)
    follow = jnp.minimum(flat + 1, n_dev - 1)
    ahead = jnp.maximum(flat - 1, 0)
    next_id = (lax.div(follow, wa_count), lax.rem(follow, wa_count))
    prev_id = (lax.div(ahead, wa_count), lax.rem(ahead, wa_count))
    order = [zz * IN_COUNT + pp for pp in range(IN_COUNT) for zz in range(n_out)]

    def remote(src, dst, send, recv, where):
        return pltpu.make_async_remote_copy(
            src, dst, send, recv, device_id=where, device_id_type=MESH
        )

    def permuted(v):
        t = v.astype(BF).astype(F32).T
        return jnp.concatenate([t[i * rows : (i + 1) * rows] for i in order], axis=0).astype(BF)

    def per_rows(body):
        def run(i, carry):
            body(aligned(i * step, step))
            return carry

        lax.fori_loop(0, tok // step, run, 0)

    out_rows = aligned(w * tok, tok)
    tok_in = pltpu.make_async_copy(s.tok_ref.at[out_rows], s.tk, s.tsem.at[0])
    cot_in = pltpu.make_async_copy(s.cot_ref.at[out_rows], s.ct, s.tsem.at[1])
    tables = [
        pltpu.make_async_copy(s.cosi_ref, s.cs, s.tsem.at[2]),
        pltpu.make_async_copy(s.sini_ref, s.sn, s.tsem.at[3]),
    ]
    tok_in.start()
    for cp in tables:
        cp.start()
    cot_in.start()

    wk_refs = (
        (s.wq_ref, s.wq.at[w]),
        (s.wo_ref, s.wo.at[aligned(w * (HQ // 2), HQ // 2)]),
        (s.wgu_ref.at[0], s.wg.at[w]),
        (s.wgu_ref.at[1], s.wu.at[w]),
        (s.wd_ref, s.wd.at[aligned(w * half_ff, half_ff)]),
    )
    w_far = [remote(a, b, s.wsend.at[i], s.wrecv.at[i], partner) for i, (a, b) in enumerate(wk_refs)]
    w_own = [pltpu.make_async_copy(a, b, s.wown.at[i]) for i, (a, b) in enumerate(wk_refs)]

    def weights_start(first, last):
        for i in range(first, last):
            w_far[i].start()
            w_own[i].start()

    weights_start(0, 1)

    def weights_ready(i):
        w_own[i].wait()
        w_far[i].wait_recv()

    tok_in.wait()

    def first(rs):
        x = s.tk[rs].astype(F32)
        _, zed, g1 = norm_parts(x, s.gain_ref[0:1])
        s.xa[rs] = (zed * g1).astype(BF)

    per_rows(first)

    cb, sb_ = s.cosb_ref[pl.ds(flat, 1), :], s.sinb_ref[pl.ds(flat, 1), :]
    for cp in tables:
        cp.wait()
    cosi, sini = s.cs[...], s.sn[...]
    s.cs[...] = cb * cosi - sb_ * sini
    s.sn[...] = sb_ * cosi + cb * sini
    hh = HD // 2

    def turn(v, cosine, sine):
        a, b = v[:, :hh], v[:, hh:]
        return jnp.concatenate([a * cosine - b * sine, b * cosine + a * sine], axis=1)

    def turn_back(v, cosine, sine):
        a, b = v[:, :hh], v[:, hh:]
        return jnp.concatenate([a * cosine + b * sine, b * cosine - a * sine], axis=1)

    s.ka[WINDOW:, :] = turn(dot32(s.xa[...], s.wkv_ref[0]), s.cs[...], s.sn[...]).astype(BF)
    s.idown[...] = jnp.broadcast_to(s.ids_ref[:, aligned(w * tok, tok)], (8, tok))
    halo = [
        remote(src, dst, s.ksend.at[i], s.krecv.at[i], next_id)
        for i, (src, dst) in enumerate(
            (
                (s.ka.at[pl.ds(tok, WINDOW)], s.ka.at[pl.ds(0, WINDOW)]),
                (s.va.at[pl.ds(tok, WINDOW)], s.va.at[pl.ds(0, WINDOW)]),
                (s.idown, s.idprev),
            )
        )
    ]

    @pl.when(flat < n_dev - 1)
    def _():
        halo[2].start()
        halo[0].start()

    s.va[WINDOW:, :] = dot32(s.xa[...], s.wkv_ref[1]).astype(BF)

    @pl.when(flat < n_dev - 1)
    def _():
        halo[1].start()

    weights_start(1, 5)

    def flip(rs):
        s.xat[:, rs] = permuted(s.xa[rs])

    weights_ready(0)

    def project(h, carry):
        v, u = lax.div(h, heads // 2), lax.rem(h, heads // 2)
        q = dot32(s.xa[...], s.wq[v, :, aligned(u * HD, HD)])
        q = (turn(q, s.cs[...], s.sn[...]) * HD ** (-0.5)).astype(BF)
        for a in range(tiles):
            s.qs[a * heads + h] = q[a * TILE : (a + 1) * TILE]
        return carry

    lax.fori_loop(0, heads, project, 0)
    per_rows(flip)

    @pl.when(flat > 0)
    def _():
        halo[2].wait_recv()

    @pl.when(flat == 0)
    def _():
        s.idprev[...] = jnp.full((8, tok), -1, jnp.int32)

    row_ids = jnp.concatenate([s.idprev[0:1, :], s.idown[0:1, :]], axis=1)
    own_col = jnp.broadcast_to(s.idown[0:1, :], (128, tok)).T[:, 0:1]
    gap = lax.broadcasted_iota(jnp.int32, (TILE, win), 1) - lax.broadcasted_iota(
        jnp.int32, (TILE, win), 0
    )
    for a in range(tiles):
        same = own_col[a * TILE : (a + 1) * TILE] == row_ids[:, a * TILE : a * TILE + win]
        ok = jnp.logical_and(same, jnp.logical_and(gap > 0, gap <= WINDOW))
        s.ffb[a, 0:TILE, 0:win] = jnp.where(ok, 1.0, 0.0).astype(BF)

    @pl.when(flat > 0)
    def _():
        halo[0].wait_recv()
        halo[1].wait_recv()

    @pl.when(flat == 0)
    def _():
        s.ka[0:WINDOW, :] = jnp.zeros((WINDOW, HD), BF)
        s.va[0:WINDOW, :] = jnp.zeros((WINDOW, HD), BF)

    def attend(i, carry):
        a, h = lax.div(i, heads), lax.rem(i, heads)
        ks = pl.ds(pl.multiple_of(a * TILE, TILE), win)
        t = jnp.tanh(dot_nt(s.qs[i], s.ka[ks, :]) * (1.0 / SOFT_CAP))
        e = jnp.exp(SOFT_CAP * t) * s.ffb[a, 0:TILE, 0:win].astype(F32)
        pr = e * (1.0 / jnp.sum(e, axis=-1, keepdims=True))
        pr = pr.astype(BF)
        s.ps[i] = pr
        s.ts[i] = (1.0 - t * t).astype(BF)
        o = dot32(pr, s.va[ks, :])
        s.att[aligned(a * TILE, TILE), aligned(h * HD, HD)] = o.astype(BF)
        return carry

    lax.fori_loop(0, tiles * heads, attend, 0)

    weights_ready(1)
    s.ao[...] = dot32(s.att[...], s.wo[...])

    def second(rs):
        _, zed, g1 = norm_parts(s.ao[rs], s.gain_ref[1:2])
        h = s.tk[rs].astype(F32) + zed * g1
        s.h1[rs] = h
        _, zed, g1 = norm_parts(h, s.gain_ref[2:3])
        n = zed * g1
        s.xa[rs] = n.astype(BF)
        s.fit[:, rs] = permuted(n)

    per_rows(second)

    weights_ready(2)
    weights_ready(3)
    root = 0.7978845608028654

    def forward(i, carry):
        v, u = lax.div(i, 4), lax.rem(i, 4)
        us = aligned(u * TILE, TILE)
        gt = dot32(s.xa[...], s.wg[v, :, us])
        up = dot32(s.xa[...], s.wu[v, :, us])
        g2 = gt * gt
        th = jnp.tanh(root * gt * (1.0 + 0.044715 * g2))
        lift = 0.5 * (1.0 + th)
        act = gt * lift
        slope = lift + 0.5 * gt * (1.0 - th * th) * (root * (1.0 + 3.0 * 0.044715 * g2))
        s.ffb[v, :, us] = (act * up).astype(BF)
        s.ffb[2 + v, :, us] = (up * slope).astype(BF)
        s.ffb[4 + v, :, us] = act.astype(BF)
        return carry

    lax.fori_loop(0, 8, forward, 0)
    weights_ready(4)
    s.dn[...] = dot32(s.ffb[0], s.wd[:half_ff]) + dot32(s.ffb[1], s.wd[half_ff:])
    s.dg_ref[...] = jnp.zeros_like(s.dg_ref)

    def third(rs):
        dn = s.dn[rs]
        _, zed, g1 = norm_parts(dn, s.gain_ref[3:4])
        s.xa[rs] = (s.h1[rs] + zed * g1).astype(BF)
        dv, dg = norm_back(dn, s.gain_ref[3:4], s.ct[rs].astype(F32))
        s.dg_ref[3:4] += dg
        s.ddn[rs] = dv.astype(BF)
        s.ddnt[:, rs] = permuted(dv)

    cot_in.wait()
    per_rows(third)
    y_far = remote(s.xa, s.y_ref.at[out_rows], s.osend.at[0], s.orecv.at[0], partner)
    y_own = pltpu.make_async_copy(s.xa, s.y_ref.at[out_rows], s.oown.at[0])
    y_far.start()
    y_own.start()

    def part(m, u, width):
        return pl.ds(pl.multiple_of(offs[m] + u * width, 128), width)

    def slot(m, u):
        return lax.rem(u, 2) * 3 + m if m < 3 else (0, 2, 4, 5)[m - 3] + u

    def exchange(m, u, width):
        return remote(
            s.sb.at[slot(m, u), :, :, pl.ds(0, width)],
            s.gb.at[:, :, part(m, u, width)],
            s.csend.at[m, u],
            s.crecv.at[m, u],
            partner,
        )

    def give(m, u, width, value):
        if m < 3:

            @pl.when(u >= 2)
            def _():
                exchange(m, u - 2, width).wait_send()

        s.sb[slot(m, u), :, :, 0:width] = value.astype(BF).reshape(
            IN_COUNT, D // IN_COUNT, width
        )
        exchange(m, u, width).start()

    def keep(m, u, width, value):
        ps = part(m, u, width)
        exchange(m, u, width).wait_recv()
        total = value.reshape(IN_COUNT, D // IN_COUNT, width) + s.gb[:, :, ps].astype(F32)
        s.gb[:, :, ps] = total.astype(BF)

    def down_back(v, put):
        def run(u, carry):
            put(0, u, TILE, dot32(s.ddnt[...], s.ffb[v, :, aligned(u * TILE, TILE)]))
            return carry

        lax.fori_loop(0, 4, run, 0)

    def gate_back(v, put):
        def run(u, carry):
            us = aligned(u * TILE, TILE)
            dh = dot_nt(s.ddn[...], s.wd[aligned((v * 4 + u) * TILE, TILE), :])
            dgt = (dh * s.ffb[2 + v, :, us].astype(F32)).astype(BF)
            dup = (dh * s.ffb[4 + v, :, us].astype(F32)).astype(BF)
            s.ffb[2 + v, :, us] = dgt
            s.ffb[4 + v, :, us] = dup
            put(1, u, TILE, dot32(s.fit[...], dgt))
            return carry

        lax.fori_loop(0, 4, run, 0)

    def up_back(v, put):
        def run(u, carry):
            put(2, u, TILE, dot32(s.fit[...], s.ffb[4 + v, :, aligned(u * TILE, TILE)]))
            return carry

        lax.fori_loop(0, 4, run, 0)

    down_back(other, give)
    down_back(w, keep)
    s.plane_start(0)
    s.plane_start(1)
    gate_back(other, give)
    gate_back(w, keep)
    s.down_free()
    up_back(other, give)
    s.plane_start(2)
    s.plane_start(3)
    s.plane_mid(0)
    s.plane_mid(1)
    up_back(w, keep)
    s.dn[...] = dot_nt(s.ffb[2], s.wg[0]) + dot_nt(s.ffb[3], s.wg[1])
    s.dn[...] += dot_nt(s.ffb[4], s.wu[0]) + dot_nt(s.ffb[5], s.wu[1])

    s.buffers_free()

    def fourth(rs):
        dv, dg = norm_back(s.h1[rs], s.gain_ref[2:3], s.dn[rs])
        s.dg_ref[2:3] += dg
        dh = s.ct[rs].astype(F32) + dv
        s.h1[rs] = dh
        dv, dg = norm_back(s.ao[rs], s.gain_ref[1:2], dh)
        s.dg_ref[1:2] += dg
        s.ddn[rs] = dv.astype(BF)
        s.ddnt[:, rs] = permuted(dv)

    per_rows(fourth)
    s.plane_start(4)
    s.plane_start(5)
    for m in range(3):
        for u in (2, 3):
            exchange(m, u, TILE).wait_send()

    def out_back(v, put):
        def run(u, carry):
            hs = aligned((v * 2 + u) * HD, HD)
            s.datt[:, hs] = dot_nt(s.ddn[...], s.wo[hs, :]).astype(BF)
            put(3, u, HD, dot32(s.ddnt[...], s.att[:, hs]))
            return carry

        lax.fori_loop(0, 2, run, 0)

    out_back(other, give)
    out_back(w, keep)
    s.plane_finish(0)
    s.plane_finish(1)

    s.dka[...] = jnp.zeros_like(s.dka)
    s.dva[...] = jnp.zeros_like(s.dva)

    def attend_back(i, carry):
        a, h = lax.div(i, heads), lax.rem(i, heads)
        ks = pl.ds(pl.multiple_of(a * TILE, TILE), win)
        qr = aligned(a * TILE, TILE)
        hs = aligned(h * HD, HD)
        do = s.datt[qr, hs]
        pr = s.ps[i]
        s.dva[ks, :] += dot_tn(pr, do)
        dp = dot_nt(do, s.va[ks, :])
        pr = pr.astype(F32)
        inner = jnp.sum(pr * dp, axis=-1, keepdims=True)
        ds = (pr * (dp - inner) * s.ts[i].astype(F32)).astype(BF)
        s.dka[ks, :] += dot_tn(ds, s.qs[i])
        dq = dot32(ds, s.ka[ks, :])
        s.datt[qr, hs] = (turn_back(dq, s.cs[qr], s.sn[qr]) * HD ** (-0.5)).astype(BF)
        return carry

    def d_part(i, half):
        rs = pl.ds(half * TILE, TILE)
        return remote(
            s.dks.at[i, rs], s.dkr.at[i, rs], s.dsend.at[i, half], s.drecv.at[i, half], prev_id
        )

    d_halo = [d_part(i, half) for half in range(2) for i in range(2)]

    def d_send(half):
        rs = slice(half * TILE, (half + 1) * TILE)
        s.dks[0, rs] = s.dka[rs].astype(BF)
        s.dks[1, rs] = s.dva[rs].astype(BF)

        @pl.when(flat > 0)
        def _():
            for cp in d_halo[half * 2 : half * 2 + 2]:
                cp.start()

    lax.fori_loop(0, heads, attend_back, 0)
    d_send(0)
    s.plane_mid(2)
    s.plane_mid(3)
    lax.fori_loop(heads, tiles * heads, attend_back, 0)
    d_send(1)
    s.plane_start(6)

    def query_back(v, put):
        def run(u, carry):
            hs = aligned((v * 2 + u) * HD, HD)
            put(4, u, HD, dot32(s.xat[...], s.datt[:, hs]))
            return carry

        lax.fori_loop(0, 2, run, 0)

    query_back(other, give)
    s.plane_mid(4)
    s.plane_mid(5)
    s.dn[...] = dot_nt(s.datt[:, : HQ // 2], s.wq[0]) + dot_nt(s.datt[:, HQ // 2 :], s.wq[1])
    query_back(w, keep)
    s.plane_start(7)
    s.plane_finish(2)
    s.plane_finish(3)

    @pl.when(flat < n_dev - 1)
    def _():
        for cp in d_halo:
            cp.wait_recv()

    @pl.when(flat == n_dev - 1)
    def _():
        s.dkr[...] = jnp.zeros_like(s.dkr)

    dk = s.dka[tok:, :] + s.dkr[0].astype(F32)
    s.dkv[0] = turn_back(dk, s.cs[...], s.sn[...]).astype(BF)
    s.dkv[1] = (s.dva[tok:, :] + s.dkr[1].astype(F32)).astype(BF)
    kvw = HD // 2
    for i in range(2):
        give(5 + i, 0, kvw, dot32(s.xat[...], s.dkv[i, :, aligned(other * kvw, kvw)]))
    for i in range(2):
        keep(5 + i, 0, kvw, dot32(s.xat[...], s.dkv[i, :, aligned(w * kvw, kvw)]))
    s.plane_start(8)
    s.plane_mid(6)
    s.plane_finish(4)
    s.plane_finish(5)
    s.dn[...] += dot_nt(s.dkv[0], s.wkv_ref[0]) + dot_nt(s.dkv[1], s.wkv_ref[1])

    def fifth(rs):
        dv, dg = norm_back(s.tk[rs].astype(F32), s.gain_ref[0:1], s.dn[rs])
        s.dg_ref[0:1] += dg
        s.h1[rs] = s.h1[rs] + dv

    per_rows(fifth)
    s.gains_core()
    x_far = remote(s.h1, s.x_ref.at[out_rows], s.osend.at[1], s.orecv.at[1], partner)
    x_own = pltpu.make_async_copy(s.h1, s.x_ref.at[out_rows], s.oown.at[1])
    x_far.start()
    x_own.start()

    def finish():
        for cp in w_far:
            cp.wait_send()

        @pl.when(flat < n_dev - 1)
        def _():
            for cp in halo:
                cp.wait_send()

        @pl.when(flat > 0)
        def _():
            for cp in d_halo:
                cp.wait_send()

        for m, count, width in ((3, 2, HD), (4, 2, HD), (5, 1, kvw), (6, 1, kvw)):
            for u in range(count):
                exchange(m, u, width).wait_send()
        y_own.wait()
        x_own.wait()
        y_far.wait()
        x_far.wait()

    return finish


LAYER_INPUTS = (
    "tok_ref",
    "cot_ref",
    "cosi_ref",
    "sini_ref",
    "mq_ref",
    "mkv_ref",
    "mgu_ref",
    "mo_ref",
    "md_ref",
    "ids_ref",
    "gain_ref",
    "wkv_ref",
    "cosb_ref",
    "sinb_ref",
    "wq_ref",
    "wo_ref",
    "wgu_ref",
    "wd_ref",
)
LAYER_OUTPUTS = ("y_ref", "x_ref", "sum_ref", "nm_ref", "ub", "ubk", "gs_ref")
VMEM_BYTES = 63 << 20


def whole_kernel(ctx_count, wa_count, names, *refs):
    s = Refs()
    for name, ref in zip(names, refs):
        setattr(s, name, ref)
    c = lax.axis_index("ctx")
    w = lax.axis_index("wa")
    flat = c * wa_count + w
    n_dev = ctx_count * wa_count
    barrier = pltpu.get_barrier_semaphore()

    def greet(i, carry):
        other = lax.rem(flat + i, n_dev)
        pl.semaphore_signal(
            barrier,
            inc=1,
            device_id=(lax.div(other, wa_count), lax.rem(other, wa_count)),
            device_id_type=MESH,
        )
        return carry

    lax.fori_loop(1, n_dev, greet, 0)
    pl.semaphore_wait(barrier, n_dev - 1)
    tail = tail_phases(s, ctx_count, wa_count)
    finish = layer_phases(s, ctx_count, wa_count)
    tail()
    finish()


def rotation_tables(tok, n_dev):
    freq = ROPE_BASE ** (-2.0 * np.arange(HD // 2) / HD)
    inner = np.arange(tok)[:, None] * freq[None, :]
    base = (np.arange(n_dev) * tok)[:, None] * freq[None, :]
    return [jnp.asarray(f(a), F32) for a in (inner, base) for f in (np.cos, np.sin)]


def run_whole(
    tokens, cotangent, seq_ids, gains, wkv, moms, wq, wo, wgu, wd, ctx_count, wa_count
):
    block = tokens.shape[0]
    tok = block // wa_count
    n_dev = ctx_count * wa_count
    mom_query, mom_keyval, mom_out, mom_gateup, mom_down = moms
    cosi, sini, cosb, sinb = rotation_tables(tok, n_dev)
    scratch = layer_scratch(tok) | tail_scratch(ctx_count, wa_count)
    names = LAYER_INPUTS + LAYER_OUTPUTS + tuple(scratch)
    any_space = pl.BlockSpec(memory_space=pl.ANY)
    vmem = pl.BlockSpec(memory_space=pltpu.VMEM)
    _, offs, cols = layout(wa_count)
    shard = jax.ShapeDtypeStruct((D // ctx_count, cols), F32)
    return pl.pallas_call(
        partial(whole_kernel, ctx_count, wa_count, names),
        out_shape=(
            jax.ShapeDtypeStruct((block, D), BF),
            jax.ShapeDtypeStruct((block, D), F32),
            shard,
            shard,
            jax.ShapeDtypeStruct((packed_rows(D // ctx_count), offs[5] // 2), BF),
            jax.ShapeDtypeStruct((2, -(-(D // ctx_count) // 16) * 16, HD // 2), BF),
            jax.ShapeDtypeStruct((8, 128), F32),
        ),
        in_specs=[any_space] * 9 + [vmem] * 5 + [any_space] * 4,
        out_specs=(any_space, any_space) + (vmem,) * 5,
        scratch_shapes=list(scratch.values()),
        compiler_params=pltpu.CompilerParams(
            collective_id=0, has_side_effects=True, vmem_limit_bytes=VMEM_BYTES
        ),
        name="whole",
    )(
        tokens,
        cotangent,
        cosi,
        sini,
        mom_query,
        mom_keyval,
        mom_gateup,
        mom_out.T,
        mom_down.T,
        seq_ids[None],
        gains,
        wkv,
        cosb,
        sinb,
        wq,
        wo,
        wgu,
        wd,
    )


def format_kernel(
    ctx_count,
    wa_count,
    sum_ref,
    nm_ref,
    ub_ref,
    ubk_ref,
    gs_ref,
    first_ref,
    second_ref,
    y_ref,
    x_ref,
    *rest,
):
    outs, (sumv, nmv, ubv, ubkv, gsv, fv, sv, yv, xv, sem) = rest[:21], rest[21:]
    rows = D // ctx_count
    halves, offs, _ = layout(wa_count)

    def copies(pairs, first):
        return [pltpu.make_async_copy(a, b, sem.at[first + i]) for i, (a, b) in enumerate(pairs)]

    def places(group):
        query, keyval, out, gateup, down = group
        return (down, gateup.at[0], gateup.at[1], out, query, keyval.at[0], keyval.at[1])

    fetched = copies(
        (
            (x_ref, xv),
            (y_ref, yv),
            (sum_ref, sumv),
            (nm_ref, nmv),
            (ub_ref, ubv),
            (ubk_ref, ubkv),
            (gs_ref, gsv),
            (first_ref, fv),
            (second_ref, sv),
        ),
        0,
    )
    for cp in fetched:
        cp.start()
    stored = copies(((xv, outs[1]), (yv, outs[0])), 9)
    for src, group, first in ((sumv, outs[2:7], 11), (nmv, outs[8:13], 18)):
        stored += copies(
            [
                (src.at[:, pl.ds(offs[m], halves[m])], dst)
                for m, dst in enumerate(places(group))
            ],
            first,
        )
    starts = ((0, 1), (1, 2), (2, 9), (9, 16))
    for cp, (a, b) in zip(fetched[:4], starts):
        cp.wait()
        for out in stored[a:b]:
            out.start()
    for cp in fetched[4:]:
        cp.wait()
    for m, dst in enumerate(places(outs[13:18])):
        if m < 5:
            for q in range(halves[m] // 512):
                at = offs[m] // 2 + q * 256
                for side, part in enumerate(unpack(ubv[:, at : at + 256], rows)):
                    dst[:, q * 512 + side * 256 : q * 512 + (side + 1) * 256] = part
        else:
            dst[...] = ubkv[m - 5].astype(F32)[:rows]
    g = gsv[0:4, 0:rows]
    first = ADAM_ONE * fv[...] + (1.0 - ADAM_ONE) * g
    second = ADAM_TWO * sv[...] + (1.0 - ADAM_TWO) * g * g
    outs[7][...] = g
    outs[18][...] = first
    outs[19][...] = second
    outs[20][...] = -GAIN_RATE * first / (jnp.sqrt(second) + ADAM_EPS)
    for cp in stored:
        cp.wait()


def run_format(sums, fresh, updates, small, gsum, gain_first, gain_second, y, x, ctx_count, wa_count):
    rows = D // ctx_count
    halves = layout(wa_count)[0]
    down, gate, _, out, query, key, _ = halves
    f = lambda *shape: jax.ShapeDtypeStruct(shape, F32)
    weights = [f(rows, query), f(2, rows, key), f(rows, out), f(2, rows, gate), f(rows, down)]
    any_space = pl.BlockSpec(memory_space=pl.ANY)
    vmem = pl.BlockSpec(memory_space=pltpu.VMEM)
    gain = f(4, rows)
    shapes = [jax.ShapeDtypeStruct(y.shape, y.dtype), jax.ShapeDtypeStruct(x.shape, x.dtype)]
    shapes += weights + [gain] + weights + weights + [gain] * 3
    outs = pl.pallas_call(
        partial(format_kernel, ctx_count, wa_count),
        out_shape=shapes,
        in_specs=[any_space] * 9,
        out_specs=[any_space] * 7 + [vmem] + [any_space] * 5 + [vmem] * 8,
        scratch_shapes=[
            *[
                pltpu.VMEM(a.shape, a.dtype)
                for a in (sums, fresh, updates, small, gsum, gain_first, gain_second, y, x)
            ],
            pltpu.SemaphoreType.DMA((25,)),
        ],
        compiler_params=pltpu.CompilerParams(vmem_limit_bytes=VMEM_BYTES),
        name="format",
    )(sums, fresh, updates, small, gsum, gain_first, gain_second, y, x)
    return tuple(o.T if i in (4, 6, 10, 12, 15, 17) else o for i, o in enumerate(outs))


def per_device(
    tokens,
    cotangent,
    seq_ids,
    w_query,
    w_keyval,
    w_out,
    w_gateup,
    w_down,
    norm_gains,
    mom_query,
    mom_keyval,
    mom_out,
    mom_gateup,
    mom_down,
    gain_first,
    gain_second,
):
    ctx_count = lax.axis_size("ctx")
    wa_count = lax.axis_size("wa")
    y, x, sums, fresh, updates, small, gsum = run_whole(
        tokens,
        cotangent,
        seq_ids,
        norm_gains,
        w_keyval,
        (mom_query, mom_keyval, mom_out, mom_gateup, mom_down),
        w_query,
        w_out,
        w_gateup,
        w_down,
        ctx_count,
        wa_count,
    )
    return tuple(
        run_format(
            sums, fresh, updates, small, gsum, gain_first, gain_second, y, x, ctx_count, wa_count
        )
    )


def solution(mesh):
    in_specs = (
        P("ctx", None),
        P("ctx", None),
        P("ctx"),
        P(None, "wa"),
        P(),
        P("wa", None),
        P(None, None, "wa"),
        P("wa", None),
        P(),
        P("ctx", "wa"),
        P(None, "ctx", "wa"),
        P("wa", "ctx"),
        P(None, "ctx", "wa"),
        P("wa", "ctx"),
        P(None, "ctx"),
        P(None, "ctx"),
    )
    out_specs = (
        P("ctx", None),
        P("ctx", None),
        P("ctx", "wa"),
        P(None, "ctx", "wa"),
        P("wa", "ctx"),
        P(None, "ctx", "wa"),
        P("wa", "ctx"),
        P(None, "ctx"),
        P("ctx", "wa"),
        P(None, "ctx", "wa"),
        P("wa", "ctx"),
        P(None, "ctx", "wa"),
        P("wa", "ctx"),
        P("ctx", "wa"),
        P(None, "ctx", "wa"),
        P("wa", "ctx"),
        P(None, "ctx", "wa"),
        P("wa", "ctx"),
        P(None, "ctx"),
        P(None, "ctx"),
        P(None, "ctx"),
    )
    return jax.shard_map(
        per_device, mesh=mesh, in_specs=in_specs, out_specs=out_specs, check_vma=False
    )
```
